32 devices in a mesh: dp: 8 (over z, core), fsdp: 4 (over y, x).
Axes of the slice: x: 2, y: 2, z: 4, core: 2. Of those that a mesh axis runs over, the one named last changes fastest.
Arguments:
- tokens: bfloat16 [32768, 768], P(('dp', 'fsdp')), may hold values from -6 to 6
- bucket: int32 [32], P(('dp', 'fsdp')), may hold values from 0 to 1, as said below
- lengths: int32 [32, 8], P(('dp', 'fsdp')), may hold values from 0 to 512, as said below
- cotangent: bfloat16 [32768, 768], P(('dp', 'fsdp')), may hold values from -6 to 6
- query_weight: bfloat16 [768, 768], P('dp', 'fsdp'), may hold values from -0.21875 to 0.21875
- query_bias: bfloat16 [768], P('fsdp'), may hold values from -3 to 3
- key_weight: bfloat16 [768, 768], P('dp', 'fsdp'), may hold values from -0.21875 to 0.21875
- value_weight: bfloat16 [768, 768], P('dp', 'fsdp'), may hold values from -0.21875 to 0.21875
- value_bias: bfloat16 [768], P('fsdp'), may hold values from -0.625 to 0.625
- out_weight: bfloat16 [768, 768], P('dp', 'fsdp'), may hold values from -2.5 to 2.5
- out_bias: bfloat16 [768], P('fsdp'), may hold values from -3 to 3
- norm1_gain: bfloat16 [768], P('fsdp'), may hold values from 0.5 to 1.5
- norm1_bias: bfloat16 [768], P('fsdp'), may hold values from -1.75 to 1.75
- up_weight: bfloat16 [768, 3072], P('dp', 'fsdp'), may hold values from -0.21875 to 0.21875
- up_bias: bfloat16 [3072], P('fsdp'), may hold values from -3 to 3
- down_weight: bfloat16 [3072, 768], P('dp', 'fsdp'), may hold values from -0.109375 to 0.109375
- down_bias: bfloat16 [768], P('fsdp'), may hold values from -3 to 3
- norm2_gain: bfloat16 [768], P('fsdp'), may hold values from 0.5 to 1.5
- norm2_bias: bfloat16 [768], P('fsdp'), may hold values from -1.75 to 1.75
Outputs:
- out_tokens: bfloat16 [32768, 768], P(('dp', 'fsdp'))
- pooled: float32 [256, 768], P(('dp', 'fsdp'))
- input_grad: float32 [32768, 768], P(('dp', 'fsdp'))
- grad_query_weight: float32 [768, 768], P('dp', 'fsdp')
- grad_query_bias: float32 [768], P('fsdp')
- grad_key_weight: float32 [768, 768], P('dp', 'fsdp')
- grad_value_weight: float32 [768, 768], P('dp', 'fsdp')
- grad_value_bias: float32 [768], P('fsdp')
- grad_out_weight: float32 [768, 768], P('dp', 'fsdp')
- grad_out_bias: float32 [768], P('fsdp')
- grad_norm1_gain: float32 [768], P('fsdp')
- grad_norm1_bias: float32 [768], P('fsdp')
- grad_up_weight: float32 [768, 3072], P('dp', 'fsdp')
- grad_up_bias: float32 [3072], P('fsdp')
- grad_down_weight: float32 [3072, 768], P('dp', 'fsdp')
- grad_down_bias: float32 [768], P('fsdp')
- grad_norm2_gain: float32 [768], P('fsdp')
- grad_norm2_bias: float32 [768], P('fsdp')
The draws below stay inside these ranges and needn't reach their ends.
Inputs may be any that keep to these rules, and one draw needn't show every extreme that they name: `bucket`: both values occur. A device with 1 holds 2 passages of 512 rows, one with 0 holds 8 queries of 128 rows. `lengths`: entry j is the live length of the device's j-th sequence, 1 to 512 for passages and 1 to 128 for queries; entries j >= 2 of a passage device are 0. Some passage has 512 live tokens and some query 128.
All inputs are finite; a program needn't handle non-finite values.
Results may differ from the reference program's by a relative error of at most 0.02.
Values may be sent and summed in bfloat16 or wider, within the bound.
No kernel may reach another device: no remote copies, remote signals or barrier semaphores. Data moves between devices by JAX's collectives and lax.ppermute only.
A program may use at most 192 MiB of HBM per device.

```python
import jax
import jax.numpy as jnp
from jax import lax

D = 768
H = 12
HD = 64
FF = 3072
PLEN = 512
QLEN = 128
PASS_DEV = 2
TOK_DEV = 1024
Q_DEV = 8
SHARDS = 32
TOKENS = 32768
SLOTS = 256


def device_kinds(key):
    flag_key, passage_key, query_key = jax.random.split(key, 3)
    passage_flags = (jax.random.randint(flag_key, (SHARDS,), 0, 4) < 3).astype(jnp.int32)
    passage_device = jax.random.randint(passage_key, (), 0, SHARDS)
    query_device = (passage_device + jax.random.randint(query_key, (), 1, SHARDS)) % SHARDS
    device_order = jnp.arange(SHARDS)
    passage_flags = jnp.where(device_order == passage_device, 1, jnp.where(device_order == query_device, 0, passage_flags))
    return (passage_flags.astype(jnp.int32), passage_device, query_device)


def draw_bucket(key, part):
    passage_flags = device_kinds(key)[0]
    return passage_flags


def draw_lengths(key, part):
    passage_flags, passage_device, query_device = device_kinds(key)
    key = jax.random.fold_in(key, 5)
    sub_keys = jax.random.split(key, 4)
    passage_sizes = jax.random.randint(sub_keys[0], (SHARDS, Q_DEV), PLEN // 8, PLEN + 1)
    query_sizes = jax.random.randint(sub_keys[1], (SHARDS, Q_DEV), max(QLEN // 8, 1), QLEN + 1)
    slot_index = jnp.arange(Q_DEV)[None, :]
    passage_sizes = jnp.where(slot_index < PASS_DEV, passage_sizes, 0)
    length_table = jnp.where(passage_flags[:, None] == 1, passage_sizes, query_sizes)
    longest_slot = jax.random.randint(sub_keys[2], (), 0, PASS_DEV)
    full_slot = jax.random.randint(sub_keys[3], (), 0, Q_DEV)
    length_table = length_table.at[passage_device, longest_slot].set(PLEN)
    length_table = length_table.at[query_device, full_slot].set(QLEN)
    return length_table.astype(jnp.int32)


def levels(stream_key, shape, shards, least, high):
    def one(dim, parts):
        draws = jax.random.uniform(jax.random.fold_in(jax.random.fold_in(stream_key, 6), dim), (parts,), jnp.float32, least / len(shards), high / len(shards))
        return jnp.repeat(jnp.exp(draws), shape[dim] // parts).reshape((-1,) + (1,) * (len(shape) - dim - 1))

    loudness = one(*shards[0])
    for cut in shards[1:]:
        loudness = loudness * one(*cut)
    return loudness


def gaussian(stream_key, shape, width, limit, cuts=(), held_as=jnp.bfloat16):
    values = width * jax.random.normal(stream_key, shape, jnp.float32)
    if cuts:
        values = values * levels(stream_key, shape, cuts, -0.22, 0.18)
    return jnp.clip(values, -limit, limit).astype(held_as)


def setup_inputs(seed: int = 0) -> dict:
    key_of = jax.random.split(jax.random.key(seed), 20)
    return {
        "tokens": gaussian(key_of[0], (TOKENS, D), 1.0, 6.0, ((0, 32),)),
        "bucket": draw_bucket(jax.random.fold_in(key_of[19], 71), 0),
        "lengths": draw_lengths(jax.random.fold_in(key_of[19], 71), 0),
        "cotangent": gaussian(key_of[3], (TOKENS, D), 1.0, 6.0, ((0, 32),)),
        "query_weight": gaussian(key_of[4], (D, D), D ** -0.5, 0.21875, ((0, 8), (1, 4))),
        "query_bias": gaussian(key_of[5], (D,), 0.5, 3.0, ((0, 4),)),
        "key_weight": gaussian(key_of[6], (D, D), D ** -0.5, 0.21875, ((0, 8), (1, 4))),
        "value_weight": gaussian(key_of[7], (D, D), D ** -0.5, 0.21875, ((0, 8), (1, 4))),
        "value_bias": gaussian(key_of[8], (D,), 0.1, 0.625, ((0, 4),)),
        "out_weight": gaussian(key_of[9], (D, D), (max(D // 128, 2)) ** -0.5, 2.5, ((0, 8), (1, 4))),
        "out_bias": gaussian(key_of[10], (D,), 0.5, 3.0, ((0, 4),)),
        "norm1_gain": jnp.clip(1.0 + 0.1 * jax.random.normal(key_of[11], (D,), jnp.float32), 0.5, 1.5).astype(jnp.bfloat16),
        "norm1_bias": gaussian(key_of[12], (D,), 0.3, 1.75, ((0, 4),)),
        "up_weight": gaussian(key_of[13], (D, FF), D ** -0.5, 0.21875, ((0, 8), (1, 4))),
        "up_bias": gaussian(key_of[14], (FF,), 0.5, 3.0, ((0, 4),)),
        "down_weight": gaussian(key_of[15], (FF, D), FF ** -0.5, 0.109375, ((0, 8), (1, 4))),
        "down_bias": gaussian(key_of[16], (D,), 0.5, 3.0, ((0, 4),)),
        "norm2_gain": jnp.clip(1.0 + 0.1 * jax.random.normal(key_of[17], (D,), jnp.float32), 0.5, 1.5).astype(jnp.bfloat16),
        "norm2_bias": gaussian(key_of[18], (D,), 0.3, 1.75, ((0, 4),)),
    }


epsilon = 1e-06
masked_score = -1e+30

@jax.custom_vjp
def low(v):
    return lax.optimization_barrier(v.astype(jnp.bfloat16)).astype(jnp.float32)

@jax.custom_vjp
def low_back(v):
    return v

def low_keep(v):
    return (low(v), None)

def low_pass(kept, grad):
    return (grad,)

def back_keep(v):
    return (v, None)

def back_low(kept, grad):
    return (low(grad),)
low.defvjp(low_keep, low_pass)
low_back.defvjp(back_keep, back_low)

def product(left, right):
    return jnp.dot(left, right, precision=lax.Precision.HIGHEST)

def both_ways(value):
    return low(low_back(value))

def layer_norm(inputs, norm_gain, norm_shift):
    centred = inputs - lax.optimization_barrier(jnp.mean(inputs, axis=-1, keepdims=True))
    spread = lax.optimization_barrier(jnp.mean(centred * centred, axis=-1, keepdims=True))
    return centred * lax.rsqrt(spread + epsilon) * norm_gain + norm_shift

def layout(passage_flag, seq_lengths, row_count):
    row_index = jnp.arange(row_count, dtype=jnp.int32)
    segment = jnp.where(passage_flag == 1, row_index // PLEN, row_index // QLEN)
    position = jnp.where(passage_flag == 1, row_index % PLEN, row_index % QLEN)
    slot_index = jnp.arange(seq_lengths.shape[0], dtype=jnp.int32)
    member = segment[:, None] == slot_index[None, :]
    seq_limit = lax.optimization_barrier(jnp.sum(jnp.where(member, seq_lengths[None, :], 0), axis=1))
    return (segment, position < seq_limit, member)

def encode(params, inputs, passage_flag, seq_lengths):
    query_weight, query_bias, key_weight, value_weight, value_bias, out_weight, out_bias, norm1_gain, norm1_bias, up_weight, up_bias, down_weight, down_bias, norm2_gain, norm2_bias = params
    segment, alive_rows, member = layout(passage_flag, seq_lengths, TOK_DEV)
    queries = both_ways(product(inputs, query_weight) + query_bias)
    key_rows = both_ways(product(inputs, key_weight))
    values = both_ways(product(inputs, value_weight) + value_bias)
    blocks = TOK_DEV // PLEN

    def head_view(tensor):
        return tensor.reshape(blocks, PLEN, H, HD)
    block_segment = segment.reshape(blocks, PLEN)
    block_alive = alive_rows.reshape(blocks, PLEN)
    allowed = (block_segment[:, :, None] == block_segment[:, None, :]) & block_alive[:, None, :]
    raw_scores = jnp.einsum('bqhd,bkhd->bhqk', head_view(queries), head_view(key_rows), precision=lax.Precision.HIGHEST) * HD ** (-0.5)
    scores = low_back(jnp.where(allowed[:, None], raw_scores, masked_score))
    weights = low(jax.nn.softmax(scores, axis=-1))
    context = jnp.einsum('bhqk,bkhd->bqhd', weights, head_view(values), precision=lax.Precision.HIGHEST).reshape(TOK_DEV, D)
    context = both_ways(context)
    attended = low_back(product(context, out_weight) + out_bias)
    normed_one = layer_norm(inputs + attended, norm1_gain, norm1_bias)
    hidden = low_back(product(low(normed_one), up_weight) + up_bias)
    active = low(jax.nn.gelu(hidden, approximate=False))
    branch = low_back(product(active, down_weight) + down_bias)
    return layer_norm(normed_one + branch, norm2_gain, norm2_bias)

def pool_rows(outputs, passage_flag, seq_lengths):
    segment, alive_rows, member = layout(passage_flag, seq_lengths, TOK_DEV)
    chosen = (member & alive_rows[:, None]).astype(jnp.float32)
    summed = jnp.einsum('tj,td->jd', chosen, outputs, precision=lax.Precision.HIGHEST)
    counted = lax.optimization_barrier(jnp.sum(chosen, axis=0))
    return summed / jnp.maximum(counted, 1.0)[:, None]

def encode_and_pool(params, inputs, passage_flag, seq_lengths):
    outputs = encode(params, inputs, passage_flag, seq_lengths)
    return (outputs, pool_rows(outputs, passage_flag, seq_lengths))

def reference(tokens, bucket, lengths, cotangent, query_weight, query_bias, key_weight, value_weight, value_bias, out_weight, out_bias, norm1_gain, norm1_bias, up_weight, up_bias, down_weight, down_bias, norm2_gain, norm2_bias):
    params = tuple((weight.astype(jnp.float32) for weight in (query_weight, query_bias, key_weight, value_weight, value_bias, out_weight, out_bias, norm1_gain, norm1_bias, up_weight, up_bias, down_weight, down_bias, norm2_gain, norm2_bias)))
    inputs = tokens.astype(jnp.float32).reshape(SHARDS, TOK_DEV, D)

    def forward(all_inputs, all_params):

        def scan_step(scan_carry, scan_item):
            return (scan_carry, jax.checkpoint(encode_and_pool)(all_params, scan_item[0], scan_item[1], scan_item[2]))
        return lax.scan(scan_step, jnp.zeros((), jnp.float32), (all_inputs, bucket, lengths))[1]
    (outputs, pooled), pullback = jax.vjp(forward, inputs, params)
    grad_inputs, weight_grads = pullback((cotangent.astype(jnp.float32).reshape(SHARDS, TOK_DEV, D), jnp.zeros_like(pooled)))
    return (outputs.reshape(TOKENS, D).astype(jnp.bfloat16), pooled.reshape(SLOTS, D), grad_inputs.reshape(TOKENS, D), weight_grads[0], weight_grads[1], weight_grads[2], weight_grads[3], weight_grads[4], weight_grads[5], weight_grads[6], weight_grads[7], weight_grads[8], weight_grads[9], weight_grads[10], weight_grads[11], weight_grads[12], weight_grads[13], weight_grads[14])
```

```python
import functools

import jax
import jax.numpy as jnp
from jax import lax
from jax.experimental import pallas as pl
from jax.experimental.pallas import tpu as pltpu
from jax.sharding import PartitionSpec as P

H = 12
HD = 64
PLEN = 512
QLEN = 128
PAIR = 2 * HD
ROWS = 256

epsilon = 1e-06
masked_score = -1e30
f32 = jnp.float32
bf16 = jnp.bfloat16
LIMIT = 60 * 1024 * 1024


def dot(left, right):
    return jnp.dot(left, right, preferred_element_type=f32)


def dot_nt(left, right):
    return lax.dot_general(left, right, (((1,), (1,)), ((), ())), preferred_element_type=f32)


def dot_tn(left, right):
    return lax.dot_general(left, right, (((0,), (0,)), ((), ())), preferred_element_type=f32)


def call(kernel, name, grid, in_specs, out_specs, out_shape, scratch=(), prefetch=0, cost=None):
    return pl.pallas_call(
        kernel,
        name=name,
        grid_spec=pltpu.PrefetchScalarGridSpec(
            num_scalar_prefetch=prefetch,
            grid=grid,
            in_specs=in_specs,
            out_specs=out_specs,
            scratch_shapes=list(scratch),
        ),
        out_shape=out_shape,
        compiler_params=pltpu.CompilerParams(
            vmem_limit_bytes=LIMIT, dimension_semantics=("arbitrary",) * len(grid)
        ),
        cost_estimate=cost,
    )


def whole(shape):
    return pl.BlockSpec(shape, lambda *_: (0,) * len(shape))


def sds(shape, dtype):
    return jax.ShapeDtypeStruct(shape, dtype)


def guess(flops, nbytes):
    return pl.CostEstimate(flops=int(flops), bytes_accessed=int(nbytes), transcendentals=0)


def segment_lanes(bucket, lengths, queries_ext, keys_ext):
    row_count = queries_ext.shape[0]
    slots = lengths.shape[0]
    shape = (row_count, PAIR)
    row = lax.broadcasted_iota(jnp.int32, shape, 0)
    lane = lax.broadcasted_iota(jnp.int32, shape, 1) % HD
    passage = bucket[0] == 1
    segment = jnp.where(passage, row // PLEN, row // QLEN)
    position = jnp.where(passage, row % PLEN, row % QLEN)
    limit = jnp.zeros(shape, jnp.int32)
    for s in range(slots):
        limit = jnp.where(segment == s, lengths[s], limit)
    alive = position < limit
    same = segment == lane
    queries_ext[...] = jnp.where(same, 1.0, 0.0).astype(bf16)
    keys_ext[...] = jnp.where((lane < slots) & ~(same & alive), masked_score, 0.0).astype(bf16)


def attend_kernel(
    bucket, lengths, x, qw, kw, vw, qb, vb,
    q_out, k_out, v_out, context_out, lse_out,
    queries_ext, keys_ext, lse_all,
):
    pair = pl.program_id(0)
    row_count = x.shape[0]

    @pl.when(pair == 0)
    def _():
        segment_lanes(bucket, lengths, queries_ext, keys_ext)
        lse_all[...] = jnp.zeros_like(lse_all)

    weights = jnp.concatenate([qw[0], kw[0], vw[0]], axis=1)
    qb_row = qb[...]
    vb_row = vb[...]
    low_half = lax.broadcasted_iota(jnp.int32, (PLEN, PAIR), 1) < HD
    lane = lax.broadcasted_iota(jnp.int32, (PLEN, PAIR), 1)

    def block(b, carry):
        rows = pl.ds(pl.multiple_of(b * PLEN, PLEN), PLEN)
        qkv = dot(x[rows, :], weights)
        queries = ((qkv[:, :PAIR] + qb_row).astype(bf16).astype(f32) * HD ** (-0.5)).astype(bf16)
        keys = qkv[:, PAIR:2 * PAIR].astype(bf16)
        values = (qkv[:, 2 * PAIR:] + vb_row).astype(bf16)
        q_out[rows, :] = queries
        k_out[rows, :] = keys
        v_out[rows, :] = values
        q_ext = queries_ext[rows, :]
        k_ext = keys_ext[rows, :]
        ones = jnp.ones_like(values)
        sums, tops = [], []
        for half in range(2):
            mine = low_half if half == 0 else ~low_half
            scores = dot_nt(jnp.where(mine, queries, q_ext), jnp.where(mine, keys, k_ext))
            top = jnp.max(scores, axis=-1, keepdims=True)
            weight = jnp.exp(scores - top).astype(bf16)
            sums.append(dot(weight, jnp.where(mine, values, ones)))
            tops.append(top)
        numer = jnp.where(low_half, sums[0], sums[1])
        denom = pltpu.roll(jnp.where(low_half, sums[1], sums[0]), HD, 1)
        context_out[rows, :] = (numer / denom).astype(bf16)
        lse = jnp.where(low_half, tops[0], tops[1]) + jnp.log(denom)
        mine = (lane % HD) == pair
        lse_all[rows, :] = jnp.where(mine, lse, lse_all[rows, :])
        return carry

    lax.fori_loop(0, row_count // PLEN, block, 0)

    @pl.when(pair == pl.num_programs(0) - 1)
    def _():
        lse_out[...] = lse_all[...].T


def attend(bucket, lengths, x, weights, qb, vb):
    t, d = x.shape
    pairs = d // PAIR
    column = lambda m: pl.BlockSpec((1, d, PAIR), lambda p, *_: (m, 0, p))
    vector = pl.BlockSpec((1, PAIR), lambda p, *_: (0, p))
    tall = pl.BlockSpec((t, PAIR), lambda p, *_: (0, p))
    return call(
        attend_kernel, "attend", (pairs,),
        [whole((t, d)), column(0), column(1), column(2), vector, vector],
        [tall, tall, tall, tall, whole((PAIR, t))],
        [sds((t, d), bf16)] * 4 + [sds((PAIR, t), f32)],
        [pltpu.VMEM((t, PAIR), bf16), pltpu.VMEM((t, PAIR), bf16), pltpu.VMEM((t, PAIR), f32)],
        prefetch=2, cost=guess(15e9, 12e6),
    )(bucket, lengths, x, weights, weights, weights, qb, vb)


def attend_back_kernel(
    bucket, lengths, x_t, q, k, v, grad_context, lse, delta, qw, kw, vw, grad_inner,
    gqw, gkw, gvw, gqb, gvb, input_grad,
    queries_ext, keys_ext, grads,
):
    pair = pl.program_id(0)
    row_count = q.shape[0]

    @pl.when(pair == 0)
    def _():
        segment_lanes(bucket, lengths, queries_ext, keys_ext)

    low_half = lax.broadcasted_iota(jnp.int32, (PLEN, PAIR), 1) < HD

    def block(b, carry):
        rows = pl.ds(pl.multiple_of(b * PLEN, PLEN), PLEN)
        queries, keys, values, grad_ctx = q[rows, :], k[rows, :], v[rows, :], grad_context[rows, :]
        q_ext, k_ext = queries_ext[rows, :], keys_ext[rows, :]
        nothing = jnp.zeros_like(values)
        got = []
        for half in range(2):
            mine = low_half if half == 0 else ~low_half
            lse_row = lse[pl.ds(half * HD + pair, 1), rows]
            delta_row = delta[pl.ds(half * HD + pair, 1), rows]
            scores = dot_nt(jnp.where(mine, keys, k_ext), jnp.where(mine, queries, q_ext))
            probs = jnp.exp(scores - lse_row)
            grad_probs = dot_nt(jnp.where(mine, values, nothing), grad_ctx)
            grad_scores = (probs * (grad_probs - delta_row)).astype(bf16)
            grad_v = dot(probs.astype(bf16), grad_ctx)
            grad_k = dot(grad_scores, queries)
            grad_q = dot_tn(grad_scores, keys)
            got.append((grad_q, grad_k, grad_v))
        gq = (jnp.where(low_half, got[0][0], got[1][0]) * HD ** (-0.5)).astype(bf16)
        gk = jnp.where(low_half, got[0][1], got[1][1]).astype(bf16)
        gv = jnp.where(low_half, got[0][2], got[1][2]).astype(bf16)
        grads[rows, :PAIR] = gq
        grads[rows, PAIR:2 * PAIR] = gk
        grads[rows, 2 * PAIR:] = gv
        sum_q = jnp.sum(gq.astype(f32), axis=0, keepdims=True)
        sum_v = jnp.sum(gv.astype(f32), axis=0, keepdims=True)
        return (carry[0] + sum_q, carry[1] + sum_v)

    start = jnp.zeros((1, PAIR), f32)
    gqb[...], gvb[...] = lax.fori_loop(0, row_count // PLEN, block, (start, start))

    columns = grads[...]
    weight_grads = dot(x_t[...], columns)
    gqw[...] = weight_grads[:, :PAIR].astype(gqw.dtype)
    gkw[...] = weight_grads[:, PAIR:2 * PAIR].astype(gkw.dtype)
    gvw[...] = weight_grads[:, 2 * PAIR:].astype(gvw.dtype)

    @pl.when(pair == 0)
    def _():
        input_grad[...] = grad_inner[...]

    weights = jnp.concatenate([qw[0], kw[0], vw[0]], axis=1)
    input_grad[...] += dot_nt(columns, weights)


def attend_back(bucket, lengths, x_t, q, k, v, grad_context, lse, delta, weights, grad_inner):
    t, d = q.shape
    pairs = d // PAIR
    column = lambda m: pl.BlockSpec((1, d, PAIR), lambda p, *_: (m, 0, p))
    vector = pl.BlockSpec((1, PAIR), lambda p, *_: (0, p))
    tall = pl.BlockSpec((t, PAIR), lambda p, *_: (0, p))
    made = pl.BlockSpec((d, PAIR), lambda p, *_: (0, p))
    return call(
        attend_back_kernel, "attend_back", (pairs,),
        [whole((d, t)), tall, tall, tall, tall, whole((PAIR, t)), whole((PAIR, t)),
         column(0), column(1), column(2), whole((t, d))],
        [made, made, made, vector, vector, whole((t, d))],
        [sds((d, d), bf16)] * 3 + [sds((1, d), f32)] * 2 + [sds((t, d), f32)],
        [pltpu.VMEM((t, PAIR), bf16), pltpu.VMEM((t, PAIR), bf16), pltpu.VMEM((t, 3 * PAIR), bf16)],
        prefetch=2, cost=guess(30e9, 25e6),
    )(bucket, lengths, x_t, q, k, v, grad_context, lse, delta, weights, weights, weights, grad_inner)


def normed(v):
    centred = v - jnp.mean(v, axis=-1, keepdims=True)
    r = lax.rsqrt(jnp.mean(centred * centred, axis=-1, keepdims=True) + epsilon)
    return centred * r, r


def norm_back(dy, n, r, gain):
    dn = dy * gain
    return r * (dn - jnp.mean(dn, axis=-1, keepdims=True) - n * jnp.mean(dn * n, axis=-1, keepdims=True))


def gelu_parts(u):
    size = jnp.abs(u)
    below = 1.0 + (0.3275911 * 0.7071067811865476) * size
    t = pl.reciprocal(below, approx=True)
    t = t * (2.0 - below * t)
    poly = 0.5 * 1.061405429
    for c in (-1.453152027, 1.421413741, -0.284496736, 0.254829592):
        poly = poly * t + 0.5 * c
    bell = jnp.exp(u * u * -0.5)
    tail = poly * t * bell
    phi = jnp.where(u >= 0, 1.0 - tail, tail)
    return u * phi, phi + u * bell * 0.3989422804014327


def up_kernel(x, context, ow, ob, g1, b1, uw, ub, n1_out, r1_out, low_out, act_out, slope_out):
    parts, _, wide = act_out.shape
    attended = dot(context[...], ow[0]) + ob[...]
    n1, r1 = normed(x[...].astype(f32) + attended)
    n1_out[...] = n1
    r1_out[...] = jnp.broadcast_to(r1, r1_out.shape)
    low = (n1 * g1[...] + b1[...]).astype(bf16)
    low_out[...] = low
    each = uw.shape[2] // wide
    for j in range(uw.shape[0]):
        hidden = dot(low, uw[j]) + ub[j:j + 1, :]
        active, slope = gelu_parts(hidden)
        active, slope = active.astype(bf16), slope.astype(bf16)
        for c in range(each):
            act_out[j * each + c] = active[:, c * wide:(c + 1) * wide]
            slope_out[j * each + c] = slope[:, c * wide:(c + 1) * wide]


def up(x, context, weights, ob, g1, b1, uw, ub, parts):
    t, d = x.shape
    f, _, wide = uw.shape
    narrow = f * wide // parts
    rows = pl.BlockSpec((ROWS, d), lambda r: (r, 0))
    tall = pl.BlockSpec((parts, ROWS, narrow), lambda r: (0, r, 0))
    return call(
        up_kernel, "up", (t // ROWS,),
        [rows, rows, pl.BlockSpec((1, d, d), lambda r: (3, 0, 0)), whole((1, d)), whole((1, d)), whole((1, d)),
         whole(uw.shape), whole(ub.shape)],
        [rows, pl.BlockSpec((ROWS, 128), lambda r: (r, 0)), rows, tall, tall],
        [sds((t, d), f32), sds((t, 128), f32), sds((t, d), bf16), sds((parts, t, narrow), bf16),
         sds((parts, t, narrow), bf16)],
        cost=guess(12e9, 26e6),
    )(x, context, weights, ob, g1, b1, uw, ub)


def down_kernel(
    bucket, lengths, act_rows, n1, g1, b1, dw, db, g2, b2, cotangent, act_part,
    out, pooled, mixed_out, branch_out, gdb, gg2, gb2, gdw,
    branch_t, counts,
):
    step = pl.program_id(0)
    tiles = branch_t.shape[1] // ROWS
    parts = dw.shape[0]

    @pl.when(step == 0)
    def _():
        pooled[...] = jnp.zeros_like(pooled)
        counts[...] = jnp.zeros_like(counts)
        gdb[...] = jnp.zeros_like(gdb)
        gg2[...] = jnp.zeros_like(gg2)
        gb2[...] = jnp.zeros_like(gb2)

    @pl.when(step < tiles)
    def _():
        branch = dot_nt(act_rows[0], dw[0])
        for i in range(1, parts):
            branch += dot_nt(act_rows[i], dw[i])
        residual = n1[...] * g1[...] + b1[...] + (branch + db[...])
        n2, r2 = normed(residual)
        result = n2 * g2[...] + b2[...]
        out[...] = result.astype(bf16)
        slots = pooled.shape[0]
        shape = (slots, ROWS)
        slot = lax.broadcasted_iota(jnp.int32, shape, 0)
        row = lax.broadcasted_iota(jnp.int32, shape, 1) + step * ROWS
        passage = bucket[0] == 1
        segment = jnp.where(passage, row // PLEN, row // QLEN)
        position = jnp.where(passage, row % PLEN, row % QLEN)
        limit = jnp.zeros(shape, jnp.int32)
        for s in range(slots):
            limit = jnp.where(slot == s, lengths[s], limit)
        chosen = jnp.where((segment == slot) & (position < limit), 1.0, 0.0)
        picked = chosen.astype(bf16)
        high = result.astype(bf16)
        rest = result - high.astype(f32)
        middle = rest.astype(bf16)
        last = (rest - middle.astype(f32)).astype(bf16)
        pooled[...] += dot(picked, high) + dot(picked, middle) + dot(picked, last)
        counts[...] += jnp.broadcast_to(jnp.sum(chosen, axis=1, keepdims=True), counts.shape)
        dy = cotangent[...].astype(f32)
        gg2[...] += jnp.sum(dy * n2, axis=0, keepdims=True)
        gb2[...] += jnp.sum(dy, axis=0, keepdims=True)
        mixed = norm_back(dy, n2, r2, g2[...])
        mixed_out[...] = mixed
        low = mixed.astype(bf16)
        branch_out[...] = low
        gdb[...] += jnp.sum(low.astype(f32), axis=0, keepdims=True)
        for tile in range(tiles):
            @pl.when(step == tile)
            def _():
                branch_t[:, tile * ROWS:(tile + 1) * ROWS] = low.T

    @pl.when(step == tiles - 1)
    def _():
        pooled[...] = pooled[...] / jnp.maximum(counts[...], 1.0)[:, :1]

    @pl.when(step >= tiles)
    def _():
        gdw[0] = dot(branch_t[...], act_part[0]).astype(bf16)


def down(bucket, lengths, active, n1, g1, b1, dw, db, g2, b2, cotangent):
    parts, t, narrow = active.shape
    d = n1.shape[1]
    tiles = t // ROWS
    slots = lengths.shape[0]
    early = lambda s: jnp.minimum(s, tiles - 1)
    late = lambda s: jnp.maximum(s - tiles, 0)
    rows = pl.BlockSpec((ROWS, d), lambda s, *_: (early(s), 0))
    vector = whole((1, d))
    return call(
        down_kernel, "down", (tiles + parts,),
        [pl.BlockSpec((parts, ROWS, narrow), lambda s, *_: (0, early(s), 0)), rows, vector, vector,
         whole(dw.shape), vector, vector, vector, rows,
         pl.BlockSpec((1, t, narrow), lambda s, *_: (late(s), 0, 0))],
        [rows, whole((slots, d)), rows, rows, vector, vector, vector,
         pl.BlockSpec((1, d, narrow), lambda s, *_: (late(s), 0, 0))],
        [sds((t, d), bf16), sds((slots, d), f32), sds((t, d), f32), sds((t, d), bf16)]
        + [sds((1, d), f32)] * 3 + [sds((parts, d, narrow), bf16)],
        [pltpu.VMEM((d, t), bf16), pltpu.VMEM((slots, 128), f32)],
        prefetch=2, cost=guess(12e9, 30e6),
    )(bucket, lengths, active, n1, g1, b1, dw, db, g2, b2, cotangent, active)


def feed_back_kernel(
    branch, slope, dw, uw, low_t, mixed, n1, r1, g1, context, ow,
    guw, gub, inner_out, gg1, gb1, gob, gow, grad_context, delta_out,
    hidden, grad_normed, attended,
):
    j = pl.program_id(0)
    each, t, narrow = slope.shape
    d = branch.shape[1]
    tiles = t // ROWS

    def gelu_rows(r, sums):
        rows = pl.ds(pl.multiple_of(r * ROWS, ROWS), ROWS)
        found = []
        for c in range(each):
            grad = (slope[c, rows, :].astype(f32) * dot(branch[rows, :], dw[c])).astype(bf16)
            hidden[rows, c * narrow:(c + 1) * narrow] = grad
            found.append(sums[c] + jnp.sum(grad.astype(f32), axis=0, keepdims=True))
        return tuple(found)

    sums = lax.fori_loop(0, tiles, gelu_rows, (jnp.zeros((1, narrow), f32),) * each)
    for c in range(each):
        gub[0, :, c * narrow:(c + 1) * narrow] = sums[c]
    guw[0] = dot(low_t[...], hidden[...]).astype(bf16)

    @pl.when(j == 0)
    def _():
        grad_normed[...] = mixed[...]

    def normed_rows(r, carry):
        rows = pl.ds(pl.multiple_of(r * ROWS, ROWS), ROWS)
        grad_normed[rows, :] += dot_nt(hidden[rows, :], uw[0])
        return carry

    lax.fori_loop(0, tiles, normed_rows, 0)

    @pl.when(j == pl.num_programs(0) - 1)
    def _():
        feature = lax.broadcasted_iota(jnp.int32, (128, d), 1)
        slot = lax.broadcasted_iota(jnp.int32, (128, d), 0)
        head = jnp.where(slot < HD, 2 * slot, 2 * (slot - HD) + 1)
        pick = jnp.where(feature // HD == head, 1.0, 0.0).astype(bf16)

        def inner_rows(r, sums):
            rows = pl.ds(pl.multiple_of(r * ROWS, ROWS), ROWS)
            dy, n = grad_normed[rows, :], n1[rows, :]
            inner = norm_back(dy, n, r1[rows, :1], g1[...])
            inner_out[rows, :] = inner
            low = inner.astype(bf16)
            attended[rows, :] = low
            grad_ctx = dot_nt(low, ow[0]).astype(bf16)
            grad_context[rows, :] = grad_ctx
            both = grad_ctx.astype(f32) * context[rows, :].astype(f32)
            high = both.astype(bf16)
            rest = (both - high.astype(f32)).astype(bf16)
            delta_out[:, rows] = dot_nt(pick, high) + dot_nt(pick, rest)
            return (
                sums[0] + jnp.sum(dy * n, axis=0, keepdims=True),
                sums[1] + jnp.sum(dy, axis=0, keepdims=True),
                sums[2] + jnp.sum(low.astype(f32), axis=0, keepdims=True),
            )

        gg1[...], gb1[...], gob[...] = lax.fori_loop(0, tiles, inner_rows, (jnp.zeros((1, d), f32),) * 3)
        gow[...] = dot_tn(context[...], attended[...]).astype(bf16)


def feed_back(branch, slope, dw, uw, low_t, mixed, n1, r1, g1, context, weights):
    parts, t, narrow = slope.shape
    f, d, wide = uw.shape
    each = parts // f
    vector = whole((1, d))
    return call(
        feed_back_kernel, "feed_back", (f,),
        [whole((t, d)), pl.BlockSpec((each, t, narrow), lambda j: (j, 0, 0)),
         pl.BlockSpec((each, d, narrow), lambda j: (j, 0, 0)), pl.BlockSpec((1, d, wide), lambda j: (j, 0, 0)),
         whole((d, t)), whole((t, d)), whole((t, d)), whole((t, 128)), vector, whole((t, d)),
         pl.BlockSpec((1, d, d), lambda j: (3, 0, 0))],
        [pl.BlockSpec((1, d, wide), lambda j: (j, 0, 0)), pl.BlockSpec((1, 1, wide), lambda j: (j, 0, 0)),
         whole((t, d)), vector, vector, vector, whole((d, d)), whole((t, d)), whole((128, t))],
        [sds((f, d, wide), bf16), sds((f, 1, wide), f32), sds((t, d), f32)] + [sds((1, d), f32)] * 3
        + [sds((d, d), bf16), sds((t, d), bf16), sds((128, t), f32)],
        [pltpu.VMEM((t, wide), bf16), pltpu.VMEM((t, d), f32), pltpu.VMEM((t, d), bf16)],
        cost=guess(18e9, 45e6),
    )(branch, slope, dw, uw, low_t, mixed, n1, r1, g1, context, weights)


def shards(
    tokens, bucket, lengths, cotangent,
    query_weight, query_bias, key_weight, value_weight, value_bias, out_weight, out_bias,
    norm1_gain, norm1_bias, up_weight, up_bias, down_weight, down_bias, norm2_gain, norm2_bias,
):
    t, d = tokens.shape
    dp, fsdp = lax.axis_size("dp"), lax.axis_size("fsdp")
    lengths = lengths[0]

    def gather(v, axis, dim, tiled=True):
        return lax.all_gather(v, axis, axis=dim, tiled=tiled)

    stack = jnp.stack([query_weight, key_weight, value_weight, out_weight])
    weights = gather(gather(stack, "fsdp", 2), "dp", 1)
    uw = gather(gather(up_weight, "dp", 0), "fsdp", 0, False)
    dw = gather(gather(down_weight.T, "fsdp", 0), "dp", 0, False)
    vectors = jnp.stack([query_bias, value_bias, out_bias, norm1_gain, norm1_bias, down_bias, norm2_gain, norm2_bias])
    vectors = gather(vectors, "fsdp", 1).astype(f32)
    qb, vb, ob, g1, b1, db, g2, b2 = (vectors[n:n + 1] for n in range(8))
    ub = gather(up_bias, "fsdp", 0, False).astype(f32)

    q, k, v, context, lse = attend(bucket, lengths, tokens, weights, qb, vb)
    n1, r1, low, active, slope = up(tokens, context, weights, ob, g1, b1, uw, ub, dp)
    out, pooled, mixed, branch, gdb, gg2, gb2, gdw = down(
        bucket, lengths, active, n1, g1, b1, dw, db, g2, b2, cotangent
    )
    guw, gub, inner, gg1, gb1, gob, gow, grad_context, delta = feed_back(
        branch, slope, dw, uw, low.T, mixed, n1, r1, g1, context, weights
    )
    gqw, gkw, gvw, gqb, gvb, input_grad = attend_back(
        bucket, lengths, tokens.T, q, k, v, grad_context, lse, delta, weights, inner
    )

    def scatter(g, axis, dim, tiled=True):
        return lax.psum_scatter(g, axis, scatter_dimension=dim, tiled=tiled)

    made_u = scatter(scatter(guw, "fsdp", 0, False), "dp", 0).astype(f32)
    made_d = scatter(scatter(gdw, "dp", 0, False), "fsdp", 0).T.astype(f32)
    made = [scatter(scatter(g, "dp", 0), "fsdp", 1).astype(f32) for g in (gqw, gkw, gvw, gow)]
    rows = jnp.concatenate([gqb, gvb, gob, gg1, gb1, gdb, gg2, gb2], axis=0)
    rows = lax.psum(scatter(rows, "fsdp", 1), "dp")
    gub = lax.psum(scatter(gub.reshape(-1), "fsdp", 0), "dp")
    return (
        out, pooled, input_grad, made[0], rows[0], made[1], made[2], rows[1], made[3], rows[2], rows[3], rows[4],
        made_u, gub, made_d, rows[5], rows[6], rows[7],
    )


def solution(mesh):
    tall, square, vector = P(("dp", "fsdp"), None), P("dp", "fsdp"), P("fsdp")
    in_specs = (
        tall, P(("dp", "fsdp")), tall, tall, square, vector, square, square, vector, square, vector,
        vector, vector, square, vector, square, vector, vector, vector,
    )
    out_specs = (
        tall, tall, tall, square, vector, square, square, vector, square, vector, vector, vector,
        square, vector, square, vector, vector, vector,
    )
    return jax.shard_map(shards, mesh=mesh, in_specs=in_specs, out_specs=out_specs, check_vma=False)
```

```python
import functools

import jax
import jax.numpy as jnp
from jax import lax
from jax.experimental import pallas as pl
from jax.experimental.pallas import tpu as pltpu
from jax.sharding import PartitionSpec as P

H = 12
HD = 64
PLEN = 512
QLEN = 128
PAIR = 2 * HD
ROWS = 256

epsilon = 1e-06
masked_score = -1e30
f32 = jnp.float32
bf16 = jnp.bfloat16
LIMIT = 60 * 1024 * 1024


def dot(left, right):
    return jnp.dot(left, right, preferred_element_type=f32)


def dot_nt(left, right):
    return lax.dot_general(left, right, (((1,), (1,)), ((), ())), preferred_element_type=f32)


def dot_tn(left, right):
    return lax.dot_general(left, right, (((0,), (0,)), ((), ())), preferred_element_type=f32)


def call(kernel, name, grid, in_specs, out_specs, out_shape, scratch=(), prefetch=0, cost=None):
    return pl.pallas_call(
        kernel,
        name=name,
        grid_spec=pltpu.PrefetchScalarGridSpec(
            num_scalar_prefetch=prefetch,
            grid=grid,
            in_specs=in_specs,
            out_specs=out_specs,
            scratch_shapes=list(scratch),
        ),
        out_shape=out_shape,
        compiler_params=pltpu.CompilerParams(
            vmem_limit_bytes=LIMIT, dimension_semantics=("arbitrary",) * len(grid)
        ),
        cost_estimate=cost,
    )


def whole(shape):
    return pl.BlockSpec(shape, lambda *_: (0,) * len(shape))


def sds(shape, dtype):
    return jax.ShapeDtypeStruct(shape, dtype)


def guess(flops, nbytes):
    return pl.CostEstimate(flops=int(flops), bytes_accessed=int(nbytes), transcendentals=0)


def reverse(s, bits):
    return sum(((s >> b) & 1) << (bits - 1 - b) for b in range(bits))


def axis_facts():
    dp, fsdp = lax.axis_size("dp"), lax.axis_size("fsdp")
    return dp, fsdp, dp // 2, fsdp.bit_length() - 1


def along_z(hop):
    dp = lax.axis_size("dp")
    return [(d, (d + 2 * hop) % dp) for d in range(dp)]


def across_cores():
    return [(d, d ^ 1) for d in range(lax.axis_size("dp"))]


def along_bit(r):
    dp, fsdp, _, bits = axis_facts()
    pairs = []
    for d in range(dp):
        flip = 1 << (r if d % 2 == 0 else bits - 1 - r)
        pairs += [(d * fsdp + f, d * fsdp + (f ^ flip)) for f in range(fsdp)]
    return pairs


def gather_blocks(block):
    _, _, depth, bits = axis_facts()
    parts = [block] + [lax.ppermute(block, "dp", along_z(s)) for s in range(1, depth)]
    held = jnp.stack(parts)[None]
    for r in range(bits):
        got = lax.ppermute(held, ("dp", "fsdp"), along_bit(r))
        if r < bits - 1:
            held = jnp.concatenate([held, got])
    own = [held, got]
    return own + [lax.ppermute(v, "dp", across_cores()) for v in own]


def add(left, right):
    return (left.astype(f32) + right.astype(f32)).astype(bf16)


def scatter_blocks(keep, send):
    _, _, depth, bits = axis_facts()
    got = lax.ppermute(send, "dp", across_cores())
    for r in reversed(range(bits)):
        half = keep.shape[0] // 2
        upper = add(keep[half:], got[half:])
        keep = add(keep[:half], got[:half])
        got = lax.ppermute(upper, ("dp", "fsdp"), along_bit(r))
    mine = [add(keep[0, s], got[0, s]) for s in range(1, depth)]
    total = keep[0, 0].astype(f32) + got[0, 0].astype(f32)
    for s in range(1, depth):
        total = total + lax.ppermute(mine[s - 1], "dp", along_z(-s)).astype(f32)
    return total


def places():
    dp, fsdp, depth, bits = axis_facts()
    d, f = lax.axis_index("dp"), lax.axis_index("fsdp")
    z, core = d // 2, d % 2
    slot = jnp.arange(depth, dtype=jnp.int32)
    index = jnp.arange(fsdp, dtype=jnp.int32)
    mirror = sum((((index >> b) & 1) << (bits - 1 - b) for b in range(bits)), jnp.zeros_like(index))
    rows, slots, columns = [], [], []
    for n in range(2):
        there = core ^ n
        rows.append(2 * ((z - slot) % depth) + there)
        away = index ^ f
        mirrored = sum((((away >> b) & 1) << (bits - 1 - b) for b in range(bits)), jnp.zeros_like(index))
        slots.append(jnp.where(there == 0, away, mirrored))
        columns.append(f ^ jnp.where(there == 0, index, mirror))
    return jnp.concatenate(rows + slots + columns).astype(jnp.int32)


def row_of(place, n, slot, depth):
    return place[n * depth + slot]


def slot_of(place, n, j, depth, fsdp):
    return place[2 * depth + n * fsdp + j]


def column_of(place, n, s, depth, fsdp):
    return place[2 * depth + 2 * fsdp + n * fsdp + s]


def block_copies(place, arrays, target, sems):
    half, depth = arrays[0].shape[:2]
    fsdp = 2 * half
    copies = []
    for a, array in enumerate(arrays):
        for q in range(half):
            for slot in range(depth):
                i = row_of(place, a // 2, slot, depth)
                j = column_of(place, a // 2, (a % 2) * half + q, depth, fsdp)
                copies.append(pltpu.make_async_copy(array.at[q, slot], target(i, j), sems.at[len(copies)]))
    return copies


def assemble_kernel(place, own_low, own_high, other_low, other_high, weights, vectors, ub):
    step = pl.program_id(0)
    half, _, height, width = own_low.shape
    fsdp, depth, tall = 2 * half, pl.num_programs(0) // 2, height - 16
    narrow = width // 4

    def fill(n, low, high):
        pieces = []
        for j in range(fsdp):
            slot = slot_of(place, n, j, depth, fsdp)
            upper, q = slot >= half, lax.rem(slot, half)
            pieces.append(jnp.where(upper, high[q, 0].astype(f32), low[q, 0].astype(f32)))
        for m in range(4):
            row = jnp.concatenate([p[:, m * narrow:(m + 1) * narrow] for p in pieces], axis=1)
            weights[m] = row[:tall].astype(bf16)
            vectors[m] = row[tall:]
        for j in range(fsdp):
            ub[j] = pieces[j][tall:]

    @pl.when(step < depth)
    def _():
        fill(0, own_low, own_high)

    @pl.when(step >= depth)
    def _():
        fill(1, other_low, other_high)


def assemble(place, arrays):
    half, depth, height, width = arrays[0].shape
    fsdp, tall, d = 2 * half, height - 16, half * width // 2
    own = pl.BlockSpec((half, 1, height, width), lambda s, place: (0, jnp.minimum(s, depth - 1), 0, 0))
    other = pl.BlockSpec((half, 1, height, width), lambda s, place: (0, jnp.maximum(s - depth, 0), 0, 0))
    return call(
        assemble_kernel, "assemble", (2 * depth,),
        [own, own, other, other],
        [pl.BlockSpec((4, tall, d), lambda s, place: (0, place[s], 0)), whole((4, 16, d)), whole((fsdp, 16, width))],
        [sds((4, 2 * depth * tall, d), bf16), sds((4, 16, d), f32), sds((fsdp, 16, width), f32)],
        prefetch=1, cost=guess(1e9, 11e6),
    )(place, *arrays)


def pack_kernel(place, gq, gk, gv, go, vectors, gub, send, keep):
    step = pl.program_id(0)
    fsdp, _, height, width = send.shape
    depth, tall, narrow = pl.num_programs(0) // 2, height - 16, width // 4

    def fill(n, out):
        for j in range(fsdp):
            slot = slot_of(place, n, j, depth, fsdp)
            columns = slice(j * narrow, (j + 1) * narrow)
            out[slot, 0, :tall, :] = jnp.concatenate(
                [g[:, columns].astype(f32) for g in (gq, gk, gv, go)], axis=1
            ).astype(bf16)
            slab = jnp.concatenate([vectors[m, :, columns] for m in range(4)], axis=1)
            third = lax.broadcasted_iota(jnp.int32, slab.shape, 0) == 2
            out[slot, 0, tall:, :] = jnp.where(third, gub[j], slab).astype(bf16)

    @pl.when(step < depth)
    def _():
        fill(1, send)

    @pl.when(step >= depth)
    def _():
        fill(0, keep)


def pack(place, grads, vectors, gub):
    d = grads[0].shape[0]
    dp, fsdp, depth, _ = axis_facts()
    tall, width = d // dp, 4 * d // fsdp
    rows = pl.BlockSpec((tall, d), lambda s, place: (place[(s + depth) % (2 * depth)], 0))
    sent = pl.BlockSpec((fsdp, 1, tall + 16, width), lambda s, place: (0, jnp.minimum(s, depth - 1), 0, 0))
    kept = pl.BlockSpec((fsdp, 1, tall + 16, width), lambda s, place: (0, jnp.maximum(s - depth, 0), 0, 0))
    return call(
        pack_kernel, "pack", (2 * depth,),
        [rows, rows, rows, rows, whole((4, 16, d)), whole((fsdp, 1, width))],
        [sent, kept],
        [sds((fsdp, depth, tall + 16, width), bf16)] * 2,
        prefetch=1, cost=guess(1e9, 11e6),
    )(place, *grads, vectors, gub)


def segment_lanes(bucket, lengths, queries_ext, keys_ext):
    row_count = queries_ext.shape[0]
    slots = lengths.shape[0]
    shape = (row_count, PAIR)
    row = lax.broadcasted_iota(jnp.int32, shape, 0)
    lane = lax.broadcasted_iota(jnp.int32, shape, 1) % HD
    passage = bucket[0] == 1
    segment = jnp.where(passage, row // PLEN, row // QLEN)
    position = jnp.where(passage, row % PLEN, row % QLEN)
    limit = jnp.zeros(shape, jnp.int32)
    for s in range(slots):
        limit = jnp.where(segment == s, lengths[s], limit)
    alive = position < limit
    same = segment == lane
    queries_ext[...] = jnp.where(same, 1.0, 0.0).astype(bf16)
    keys_ext[...] = jnp.where((lane < slots) & ~(same & alive), masked_score, 0.0).astype(bf16)


def attend_kernel(
    bucket, lengths, x, qw, kw, vw, qb, vb,
    q_out, k_out, v_out, context_out, lse_out,
    queries_ext, keys_ext, lse_all,
):
    pair = pl.program_id(0)
    row_count = x.shape[0]

    @pl.when(pair == 0)
    def _():
        segment_lanes(bucket, lengths, queries_ext, keys_ext)
        lse_all[...] = jnp.zeros_like(lse_all)

    weights = jnp.concatenate([qw[0], kw[0], vw[0]], axis=1)
    qb_row = qb[...]
    vb_row = vb[...]
    low_half = lax.broadcasted_iota(jnp.int32, (PLEN, PAIR), 1) < HD
    lane = lax.broadcasted_iota(jnp.int32, (PLEN, PAIR), 1)

    def block(b, carry):
        rows = pl.ds(pl.multiple_of(b * PLEN, PLEN), PLEN)
        qkv = dot(x[rows, :], weights)
        queries = ((qkv[:, :PAIR] + qb_row).astype(bf16).astype(f32) * HD ** (-0.5)).astype(bf16)
        keys = qkv[:, PAIR:2 * PAIR].astype(bf16)
        values = (qkv[:, 2 * PAIR:] + vb_row).astype(bf16)
        q_out[rows, :] = queries
        k_out[rows, :] = keys
        v_out[rows, :] = values
        q_ext = queries_ext[rows, :]
        k_ext = keys_ext[rows, :]
        ones = jnp.ones_like(values)
        sums, tops = [], []
        for half in range(2):
            mine = low_half if half == 0 else ~low_half
            scores = dot_nt(jnp.where(mine, queries, q_ext), jnp.where(mine, keys, k_ext))
            top = jnp.max(scores, axis=-1, keepdims=True)
            weight = jnp.exp(scores - top).astype(bf16)
            sums.append(dot(weight, jnp.where(mine, values, ones)))
            tops.append(top)
        numer = jnp.where(low_half, sums[0], sums[1])
        denom = pltpu.roll(jnp.where(low_half, sums[1], sums[0]), HD, 1)
        context_out[rows, :] = (numer / denom).astype(bf16)
        lse = jnp.where(low_half, tops[0], tops[1]) + jnp.log(denom)
        mine = (lane % HD) == pair
        lse_all[rows, :] = jnp.where(mine, lse, lse_all[rows, :])
        return carry

    lax.fori_loop(0, row_count // PLEN, block, 0)

    @pl.when(pair == pl.num_programs(0) - 1)
    def _():
        lse_out[...] = lse_all[...].T


def attend(bucket, lengths, x, weights, qb, vb):
    t, d = x.shape
    pairs = d // PAIR
    column = lambda m: pl.BlockSpec((1, d, PAIR), lambda p, *_: (m, 0, p))
    vector = pl.BlockSpec((1, PAIR), lambda p, *_: (0, p))
    tall = pl.BlockSpec((t, PAIR), lambda p, *_: (0, p))
    return call(
        attend_kernel, "attend", (pairs,),
        [whole((t, d)), column(0), column(1), column(2), vector, vector],
        [tall, tall, tall, tall, whole((PAIR, t))],
        [sds((t, d), bf16)] * 4 + [sds((PAIR, t), f32)],
        [pltpu.VMEM((t, PAIR), bf16), pltpu.VMEM((t, PAIR), bf16), pltpu.VMEM((t, PAIR), f32)],
        prefetch=2, cost=guess(15e9, 12e6),
    )(bucket, lengths, x, weights, weights, weights, qb, vb)


def attend_back_kernel(
    bucket, lengths, x_t, q, k, v, grad_context, lse, delta, qw, kw, vw, grad_inner,
    gqw, gkw, gvw, gqb, gvb, input_grad,
    queries_ext, keys_ext, grads,
):
    pair = pl.program_id(0)
    row_count = q.shape[0]

    @pl.when(pair == 0)
    def _():
        segment_lanes(bucket, lengths, queries_ext, keys_ext)

    low_half = lax.broadcasted_iota(jnp.int32, (PLEN, PAIR), 1) < HD

    def block(b, carry):
        rows = pl.ds(pl.multiple_of(b * PLEN, PLEN), PLEN)
        queries, keys, values, grad_ctx = q[rows, :], k[rows, :], v[rows, :], grad_context[rows, :]
        q_ext, k_ext = queries_ext[rows, :], keys_ext[rows, :]
        nothing = jnp.zeros_like(values)
        got = []
        for half in range(2):
            mine = low_half if half == 0 else ~low_half
            lse_row = lse[pl.ds(half * HD + pair, 1), rows]
            delta_row = delta[pl.ds(half * HD + pair, 1), rows]
            scores = dot_nt(jnp.where(mine, keys, k_ext), jnp.where(mine, queries, q_ext))
            probs = jnp.exp(scores - lse_row)
            grad_probs = dot_nt(jnp.where(mine, values, nothing), grad_ctx)
            grad_scores = (probs * (grad_probs - delta_row)).astype(bf16)
            grad_v = dot(probs.astype(bf16), grad_ctx)
            grad_k = dot(grad_scores, queries)
            grad_q = dot_tn(grad_scores, keys)
            got.append((grad_q, grad_k, grad_v))
        gq = (jnp.where(low_half, got[0][0], got[1][0]) * HD ** (-0.5)).astype(bf16)
        gk = jnp.where(low_half, got[0][1], got[1][1]).astype(bf16)
        gv = jnp.where(low_half, got[0][2], got[1][2]).astype(bf16)
        grads[rows, :PAIR] = gq
        grads[rows, PAIR:2 * PAIR] = gk
        grads[rows, 2 * PAIR:] = gv
        sum_q = jnp.sum(gq.astype(f32), axis=0, keepdims=True)
        sum_v = jnp.sum(gv.astype(f32), axis=0, keepdims=True)
        return (carry[0] + sum_q, carry[1] + sum_v)

    start = jnp.zeros((1, PAIR), f32)
    gqb[...], gvb[...] = lax.fori_loop(0, row_count // PLEN, block, (start, start))

    columns = grads[...]
    weight_grads = dot(x_t[...], columns)
    gqw[...] = weight_grads[:, :PAIR].astype(gqw.dtype)
    gkw[...] = weight_grads[:, PAIR:2 * PAIR].astype(gkw.dtype)
    gvw[...] = weight_grads[:, 2 * PAIR:].astype(gvw.dtype)

    @pl.when(pair == 0)
    def _():
        input_grad[...] = grad_inner[...]

    weights = jnp.concatenate([qw[0], kw[0], vw[0]], axis=1)
    input_grad[...] += dot_nt(columns, weights)


def attend_back(bucket, lengths, x_t, q, k, v, grad_context, lse, delta, weights, grad_inner):
    t, d = q.shape
    pairs = d // PAIR
    column = lambda m: pl.BlockSpec((1, d, PAIR), lambda p, *_: (m, 0, p))
    vector = pl.BlockSpec((1, PAIR), lambda p, *_: (0, p))
    tall = pl.BlockSpec((t, PAIR), lambda p, *_: (0, p))
    made = pl.BlockSpec((d, PAIR), lambda p, *_: (0, p))
    return call(
        attend_back_kernel, "attend_back", (pairs,),
        [whole((d, t)), tall, tall, tall, tall, whole((PAIR, t)), whole((PAIR, t)),
         column(0), column(1), column(2), whole((t, d))],
        [made, made, made, vector, vector, whole((t, d))],
        [sds((d, d), bf16)] * 3 + [sds((1, d), f32)] * 2 + [sds((t, d), f32)],
        [pltpu.VMEM((t, PAIR), bf16), pltpu.VMEM((t, PAIR), bf16), pltpu.VMEM((t, 3 * PAIR), bf16)],
        prefetch=2, cost=guess(30e9, 25e6),
    )(bucket, lengths, x_t, q, k, v, grad_context, lse, delta, weights, weights, weights, grad_inner)


def normed(v):
    centred = v - jnp.mean(v, axis=-1, keepdims=True)
    r = lax.rsqrt(jnp.mean(centred * centred, axis=-1, keepdims=True) + epsilon)
    return centred * r, r


def norm_back(dy, n, r, gain):
    dn = dy * gain
    return r * (dn - jnp.mean(dn, axis=-1, keepdims=True) - n * jnp.mean(dn * n, axis=-1, keepdims=True))


def gelu_parts(u):
    size = jnp.abs(u)
    below = 1.0 + (0.3275911 * 0.7071067811865476) * size
    t = pl.reciprocal(below, approx=True)
    t = t * (2.0 - below * t)
    poly = 0.5 * 1.061405429
    for c in (-1.453152027, 1.421413741, -0.284496736, 0.254829592):
        poly = poly * t + 0.5 * c
    bell = jnp.exp(u * u * -0.5)
    tail = poly * t * bell
    phi = jnp.where(u >= 0, 1.0 - tail, tail)
    return u * phi, phi + u * bell * 0.3989422804014327


def up_kernel(
    place, x, context, ow, ob, g1, b1, ub, u0, u1, u2, u3,
    n1_out, r1_out, low_out, act_out, slope_out, uw, sems,
):
    wide = act_out.shape[2]
    tall = u0.shape[2]
    copies = block_copies(
        place, (u0, u1, u2, u3), lambda i, j: uw.at[j, pl.ds(pl.multiple_of(i * tall, 16), tall), :], sems
    )

    @pl.when(pl.program_id(0) == 0)
    def _():
        for copy in copies:
            copy.start()

    attended = dot(context[...], ow[0]) + ob[...]
    n1, r1 = normed(x[...].astype(f32) + attended)
    n1_out[...] = n1
    r1_out[...] = jnp.broadcast_to(r1, r1_out.shape)
    low = (n1 * g1[...] + b1[...]).astype(bf16)
    low_out[...] = low

    @pl.when(pl.program_id(0) == 0)
    def _():
        for copy in copies:
            copy.wait()

    each = uw.shape[2] // wide
    for j in range(uw.shape[0]):
        hidden = dot(low, uw[j]) + ub[j:j + 1, :]
        active, slope = gelu_parts(hidden)
        active, slope = active.astype(bf16), slope.astype(bf16)
        for c in range(each):
            act_out[j * each + c] = active[:, c * wide:(c + 1) * wide]
            slope_out[j * each + c] = slope[:, c * wide:(c + 1) * wide]


def up(place, x, context, weights, ob, g1, b1, ub, blocks):
    t, d = x.shape
    half, depth, tall, wide = blocks[0].shape
    f, parts = 2 * half, 2 * depth
    narrow = f * wide // parts
    rows = pl.BlockSpec((ROWS, d), lambda r, *_: (r, 0))
    high = pl.BlockSpec((parts, ROWS, narrow), lambda r, *_: (0, r, 0))
    return call(
        up_kernel, "up", (t // ROWS,),
        [rows, rows, pl.BlockSpec((1, d, d), lambda r, *_: (3, 0, 0)), whole((1, d)), whole((1, d)), whole((1, d)),
         whole(ub.shape)] + [pl.BlockSpec(memory_space=pl.ANY)] * 4,
        [rows, pl.BlockSpec((ROWS, 128), lambda r, *_: (r, 0)), rows, high, high, whole((f, d, wide))],
        [sds((t, d), f32), sds((t, 128), f32), sds((t, d), bf16), sds((parts, t, narrow), bf16),
         sds((parts, t, narrow), bf16), sds((f, d, wide), bf16)],
        [pltpu.SemaphoreType.DMA((f * parts,))],
        prefetch=1, cost=guess(12e9, 31e6),
    )(place, x, context, weights, ob, g1, b1, ub, *blocks)


def down_kernel(
    place, bucket, lengths, act_rows, n1, g1, b1, db, g2, b2, cotangent, act_part, d0, d1, d2, d3,
    out, pooled, mixed_out, branch_out, gdb, gg2, gb2, send, keep, dw,
    branch_t, counts, sems,
):
    step = pl.program_id(0)
    tiles = branch_t.shape[1] // ROWS
    parts = dw.shape[0]
    f, _, tall, _ = send.shape
    depth = parts // 2
    copies = block_copies(
        place, (d0, d1, d2, d3), lambda i, j: dw.at[i, pl.ds(pl.multiple_of(j * tall, 16), tall), :], sems
    )

    @pl.when(step == 0)
    def _():
        for copy in copies:
            copy.start()
        pooled[...] = jnp.zeros_like(pooled)
        counts[...] = jnp.zeros_like(counts)
        gdb[...] = jnp.zeros_like(gdb)
        gg2[...] = jnp.zeros_like(gg2)
        gb2[...] = jnp.zeros_like(gb2)
        for copy in copies:
            copy.wait()

    @pl.when(step < tiles)
    def _():
        branch = dot_nt(act_rows[0], dw[0])
        for i in range(1, parts):
            branch += dot_nt(act_rows[i], dw[i])
        residual = n1[...] * g1[...] + b1[...] + (branch + db[...])
        n2, r2 = normed(residual)
        result = n2 * g2[...] + b2[...]
        out[...] = result.astype(bf16)
        slots = pooled.shape[0]
        shape = (slots, ROWS)
        slot = lax.broadcasted_iota(jnp.int32, shape, 0)
        row = lax.broadcasted_iota(jnp.int32, shape, 1) + step * ROWS
        passage = bucket[0] == 1
        segment = jnp.where(passage, row // PLEN, row // QLEN)
        position = jnp.where(passage, row % PLEN, row % QLEN)
        limit = jnp.zeros(shape, jnp.int32)
        for s in range(slots):
            limit = jnp.where(slot == s, lengths[s], limit)
        chosen = jnp.where((segment == slot) & (position < limit), 1.0, 0.0)
        picked = chosen.astype(bf16)
        high = result.astype(bf16)
        rest = result - high.astype(f32)
        middle = rest.astype(bf16)
        last = (rest - middle.astype(f32)).astype(bf16)
        pooled[...] += dot(picked, high) + dot(picked, middle) + dot(picked, last)
        counts[...] += jnp.broadcast_to(jnp.sum(chosen, axis=1, keepdims=True), counts.shape)
        dy = cotangent[...].astype(f32)
        gg2[...] += jnp.sum(dy * n2, axis=0, keepdims=True)
        gb2[...] += jnp.sum(dy, axis=0, keepdims=True)
        mixed = norm_back(dy, n2, r2, g2[...])
        mixed_out[...] = mixed
        low = mixed.astype(bf16)
        branch_out[...] = low
        gdb[...] += jnp.sum(low.astype(f32), axis=0, keepdims=True)
        for tile in range(tiles):
            @pl.when(step == tile)
            def _():
                branch_t[:, tile * ROWS:(tile + 1) * ROWS] = low.T

    @pl.when(step == tiles - 1)
    def _():
        pooled[...] = pooled[...] / jnp.maximum(counts[...], 1.0)[:, :1]

    def part(n, target):
        found = dot(branch_t[...], act_part[0]).astype(bf16)
        for j in range(f):
            target[slot_of(place, n, j, depth, f), 0] = found[j * tall:(j + 1) * tall]

    @pl.when((step >= tiles) & (step < tiles + depth))
    def _():
        part(1, send)

    @pl.when(step >= tiles + depth)
    def _():
        part(0, keep)


def down(place, bucket, lengths, active, n1, g1, b1, db, g2, b2, cotangent, blocks):
    parts, t, narrow = active.shape
    d = n1.shape[1]
    tiles = t // ROWS
    slots = lengths.shape[0]
    half, depth, tall, _ = blocks[0].shape
    f = 2 * half
    early = lambda s: jnp.minimum(s, tiles - 1)
    late = lambda s, place: place[(jnp.maximum(s - tiles, 0) + depth) % parts]
    made = lambda first: pl.BlockSpec(
        (f, 1, tall, narrow), lambda s, *_: (0, jnp.clip(s - tiles - first, 0, depth - 1), 0, 0)
    )
    rows = pl.BlockSpec((ROWS, d), lambda s, *_: (early(s), 0))
    vector = whole((1, d))
    return call(
        down_kernel, "down", (tiles + parts,),
        [pl.BlockSpec((parts, ROWS, narrow), lambda s, *_: (0, early(s), 0)), rows, vector, vector,
         vector, vector, vector, rows,
         pl.BlockSpec((1, t, narrow), lambda s, place, *_: (late(s, place), 0, 0))]
        + [pl.BlockSpec(memory_space=pl.ANY)] * 4,
        [rows, whole((slots, d)), rows, rows, vector, vector, vector, made(0), made(depth),
         whole((parts, d, narrow))],
        [sds((t, d), bf16), sds((slots, d), f32), sds((t, d), f32), sds((t, d), bf16)]
        + [sds((1, d), f32)] * 3 + [sds((f, depth, tall, narrow), bf16)] * 2 + [sds((parts, d, narrow), bf16)],
        [pltpu.VMEM((d, t), bf16), pltpu.VMEM((slots, 128), f32), pltpu.SemaphoreType.DMA((f * parts,))],
        prefetch=3, cost=guess(12e9, 35e6),
    )(place, bucket, lengths, active, n1, g1, b1, db, g2, b2, cotangent, active, *blocks)


def feed_back_kernel(
    place, branch, slope, dw, uw, low_t, mixed, n1, r1, g1, context, ow,
    send, keep, gub, inner_out, gg1, gb1, gob, gow, grad_context, delta_out,
    hidden, grad_normed, attended, found,
):
    j = pl.program_id(0)
    _, depth, tall, _ = send.shape
    each, t, narrow = slope.shape
    d = branch.shape[1]
    tiles = t // ROWS

    def gelu_rows(r, sums):
        rows = pl.ds(pl.multiple_of(r * ROWS, ROWS), ROWS)
        found = []
        for c in range(each):
            grad = (slope[c, rows, :].astype(f32) * dot(branch[rows, :], dw[c])).astype(bf16)
            hidden[rows, c * narrow:(c + 1) * narrow] = grad
            found.append(sums[c] + jnp.sum(grad.astype(f32), axis=0, keepdims=True))
        return tuple(found)

    sums = lax.fori_loop(0, tiles, gelu_rows, (jnp.zeros((1, narrow), f32),) * each)
    for c in range(each):
        gub[0, :, c * narrow:(c + 1) * narrow] = sums[c]
    found[...] = dot(low_t[...], hidden[...]).astype(bf16)
    for n, target in ((1, send), (0, keep)):
        for slot in range(depth):
            i = row_of(place, n, slot, depth)
            target[0, slot] = found[pl.ds(pl.multiple_of(i * tall, 16), tall), :]

    @pl.when(j == 0)
    def _():
        grad_normed[...] = mixed[...]

    def normed_rows(r, carry):
        rows = pl.ds(pl.multiple_of(r * ROWS, ROWS), ROWS)
        grad_normed[rows, :] += dot_nt(hidden[rows, :], uw[0])
        return carry

    lax.fori_loop(0, tiles, normed_rows, 0)

    @pl.when(j == pl.num_programs(0) - 1)
    def _():
        feature = lax.broadcasted_iota(jnp.int32, (128, d), 1)
        slot = lax.broadcasted_iota(jnp.int32, (128, d), 0)
        head = jnp.where(slot < HD, 2 * slot, 2 * (slot - HD) + 1)
        pick = jnp.where(feature // HD == head, 1.0, 0.0).astype(bf16)

        def inner_rows(r, sums):
            rows = pl.ds(pl.multiple_of(r * ROWS, ROWS), ROWS)
            dy, n = grad_normed[rows, :], n1[rows, :]
            inner = norm_back(dy, n, r1[rows, :1], g1[...])
            inner_out[rows, :] = inner
            low = inner.astype(bf16)
            attended[rows, :] = low
            grad_ctx = dot_nt(low, ow[0]).astype(bf16)
            grad_context[rows, :] = grad_ctx
            both = grad_ctx.astype(f32) * context[rows, :].astype(f32)
            high = both.astype(bf16)
            rest = (both - high.astype(f32)).astype(bf16)
            delta_out[:, rows] = dot_nt(pick, high) + dot_nt(pick, rest)
            return (
                sums[0] + jnp.sum(dy * n, axis=0, keepdims=True),
                sums[1] + jnp.sum(dy, axis=0, keepdims=True),
                sums[2] + jnp.sum(low.astype(f32), axis=0, keepdims=True),
            )

        gg1[...], gb1[...], gob[...] = lax.fori_loop(0, tiles, inner_rows, (jnp.zeros((1, d), f32),) * 3)
        gow[...] = dot_tn(context[...], attended[...]).astype(bf16)


def feed_back(place, branch, slope, dw, uw, low_t, mixed, n1, r1, g1, context, weights):
    parts, t, narrow = slope.shape
    f, d, wide = uw.shape
    each, depth, tall = parts // f, parts // 2, d // parts
    made = lambda n: pl.BlockSpec(
        (1, depth, tall, wide), lambda j, place: (slot_of(place, n, j, depth, f), 0, 0, 0)
    )
    vector = whole((1, d))
    return call(
        feed_back_kernel, "feed_back", (f,),
        [whole((t, d)), pl.BlockSpec((each, t, narrow), lambda j, *_: (j, 0, 0)),
         pl.BlockSpec((each, d, narrow), lambda j, *_: (j, 0, 0)), pl.BlockSpec((1, d, wide), lambda j, *_: (j, 0, 0)),
         whole((d, t)), whole((t, d)), whole((t, d)), whole((t, 128)), vector, whole((t, d)),
         pl.BlockSpec((1, d, d), lambda j, *_: (3, 0, 0))],
        [made(1), made(0), pl.BlockSpec((1, 1, wide), lambda j, *_: (j, 0, 0)),
         whole((t, d)), vector, vector, vector, whole((d, d)), whole((t, d)), whole((128, t))],
        [sds((f, depth, tall, wide), bf16)] * 2 + [sds((f, 1, wide), f32), sds((t, d), f32)] + [sds((1, d), f32)] * 3
        + [sds((d, d), bf16), sds((t, d), bf16), sds((128, t), f32)],
        [pltpu.VMEM((t, wide), bf16), pltpu.VMEM((t, d), f32), pltpu.VMEM((t, d), bf16), pltpu.VMEM((d, wide), bf16)],
        prefetch=1, cost=guess(18e9, 45e6),
    )(place, branch, slope, dw, uw, low_t, mixed, n1, r1, g1, context, weights)


def shards(
    tokens, bucket, lengths, cotangent,
    query_weight, query_bias, key_weight, value_weight, value_bias, out_weight, out_bias,
    norm1_gain, norm1_bias, up_weight, up_bias, down_weight, down_bias, norm2_gain, norm2_bias,
):
    t, d = tokens.shape
    dp, fsdp = lax.axis_size("dp"), lax.axis_size("fsdp")
    lengths = lengths[0]

    place = places()
    spare = jnp.zeros((13, 4 * d // fsdp), bf16)
    block = jnp.concatenate([
        jnp.concatenate([query_weight, key_weight, value_weight, out_weight], axis=1),
        jnp.concatenate([query_bias, value_bias, out_bias, norm1_gain])[None],
        jnp.concatenate([norm1_bias, down_bias, norm2_gain, norm2_bias])[None],
        up_bias[None],
        spare,
    ])
    attention_blocks = gather_blocks(block)
    up_blocks = gather_blocks(up_weight)
    down_blocks = gather_blocks(down_weight.T)

    weights, vectors, ub = assemble(place, attention_blocks)
    qb, vb, ob, g1 = (vectors[m, 0:1] for m in range(4))
    b1, db, g2, b2 = (vectors[m, 1:2] for m in range(4))
    ub = ub[:, 2]

    q, k, v, context, lse = attend(bucket, lengths, tokens, weights, qb, vb)
    n1, r1, low, active, slope, uw = up(place, tokens, context, weights, ob, g1, b1, ub, up_blocks)
    out, pooled, mixed, branch, gdb, gg2, gb2, send_d, keep_d, dw = down(
        place, bucket, lengths, active, n1, g1, b1, db, g2, b2, cotangent, down_blocks
    )
    made_d = scatter_blocks(keep_d, send_d)
    send_u, keep_u, gub, inner, gg1, gb1, gob, gow, grad_context, delta = feed_back(
        place, branch, slope, dw, uw, low.T, mixed, n1, r1, g1, context, weights
    )
    made_u = scatter_blocks(keep_u, send_u)
    gqw, gkw, gvw, gqb, gvb, input_grad = attend_back(
        bucket, lengths, tokens.T, q, k, v, grad_context, lse, delta, weights, inner
    )
    firsts = jnp.stack([gqb, gvb, gob, gg1])
    seconds = jnp.stack([gb1, gdb, gg2, gb2])
    vectors = jnp.concatenate([firsts, seconds, jnp.zeros((4, 14, d), f32)], axis=1)
    send_a, keep_a = pack(place, (gqw, gkw, gvw, gow), vectors, gub)
    made_a = scatter_blocks(keep_a, send_a)

    tall, narrow = d // dp, d // fsdp
    made = [made_a[:tall, m * narrow:(m + 1) * narrow] for m in range(4)]
    rows = [made_a[tall + n, m * narrow:(m + 1) * narrow] for n in range(2) for m in range(4)]
    return (
        out, pooled, input_grad, made[0], rows[0], made[1], made[2], rows[1], made[3], rows[2], rows[3], rows[4],
        made_u, made_a[tall + 2], made_d.T, rows[5], rows[6], rows[7],
    )


def solution(mesh):
    tall, square, vector = P(("dp", "fsdp"), None), P("dp", "fsdp"), P("fsdp")
    in_specs = (
        tall, P(("dp", "fsdp")), tall, tall, square, vector, square, square, vector, square, vector,
        vector, vector, square, vector, square, vector, vector, vector,
    )
    out_specs = (
        tall, tall, tall, square, vector, square, square, vector, square, vector, vector, vector,
        square, vector, square, vector, vector, vector,
    )
    return jax.shard_map(shards, mesh=mesh, in_specs=in_specs, out_specs=out_specs, check_vma=False)
```

```python
import functools

import jax
import jax.numpy as jnp
from jax import lax
from jax.experimental import pallas as pl
from jax.experimental.pallas import tpu as pltpu
from jax.sharding import PartitionSpec as P

H = 12
HD = 64
PLEN = 512
QLEN = 128
PAIR = 2 * HD
ROWS = 256

epsilon = 1e-06
masked_score = -1e30
f32 = jnp.float32
bf16 = jnp.bfloat16
LIMIT = 60 * 1024 * 1024


def dot(left, right):
    return jnp.dot(left, right, preferred_element_type=f32)


def dot_nt(left, right):
    return lax.dot_general(left, right, (((1,), (1,)), ((), ())), preferred_element_type=f32)


def dot_tn(left, right):
    return lax.dot_general(left, right, (((0,), (0,)), ((), ())), preferred_element_type=f32)


def call(kernel, name, grid, in_specs, out_specs, out_shape, scratch=(), prefetch=0, cost=None):
    return pl.pallas_call(
        kernel,
        name=name,
        grid_spec=pltpu.PrefetchScalarGridSpec(
            num_scalar_prefetch=prefetch,
            grid=grid,
            in_specs=in_specs,
            out_specs=out_specs,
            scratch_shapes=list(scratch),
        ),
        out_shape=out_shape,
        compiler_params=pltpu.CompilerParams(
            vmem_limit_bytes=LIMIT, dimension_semantics=("arbitrary",) * len(grid)
        ),
        cost_estimate=cost,
    )


def whole(shape):
    return pl.BlockSpec(shape, lambda *_: (0,) * len(shape))


def sds(shape, dtype):
    return jax.ShapeDtypeStruct(shape, dtype)


def guess(flops, nbytes):
    return pl.CostEstimate(flops=int(flops), bytes_accessed=int(nbytes), transcendentals=0)


def reverse(s, bits):
    return sum(((s >> b) & 1) << (bits - 1 - b) for b in range(bits))


def axis_facts():
    dp, fsdp = lax.axis_size("dp"), lax.axis_size("fsdp")
    return dp, fsdp, dp // 2, fsdp.bit_length() - 1


def along_z(hop):
    dp = lax.axis_size("dp")
    return [(d, (d + 2 * hop) % dp) for d in range(dp)]


def across_cores():
    return [(d, d ^ 1) for d in range(lax.axis_size("dp"))]


def along_bit(r):
    dp, fsdp, _, bits = axis_facts()
    pairs = []
    for d in range(dp):
        flip = 1 << (r if d % 2 == 0 else bits - 1 - r)
        pairs += [(d * fsdp + f, d * fsdp + (f ^ flip)) for f in range(fsdp)]
    return pairs


class Gather:
    def __init__(self, block):
        self.block, self.round, self.blocks = block, -1, None

    def stage(self):
        _, _, depth, bits = axis_facts()
        if self.round < 0:
            return [(self.block, "dp", along_z(s)) for s in range(1, depth)]
        if self.round < bits:
            return [(self.held, ("dp", "fsdp"), along_bit(self.round))]
        return [(v, "dp", across_cores()) for v in self.own]

    def take(self, got):
        bits = axis_facts()[3]
        if self.round < 0:
            self.held = jnp.stack([self.block] + got)[None]
        elif self.round < bits - 1:
            self.held = jnp.concatenate([self.held] + got)
        elif self.round < bits:
            self.own = [self.held] + got
        else:
            self.blocks = self.own + got
        self.round += 1

    def done(self):
        return self.blocks is not None


def add(left, right):
    return (left.astype(f32) + right.astype(f32)).astype(bf16)


class Scatter:
    def __init__(self, keep, send):
        self.keep, self.send, self.round, self.total = keep, [send], axis_facts()[3], None

    def stage(self):
        _, _, depth, bits = axis_facts()
        if self.round == bits:
            return [(self.send[0], "dp", across_cores())]
        if self.round >= 0:
            return [(self.send[0], ("dp", "fsdp"), along_bit(self.round))]
        return [(self.send[s - 1], "dp", along_z(-s)) for s in range(1, depth)]

    def take(self, got):
        depth = axis_facts()[2]
        keep = self.keep
        if self.round > 0:
            half = keep.shape[0] // 2
            self.send = [add(keep[half:], got[0][half:])]
            self.keep = add(keep[:half], got[0][:half])
        elif self.round == 0:
            self.send = [add(keep[0, s], got[0][0, s]) for s in range(1, depth)]
            self.keep = keep[0, 0].astype(f32) + got[0][0, 0].astype(f32)
        else:
            for part in got:
                keep = keep + part.astype(f32)
            self.total = keep
        self.round -= 1

    def done(self):
        return self.total is not None


def beside(moves, compute=None, args=()):
    moves = [move for move in moves if not move.done()]
    stages = [move.stage() for move in moves]
    args, arrays = lax.optimization_barrier((args, [[v for v, _, _ in stage] for stage in stages]))
    results = compute(*args) if compute else ()
    got = [
        [lax.ppermute(v, axis, perm) for v, (_, axis, perm) in zip(held, stage)]
        for held, stage in zip(arrays, stages)
    ]
    results, got = lax.optimization_barrier((results, got))
    for move, parts in zip(moves, got):
        move.take(parts)
    return results


def finish(move):
    while not move.done():
        beside([move])


def places():
    dp, fsdp, depth, bits = axis_facts()
    d, f = lax.axis_index("dp"), lax.axis_index("fsdp")
    z, core = d // 2, d % 2
    slot = jnp.arange(depth, dtype=jnp.int32)
    index = jnp.arange(fsdp, dtype=jnp.int32)
    mirror = sum((((index >> b) & 1) << (bits - 1 - b) for b in range(bits)), jnp.zeros_like(index))
    rows, slots, columns = [], [], []
    for n in range(2):
        there = core ^ n
        rows.append(2 * ((z - slot) % depth) + there)
        away = index ^ f
        mirrored = sum((((away >> b) & 1) << (bits - 1 - b) for b in range(bits)), jnp.zeros_like(index))
        slots.append(jnp.where(there == 0, away, mirrored))
        columns.append(f ^ jnp.where(there == 0, index, mirror))
    return jnp.concatenate(rows + slots + columns).astype(jnp.int32)


def row_of(place, n, slot, depth):
    return place[n * depth + slot]


def slot_of(place, n, j, depth, fsdp):
    return place[2 * depth + n * fsdp + j]


def column_of(place, n, s, depth, fsdp):
    return place[2 * depth + 2 * fsdp + n * fsdp + s]


def block_copies(place, arrays, target, sems):
    half, depth = arrays[0].shape[:2]
    fsdp = 2 * half
    copies = []
    for a, array in enumerate(arrays):
        for q in range(half):
            for slot in range(depth):
                i = row_of(place, a // 2, slot, depth)
                j = column_of(place, a // 2, (a % 2) * half + q, depth, fsdp)
                copies.append(pltpu.make_async_copy(array.at[q, slot], target(i, j), sems.at[len(copies)]))
    return copies


def assemble_kernel(place, own_low, own_high, other_low, other_high, weights, vectors, ub):
    step = pl.program_id(0)
    half, _, height, width = own_low.shape
    fsdp, depth, tall = 2 * half, pl.num_programs(0) // 2, height - 16
    narrow = width // 4

    def fill(n, low, high):
        pieces = []
        for j in range(fsdp):
            slot = slot_of(place, n, j, depth, fsdp)
            upper, q = slot >= half, lax.rem(slot, half)
            pieces.append(jnp.where(upper, high[q, 0].astype(f32), low[q, 0].astype(f32)))
        for m in range(4):
            row = jnp.concatenate([p[:, m * narrow:(m + 1) * narrow] for p in pieces], axis=1)
            weights[m] = row[:tall].astype(bf16)
            vectors[m] = row[tall:]
        for j in range(fsdp):
            ub[j] = pieces[j][tall:]

    @pl.when(step < depth)
    def _():
        fill(0, own_low, own_high)

    @pl.when(step >= depth)
    def _():
        fill(1, other_low, other_high)


def assemble(place, arrays):
    half, depth, height, width = arrays[0].shape
    fsdp, tall, d = 2 * half, height - 16, half * width // 2
    own = pl.BlockSpec((half, 1, height, width), lambda s, place: (0, jnp.minimum(s, depth - 1), 0, 0))
    other = pl.BlockSpec((half, 1, height, width), lambda s, place: (0, jnp.maximum(s - depth, 0), 0, 0))
    return call(
        assemble_kernel, "assemble", (2 * depth,),
        [own, own, other, other],
        [pl.BlockSpec((4, tall, d), lambda s, place: (0, place[s], 0)), whole((4, 16, d)), whole((fsdp, 16, width))],
        [sds((4, 2 * depth * tall, d), bf16), sds((4, 16, d), f32), sds((fsdp, 16, width), f32)],
        prefetch=1, cost=guess(1e9, 11e6),
    )(place, *arrays)


def pack_kernel(place, gq, gk, gv, go, vectors, gub, send, keep):
    step = pl.program_id(0)
    fsdp, _, height, width = send.shape
    depth, tall, narrow = pl.num_programs(0) // 2, height - 16, width // 4

    def fill(n, out):
        for j in range(fsdp):
            slot = slot_of(place, n, j, depth, fsdp)
            columns = slice(j * narrow, (j + 1) * narrow)
            out[slot, 0, :tall, :] = jnp.concatenate(
                [g[:, columns].astype(f32) for g in (gq, gk, gv, go)], axis=1
            ).astype(bf16)
            slab = jnp.concatenate([vectors[m, :, columns] for m in range(4)], axis=1)
            third = lax.broadcasted_iota(jnp.int32, slab.shape, 0) == 2
            out[slot, 0, tall:, :] = jnp.where(third, gub[j], slab).astype(bf16)

    @pl.when(step < depth)
    def _():
        fill(1, send)

    @pl.when(step >= depth)
    def _():
        fill(0, keep)


def pack(place, grads, vectors, gub):
    d = grads[0].shape[0]
    dp, fsdp, depth, _ = axis_facts()
    tall, width = d // dp, 4 * d // fsdp
    rows = pl.BlockSpec((tall, d), lambda s, place: (place[(s + depth) % (2 * depth)], 0))
    sent = pl.BlockSpec((fsdp, 1, tall + 16, width), lambda s, place: (0, jnp.minimum(s, depth - 1), 0, 0))
    kept = pl.BlockSpec((fsdp, 1, tall + 16, width), lambda s, place: (0, jnp.maximum(s - depth, 0), 0, 0))
    return call(
        pack_kernel, "pack", (2 * depth,),
        [rows, rows, rows, rows, whole((4, 16, d)), whole((fsdp, 1, width))],
        [sent, kept],
        [sds((fsdp, depth, tall + 16, width), bf16)] * 2,
        prefetch=1, cost=guess(1e9, 11e6),
    )(place, *grads, vectors, gub)


def segment_lanes(bucket, lengths, queries_ext, keys_ext):
    row_count = queries_ext.shape[0]
    slots = lengths.shape[0]
    shape = (row_count, PAIR)
    row = lax.broadcasted_iota(jnp.int32, shape, 0)
    lane = lax.broadcasted_iota(jnp.int32, shape, 1) % HD
    passage = bucket[0] == 1
    segment = jnp.where(passage, row // PLEN, row // QLEN)
    position = jnp.where(passage, row % PLEN, row % QLEN)
    limit = jnp.zeros(shape, jnp.int32)
    for s in range(slots):
        limit = jnp.where(segment == s, lengths[s], limit)
    alive = position < limit
    same = segment == lane
    queries_ext[...] = jnp.where(same, 1.0, 0.0).astype(bf16)
    keys_ext[...] = jnp.where((lane < slots) & ~(same & alive), masked_score, 0.0).astype(bf16)


def attend_kernel(
    bucket, lengths, x, qw, kw, vw, qb, vb,
    q_out, k_out, v_out, context_out, lse_out,
    queries_ext, keys_ext, lse_all,
):
    pair = pl.program_id(0)
    row_count = x.shape[0]

    @pl.when(pair == 0)
    def _():
        segment_lanes(bucket, lengths, queries_ext, keys_ext)
        lse_all[...] = jnp.zeros_like(lse_all)

    weights = jnp.concatenate([qw[0], kw[0], vw[0]], axis=1)
    qb_row = qb[...]
    vb_row = vb[...]
    low_half = lax.broadcasted_iota(jnp.int32, (PLEN, PAIR), 1) < HD
    lane = lax.broadcasted_iota(jnp.int32, (PLEN, PAIR), 1)

    def block(b, carry):
        rows = pl.ds(pl.multiple_of(b * PLEN, PLEN), PLEN)
        qkv = dot(x[rows, :], weights)
        queries = ((qkv[:, :PAIR] + qb_row).astype(bf16).astype(f32) * HD ** (-0.5)).astype(bf16)
        keys = qkv[:, PAIR:2 * PAIR].astype(bf16)
        values = (qkv[:, 2 * PAIR:] + vb_row).astype(bf16)
        q_out[rows, :] = queries
        k_out[rows, :] = keys
        v_out[rows, :] = values
        q_ext = queries_ext[rows, :]
        k_ext = keys_ext[rows, :]
        ones = jnp.ones_like(values)
        sums, tops = [], []
        for half in range(2):
            mine = low_half if half == 0 else ~low_half
            scores = dot_nt(jnp.where(mine, queries, q_ext), jnp.where(mine, keys, k_ext))
            top = jnp.max(scores, axis=-1, keepdims=True)
            weight = jnp.exp(scores - top).astype(bf16)
            sums.append(dot(weight, jnp.where(mine, values, ones)))
            tops.append(top)
        numer = jnp.where(low_half, sums[0], sums[1])
        denom = pltpu.roll(jnp.where(low_half, sums[1], sums[0]), HD, 1)
        context_out[rows, :] = (numer / denom).astype(bf16)
        lse = jnp.where(low_half, tops[0], tops[1]) + jnp.log(denom)
        mine = (lane % HD) == pair
        lse_all[rows, :] = jnp.where(mine, lse, lse_all[rows, :])
        return carry

    lax.fori_loop(0, row_count // PLEN, block, 0)

    @pl.when(pair == pl.num_programs(0) - 1)
    def _():
        lse_out[...] = lse_all[...].T


def attend(bucket, lengths, x, weights, qb, vb):
    t, d = x.shape
    pairs = d // PAIR
    column = lambda m: pl.BlockSpec((1, d, PAIR), lambda p, *_: (m, 0, p))
    vector = pl.BlockSpec((1, PAIR), lambda p, *_: (0, p))
    tall = pl.BlockSpec((t, PAIR), lambda p, *_: (0, p))
    return call(
        attend_kernel, "attend", (pairs,),
        [whole((t, d)), column(0), column(1), column(2), vector, vector],
        [tall, tall, tall, tall, whole((PAIR, t))],
        [sds((t, d), bf16)] * 4 + [sds((PAIR, t), f32)],
        [pltpu.VMEM((t, PAIR), bf16), pltpu.VMEM((t, PAIR), bf16), pltpu.VMEM((t, PAIR), f32)],
        prefetch=2, cost=guess(15e9, 12e6),
    )(bucket, lengths, x, weights, weights, weights, qb, vb)


def attend_back_kernel(
    bucket, lengths, x_t, q, k, v, grad_context, lse, delta, qw, kw, vw, grad_inner,
    gqw, gkw, gvw, gqb, gvb, input_grad,
    queries_ext, keys_ext, grads,
):
    pair = pl.program_id(0)
    row_count = q.shape[0]

    @pl.when(pair == 0)
    def _():
        segment_lanes(bucket, lengths, queries_ext, keys_ext)

    low_half = lax.broadcasted_iota(jnp.int32, (PLEN, PAIR), 1) < HD

    def block(b, carry):
        rows = pl.ds(pl.multiple_of(b * PLEN, PLEN), PLEN)
        queries, keys, values, grad_ctx = q[rows, :], k[rows, :], v[rows, :], grad_context[rows, :]
        q_ext, k_ext = queries_ext[rows, :], keys_ext[rows, :]
        nothing = jnp.zeros_like(values)
        got = []
        for half in range(2):
            mine = low_half if half == 0 else ~low_half
            lse_row = lse[pl.ds(half * HD + pair, 1), rows]
            delta_row = delta[pl.ds(half * HD + pair, 1), rows]
            scores = dot_nt(jnp.where(mine, keys, k_ext), jnp.where(mine, queries, q_ext))
            probs = jnp.exp(scores - lse_row)
            grad_probs = dot_nt(jnp.where(mine, values, nothing), grad_ctx)
            grad_scores = (probs * (grad_probs - delta_row)).astype(bf16)
            grad_v = dot(probs.astype(bf16), grad_ctx)
            grad_k = dot(grad_scores, queries)
            grad_q = dot_tn(grad_scores, keys)
            got.append((grad_q, grad_k, grad_v))
        gq = (jnp.where(low_half, got[0][0], got[1][0]) * HD ** (-0.5)).astype(bf16)
        gk = jnp.where(low_half, got[0][1], got[1][1]).astype(bf16)
        gv = jnp.where(low_half, got[0][2], got[1][2]).astype(bf16)
        grads[rows, :PAIR] = gq
        grads[rows, PAIR:2 * PAIR] = gk
        grads[rows, 2 * PAIR:] = gv
        sum_q = jnp.sum(gq.astype(f32), axis=0, keepdims=True)
        sum_v = jnp.sum(gv.astype(f32), axis=0, keepdims=True)
        return (carry[0] + sum_q, carry[1] + sum_v)

    start = jnp.zeros((1, PAIR), f32)
    gqb[...], gvb[...] = lax.fori_loop(0, row_count // PLEN, block, (start, start))

    columns = grads[...]
    weight_grads = dot(x_t[...], columns)
    gqw[...] = weight_grads[:, :PAIR].astype(gqw.dtype)
    gkw[...] = weight_grads[:, PAIR:2 * PAIR].astype(gkw.dtype)
    gvw[...] = weight_grads[:, 2 * PAIR:].astype(gvw.dtype)

    @pl.when(pair == 0)
    def _():
        input_grad[...] = grad_inner[...]

    weights = jnp.concatenate([qw[0], kw[0], vw[0]], axis=1)
    input_grad[...] += dot_nt(columns, weights)


def attend_back(bucket, lengths, x_t, q, k, v, grad_context, lse, delta, weights, grad_inner):
    t, d = q.shape
    pairs = d // PAIR
    column = lambda m: pl.BlockSpec((1, d, PAIR), lambda p, *_: (m, 0, p))
    vector = pl.BlockSpec((1, PAIR), lambda p, *_: (0, p))
    tall = pl.BlockSpec((t, PAIR), lambda p, *_: (0, p))
    made = pl.BlockSpec((d, PAIR), lambda p, *_: (0, p))
    return call(
        attend_back_kernel, "attend_back", (pairs,),
        [whole((d, t)), tall, tall, tall, tall, whole((PAIR, t)), whole((PAIR, t)),
         column(0), column(1), column(2), whole((t, d))],
        [made, made, made, vector, vector, whole((t, d))],
        [sds((d, d), bf16)] * 3 + [sds((1, d), f32)] * 2 + [sds((t, d), f32)],
        [pltpu.VMEM((t, PAIR), bf16), pltpu.VMEM((t, PAIR), bf16), pltpu.VMEM((t, 3 * PAIR), bf16)],
        prefetch=2, cost=guess(30e9, 25e6),
    )(bucket, lengths, x_t, q, k, v, grad_context, lse, delta, weights, weights, weights, grad_inner)


def normed(v):
    centred = v - jnp.mean(v, axis=-1, keepdims=True)
    r = lax.rsqrt(jnp.mean(centred * centred, axis=-1, keepdims=True) + epsilon)
    return centred * r, r


def norm_back(dy, n, r, gain):
    dn = dy * gain
    return r * (dn - jnp.mean(dn, axis=-1, keepdims=True) - n * jnp.mean(dn * n, axis=-1, keepdims=True))


def gelu_parts(u):
    size = jnp.abs(u)
    below = 1.0 + (0.3275911 * 0.7071067811865476) * size
    t = pl.reciprocal(below, approx=True)
    t = t * (2.0 - below * t)
    poly = 0.5 * 1.061405429
    for c in (-1.453152027, 1.421413741, -0.284496736, 0.254829592):
        poly = poly * t + 0.5 * c
    bell = jnp.exp(u * u * -0.5)
    tail = poly * t * bell
    phi = jnp.where(u >= 0, 1.0 - tail, tail)
    return u * phi, phi + u * bell * 0.3989422804014327


def up_kernel(
    place, x, context, ow, ob, g1, b1, ub, u0, u1, u2, u3,
    n1_out, r1_out, low_out, act_out, slope_out, uw, sems,
):
    wide = act_out.shape[2]
    tall = u0.shape[2]
    copies = block_copies(
        place, (u0, u1, u2, u3), lambda i, j: uw.at[j, pl.ds(pl.multiple_of(i * tall, 16), tall), :], sems
    )

    @pl.when(pl.program_id(0) == 0)
    def _():
        for copy in copies:
            copy.start()

    attended = dot(context[...], ow[0]) + ob[...]
    n1, r1 = normed(x[...].astype(f32) + attended)
    n1_out[...] = n1
    r1_out[...] = jnp.broadcast_to(r1, r1_out.shape)
    low = (n1 * g1[...] + b1[...]).astype(bf16)
    low_out[...] = low

    @pl.when(pl.program_id(0) == 0)
    def _():
        for copy in copies:
            copy.wait()

    each = uw.shape[2] // wide
    for j in range(uw.shape[0]):
        hidden = dot(low, uw[j]) + ub[j:j + 1, :]
        active, slope = gelu_parts(hidden)
        active, slope = active.astype(bf16), slope.astype(bf16)
        for c in range(each):
            act_out[j * each + c] = active[:, c * wide:(c + 1) * wide]
            slope_out[j * each + c] = slope[:, c * wide:(c + 1) * wide]


def up(place, x, context, weights, ob, g1, b1, ub, blocks):
    t, d = x.shape
    half, depth, tall, wide = blocks[0].shape
    f, parts = 2 * half, 2 * depth
    narrow = f * wide // parts
    rows = pl.BlockSpec((ROWS, d), lambda r, *_: (r, 0))
    high = pl.BlockSpec((parts, ROWS, narrow), lambda r, *_: (0, r, 0))
    return call(
        up_kernel, "up", (t // ROWS,),
        [rows, rows, pl.BlockSpec((1, d, d), lambda r, *_: (3, 0, 0)), whole((1, d)), whole((1, d)), whole((1, d)),
         whole(ub.shape)] + [pl.BlockSpec(memory_space=pl.ANY)] * 4,
        [rows, pl.BlockSpec((ROWS, 128), lambda r, *_: (r, 0)), rows, high, high, whole((f, d, wide))],
        [sds((t, d), f32), sds((t, 128), f32), sds((t, d), bf16), sds((parts, t, narrow), bf16),
         sds((parts, t, narrow), bf16), sds((f, d, wide), bf16)],
        [pltpu.SemaphoreType.DMA((f * parts,))],
        prefetch=1, cost=guess(12e9, 31e6),
    )(place, x, context, weights, ob, g1, b1, ub, *blocks)


def down_kernel(
    place, bucket, lengths, act_rows, n1, g1, b1, db, g2, b2, cotangent, act_part, d0, d1, d2, d3,
    out, pooled, mixed_out, branch_out, gdb, gg2, gb2, send, keep, dw,
    branch_t, counts, sems,
):
    step = pl.program_id(0)
    tiles = branch_t.shape[1] // ROWS
    parts = dw.shape[0]
    f, _, tall, _ = send.shape
    depth = parts // 2
    copies = block_copies(
        place, (d0, d1, d2, d3), lambda i, j: dw.at[i, pl.ds(pl.multiple_of(j * tall, 16), tall), :], sems
    )

    @pl.when(step == 0)
    def _():
        for copy in copies:
            copy.start()
        pooled[...] = jnp.zeros_like(pooled)
        counts[...] = jnp.zeros_like(counts)
        gdb[...] = jnp.zeros_like(gdb)
        gg2[...] = jnp.zeros_like(gg2)
        gb2[...] = jnp.zeros_like(gb2)
        for copy in copies:
            copy.wait()

    @pl.when(step < tiles)
    def _():
        branch = dot_nt(act_rows[0], dw[0])
        for i in range(1, parts):
            branch += dot_nt(act_rows[i], dw[i])
        residual = n1[...] * g1[...] + b1[...] + (branch + db[...])
        n2, r2 = normed(residual)
        result = n2 * g2[...] + b2[...]
        out[...] = result.astype(bf16)
        slots = pooled.shape[0]
        shape = (slots, ROWS)
        slot = lax.broadcasted_iota(jnp.int32, shape, 0)
        row = lax.broadcasted_iota(jnp.int32, shape, 1) + step * ROWS
        passage = bucket[0] == 1
        segment = jnp.where(passage, row // PLEN, row // QLEN)
        position = jnp.where(passage, row % PLEN, row % QLEN)
        limit = jnp.zeros(shape, jnp.int32)
        for s in range(slots):
            limit = jnp.where(slot == s, lengths[s], limit)
        chosen = jnp.where((segment == slot) & (position < limit), 1.0, 0.0)
        picked = chosen.astype(bf16)
        high = result.astype(bf16)
        rest = result - high.astype(f32)
        middle = rest.astype(bf16)
        last = (rest - middle.astype(f32)).astype(bf16)
        pooled[...] += dot(picked, high) + dot(picked, middle) + dot(picked, last)
        counts[...] += jnp.broadcast_to(jnp.sum(chosen, axis=1, keepdims=True), counts.shape)
        dy = cotangent[...].astype(f32)
        gg2[...] += jnp.sum(dy * n2, axis=0, keepdims=True)
        gb2[...] += jnp.sum(dy, axis=0, keepdims=True)
        mixed = norm_back(dy, n2, r2, g2[...])
        mixed_out[...] = mixed
        low = mixed.astype(bf16)
        branch_out[...] = low
        gdb[...] += jnp.sum(low.astype(f32), axis=0, keepdims=True)
        for tile in range(tiles):
            @pl.when(step == tile)
            def _():
                branch_t[:, tile * ROWS:(tile + 1) * ROWS] = low.T

    @pl.when(step == tiles - 1)
    def _():
        pooled[...] = pooled[...] / jnp.maximum(counts[...], 1.0)[:, :1]

    def part(n, target):
        found = dot(branch_t[...], act_part[0]).astype(bf16)
        for j in range(f):
            target[slot_of(place, n, j, depth, f), 0] = found[j * tall:(j + 1) * tall]

    @pl.when((step >= tiles) & (step < tiles + depth))
    def _():
        part(1, send)

    @pl.when(step >= tiles + depth)
    def _():
        part(0, keep)


def down(place, bucket, lengths, active, n1, g1, b1, db, g2, b2, cotangent, blocks):
    parts, t, narrow = active.shape
    d = n1.shape[1]
    tiles = t // ROWS
    slots = lengths.shape[0]
    half, depth, tall, _ = blocks[0].shape
    f = 2 * half
    early = lambda s: jnp.minimum(s, tiles - 1)
    late = lambda s, place: place[(jnp.maximum(s - tiles, 0) + depth) % parts]
    made = lambda first: pl.BlockSpec(
        (f, 1, tall, narrow), lambda s, *_: (0, jnp.clip(s - tiles - first, 0, depth - 1), 0, 0)
    )
    rows = pl.BlockSpec((ROWS, d), lambda s, *_: (early(s), 0))
    vector = whole((1, d))
    return call(
        down_kernel, "down", (tiles + parts,),
        [pl.BlockSpec((parts, ROWS, narrow), lambda s, *_: (0, early(s), 0)), rows, vector, vector,
         vector, vector, vector, rows,
         pl.BlockSpec((1, t, narrow), lambda s, place, *_: (late(s, place), 0, 0))]
        + [pl.BlockSpec(memory_space=pl.ANY)] * 4,
        [rows, whole((slots, d)), rows, rows, vector, vector, vector, made(0), made(depth),
         whole((parts, d, narrow))],
        [sds((t, d), bf16), sds((slots, d), f32), sds((t, d), f32), sds((t, d), bf16)]
        + [sds((1, d), f32)] * 3 + [sds((f, depth, tall, narrow), bf16)] * 2 + [sds((parts, d, narrow), bf16)],
        [pltpu.VMEM((d, t), bf16), pltpu.VMEM((slots, 128), f32), pltpu.SemaphoreType.DMA((f * parts,))],
        prefetch=3, cost=guess(12e9, 35e6),
    )(place, bucket, lengths, active, n1, g1, b1, db, g2, b2, cotangent, active, *blocks)


def feed_back_kernel(
    place, branch, slope, dw, uw, low_t, mixed,
    send, keep, gub, grad_normed,
    hidden, found,
):
    j = pl.program_id(0)
    _, depth, tall, _ = send.shape
    each, t, narrow = slope.shape
    tiles = t // ROWS

    def gelu_rows(r, sums):
        rows = pl.ds(pl.multiple_of(r * ROWS, ROWS), ROWS)
        sums_now = []
        for c in range(each):
            grad = (slope[c, rows, :].astype(f32) * dot(branch[rows, :], dw[c])).astype(bf16)
            hidden[rows, c * narrow:(c + 1) * narrow] = grad
            sums_now.append(sums[c] + jnp.sum(grad.astype(f32), axis=0, keepdims=True))
        return tuple(sums_now)

    sums = lax.fori_loop(0, tiles, gelu_rows, (jnp.zeros((1, narrow), f32),) * each)
    for c in range(each):
        gub[0, :, c * narrow:(c + 1) * narrow] = sums[c]
    found[...] = dot(low_t[...], hidden[...]).astype(bf16)
    for n, target in ((1, send), (0, keep)):
        for slot in range(depth):
            i = row_of(place, n, slot, depth)
            target[0, slot] = found[pl.ds(pl.multiple_of(i * tall, 16), tall), :]

    @pl.when(j == 0)
    def _():
        grad_normed[...] = mixed[...]

    def normed_rows(r, carry):
        rows = pl.ds(pl.multiple_of(r * ROWS, ROWS), ROWS)
        grad_normed[rows, :] += dot_nt(hidden[rows, :], uw[0])
        return carry

    lax.fori_loop(0, tiles, normed_rows, 0)


def feed_back(place, branch, slope, dw, uw, low_t, mixed):
    parts, t, narrow = slope.shape
    f, d, wide = uw.shape
    each, depth, tall = parts // f, parts // 2, d // parts
    made = lambda n: pl.BlockSpec(
        (1, depth, tall, wide), lambda j, place: (slot_of(place, n, j, depth, f), 0, 0, 0)
    )
    return call(
        feed_back_kernel, "feed_back", (f,),
        [whole((t, d)), pl.BlockSpec((each, t, narrow), lambda j, *_: (j, 0, 0)),
         pl.BlockSpec((each, d, narrow), lambda j, *_: (j, 0, 0)), pl.BlockSpec((1, d, wide), lambda j, *_: (j, 0, 0)),
         whole((d, t)), whole((t, d))],
        [made(1), made(0), pl.BlockSpec((1, 1, wide), lambda j, *_: (j, 0, 0)), whole((t, d))],
        [sds((f, depth, tall, wide), bf16)] * 2 + [sds((f, 1, wide), f32), sds((t, d), f32)],
        [pltpu.VMEM((t, wide), bf16), pltpu.VMEM((d, wide), bf16)],
        prefetch=1, cost=guess(15e9, 35e6),
    )(place, branch, slope, dw, uw, low_t, mixed)


def inner_kernel(
    grad_normed, n1, r1, g1, context, ow,
    inner_out, gg1, gb1, gob, gow, grad_context, delta_out,
    weight_grad,
):
    step = pl.program_id(0)
    d = n1.shape[1]

    @pl.when(step == 0)
    def _():
        weight_grad[...] = jnp.zeros_like(weight_grad)
        gg1[...] = jnp.zeros_like(gg1)
        gb1[...] = jnp.zeros_like(gb1)
        gob[...] = jnp.zeros_like(gob)

    feature = lax.broadcasted_iota(jnp.int32, (128, d), 1)
    slot = lax.broadcasted_iota(jnp.int32, (128, d), 0)
    head = jnp.where(slot < HD, 2 * slot, 2 * (slot - HD) + 1)
    pick = jnp.where(feature // HD == head, 1.0, 0.0).astype(bf16)
    dy, n = grad_normed[...], n1[...]
    inner = norm_back(dy, n, r1[:, :1], g1[...])
    inner_out[...] = inner
    low = inner.astype(bf16)
    grad_ctx = dot_nt(low, ow[0]).astype(bf16)
    grad_context[...] = grad_ctx
    both = grad_ctx.astype(f32) * context[...].astype(f32)
    high = both.astype(bf16)
    rest = (both - high.astype(f32)).astype(bf16)
    delta_out[...] = dot_nt(pick, high) + dot_nt(pick, rest)
    gg1[...] += jnp.sum(dy * n, axis=0, keepdims=True)
    gb1[...] += jnp.sum(dy, axis=0, keepdims=True)
    gob[...] += jnp.sum(low.astype(f32), axis=0, keepdims=True)
    weight_grad[...] += dot_tn(context[...], low)

    @pl.when(step == pl.num_programs(0) - 1)
    def _():
        gow[...] = weight_grad[...].astype(bf16)


def inner_back(grad_normed, n1, r1, g1, context, weights):
    t, d = n1.shape
    rows = pl.BlockSpec((ROWS, d), lambda r: (r, 0))
    vector = whole((1, d))
    return call(
        inner_kernel, "inner_back", (t // ROWS,),
        [rows, rows, pl.BlockSpec((ROWS, 128), lambda r: (r, 0)), vector, rows,
         pl.BlockSpec((1, d, d), lambda r: (3, 0, 0))],
        [rows, vector, vector, vector, whole((d, d)), rows, pl.BlockSpec((128, ROWS), lambda r: (0, r))],
        [sds((t, d), f32)] + [sds((1, d), f32)] * 3
        + [sds((d, d), bf16), sds((t, d), bf16), sds((128, t), f32)],
        [pltpu.VMEM((d, d), f32)],
        cost=guess(4e9, 20e6),
    )(grad_normed, n1, r1, g1, context, weights)


def shards(
    tokens, bucket, lengths, cotangent,
    query_weight, query_bias, key_weight, value_weight, value_bias, out_weight, out_bias,
    norm1_gain, norm1_bias, up_weight, up_bias, down_weight, down_bias, norm2_gain, norm2_bias,
):
    t, d = tokens.shape
    dp, fsdp = lax.axis_size("dp"), lax.axis_size("fsdp")
    lengths = lengths[0]

    place = places()
    spare = jnp.zeros((13, 4 * d // fsdp), bf16)
    block = jnp.concatenate([
        jnp.concatenate([query_weight, key_weight, value_weight, out_weight], axis=1),
        jnp.concatenate([query_bias, value_bias, out_bias, norm1_gain])[None],
        jnp.concatenate([norm1_bias, down_bias, norm2_gain, norm2_bias])[None],
        up_bias[None],
        spare,
    ])
    to_a, to_u, to_d = Gather(block), Gather(up_weight), Gather(down_weight.T)
    beside([to_a])
    beside([to_a, to_u])
    while to_a.round < axis_facts()[3]:
        beside([to_a, to_d] if to_d.round < 0 else [to_a])
    beside([to_a, to_u])
    weights, vectors, ub = beside([to_u], assemble, (place, to_a.blocks))
    qb, vb, ob, g1 = (vectors[m, 0:1] for m in range(4))
    b1, db, g2, b2 = (vectors[m, 1:2] for m in range(4))
    ub = ub[:, 2]

    q, k, v, context, lse = beside([to_u, to_d], attend, (bucket, lengths, tokens, weights, qb, vb))
    finish(to_u)
    n1, r1, low, active, slope, uw = beside(
        [to_d], up, (place, tokens, context, weights, ob, g1, b1, ub, to_u.blocks)
    )
    finish(to_d)
    out, pooled, mixed, branch, gdb, gg2, gb2, send_d, keep_d, dw = down(
        place, bucket, lengths, active, n1, g1, b1, db, g2, b2, cotangent, to_d.blocks
    )
    of_d = Scatter(keep_d, send_d)
    send_u, keep_u, gub, grad_normed = beside(
        [of_d], feed_back, (place, branch, slope, dw, uw, low.T, mixed)
    )
    of_u = Scatter(keep_u, send_u)
    inner, gg1, gb1, gob, gow, grad_context, delta = beside(
        [of_d, of_u], inner_back, (grad_normed, n1, r1, g1, context, weights)
    )
    gqw, gkw, gvw, gqb, gvb, input_grad = beside(
        [of_d, of_u], attend_back,
        (bucket, lengths, tokens.T, q, k, v, grad_context, lse, delta, weights, inner),
    )
    firsts = jnp.stack([gqb, gvb, gob, gg1])
    seconds = jnp.stack([gb1, gdb, gg2, gb2])
    vectors = jnp.concatenate([firsts, seconds, jnp.zeros((4, 14, d), f32)], axis=1)
    send_a, keep_a = beside([of_d, of_u], pack, (place, (gqw, gkw, gvw, gow), vectors, gub))
    of_a = Scatter(keep_a, send_a)
    while not (of_a.done() and of_u.done() and of_d.done()):
        beside([of_a, of_u, of_d])
    made_a, made_u, made_d = of_a.total, of_u.total, of_d.total

    tall, narrow = d // dp, d // fsdp
    made = [made_a[:tall, m * narrow:(m + 1) * narrow] for m in range(4)]
    rows = [made_a[tall + n, m * narrow:(m + 1) * narrow] for n in range(2) for m in range(4)]
    return (
        out, pooled, input_grad, made[0], rows[0], made[1], made[2], rows[1], made[3], rows[2], rows[3], rows[4],
        made_u, made_a[tall + 2], made_d.T, rows[5], rows[6], rows[7],
    )


def solution(mesh):
    tall, square, vector = P(("dp", "fsdp"), None), P("dp", "fsdp"), P("fsdp")
    in_specs = (
        tall, P(("dp", "fsdp")), tall, tall, square, vector, square, square, vector, square, vector,
        vector, vector, square, vector, square, vector, vector, vector,
    )
    out_specs = (
        tall, tall, tall, square, vector, square, square, vector, square, vector, vector, vector,
        square, vector, square, vector, vector, vector,
    )
    return jax.shard_map(shards, mesh=mesh, in_specs=in_specs, out_specs=out_specs, check_vma=False)
```

```python
import functools

import jax
import jax.numpy as jnp
from jax import lax
from jax.experimental import pallas as pl
from jax.experimental.pallas import tpu as pltpu
from jax.sharding import PartitionSpec as P

H = 12
HD = 64
PLEN = 512
QLEN = 128
PAIR = 2 * HD
ROWS = 256
FEED_ROWS = 512

epsilon = 1e-06
masked_score = -1e30
f32 = jnp.float32
bf16 = jnp.bfloat16
LIMIT = 60 * 1024 * 1024
SMALL = 24 * 1024 * 1024


def dot(left, right):
    return jnp.dot(left, right, preferred_element_type=f32)


def dot_nt(left, right):
    return lax.dot_general(left, right, (((1,), (1,)), ((), ())), preferred_element_type=f32)


def dot_tn(left, right):
    return lax.dot_general(left, right, (((0,), (0,)), ((), ())), preferred_element_type=f32)


def call(kernel, name, grid, in_specs, out_specs, out_shape, scratch=(), prefetch=0, cost=None, limit=LIMIT):
    return pl.pallas_call(
        kernel,
        name=name,
        grid_spec=pltpu.PrefetchScalarGridSpec(
            num_scalar_prefetch=prefetch,
            grid=grid,
            in_specs=in_specs,
            out_specs=out_specs,
            scratch_shapes=list(scratch),
        ),
        out_shape=out_shape,
        compiler_params=pltpu.CompilerParams(
            vmem_limit_bytes=limit, dimension_semantics=("arbitrary",) * len(grid)
        ),
        cost_estimate=cost,
    )


def whole(shape):
    return pl.BlockSpec(shape, lambda *_: (0,) * len(shape))


def sds(shape, dtype):
    return jax.ShapeDtypeStruct(shape, dtype)


def held():
    return pl.BlockSpec(memory_space=pltpu.VMEM)


def guess(flops, nbytes):
    return pl.CostEstimate(flops=int(flops), bytes_accessed=int(nbytes), transcendentals=0)


def reverse(s, bits):
    return sum(((s >> b) & 1) << (bits - 1 - b) for b in range(bits))


def axis_facts():
    dp, fsdp = lax.axis_size("dp"), lax.axis_size("fsdp")
    return dp, fsdp, dp // 2, fsdp.bit_length() - 1


def along_z(hop):
    dp = lax.axis_size("dp")
    return [(d, (d + 2 * hop) % dp) for d in range(dp)]


def across_cores():
    return [(d, d ^ 1) for d in range(lax.axis_size("dp"))]


def along_bit(r):
    dp, fsdp, _, bits = axis_facts()
    pairs = []
    for d in range(dp):
        flip = 1 << (r if d % 2 == 0 else bits - 1 - r)
        pairs += [(d * fsdp + f, d * fsdp + (f ^ flip)) for f in range(fsdp)]
    return pairs


def select_core(even, odd):
    return jnp.where(lax.axis_index("dp") % 2 == 0, even, odd)


def gather_z(block):
    dp = lax.axis_size("dp")
    groups = [list(range(core, dp, 2)) for core in range(2)]
    return lax.all_gather(block, "dp", axis=0, axis_index_groups=groups)


class Gather:
    def __init__(self, along):
        self.held, self.round, self.blocks = along[None], 0, None

    def stage(self):
        bits = axis_facts()[3]
        if self.round < bits:
            return [(self.held, ("dp", "fsdp"), along_bit(self.round))]
        return [(v, "dp", across_cores()) for v in self.own]

    def take(self, got):
        bits = axis_facts()[3]
        if self.round < bits - 1:
            self.held = jnp.concatenate([self.held] + got)
        elif self.round < bits:
            self.own = [self.held] + got
        else:
            self.blocks = self.own + got
        self.round += 1

    def done(self):
        return self.blocks is not None


class Once:
    def __init__(self, sends):
        self.sends, self.got = sends, None

    def stage(self):
        return self.sends

    def take(self, got):
        self.got = got

    def done(self):
        return self.got is not None


def add(left, right):
    return (left.astype(f32) + right.astype(f32)).astype(bf16)


class Scatter:
    def __init__(self, keep, send):
        self.keep, self.send, self.round, self.total = keep, [send], axis_facts()[3], None

    def stage(self):
        _, _, depth, bits = axis_facts()
        if self.round == bits:
            return [(self.send[0], "dp", across_cores())]
        if self.round >= 0:
            return [(self.send[0], ("dp", "fsdp"), along_bit(self.round))]
        return [(self.send[s - 1], "dp", along_z(-s)) for s in range(1, depth)]

    def take(self, got):
        depth = axis_facts()[2]
        keep = self.keep
        if self.round > 0:
            half = keep.shape[0] // 2
            self.send = [add(keep[half:], got[0][half:])]
            self.keep = add(keep[:half], got[0][:half])
        elif self.round == 0:
            self.send = [add(keep[0, s], got[0][0, s]) for s in range(1, depth)]
            self.keep = keep[0, 0].astype(f32) + got[0][0, 0].astype(f32)
        else:
            for part in got:
                keep = keep + part.astype(f32)
            self.total = keep
        self.round -= 1

    def done(self):
        return self.total is not None


def beside(moves, compute=None, args=(), key=0, out=0):
    moves = [move for move in moves if not move.done()]
    stages = [move.stage() for move in moves]
    arrays = [[v for v, _, _ in stage] for stage in stages]
    args = list(args)
    results = ()
    if compute:
        args[key], arrays = lax.optimization_barrier((args[key], arrays))
        results = list(compute(*args))
    else:
        arrays = lax.optimization_barrier(arrays)
    got = [
        [lax.ppermute(v, axis, perm) for v, (_, axis, perm) in zip(sent, stage)]
        for sent, stage in zip(arrays, stages)
    ]
    if compute:
        results[out], got = lax.optimization_barrier((results[out], got))
    else:
        got = lax.optimization_barrier(got)
    for move, parts in zip(moves, got):
        move.take(parts)
    return results


def finish(move):
    while not move.done():
        beside([move])


def places():
    dp, fsdp, depth, bits = axis_facts()
    d, f = lax.axis_index("dp"), lax.axis_index("fsdp")
    z, core = d // 2, d % 2
    slot = jnp.arange(depth, dtype=jnp.int32)
    index = jnp.arange(fsdp, dtype=jnp.int32)
    mirror = sum((((index >> b) & 1) << (bits - 1 - b) for b in range(bits)), jnp.zeros_like(index))
    rows, slots, columns = [], [], []
    for n in range(2):
        there = core ^ n
        rows.append(2 * ((z - slot) % depth) + there)
        away = index ^ f
        mirrored = sum((((away >> b) & 1) << (bits - 1 - b) for b in range(bits)), jnp.zeros_like(index))
        slots.append(jnp.where(there == 0, away, mirrored))
        columns.append(f ^ jnp.where(there == 0, index, mirror))
    neighbours = [(f ^ s)[None] for s in range(fsdp)]
    return jnp.concatenate(rows + slots + columns + [core[None]] + neighbours).astype(jnp.int32)


def row_of(place, n, slot, depth):
    return place[n * depth + slot]


def slot_of(place, n, j, depth, fsdp):
    return place[2 * depth + n * fsdp + j]


def column_of(place, n, s, depth, fsdp):
    return place[2 * depth + 2 * fsdp + n * fsdp + s]


def core_of(place, depth, fsdp):
    return place[2 * depth + 4 * fsdp]


def neighbour_of(place, s, depth, fsdp):
    return place[2 * depth + 4 * fsdp + 1 + s]


def block_copies(place, arrays, target, sems):
    half, depth = arrays[0].shape[:2]
    fsdp = 2 * half
    copies = []
    for a, array in enumerate(arrays):
        core = lax.rem(core_of(place, depth, fsdp) + a // 2, 2)
        for q in range(half):
            j = column_of(place, a // 2, (a % 2) * half + q, depth, fsdp)
            copies.append(pltpu.make_async_copy(array.at[q], target(core, j), sems.at[len(copies)]))
    return copies


def assemble_kernel(place, own_low, own_high, other_low, other_high, weights, vectors, ub):
    step = pl.program_id(0)
    half, _, height, width = own_low.shape
    fsdp, depth, tall = 2 * half, pl.num_programs(0) // 2, height - 16
    narrow = width // 4

    def fill(n, low, high):
        pieces = []
        for j in range(fsdp):
            slot = slot_of(place, n, j, depth, fsdp)
            upper, q = slot >= half, lax.rem(slot, half)
            pieces.append(jnp.where(upper, high[q, 0].astype(f32), low[q, 0].astype(f32)))
        for m in range(4):
            row = jnp.concatenate([p[:, m * narrow:(m + 1) * narrow] for p in pieces], axis=1)
            weights[m] = row[:tall].astype(bf16)
            vectors[m] = row[tall:]
        for j in range(fsdp):
            ub[j] = pieces[j][tall:]

    @pl.when(step < depth)
    def _():
        fill(0, own_low, own_high)

    @pl.when(step >= depth)
    def _():
        fill(1, other_low, other_high)


def row_at(place, s, depth, fsdp):
    core = core_of(place, depth, fsdp)
    return 2 * lax.rem(s, depth) + lax.rem(core + s // depth, 2)


def assemble(place, arrays):
    half, depth, height, width = arrays[0].shape
    fsdp, tall, d = 2 * half, height - 16, half * width // 2
    own = pl.BlockSpec((half, 1, height, width), lambda s, place: (0, jnp.minimum(s, depth - 1), 0, 0))
    other = pl.BlockSpec((half, 1, height, width), lambda s, place: (0, jnp.maximum(s - depth, 0), 0, 0))
    return call(
        assemble_kernel, "assemble", (2 * depth,),
        [own, own, other, other],
        [pl.BlockSpec((4, tall, d), lambda s, place: (0, row_at(place, s, depth, fsdp), 0)), whole((4, 16, d)),
         whole((fsdp, 16, width))],
        [sds((4, 2 * depth * tall, d), bf16), sds((4, 16, d), f32), sds((fsdp, 16, width), f32)],
        prefetch=1, cost=guess(1e9, 11e6),
    )(place, *arrays)


def pack_kernel(place, gq, gk, gv, go, vectors, gub, send, keep):
    step = pl.program_id(0)
    fsdp, _, height, width = send.shape
    depth, tall, narrow = pl.num_programs(0) // 2, height - 16, width // 4

    def fill(n, out):
        for j in range(fsdp):
            slot = slot_of(place, n, j, depth, fsdp)
            columns = slice(j * narrow, (j + 1) * narrow)
            out[slot, 0, :tall, :] = jnp.concatenate(
                [g[:, columns].astype(f32) for g in (gq, gk, gv, go)], axis=1
            ).astype(bf16)
            slab = jnp.concatenate([vectors[m, :, columns] for m in range(4)], axis=1)
            third = lax.broadcasted_iota(jnp.int32, slab.shape, 0) == 2
            out[slot, 0, tall:, :] = jnp.where(third, gub[j], slab).astype(bf16)

    @pl.when(step < depth)
    def _():
        fill(1, send)

    @pl.when(step >= depth)
    def _():
        fill(0, keep)


def pack(place, grads, vectors, gub):
    d = grads[0].shape[0]
    dp, fsdp, depth, _ = axis_facts()
    tall, width = d // dp, 4 * d // fsdp
    rows = pl.BlockSpec((tall, d), lambda s, place: (place[(s + depth) % (2 * depth)], 0))
    sent = pl.BlockSpec((fsdp, 1, tall + 16, width), lambda s, place: (0, jnp.minimum(s, depth - 1), 0, 0))
    kept = pl.BlockSpec((fsdp, 1, tall + 16, width), lambda s, place: (0, jnp.maximum(s - depth, 0), 0, 0))
    return call(
        pack_kernel, "pack", (2 * depth,),
        [rows, rows, rows, rows, whole((4, 16, d)), whole((fsdp, 1, width))],
        [sent, kept],
        [sds((fsdp, depth, tall + 16, width), bf16)] * 2,
        prefetch=1, cost=guess(1e9, 11e6),
    )(place, *grads, vectors, gub)


def segment_lanes(bucket, lengths, queries_ext, keys_ext):
    row_count = queries_ext.shape[0]
    slots = lengths.shape[0]
    shape = (row_count, PAIR)
    row = lax.broadcasted_iota(jnp.int32, shape, 0)
    lane = lax.broadcasted_iota(jnp.int32, shape, 1) % HD
    passage = bucket[0] == 1
    segment = jnp.where(passage, row // PLEN, row // QLEN)
    position = jnp.where(passage, row % PLEN, row % QLEN)
    limit = jnp.zeros(shape, jnp.int32)
    for s in range(slots):
        limit = jnp.where(segment == s, lengths[s], limit)
    alive = position < limit
    same = segment == lane
    queries_ext[...] = jnp.where(same, 1.0, 0.0).astype(bf16)
    keys_ext[...] = jnp.where((lane < slots) & ~(same & alive), masked_score, 0.0).astype(bf16)


def attend_kernel(
    bucket, lengths, x, qw, kw, vw, qb, vb,
    q_out, k_out, v_out, context_out, lse_out,
    queries_ext, keys_ext, lse_all,
):
    pair = pl.program_id(0)
    row_count = x.shape[0]

    @pl.when(pair == 0)
    def _():
        segment_lanes(bucket, lengths, queries_ext, keys_ext)
        lse_all[...] = jnp.zeros_like(lse_all)

    weights = jnp.concatenate([qw[0], kw[0], vw[0]], axis=1)
    qb_row = qb[...]
    vb_row = vb[...]
    low_half = lax.broadcasted_iota(jnp.int32, (PLEN, PAIR), 1) < HD
    lane = lax.broadcasted_iota(jnp.int32, (PLEN, PAIR), 1)

    def block(b, carry):
        rows = pl.ds(pl.multiple_of(b * PLEN, PLEN), PLEN)
        qkv = dot(x[rows, :], weights)
        queries = ((qkv[:, :PAIR] + qb_row).astype(bf16).astype(f32) * HD ** (-0.5)).astype(bf16)
        keys = qkv[:, PAIR:2 * PAIR].astype(bf16)
        values = (qkv[:, 2 * PAIR:] + vb_row).astype(bf16)
        q_out[rows, :] = queries
        k_out[rows, :] = keys
        v_out[rows, :] = values
        q_ext = queries_ext[rows, :]
        k_ext = keys_ext[rows, :]
        ones = jnp.ones_like(values)
        sums, tops = [], []
        for half in range(2):
            mine = low_half if half == 0 else ~low_half
            scores = dot_nt(jnp.where(mine, queries, q_ext), jnp.where(mine, keys, k_ext))
            top = jnp.max(scores, axis=-1, keepdims=True)
            weight = jnp.exp(scores - top).astype(bf16)
            sums.append(dot(weight, jnp.where(mine, values, ones)))
            tops.append(top)
        numer = jnp.where(low_half, sums[0], sums[1])
        denom = pltpu.roll(jnp.where(low_half, sums[1], sums[0]), HD, 1)
        context_out[rows, :] = (numer / denom).astype(bf16)
        lse = jnp.where(low_half, tops[0], tops[1]) + jnp.log(denom)
        mine = (lane % HD) == pair
        lse_all[rows, :] = jnp.where(mine, lse, lse_all[rows, :])
        return carry

    lax.fori_loop(0, row_count // PLEN, block, 0)

    @pl.when(pair == pl.num_programs(0) - 1)
    def _():
        lse_out[...] = lse_all[...].T


def attend(bucket, lengths, x, weights, qb, vb):
    t, d = x.shape
    pairs = d // PAIR
    column = lambda m: pl.BlockSpec((1, d, PAIR), lambda p, *_: (m, 0, p))
    vector = pl.BlockSpec((1, PAIR), lambda p, *_: (0, p))
    tall = pl.BlockSpec((t, PAIR), lambda p, *_: (0, p))
    return call(
        attend_kernel, "attend", (pairs,),
        [whole((t, d)), column(0), column(1), column(2), vector, vector],
        [tall, tall, tall, tall, whole((PAIR, t))],
        [sds((t, d), bf16)] * 4 + [sds((PAIR, t), f32)],
        [pltpu.VMEM((t, PAIR), bf16), pltpu.VMEM((t, PAIR), bf16), pltpu.VMEM((t, PAIR), f32)],
        prefetch=2, cost=guess(15e9, 12e6),
    )(bucket, lengths, x, weights, weights, weights, qb, vb)


HEADS = 3
USED = 5 * PAIR


def columns_of(q, k, v, o):
    return jnp.concatenate([q[:, :PAIR], k[:, :PAIR], v[:, :PAIR], q[:, PAIR:], k[:, PAIR:], v[:, PAIR:], o], axis=1)


def columns_back(block):
    q = jnp.concatenate([block[:, :PAIR], block[:, 3 * PAIR:3 * PAIR + HD]], axis=1)
    k = jnp.concatenate([block[:, PAIR:2 * PAIR], block[:, 3 * PAIR + HD:4 * PAIR]], axis=1)
    v = jnp.concatenate([block[:, 2 * PAIR:3 * PAIR], block[:, 4 * PAIR:4 * PAIR + HD]], axis=1)
    return q, k, v, block[:, 4 * PAIR + HD:]


def line_up_kernel(place, *refs):
    out = refs[-1]
    depth = len(refs) - 1
    for s in range(depth):
        out[row_of(place, 0, s, depth) // 2] = refs[s][...]


def line_up(place, parts):
    shape = parts[0].shape
    out = (len(parts), *shape)
    return call(
        line_up_kernel, "line_up", (1,), [whole(shape)] * len(parts), whole(out), sds(out, parts[0].dtype),
        prefetch=1, cost=guess(1e6, 1e6), limit=SMALL,
    )(place, *parts)


def attend_one_kernel(
    away, place, bucket, lengths, x, own, other, *refs,
):
    context_out, w_out, slab_out, kept, lse_out, queries_ext, keys_ext, sems = refs[-8:]
    _, depth, _, tall, width = w_out.shape
    row_count = x.shape[0]
    core = core_of(place, depth, w_out_fsdp(place, depth))
    copies = [
        pltpu.make_async_copy(ref.at[:, :tall, :], w_out.at[0, :, lax.rem(core + n, 2)], sems.at[n])
        for n, ref in enumerate((own, other))
    ]
    last = pltpu.make_async_copy(own.at[0, tall:, :], slab_out.at[0], sems.at[2])
    for copy in (*copies, last):
        copy.start()
    segment_lanes(bucket, lengths, queries_ext, keys_ext)
    for copy in (*copies, last):
        copy.wait()

    bias = slab_out[0, 0:1, :USED].astype(f32)
    lane = lax.broadcasted_iota(jnp.int32, (PLEN, PAIR), 1)
    low_half = lane < HD
    scale = HD ** (-0.5)

    def block(b, carry):
        rows = pl.ds(pl.multiple_of(b * PLEN, PLEN), PLEN)
        weights = w_out[0, :, :, :, :USED].reshape(2 * depth * tall, USED)
        qkv = dot(x[rows, :], weights) + bias
        tiles = [qkv[:, n * PAIR:(n + 1) * PAIR].astype(bf16) for n in range(5)]
        tiles[0] = tiles[0] * jnp.array(scale, bf16)
        tiles[3] = jnp.where(low_half, tiles[3] * jnp.array(scale, bf16), tiles[3])
        for n in range(5):
            kept[rows, n * PAIR:(n + 1) * PAIR] = tiles[n]
        queries, keys, values, both, values_two = tiles
        keys_two = pltpu.roll(both.astype(f32), HD, 1).astype(bf16)
        q_ext, k_ext = queries_ext[rows, :], keys_ext[rows, :]
        ones = jnp.ones_like(values)

        def one(mine, q, k, v):
            scores = dot_nt(jnp.where(mine, q, q_ext), jnp.where(mine, k, k_ext))
            top = jnp.max(scores, axis=-1, keepdims=True)
            weight = jnp.exp(scores - top).astype(bf16)
            return top, dot(weight, jnp.where(mine, v, ones))

        top_a, sum_a = one(low_half, queries, keys, values)
        top_b, sum_b = one(~low_half, queries, keys, values)
        top_c, sum_c = one(low_half, both, keys_two, values_two)
        denom = pltpu.roll(jnp.where(low_half, sum_b, sum_a), HD, 1)
        denom_c = pltpu.roll(sum_c, HD, 1)
        context_out[0, rows, :PAIR] = (jnp.where(low_half, sum_a, sum_b) / denom).astype(bf16)
        context_out[0, rows, PAIR:] = (sum_c / denom_c)[:, :HD].astype(bf16)
        lse_ab = jnp.where(low_half, top_a, top_b) + jnp.log(denom)
        lse_c = top_c + jnp.log(denom_c)
        every = jnp.where((lane >= 32) & low_half, lse_c, lse_ab).T
        lse_out[0:1, rows] = every[0:1]
        lse_out[1:2, rows] = every[HD:HD + 1]
        lse_out[2:3, rows] = every[32:33]
        return carry

    lax.fori_loop(0, row_count // PLEN, block, 0)


def w_out_fsdp(place, depth):
    return (place.shape[0] - 2 * depth - 1) // 5


def attend_one(away, fsdp, place, bucket, lengths, x, own, other, shared):
    t, d = x.shape
    depth, height, width = own.shape
    tall, narrow = height - 16, d // fsdp
    shapes = [(fsdp, t, narrow), (fsdp, depth, 2, tall, width), (fsdp, 16, width)]
    j = lambda place: neighbour_of(place, away, depth, fsdp)
    any_space = pl.BlockSpec(memory_space=pl.ANY)
    return pl.pallas_call(
        functools.partial(attend_one_kernel, away),
        name="attend",
        grid_spec=pltpu.PrefetchScalarGridSpec(
            num_scalar_prefetch=3,
            grid=(1,),
            in_specs=[whole((t, d)), any_space, any_space] + [any_space] * len(shared),
            out_specs=[
                pl.BlockSpec((1, t, narrow), lambda s, place, *_: (j(place), 0, 0)),
                pl.BlockSpec((1, depth, 2, tall, width), lambda s, place, *_: (j(place), 0, 0, 0, 0)),
                pl.BlockSpec((1, 16, width), lambda s, place, *_: (j(place), 0, 0)),
                whole((t, USED)), whole((8, t)),
            ],
            scratch_shapes=[
                pltpu.VMEM((t, PAIR), bf16), pltpu.VMEM((t, PAIR), bf16), pltpu.SemaphoreType.DMA((3,)),
            ],
        ),
        out_shape=[sds(shape, bf16) for shape in shapes] + [sds((t, USED), bf16), sds((8, t), f32)],
        input_output_aliases={6 + n: n for n in range(len(shared))},
        compiler_params=pltpu.CompilerParams(vmem_limit_bytes=SMALL, dimension_semantics=("arbitrary",)),
        cost_estimate=guess(5e9, 8e6),
    )(place, bucket, lengths, x, own, other, *shared)


def attend_back_one_kernel(
    away, place, bucket, lengths, x_t, kept, grad_context, lse, delta, weights, gow, slab, grad_in,
    send, keep, grad_out,
    queries_ext, keys_ext, grads, found,
):
    depth, height, width = send.shape
    tall = height - 16
    row_count = kept.shape[0]
    segment_lanes(bucket, lengths, queries_ext, keys_ext)
    lane = lax.broadcasted_iota(jnp.int32, (PLEN, PAIR), 1)
    low_half = lane < HD
    scale = HD ** (-0.5)

    def block(b, sums):
        rows = pl.ds(pl.multiple_of(b * PLEN, PLEN), PLEN)
        queries, keys, values, both, values_two = (kept[rows, n * PAIR:(n + 1) * PAIR] for n in range(5))
        keys_two = pltpu.roll(both.astype(f32), HD, 1).astype(bf16)
        q_ext, k_ext = queries_ext[rows, :], keys_ext[rows, :]
        nothing = jnp.zeros_like(values)
        grad_two = jnp.concatenate([grad_context[0, rows, PAIR:]] * 2, axis=1)

        def one(a, mine, q, k, v, grad_ctx):
            scores = dot_nt(jnp.where(mine, k, k_ext), jnp.where(mine, q, q_ext))
            probs = jnp.exp(scores - lse[a:a + 1, rows])
            grad_probs = dot_nt(jnp.where(mine, v, nothing), grad_ctx)
            grad_scores = (probs * (grad_probs - delta[0, a:a + 1, rows])).astype(bf16)
            grad_v = dot(probs.astype(bf16), grad_ctx)
            grad_k = dot(grad_scores, q)
            grad_q = dot_tn(grad_scores, k) * scale
            return grad_q, grad_k, grad_v

        grad_pair = grad_context[0, rows, :PAIR]
        q_a, k_a, v_a = one(0, low_half, queries, keys, values, grad_pair)
        q_b, k_b, v_b = one(1, ~low_half, queries, keys, values, grad_pair)
        q_c, k_c, v_c = one(2, low_half, both, keys_two, values_two, grad_two)
        made = [
            jnp.where(low_half, q_a, q_b), jnp.where(low_half, k_a, k_b), jnp.where(low_half, v_a, v_b),
            jnp.where(low_half, q_c, pltpu.roll(k_c, HD, 1)), jnp.where(low_half, v_c, 0.0),
        ]
        found_sums = []
        for n in range(5):
            low = made[n].astype(bf16)
            grads[rows, n * PAIR:(n + 1) * PAIR] = low
            found_sums.append(sums[n] + jnp.sum(low.astype(f32), axis=0, keepdims=True))
        return tuple(found_sums)

    sums = lax.fori_loop(0, row_count // PLEN, block, (jnp.zeros((1, PAIR), f32),) * 5)
    columns = grads[...]
    made = dot(x_t[...], columns)
    found[:, :4 * PAIR] = made[:, :4 * PAIR].astype(bf16)
    found[:, 4 * PAIR:] = jnp.concatenate([made[:, 4 * PAIR:4 * PAIR + HD], gow[0].astype(f32)], axis=1).astype(bf16)
    rest = slab[0]
    first = jnp.concatenate([*sums[:4], sums[4][:, :HD], rest[0:1, 4 * PAIR + HD:]], axis=1)
    row = lax.broadcasted_iota(jnp.int32, rest.shape, 0)
    below = jnp.where(row == 0, first, rest).astype(bf16)
    core = core_of(place, depth, w_out_fsdp(place, depth))
    for n, target in ((1, send), (0, keep)):
        for z in range(depth):
            i = 2 * z + lax.rem(core + n, 2)
            target[z, :tall, :] = found[pl.ds(pl.multiple_of(i * tall, 16), tall), :]
            target[z, tall:, :] = below
    grad_out[...] = grad_in[...] + dot_nt(columns, weights[0, :, :, :, :USED].reshape(2 * depth * tall, USED))


def attend_back_one(
    away, fsdp, final, place, bucket, lengths, x_t, kept, grad_context, lse, delta, weights, gow, slab, grad_in
):
    d, t = x_t.shape
    _, depth, _, tall, width = weights.shape
    narrow = d // fsdp
    j = lambda place: neighbour_of(place, away, depth, fsdp)
    part = lambda *shape: pl.BlockSpec((1, *shape), lambda s, place, *_: (j(place),) + (0,) * len(shape))
    sent = (depth, tall + 16, width)
    return call(
        functools.partial(attend_back_one_kernel, away), "attend_back", (1,),
        [whole((d, t)), whole((t, USED)), part(t, narrow), whole((8, t)), part(8, t), part(depth, 2, tall, width),
         part(d, narrow), part(16, width), held()],
        [whole(sent), whole(sent), whole((t, d)) if final else held()],
        [sds(sent, bf16)] * 2 + [sds((t, d), f32) if final else pltpu.VMEM((t, d), f32)],
        [pltpu.VMEM((t, PAIR), bf16), pltpu.VMEM((t, PAIR), bf16), pltpu.VMEM((t, USED), bf16),
         pltpu.VMEM((d, width), bf16)],
        prefetch=3, cost=guess(10e9, 12e6), limit=40 * 1024 * 1024,
    )(place, bucket, lengths, x_t, kept, grad_context, lse, delta, weights, gow, slab, grad_in)


def attend_back_kernel(
    bucket, lengths, x_t, q, k, v, grad_context, lse, delta, qw, kw, vw, grad_inner,
    gqw, gkw, gvw, gqb, gvb, input_grad,
    queries_ext, keys_ext, grads,
):
    pair = pl.program_id(0)
    row_count = q.shape[0]

    @pl.when(pair == 0)
    def _():
        segment_lanes(bucket, lengths, queries_ext, keys_ext)

    low_half = lax.broadcasted_iota(jnp.int32, (PLEN, PAIR), 1) < HD

    def block(b, carry):
        rows = pl.ds(pl.multiple_of(b * PLEN, PLEN), PLEN)
        queries, keys, values, grad_ctx = q[rows, :], k[rows, :], v[rows, :], grad_context[rows, :]
        q_ext, k_ext = queries_ext[rows, :], keys_ext[rows, :]
        nothing = jnp.zeros_like(values)
        got = []
        for half in range(2):
            mine = low_half if half == 0 else ~low_half
            lse_row = lse[pl.ds(half * HD + pair, 1), rows]
            delta_row = delta[pl.ds(half * HD + pair, 1), rows]
            scores = dot_nt(jnp.where(mine, keys, k_ext), jnp.where(mine, queries, q_ext))
            probs = jnp.exp(scores - lse_row)
            grad_probs = dot_nt(jnp.where(mine, values, nothing), grad_ctx)
            grad_scores = (probs * (grad_probs - delta_row)).astype(bf16)
            grad_v = dot(probs.astype(bf16), grad_ctx)
            grad_k = dot(grad_scores, queries)
            grad_q = dot_tn(grad_scores, keys)
            got.append((grad_q, grad_k, grad_v))
        gq = (jnp.where(low_half, got[0][0], got[1][0]) * HD ** (-0.5)).astype(bf16)
        gk = jnp.where(low_half, got[0][1], got[1][1]).astype(bf16)
        gv = jnp.where(low_half, got[0][2], got[1][2]).astype(bf16)
        grads[rows, :PAIR] = gq
        grads[rows, PAIR:2 * PAIR] = gk
        grads[rows, 2 * PAIR:] = gv
        sum_q = jnp.sum(gq.astype(f32), axis=0, keepdims=True)
        sum_v = jnp.sum(gv.astype(f32), axis=0, keepdims=True)
        return (carry[0] + sum_q, carry[1] + sum_v)

    start = jnp.zeros((1, PAIR), f32)
    gqb[...], gvb[...] = lax.fori_loop(0, row_count // PLEN, block, (start, start))

    columns = grads[...]
    weight_grads = dot(x_t[...], columns)
    gqw[...] = weight_grads[:, :PAIR].astype(gqw.dtype)
    gkw[...] = weight_grads[:, PAIR:2 * PAIR].astype(gkw.dtype)
    gvw[...] = weight_grads[:, 2 * PAIR:].astype(gvw.dtype)

    @pl.when(pair == 0)
    def _():
        input_grad[...] = grad_inner[...]

    weights = jnp.concatenate([qw[0], kw[0], vw[0]], axis=1)
    input_grad[...] += dot_nt(columns, weights)


def attend_back(bucket, lengths, x_t, q, k, v, grad_context, lse, delta, weights, grad_inner):
    t, d = q.shape
    pairs = d // PAIR
    column = lambda m: pl.BlockSpec((1, d, PAIR), lambda p, *_: (m, 0, p))
    vector = pl.BlockSpec((1, PAIR), lambda p, *_: (0, p))
    tall = pl.BlockSpec((t, PAIR), lambda p, *_: (0, p))
    made = pl.BlockSpec((d, PAIR), lambda p, *_: (0, p))
    return call(
        attend_back_kernel, "attend_back", (pairs,),
        [whole((d, t)), tall, tall, tall, tall, whole((PAIR, t)), whole((PAIR, t)),
         column(0), column(1), column(2), whole((t, d))],
        [made, made, made, vector, vector, whole((t, d))],
        [sds((d, d), bf16)] * 3 + [sds((1, d), f32)] * 2 + [sds((t, d), f32)],
        [pltpu.VMEM((t, PAIR), bf16), pltpu.VMEM((t, PAIR), bf16), pltpu.VMEM((t, 3 * PAIR), bf16)],
        prefetch=2, cost=guess(30e9, 25e6),
    )(bucket, lengths, x_t, q, k, v, grad_context, lse, delta, weights, weights, weights, grad_inner)


def normed(v):
    centred = v - jnp.mean(v, axis=-1, keepdims=True)
    r = lax.rsqrt(jnp.mean(centred * centred, axis=-1, keepdims=True) + epsilon)
    return centred * r, r


def norm_back(dy, n, r, gain):
    dn = dy * gain
    return r * (dn - jnp.mean(dn, axis=-1, keepdims=True) - n * jnp.mean(dn * n, axis=-1, keepdims=True))


def gelu_parts(u):
    size = jnp.abs(u)
    below = 1.0 + (0.3275911 * 0.7071067811865476) * size
    t = pl.reciprocal(below, approx=True)
    t = t * (2.0 - below * t)
    poly = 0.5 * 1.061405429
    for c in (-1.453152027, 1.421413741, -0.284496736, 0.254829592):
        poly = poly * t + 0.5 * c
    bell = jnp.exp(u * u * -0.5)
    tail = poly * t * bell
    phi = jnp.where(u >= 0, 1.0 - tail, tail)
    return u * phi, phi + u * bell * 0.3989422804014327


def attended_kernel(x, context, ow, ob, g1, b1, n1_out, r1_out, low_out, low_t, ow_out):
    rows = pl.ds(pl.multiple_of(pl.program_id(0) * ROWS, ROWS), ROWS)
    parts, _, narrow = context.shape

    @pl.when(pl.program_id(0) == 0)
    def _():
        ow_out[...] = jnp.concatenate([ow[j][:, ow.shape[2] - narrow:] for j in range(parts)], axis=1)

    joined = jnp.concatenate([context[j] for j in range(parts)], axis=1)
    attended = dot(joined, ow_out[...]) + ob[...]
    n1, r1 = normed(x[...].astype(f32) + attended)
    n1_out[rows, :] = n1
    r1_out[rows, :] = jnp.broadcast_to(r1, (ROWS, r1_out.shape[1]))
    low = (n1 * g1[...] + b1[...]).astype(bf16)
    low_out[rows, :] = low
    low_t[:, rows] = low.T


def attended(x, context, ow, last, ob, g1, b1):
    t, d = x.shape
    parts, _, narrow = context.shape
    wide = ow.shape[2] // (last + 1)
    rows = pl.BlockSpec((ROWS, d), lambda r: (r, 0))
    return call(
        attended_kernel, "attended", (t // ROWS,),
        [rows, pl.BlockSpec((parts, ROWS, narrow), lambda r: (0, r, 0)),
         pl.BlockSpec((parts, d, wide), lambda r: (0, 0, last)), whole((1, d)), whole((1, d)), whole((1, d))],
        [held()] * 5,
        [pltpu.VMEM((t, d), f32), pltpu.VMEM((t, 128), f32), pltpu.VMEM((t, d), bf16), pltpu.VMEM((d, t), bf16),
         pltpu.VMEM((d, d), bf16)],
        cost=guess(3e9, 10e6), limit=SMALL,
    )(x, context, ow, ob, g1, b1)


def up_kernel(place, low, ub, u0, u1, u2, u3, act_out, slope_out, uw, sems):
    wide = act_out.shape[2]
    rows = pl.ds(pl.multiple_of(pl.program_id(0) * ROWS, ROWS), ROWS)
    copies = block_copies(place, (u0, u1, u2, u3), lambda core, j: uw.at[j, :, core], sems)

    @pl.when(pl.program_id(0) == 0)
    def _():
        for copy in copies:
            copy.start()
        for copy in copies:
            copy.wait()

    tile = low[rows, :]
    f, depth, _, tall, columns = uw.shape
    each = columns // wide
    for j in range(f):
        hidden = dot(tile, uw[j].reshape(2 * depth * tall, columns)) + ub[j:j + 1, :]
        active, slope = gelu_parts(hidden)
        active, slope = active.astype(bf16), slope.astype(bf16)
        for c in range(each):
            act_out[j * each + c] = active[:, c * wide:(c + 1) * wide]
            slope_out[j * each + c] = slope[:, c * wide:(c + 1) * wide]


def up(place, low, ub, blocks):
    t, d = low.shape
    half, depth, tall, wide = blocks[0].shape
    f, parts = 2 * half, 2 * depth
    narrow = f * wide // parts
    high = pl.BlockSpec((parts, ROWS, narrow), lambda r, *_: (0, r, 0))
    return call(
        up_kernel, "up", (t // ROWS,),
        [held(), whole(ub.shape)] + [pl.BlockSpec(memory_space=pl.ANY)] * 4,
        [high, high, whole((f, depth, 2, tall, wide))],
        [sds((parts, t, narrow), bf16), sds((parts, t, narrow), bf16), sds((f, depth, 2, tall, wide), bf16)],
        [pltpu.SemaphoreType.DMA((2 * f,))],
        prefetch=1, cost=guess(12e9, 31e6), limit=SMALL,
    )(place, low, ub, *blocks)


def down_kernel(
    place, bucket, lengths, act_rows, n1, g1, b1, db, g2, b2, cotangent, act_part, d0, d1, d2, d3,
    out, pooled, mixed_out, branch_out, gdb, gg2, gb2, send, keep, dw,
    branch_t, counts, sems,
):
    step = pl.program_id(0)
    tiles = branch_t.shape[1] // ROWS
    depth = dw.shape[0]
    parts = 2 * depth
    f, _, tall, _ = send.shape
    copies = block_copies(
        place, (d0, d1, d2, d3),
        lambda core, j: dw.at[:, core, pl.ds(pl.multiple_of(j * tall, 16), tall), :], sems,
    )

    @pl.when(step == 0)
    def _():
        for copy in copies:
            copy.start()
        pooled[...] = jnp.zeros_like(pooled)
        counts[...] = jnp.zeros_like(counts)
        gdb[...] = jnp.zeros_like(gdb)
        gg2[...] = jnp.zeros_like(gg2)
        gb2[...] = jnp.zeros_like(gb2)
        for copy in copies:
            copy.wait()

    @pl.when(step < tiles)
    def _():
        rows = pl.ds(pl.multiple_of(step * ROWS, ROWS), ROWS)
        branch = dot_nt(act_rows[0], dw[0, 0])
        for i in range(1, parts):
            branch += dot_nt(act_rows[i], dw[i // 2, i % 2])
        residual = n1[rows, :] * g1[...] + b1[...] + (branch + db[...])
        n2, r2 = normed(residual)
        result = n2 * g2[...] + b2[...]
        out[...] = result.astype(bf16)
        slots = pooled.shape[0]
        shape = (slots, ROWS)
        slot = lax.broadcasted_iota(jnp.int32, shape, 0)
        row = lax.broadcasted_iota(jnp.int32, shape, 1) + step * ROWS
        passage = bucket[0] == 1
        segment = jnp.where(passage, row // PLEN, row // QLEN)
        position = jnp.where(passage, row % PLEN, row % QLEN)
        limit = jnp.zeros(shape, jnp.int32)
        for s in range(slots):
            limit = jnp.where(slot == s, lengths[s], limit)
        chosen = jnp.where((segment == slot) & (position < limit), 1.0, 0.0)
        picked = chosen.astype(bf16)
        high = result.astype(bf16)
        rest = result - high.astype(f32)
        middle = rest.astype(bf16)
        last = (rest - middle.astype(f32)).astype(bf16)
        pooled[...] += dot(picked, high) + dot(picked, middle) + dot(picked, last)
        counts[...] += jnp.broadcast_to(jnp.sum(chosen, axis=1, keepdims=True), counts.shape)
        dy = cotangent[...].astype(f32)
        gg2[...] += jnp.sum(dy * n2, axis=0, keepdims=True)
        gb2[...] += jnp.sum(dy, axis=0, keepdims=True)
        mixed = norm_back(dy, n2, r2, g2[...])
        mixed_out[rows, :] = mixed
        low = mixed.astype(bf16)
        branch_out[rows, :] = low
        gdb[...] += jnp.sum(low.astype(f32), axis=0, keepdims=True)
        branch_t[:, rows] = low.T

    @pl.when(step == tiles - 1)
    def _():
        pooled[...] = pooled[...] / jnp.maximum(counts[...], 1.0)[:, :1]

    def part(n, target):
        found = dot(branch_t[...], act_part[0]).astype(bf16)
        for j in range(f):
            target[slot_of(place, n, j, depth, f), 0] = found[j * tall:(j + 1) * tall]

    @pl.when((step >= tiles) & (step < tiles + depth))
    def _():
        part(1, send)

    @pl.when(step >= tiles + depth)
    def _():
        part(0, keep)


def down(place, bucket, lengths, active, n1, g1, b1, db, g2, b2, cotangent, blocks):
    parts, t, narrow = active.shape
    d = n1.shape[1]
    tiles = t // ROWS
    slots = lengths.shape[0]
    half, depth, tall, _ = blocks[0].shape
    f = 2 * half
    early = lambda s: jnp.minimum(s, tiles - 1)
    late = lambda s, place: place[(jnp.maximum(s - tiles, 0) + depth) % parts]
    made = lambda first: pl.BlockSpec(
        (f, 1, tall, narrow), lambda s, *_: (0, jnp.clip(s - tiles - first, 0, depth - 1), 0, 0)
    )
    rows = pl.BlockSpec((ROWS, d), lambda s, *_: (early(s), 0))
    vector = whole((1, d))
    return call(
        down_kernel, "down", (tiles + parts,),
        [pl.BlockSpec((parts, ROWS, narrow), lambda s, *_: (0, early(s), 0)), held(), vector, vector, vector, vector,
         vector, rows, pl.BlockSpec((1, t, narrow), lambda s, place, *_: (late(s, place), 0, 0))]
        + [pl.BlockSpec(memory_space=pl.ANY)] * 4,
        [rows, whole((slots, d)), held(), held(), vector, vector, vector, made(0), made(depth),
         whole((depth, 2, d, narrow))],
        [sds((t, d), bf16), sds((slots, d), f32), pltpu.VMEM((t, d), f32), pltpu.VMEM((t, d), bf16)]
        + [sds((1, d), f32)] * 3 + [sds((f, depth, tall, narrow), bf16)] * 2
        + [sds((depth, 2, d, narrow), bf16)],
        [pltpu.VMEM((d, t), bf16), pltpu.VMEM((slots, 128), f32), pltpu.SemaphoreType.DMA((2 * f,))],
        prefetch=3, cost=guess(12e9, 35e6), limit=SMALL,
    )(place, bucket, lengths, active, n1, g1, b1, db, g2, b2, cotangent, active, *blocks)


def feed_back_kernel(
    place, branch, slope, dw, uw, low_t, mixed,
    send, keep, gub, grad_normed,
    hidden, found,
):
    j = pl.program_id(0)
    _, depth, tall, _ = send.shape
    each, t, narrow = slope.shape
    tiles = t // FEED_ROWS

    def gelu_rows(r, sums):
        rows = pl.ds(pl.multiple_of(r * FEED_ROWS, FEED_ROWS), FEED_ROWS)
        sums_now = []
        for c in range(each):
            grad = (slope[c, rows, :].astype(f32) * dot(branch[rows, :], dw[c])).astype(bf16)
            hidden[rows, c * narrow:(c + 1) * narrow] = grad
            sums_now.append(sums[c] + jnp.sum(grad.astype(f32), axis=0, keepdims=True))
        return tuple(sums_now)

    sums = lax.fori_loop(0, tiles, gelu_rows, (jnp.zeros((1, narrow), f32),) * each)
    for c in range(each):
        gub[0, :, c * narrow:(c + 1) * narrow] = sums[c]
    found[...] = dot(low_t[...], hidden[...]).astype(bf16)
    for n, target in ((1, send), (0, keep)):
        for slot in range(depth):
            i = row_of(place, n, slot, depth)
            target[0, slot] = found[pl.ds(pl.multiple_of(i * tall, 16), tall), :]

    @pl.when(j == 0)
    def _():
        grad_normed[...] = mixed[...]

    def normed_rows(r, carry):
        rows = pl.ds(pl.multiple_of(r * FEED_ROWS, FEED_ROWS), FEED_ROWS)
        grad_normed[rows, :] += dot_nt(hidden[rows, :], uw[0])
        return carry

    lax.fori_loop(0, tiles, normed_rows, 0)


def feed_back(place, branch, slope, dw, uw, low_t, mixed):
    parts, t, narrow = slope.shape
    f, d, wide = uw.shape
    each, depth, tall = parts // f, parts // 2, d // parts
    made = lambda n: pl.BlockSpec(
        (1, depth, tall, wide), lambda j, place: (slot_of(place, n, j, depth, f), 0, 0, 0)
    )
    return call(
        feed_back_kernel, "feed_back", (f,),
        [held(), pl.BlockSpec((each, t, narrow), lambda j, *_: (j, 0, 0)),
         pl.BlockSpec((each, d, narrow), lambda j, *_: (j, 0, 0)), pl.BlockSpec((1, d, wide), lambda j, *_: (j, 0, 0)),
         held(), held()],
        [made(1), made(0), pl.BlockSpec((1, 1, wide), lambda j, *_: (j, 0, 0)), held()],
        [sds((f, depth, tall, wide), bf16)] * 2 + [sds((f, 1, wide), f32), pltpu.VMEM((t, d), f32)],
        [pltpu.VMEM((t, wide), bf16), pltpu.VMEM((d, wide), bf16)],
        prefetch=1, cost=guess(15e9, 35e6), limit=SMALL,
    )(place, branch, slope, dw, uw, low_t, mixed)


def inner_kernel(
    grad_normed, n1, r1, g1, context, ow, pick,
    inner_out, gg1, gb1, gob, gow, grad_context, delta_out,
    weight_grad,
):
    step = pl.program_id(0)
    d = n1.shape[1]
    parts, _, narrow = context.shape

    @pl.when(step == 0)
    def _():
        weight_grad[...] = jnp.zeros_like(weight_grad)
        gg1[...] = jnp.zeros_like(gg1)
        gb1[...] = jnp.zeros_like(gb1)
        gob[...] = jnp.zeros_like(gob)

    rows = pl.ds(pl.multiple_of(step * ROWS, ROWS), ROWS)
    dy, n = grad_normed[rows, :], n1[rows, :]
    inner = norm_back(dy, n, r1[rows, :1], g1[...])
    inner_out[rows, :] = inner
    low = inner.astype(bf16)
    grad_ctx = dot_nt(low, ow[...]).astype(bf16)
    for j in range(parts):
        grad_context[j] = grad_ctx[:, j * narrow:(j + 1) * narrow]
    joined = jnp.concatenate([context[j] for j in range(parts)], axis=1)
    both = grad_ctx.astype(f32) * joined.astype(f32)
    high = both.astype(bf16)
    rest = (both - high.astype(f32)).astype(bf16)
    delta_out[...] = dot_nt(pick[...], high) + dot_nt(pick[...], rest)
    gg1[...] += jnp.sum(dy * n, axis=0, keepdims=True)
    gb1[...] += jnp.sum(dy, axis=0, keepdims=True)
    gob[...] += jnp.sum(low.astype(f32), axis=0, keepdims=True)
    weight_grad[...] += dot_tn(joined, low)

    @pl.when(step == pl.num_programs(0) - 1)
    def _():
        for j in range(parts):
            gow[j] = weight_grad[:, j * narrow:(j + 1) * narrow].astype(bf16)


def inner_back(grad_normed, n1, r1, g1, context, ow, head_of_row):
    t, d = n1.shape
    parts, _, narrow = context.shape
    count = len(head_of_row)
    feature = jnp.arange(d, dtype=jnp.int32) // HD
    pick = (feature[None, :] == jnp.array(head_of_row, jnp.int32)[:, None]).astype(bf16)
    tile = pl.BlockSpec((parts, ROWS, narrow), lambda r: (0, r, 0))
    vector = whole((1, d))
    return call(
        inner_kernel, "inner_back", (t // ROWS,),
        [held(), held(), held(), vector, tile, held(), whole((count, d))],
        [held(), vector, vector, vector, whole((parts, d, narrow)), tile,
         pl.BlockSpec((count, ROWS), lambda r: (0, r))],
        [pltpu.VMEM((t, d), f32)] + [sds((1, d), f32)] * 3
        + [sds((parts, d, narrow), bf16), sds((parts, t, narrow), bf16), sds((count, t), f32)],
        [pltpu.VMEM((d, d), f32)],
        cost=guess(4e9, 10e6), limit=SMALL,
    )(grad_normed, n1, r1, g1, context, ow, pick)


def shards(
    tokens, bucket, lengths, cotangent,
    query_weight, query_bias, key_weight, value_weight, value_bias, out_weight, out_bias,
    norm1_gain, norm1_bias, up_weight, up_bias, down_weight, down_bias, norm2_gain, norm2_bias,
):
    t, d = tokens.shape
    dp, fsdp = lax.axis_size("dp"), lax.axis_size("fsdp")
    lengths = lengths[0]

    place = places()
    depth = dp // 2
    tall, narrow = d // dp, d // fsdp
    width = 4 * narrow
    by_head = narrow == HEADS * HD and fsdp == 4
    down_t = down_weight.T

    if by_head:
        join = lambda *v: jnp.concatenate(v)[None]
        blank = jnp.zeros((narrow,), bf16)
        block = jnp.concatenate([
            columns_of(query_weight, key_weight, value_weight, out_weight),
            columns_of(query_bias[None], blank[None], value_bias[None], out_bias[None]),
            join(norm1_gain, norm1_bias, down_bias, norm2_gain),
            join(norm2_bias, blank, blank, blank),
            up_bias[None],
            jnp.zeros((12, width), bf16),
        ])
        along = Once([(block, "dp", along_z(s)) for s in range(1, depth)])
        x_t, = beside([along], lambda x: (x.T,), (tokens,))
        up_weight, down_t, own = lax.optimization_barrier((up_weight, down_t, [block] + along.got))
        up_z, down_z = gather_z(up_weight), gather_z(down_t)
        own = line_up(place, own)
        swap = lambda v: (v, "dp", across_cores())
        in_plane = lambda v, s: (v, "fsdp", [(f, f ^ s) for f in range(fsdp)])
        paired = Once([swap(own)])
        beside([paired])
        sides = Once([in_plane(own, 1), in_plane(own, 2)])
        one = lambda away: functools.partial(attend_one, away, fsdp)
        run = (bucket, lengths, tokens)
        *shared, kept_0, lse_0 = beside([sides], one(0), (place, *run, own, paired.got[0], []), out=3)
        own_x, own_y = sides.got
        paired = Once([swap(own_x), swap(own_y)])
        corner = Once([(select_core(own_y, own_x), ("dp", "fsdp"), along_bit(0))])
        to_u, to_d = Gather(up_z), Gather(down_z)
        beside([paired])
        pair_x, pair_y = paired.got
        *shared, kept_1, lse_1 = beside([corner], one(1), (place, *run, own_x, pair_x, shared), out=3)
        own_c = corner.got[0]
        paired = Once([swap(own_c)])
        *shared, kept_2, lse_2 = beside([paired, to_u], one(2), (place, *run, own_y, pair_y, shared), out=3)
        *shared, kept_3, lse_3 = beside([to_u], one(3), (place, *run, own_c, paired.got[0], shared), out=3)
        context, weights, slabs = shared
        slabs = slabs.astype(f32)
        spread = lambda r, m: slabs[:, r, m * narrow:(m + 1) * narrow].reshape(1, d)
        ob = slabs[:, 0, width - narrow:].reshape(1, d)
        g1, b1, db, g2, b2 = spread(1, 0), spread(1, 1), spread(1, 2), spread(1, 3), spread(2, 0)
        ub = slabs[:, 3]
        ow, last = weights.reshape(fsdp, d, width), 2
        head_of_row = [j * HEADS + a if a < HEADS else -1 for j in range(fsdp) for a in range(8)]
    else:
        block = jnp.concatenate([
            jnp.concatenate([query_weight, key_weight, value_weight, out_weight], axis=1),
            jnp.concatenate([query_bias, value_bias, out_bias, norm1_gain])[None],
            jnp.concatenate([norm1_bias, down_bias, norm2_gain, norm2_bias])[None],
            up_bias[None],
            jnp.zeros((13, width), bf16),
        ])
        to_a, to_u, to_d = Gather(gather_z(block)), Gather(gather_z(up_weight)), Gather(gather_z(down_t))
        finish(to_a)
        weights, vectors, ub = assemble(place, to_a.blocks)
        qb, vb, ob, g1 = (vectors[m, 0:1] for m in range(4))
        b1, db, g2, b2 = (vectors[m, 1:2] for m in range(4))
        ub = ub[:, 2]
        q, k, v, context, lse = attend(bucket, lengths, tokens, weights, qb, vb)
        context, ow, last = context[None], weights[3:], 0
        pairs = d // PAIR
        head_of_row = [2 * p + half if p < pairs else -1 for half in range(2) for p in range(HD)]

    n1, r1, low, low_t, ow = beside([to_u, to_d], attended, (tokens, context, ow, last, ob, g1, b1), key=4, out=1)
    finish(to_u)
    active, slope, uw = beside([to_d], up, (place, low, ub, to_u.blocks))
    finish(to_d)
    out, pooled, mixed, branch, gdb, gg2, gb2, send_d, keep_d, dw = down(
        place, bucket, lengths, active, n1, g1, b1, db, g2, b2, cotangent, to_d.blocks
    )
    of_d = Scatter(keep_d, send_d)
    send_u, keep_u, gub, grad_normed = beside(
        [of_d], feed_back,
        (place, branch, slope, dw.reshape(dp, d, -1), uw.reshape(fsdp, d, -1), low_t, mixed),
    )
    of_u = Scatter(keep_u, send_u)
    inner, gg1, gb1, gob, gow, grad_context, delta = beside(
        [of_d, of_u], inner_back, (grad_normed, n1, r1, g1, context, ow, head_of_row), key=3, out=4
    )

    if by_head:
        cut = lambda v: v.reshape(fsdp, 1, narrow)
        nothing = jnp.zeros((fsdp, 1, narrow), f32)
        slab = jnp.concatenate([
            jnp.concatenate([nothing, nothing, nothing, cut(gob)], axis=2),
            jnp.concatenate([cut(gg1), cut(gb1), cut(gdb), cut(gg2)], axis=2),
            jnp.concatenate([cut(gb2), nothing, nothing, nothing], axis=2),
            gub.reshape(fsdp, 1, width),
            jnp.zeros((fsdp, 12, width), f32),
        ], axis=1)
        delta = delta.reshape(fsdp, 8, t)

        def back(away, moves, kept, lse, grad_in):
            args = (place, bucket, lengths, x_t, kept, grad_context, lse, delta, weights, gow, slab, grad_in)
            return beside(moves, functools.partial(attend_back_one, away, fsdp, away == 0), args)

        send_3, keep_3, so_far = back(3, [of_d, of_u], kept_3, lse_3, inner)
        swap_3 = Once([swap(send_3)])
        send_1, keep_1, so_far = back(1, [swap_3, of_d, of_u], kept_1, lse_1, so_far)
        corner = Once([(add(keep_3, swap_3.got[0]), ("dp", "fsdp"), along_bit(0))])
        send_2, keep_2, so_far = back(2, [corner, of_u], kept_2, lse_2, so_far)
        sums = Once([swap(send_1), swap(send_2)])
        beside([sums])
        add_both = lambda *v: sum(u.astype(f32) for u in v)
        through = corner.got[0]
        sum_1 = add_both(keep_1, sums.got[0]) + select_core(jnp.zeros_like(through), through).astype(f32)
        sum_2 = add_both(keep_2, sums.got[1]) + select_core(through, jnp.zeros_like(through)).astype(f32)
        sides = Once([in_plane(sum_1.astype(bf16), 1), in_plane(sum_2.astype(bf16), 2)])
        send_0, keep_0, input_grad = back(0, [sides, of_u], kept_0, lse_0, so_far)
        sums = Once([swap(send_0)])
        beside([sums, of_u])
        total = add_both(keep_0, sums.got[0], *sides.got)
        z = lax.axis_index("dp") // 2
        at = lambda s: lax.dynamic_index_in_dim(total, (z - s) % depth, 0, keepdims=False)
        along = Once([(at(s).astype(bf16), "dp", along_z(-s)) for s in range(1, depth)])
        beside([along, of_u])
        made_a = add_both(at(0), *along.got)
        finish(of_d)
        finish(of_u)
        made = columns_back(made_a[:tall])
        gqb, _, gvb, gob = (v[0] for v in columns_back(made_a[tall:tall + 1]))
        piece = lambda r, m: made_a[tall + r, m * narrow:(m + 1) * narrow]
        vectors = (gqb, gvb, gob, piece(1, 0), piece(1, 1), piece(1, 2), piece(1, 3), piece(2, 0))
        gub = made_a[tall + 3]
    else:
        gqw, gkw, gvw, gqb, gvb, input_grad = attend_back(
            bucket, lengths, tokens.T, q, k, v, grad_context[0], lse, delta, weights, inner
        )
        firsts = jnp.stack([gqb, gvb, gob, gg1])
        seconds = jnp.stack([gb1, gdb, gg2, gb2])
        vectors = jnp.concatenate([firsts, seconds, jnp.zeros((4, 14, d), f32)], axis=1)
        of_a = Scatter(*reversed(pack(place, (gqw, gkw, gvw, gow[0]), vectors, gub)))
        while not (of_a.done() and of_u.done() and of_d.done()):
            beside([of_a, of_u, of_d])
        made_a = of_a.total
        made = [made_a[:tall, m * narrow:(m + 1) * narrow] for m in range(4)]
        vectors = [made_a[tall + n, m * narrow:(m + 1) * narrow] for n in range(2) for m in range(4)]
        gub = made_a[tall + 2]
    return (
        out, pooled, input_grad, made[0], vectors[0], made[1], made[2], vectors[1], made[3], vectors[2], vectors[3],
        vectors[4], of_u.total, gub, of_d.total.T, vectors[5], vectors[6], vectors[7],
    )


def solution(mesh):
    tall, square, vector = P(("dp", "fsdp"), None), P("dp", "fsdp"), P("fsdp")
    in_specs = (
        tall, P(("dp", "fsdp")), tall, tall, square, vector, square, square, vector, square, vector,
        vector, vector, square, vector, square, vector, vector, vector,
    )
    out_specs = (
        tall, tall, tall, square, vector, square, square, vector, square, vector, vector, vector,
        square, vector, square, vector, vector, vector,
    )
    return jax.shard_map(shards, mesh=mesh, in_specs=in_specs, out_specs=out_specs, check_vma=False)
```

```python
import functools

import jax
import jax.numpy as jnp
from jax import lax
from jax.experimental import pallas as pl
from jax.experimental.pallas import tpu as pltpu
from jax.sharding import PartitionSpec as P

H = 12
HD = 64
PLEN = 512
QLEN = 128
PAIR = 2 * HD
ROWS = 256
FEED_ROWS = 512

epsilon = 1e-06
masked_score = -1e30
f32 = jnp.float32
bf16 = jnp.bfloat16
LIMIT = 60 * 1024 * 1024
SMALL = 24 * 1024 * 1024


def dot(left, right):
    return jnp.dot(left, right, preferred_element_type=f32)


def dot_nt(left, right):
    return lax.dot_general(left, right, (((1,), (1,)), ((), ())), preferred_element_type=f32)


def dot_tn(left, right):
    return lax.dot_general(left, right, (((0,), (0,)), ((), ())), preferred_element_type=f32)


BIG = 16 * 1024


def far(v, least):
    if v.size * v.dtype.itemsize < least:
        return v
    return pltpu.with_memory_space_constraint(v, pltpu.HBM)


def call(
    kernel, name, grid, in_specs, out_specs, out_shape, scratch=(), prefetch=0, cost=None, limit=LIMIT, aliases={},
    least=BIG, free=pltpu.VMEM,
):
    several = isinstance(out_shape, list)
    shapes = [
        pltpu.HBM(v.shape, v.dtype)
        if isinstance(v, jax.ShapeDtypeStruct) and v.size * v.dtype.itemsize >= BIG else v
        for v in (out_shape if several else [out_shape])
    ]
    run = pl.pallas_call(
        kernel,
        name=name,
        grid_spec=pltpu.PrefetchScalarGridSpec(
            num_scalar_prefetch=prefetch,
            grid=grid,
            in_specs=in_specs,
            out_specs=out_specs,
            scratch_shapes=list(scratch),
        ),
        out_shape=shapes if several else shapes[0],
        input_output_aliases=aliases,
        compiler_params=pltpu.CompilerParams(
            vmem_limit_bytes=limit, dimension_semantics=("arbitrary",) * len(grid)
        ),
        cost_estimate=cost,
    )

    def run_far(*args):
        given = [
            v if spec.memory_space in (pltpu.VMEM, free) else far(v, least) for v, spec in zip(args[prefetch:], in_specs)
        ]
        return run(*args[:prefetch], *given)

    return run_far


def whole(shape):
    return pl.BlockSpec(shape, lambda *_: (0,) * len(shape))


def sds(shape, dtype):
    return jax.ShapeDtypeStruct(shape, dtype)


def held():
    return pl.BlockSpec(memory_space=pltpu.VMEM)


def guess(flops, nbytes):
    return pl.CostEstimate(flops=int(flops), bytes_accessed=int(nbytes), transcendentals=0)


def reverse(s, bits):
    return sum(((s >> b) & 1) << (bits - 1 - b) for b in range(bits))


def axis_facts():
    dp, fsdp = lax.axis_size("dp"), lax.axis_size("fsdp")
    return dp, fsdp, dp // 2, fsdp.bit_length() - 1


def along_z(hop):
    dp = lax.axis_size("dp")
    return [(d, (d + 2 * hop) % dp) for d in range(dp)]


def across_cores():
    return [(d, d ^ 1) for d in range(lax.axis_size("dp"))]


def along_bit(r):
    dp, fsdp, _, bits = axis_facts()
    pairs = []
    for d in range(dp):
        flip = 1 << (r if d % 2 == 0 else bits - 1 - r)
        pairs += [(d * fsdp + f, d * fsdp + (f ^ flip)) for f in range(fsdp)]
    return pairs


def select_core(even, odd):
    return jnp.where(lax.axis_index("dp") % 2 == 0, even, odd)


def gather_z(block):
    dp = lax.axis_size("dp")
    groups = [list(range(core, dp, 2)) for core in range(2)]
    return lax.all_gather(block, "dp", axis=0, axis_index_groups=groups)


class Gather:
    def __init__(self, along):
        self.held, self.round, self.blocks = along[None], 0, None

    def stage(self):
        bits = axis_facts()[3]
        if self.round < bits:
            return [(self.held, ("dp", "fsdp"), along_bit(self.round))]
        return [(v, "dp", across_cores()) for v in self.own]

    def take(self, got):
        bits = axis_facts()[3]
        if self.round < bits - 1:
            self.held = jnp.concatenate([self.held] + got)
        elif self.round < bits:
            self.own = [self.held] + got
        else:
            self.blocks = self.own + got
        self.round += 1

    def done(self):
        return self.blocks is not None


class Once:
    def __init__(self, sends):
        self.sends, self.got = sends, None

    def stage(self):
        return self.sends

    def take(self, got):
        self.got = got

    def done(self):
        return self.got is not None


def add(left, right):
    return (left.astype(f32) + right.astype(f32)).astype(bf16)


class Scatter:
    def __init__(self, keep, send):
        self.keep, self.send, self.round, self.total = keep, [send], axis_facts()[3], None

    def stage(self):
        _, _, depth, bits = axis_facts()
        if self.round == bits:
            return [(self.send[0], "dp", across_cores())]
        if self.round >= 0:
            return [(self.send[0], ("dp", "fsdp"), along_bit(self.round))]
        return [(self.send[s - 1], "dp", along_z(-s)) for s in range(1, depth)]

    def take(self, got):
        depth = axis_facts()[2]
        keep = self.keep
        if self.round > 0:
            half = keep.shape[0] // 2
            self.send = [add(keep[half:], got[0][half:])]
            self.keep = add(keep[:half], got[0][:half])
        elif self.round == 0:
            self.send = [add(keep[0, s], got[0][0, s]) for s in range(1, depth)]
            self.keep = keep[0, 0].astype(f32) + got[0][0, 0].astype(f32)
        else:
            for part in got:
                keep = keep + part.astype(f32)
            self.total = keep
        self.round -= 1

    def done(self):
        return self.total is not None


def beside(moves, compute=None, args=(), key=0, out=0):
    moves = [move for move in moves if not move.done()]
    stages = [move.stage() for move in moves]
    arrays = [[v for v, _, _ in stage] for stage in stages]
    args = list(args)
    results = ()
    if compute:
        args[key], arrays = lax.optimization_barrier((args[key], arrays))
        results = list(compute(*args))
    else:
        arrays = lax.optimization_barrier(arrays)
    got = [
        [lax.ppermute(v, axis, perm) for v, (_, axis, perm) in zip(sent, stage)]
        for sent, stage in zip(arrays, stages)
    ]
    if compute:
        results[out], got = lax.optimization_barrier((results[out], got))
    else:
        got = lax.optimization_barrier(got)
    for move, parts in zip(moves, got):
        move.take(parts)
    return results


def finish(move):
    while not move.done():
        beside([move])


def places():
    dp, fsdp, depth, bits = axis_facts()
    d, f = lax.axis_index("dp"), lax.axis_index("fsdp")
    z, core = d // 2, d % 2
    slot = jnp.arange(depth, dtype=jnp.int32)
    index = jnp.arange(fsdp, dtype=jnp.int32)
    mirror = sum((((index >> b) & 1) << (bits - 1 - b) for b in range(bits)), jnp.zeros_like(index))
    rows, slots, columns = [], [], []
    for n in range(2):
        there = core ^ n
        rows.append(2 * ((z - slot) % depth) + there)
        away = index ^ f
        mirrored = sum((((away >> b) & 1) << (bits - 1 - b) for b in range(bits)), jnp.zeros_like(index))
        slots.append(jnp.where(there == 0, away, mirrored))
        columns.append(f ^ jnp.where(there == 0, index, mirror))
    neighbours = [(f ^ s)[None] for s in range(fsdp)]
    return jnp.concatenate(rows + slots + columns + [core[None]] + neighbours).astype(jnp.int32)


def row_of(place, n, slot, depth):
    return place[n * depth + slot]


def slot_of(place, n, j, depth, fsdp):
    return place[2 * depth + n * fsdp + j]


def column_of(place, n, s, depth, fsdp):
    return place[2 * depth + 2 * fsdp + n * fsdp + s]


def core_of(place, depth, fsdp):
    return place[2 * depth + 4 * fsdp]


def neighbour_of(place, s, depth, fsdp):
    return place[2 * depth + 4 * fsdp + 1 + s]


def block_copies(place, arrays, target, sems):
    half, depth = arrays[0].shape[:2]
    fsdp = 2 * half
    copies = []
    for a, array in enumerate(arrays):
        core = lax.rem(core_of(place, depth, fsdp) + a // 2, 2)
        for q in range(half):
            j = column_of(place, a // 2, (a % 2) * half + q, depth, fsdp)
            copies.append(pltpu.make_async_copy(array.at[q], target(core, j), sems.at[len(copies)]))
    return copies


def assemble_kernel(place, own_low, own_high, other_low, other_high, weights, vectors, ub):
    step = pl.program_id(0)
    half, _, height, width = own_low.shape
    fsdp, depth, tall = 2 * half, pl.num_programs(0) // 2, height - 16
    narrow = width // 4

    def fill(n, low, high):
        pieces = []
        for j in range(fsdp):
            slot = slot_of(place, n, j, depth, fsdp)
            upper, q = slot >= half, lax.rem(slot, half)
            pieces.append(jnp.where(upper, high[q, 0].astype(f32), low[q, 0].astype(f32)))
        for m in range(4):
            row = jnp.concatenate([p[:, m * narrow:(m + 1) * narrow] for p in pieces], axis=1)
            weights[m] = row[:tall].astype(bf16)
            vectors[m] = row[tall:]
        for j in range(fsdp):
            ub[j] = pieces[j][tall:]

    @pl.when(step < depth)
    def _():
        fill(0, own_low, own_high)

    @pl.when(step >= depth)
    def _():
        fill(1, other_low, other_high)


def row_at(place, s, depth, fsdp):
    core = core_of(place, depth, fsdp)
    return 2 * lax.rem(s, depth) + lax.rem(core + s // depth, 2)


def assemble(place, arrays):
    half, depth, height, width = arrays[0].shape
    fsdp, tall, d = 2 * half, height - 16, half * width // 2
    own = pl.BlockSpec((half, 1, height, width), lambda s, place: (0, jnp.minimum(s, depth - 1), 0, 0))
    other = pl.BlockSpec((half, 1, height, width), lambda s, place: (0, jnp.maximum(s - depth, 0), 0, 0))
    return call(
        assemble_kernel, "assemble", (2 * depth,),
        [own, own, other, other],
        [pl.BlockSpec((4, tall, d), lambda s, place: (0, row_at(place, s, depth, fsdp), 0)), whole((4, 16, d)),
         whole((fsdp, 16, width))],
        [sds((4, 2 * depth * tall, d), bf16), sds((4, 16, d), f32), sds((fsdp, 16, width), f32)],
        prefetch=1, cost=guess(1e9, 11e6),
    )(place, *arrays)


def pack_kernel(place, gq, gk, gv, go, vectors, gub, send, keep):
    step = pl.program_id(0)
    fsdp, _, height, width = send.shape
    depth, tall, narrow = pl.num_programs(0) // 2, height - 16, width // 4

    def fill(n, out):
        for j in range(fsdp):
            slot = slot_of(place, n, j, depth, fsdp)
            columns = slice(j * narrow, (j + 1) * narrow)
            out[slot, 0, :tall, :] = jnp.concatenate(
                [g[:, columns].astype(f32) for g in (gq, gk, gv, go)], axis=1
            ).astype(bf16)
            slab = jnp.concatenate([vectors[m, :, columns] for m in range(4)], axis=1)
            third = lax.broadcasted_iota(jnp.int32, slab.shape, 0) == 2
            out[slot, 0, tall:, :] = jnp.where(third, gub[j], slab).astype(bf16)

    @pl.when(step < depth)
    def _():
        fill(1, send)

    @pl.when(step >= depth)
    def _():
        fill(0, keep)


def pack(place, grads, vectors, gub):
    d = grads[0].shape[0]
    dp, fsdp, depth, _ = axis_facts()
    tall, width = d // dp, 4 * d // fsdp
    rows = pl.BlockSpec((tall, d), lambda s, place: (place[(s + depth) % (2 * depth)], 0))
    sent = pl.BlockSpec((fsdp, 1, tall + 16, width), lambda s, place: (0, jnp.minimum(s, depth - 1), 0, 0))
    kept = pl.BlockSpec((fsdp, 1, tall + 16, width), lambda s, place: (0, jnp.maximum(s - depth, 0), 0, 0))
    return call(
        pack_kernel, "pack", (2 * depth,),
        [rows, rows, rows, rows, whole((4, 16, d)), whole((fsdp, 1, width))],
        [sent, kept],
        [sds((fsdp, depth, tall + 16, width), bf16)] * 2,
        prefetch=1, cost=guess(1e9, 11e6),
    )(place, *grads, vectors, gub)


def segment_lanes(bucket, lengths, queries_ext, keys_ext):
    row_count = queries_ext.shape[0]
    slots = lengths.shape[0]
    shape = (row_count, PAIR)
    row = lax.broadcasted_iota(jnp.int32, shape, 0)
    lane = lax.broadcasted_iota(jnp.int32, shape, 1) % HD
    passage = bucket[0] == 1
    segment = jnp.where(passage, row // PLEN, row // QLEN)
    position = jnp.where(passage, row % PLEN, row % QLEN)
    limit = jnp.zeros(shape, jnp.int32)
    for s in range(slots):
        limit = jnp.where(segment == s, lengths[s], limit)
    alive = position < limit
    same = segment == lane
    queries_ext[...] = jnp.where(same, 1.0, 0.0).astype(bf16)
    keys_ext[...] = jnp.where((lane < slots) & ~(same & alive), masked_score, 0.0).astype(bf16)


def attend_kernel(
    bucket, lengths, x, qw, kw, vw, qb, vb,
    q_out, k_out, v_out, context_out, lse_out,
    queries_ext, keys_ext, lse_all,
):
    pair = pl.program_id(0)
    row_count = x.shape[0]

    @pl.when(pair == 0)
    def _():
        segment_lanes(bucket, lengths, queries_ext, keys_ext)
        lse_all[...] = jnp.zeros_like(lse_all)

    weights = jnp.concatenate([qw[0], kw[0], vw[0]], axis=1)
    qb_row = qb[...]
    vb_row = vb[...]
    low_half = lax.broadcasted_iota(jnp.int32, (PLEN, PAIR), 1) < HD
    lane = lax.broadcasted_iota(jnp.int32, (PLEN, PAIR), 1)

    def block(b, carry):
        rows = pl.ds(pl.multiple_of(b * PLEN, PLEN), PLEN)
        qkv = dot(x[rows, :], weights)
        queries = ((qkv[:, :PAIR] + qb_row).astype(bf16).astype(f32) * HD ** (-0.5)).astype(bf16)
        keys = qkv[:, PAIR:2 * PAIR].astype(bf16)
        values = (qkv[:, 2 * PAIR:] + vb_row).astype(bf16)
        q_out[rows, :] = queries
        k_out[rows, :] = keys
        v_out[rows, :] = values
        q_ext = queries_ext[rows, :]
        k_ext = keys_ext[rows, :]
        ones = jnp.ones_like(values)
        sums, tops = [], []
        for half in range(2):
            mine = low_half if half == 0 else ~low_half
            scores = dot_nt(jnp.where(mine, queries, q_ext), jnp.where(mine, keys, k_ext))
            top = jnp.max(scores, axis=-1, keepdims=True)
            weight = jnp.exp(scores - top).astype(bf16)
            sums.append(dot(weight, jnp.where(mine, values, ones)))
            tops.append(top)
        numer = jnp.where(low_half, sums[0], sums[1])
        denom = pltpu.roll(jnp.where(low_half, sums[1], sums[0]), HD, 1)
        context_out[rows, :] = (numer / denom).astype(bf16)
        lse = jnp.where(low_half, tops[0], tops[1]) + jnp.log(denom)
        mine = (lane % HD) == pair
        lse_all[rows, :] = jnp.where(mine, lse, lse_all[rows, :])
        return carry

    lax.fori_loop(0, row_count // PLEN, block, 0)

    @pl.when(pair == pl.num_programs(0) - 1)
    def _():
        lse_out[...] = lse_all[...].T


def attend(bucket, lengths, x, weights, qb, vb):
    t, d = x.shape
    pairs = d // PAIR
    column = lambda m: pl.BlockSpec((1, d, PAIR), lambda p, *_: (m, 0, p))
    vector = pl.BlockSpec((1, PAIR), lambda p, *_: (0, p))
    tall = pl.BlockSpec((t, PAIR), lambda p, *_: (0, p))
    return call(
        attend_kernel, "attend", (pairs,),
        [whole((t, d)), column(0), column(1), column(2), vector, vector],
        [tall, tall, tall, tall, whole((PAIR, t))],
        [sds((t, d), bf16)] * 4 + [sds((PAIR, t), f32)],
        [pltpu.VMEM((t, PAIR), bf16), pltpu.VMEM((t, PAIR), bf16), pltpu.VMEM((t, PAIR), f32)],
        prefetch=2, cost=guess(15e9, 12e6),
    )(bucket, lengths, x, weights, weights, weights, qb, vb)


HEADS = 3
USED = 5 * PAIR


def block_kernel(q, k, v, o, *refs):
    *vectors, ub, out = refs
    tall = q.shape[0]
    out[:tall, :] = jnp.concatenate(
        [part.astype(f32) for part in (
            q[:, :PAIR], k[:, :PAIR], v[:, :PAIR], q[:, PAIR:], k[:, PAIR:], v[:, PAIR:], o[...]
        )], axis=1
    ).astype(bf16)
    each = [v[...].astype(f32)[None, :] for v in vectors]
    first, second = jnp.concatenate(each[:4], axis=1), jnp.concatenate(each[4:], axis=1)
    third = ub[...].astype(f32)[None, :]
    row = lax.broadcasted_iota(jnp.int32, (16, out.shape[1]), 0)
    out[tall:, :] = jnp.where(
        row == 0, first, jnp.where(row == 1, second, jnp.where(row == 2, third, 0.0))
    ).astype(bf16)


def make_block(q, k, v, o, *vectors):
    tall, narrow = q.shape
    out = (tall + 16, 4 * narrow)
    return call(
        block_kernel, "block", (1,), [whole(q.shape)] * 4 + [whole(u.shape) for u in vectors], whole(out),
        sds(out, bf16), cost=guess(1e6, 1e6), limit=SMALL, least=0,
    )(q, k, v, o, *vectors)


def unblock_kernel(total, *refs):
    got, (gq, gk, gv, go, *vectors) = refs[:-13], refs[-13:]
    tall, narrow = gq.shape
    block = total[...]
    for part in got:
        block = block + part[...].astype(f32)

    def split(v):
        return (
            jnp.concatenate([v[:, :PAIR], v[:, 3 * PAIR:3 * PAIR + HD]], axis=1),
            jnp.concatenate([v[:, PAIR:2 * PAIR], v[:, 3 * PAIR + HD:4 * PAIR]], axis=1),
            jnp.concatenate([v[:, 2 * PAIR:3 * PAIR], v[:, 4 * PAIR:4 * PAIR + HD]], axis=1),
            v[:, 4 * PAIR + HD:],
        )

    gq[...], gk[...], gv[...], go[...] = split(block[:tall])
    qb, _, vb, ob = split(block[tall:tall + 1])
    rest = [block[tall + r:tall + r + 1, m * narrow:(m + 1) * narrow] for r, m in ((1, 0), (1, 1), (1, 2), (1, 3), (2, 0))]
    for ref, row in zip(vectors, (qb, vb, ob, *rest, block[tall + 3:tall + 4])):
        ref[...] = row[0]


def unblock(total, got):
    height, width = total.shape
    tall, narrow = height - 16, width // 4
    shapes = [(tall, narrow)] * 4 + [(narrow,)] * 8 + [(width,)]
    return call(
        unblock_kernel, "unblock", (1,), [whole(total.shape)] * (1 + len(got)), [whole(v) for v in shapes],
        [sds(v, f32) for v in shapes], cost=guess(1e6, 1e6), limit=SMALL,
    )(total, *got)


def line_up_kernel(place, *refs):
    out = refs[-1]
    depth = len(refs) - 1
    for s in range(depth):
        out[row_of(place, 0, s, depth) // 2] = refs[s][...]


def line_up(place, parts):
    shape = parts[0].shape
    out = (len(parts), *shape)
    return call(
        line_up_kernel, "line_up", (1,), [whole(shape)] * len(parts), whole(out), sds(out, parts[0].dtype),
        prefetch=1, cost=guess(1e6, 1e6), limit=SMALL,
    )(place, *parts)


def attend_one_kernel(
    away, place, bucket, lengths, x, own, other, *refs,
):
    context_out, w_out, slab_out, kept, lse_out, queries_ext, keys_ext, weights_here, sems = refs[-9:]
    depth, _, tall, width = weights_here.shape
    step, fsdp = pl.program_id(0), w_out_fsdp(place, depth)
    core = core_of(place, depth, fsdp)
    j = neighbour_of(place, away, depth, fsdp)
    copies = [
        pltpu.make_async_copy(ref.at[:, :tall, :], weights_here.at[:, lax.rem(core + n, 2)], sems.at[n])
        for n, ref in enumerate((own, other))
    ]
    copies.append(pltpu.make_async_copy(own.at[0, tall:, :], slab_out.at[0], sems.at[2]))
    onward = pltpu.make_async_copy(weights_here, w_out.at[j], sems.at[3])

    @pl.when(step == 0)
    def _():
        for copy in copies:
            copy.start()
        segment_lanes(bucket, lengths, queries_ext, keys_ext)
        for copy in copies:
            copy.wait()
        onward.start()

    narrow = width // 4
    row = slab_out[0, 0:1, :].astype(f32)
    qb, vb = row[:, :narrow], row[:, narrow:2 * narrow]
    none = jnp.zeros((1, PAIR), f32)
    bias = jnp.concatenate(
        [qb[:, :PAIR], none, vb[:, :PAIR], qb[:, PAIR:], none[:, :HD], vb[:, PAIR:], none[:, :HD]], axis=1
    )
    lane = lax.broadcasted_iota(jnp.int32, (PLEN, PAIR), 1)
    low_half = lane < HD
    scale = HD ** (-0.5)

    rows = pl.ds(pl.multiple_of(step * PLEN, PLEN), PLEN)
    weights = weights_here[:, :, :, :USED].reshape(2 * depth * tall, USED)
    qkv = dot(x[...], weights) + bias
    tiles = [qkv[:, n * PAIR:(n + 1) * PAIR].astype(bf16) for n in range(5)]
    tiles[0] = tiles[0] * jnp.array(scale, bf16)
    tiles[3] = jnp.where(low_half, tiles[3] * jnp.array(scale, bf16), tiles[3])
    for n in range(5):
        kept[:, n * PAIR:(n + 1) * PAIR] = tiles[n]
    queries, keys, values, both, values_two = tiles
    keys_two = pltpu.roll(both.astype(f32), HD, 1).astype(bf16)
    q_ext, k_ext = queries_ext[rows, :], keys_ext[rows, :]
    ones = jnp.ones_like(values)

    def one(mine, q, k, v):
        scores = dot_nt(jnp.where(mine, q, q_ext), jnp.where(mine, k, k_ext))
        top = jnp.max(scores, axis=-1, keepdims=True)
        weight = jnp.exp(scores - top).astype(bf16)
        return top, dot(weight, jnp.where(mine, v, ones))

    top_a, sum_a = one(low_half, queries, keys, values)
    top_b, sum_b = one(~low_half, queries, keys, values)
    top_c, sum_c = one(low_half, both, keys_two, values_two)
    denom = pltpu.roll(jnp.where(low_half, sum_b, sum_a), HD, 1)
    denom_c = pltpu.roll(sum_c, HD, 1)
    context_out[0, :, :PAIR] = (jnp.where(low_half, sum_a, sum_b) / denom).astype(bf16)
    context_out[0, :, PAIR:] = (sum_c / denom_c)[:, :HD].astype(bf16)
    lse_ab = jnp.where(low_half, top_a, top_b) + jnp.log(denom)
    lse_c = top_c + jnp.log(denom_c)
    every = jnp.where((lane >= 32) & low_half, lse_c, lse_ab).T
    lse_out[0:1, :] = every[0:1]
    lse_out[1:2, :] = every[HD:HD + 1]
    lse_out[2:3, :] = every[32:33]

    @pl.when(step == pl.num_programs(0) - 1)
    def _():
        onward.wait()


def w_out_fsdp(place, depth):
    return (place.shape[0] - 2 * depth - 1) // 5


def attend_one(away, fsdp, place, bucket, lengths, x, own, other, shared):
    t, d = x.shape
    depth, height, width = own.shape
    tall, narrow = height - 16, d // fsdp
    shapes = [(fsdp, t, narrow), (fsdp, depth, 2, tall, width), (fsdp, 16, width)]
    j = lambda place: neighbour_of(place, away, depth, fsdp)
    any_space = pl.BlockSpec(memory_space=pl.ANY)
    return call(
        functools.partial(attend_one_kernel, away), "attend", (t // PLEN,),
        [pl.BlockSpec((PLEN, d), lambda s, *_: (s, 0)), any_space, any_space] + [any_space] * len(shared),
        [
            pl.BlockSpec((1, PLEN, narrow), lambda s, place, *_: (j(place), s, 0)), any_space,
            pl.BlockSpec((1, 16, width), lambda s, place, *_: (j(place), 0, 0)),
            pl.BlockSpec((PLEN, USED), lambda s, *_: (s, 0)), pl.BlockSpec((8, PLEN), lambda s, *_: (0, s)),
        ],
        [sds(shape, bf16) for shape in shapes] + [sds((t, USED), bf16), sds((8, t), f32)],
        [pltpu.VMEM((t, PAIR), bf16), pltpu.VMEM((t, PAIR), bf16), pltpu.VMEM((depth, 2, tall, width), bf16),
         pltpu.SemaphoreType.DMA((4,))],
        prefetch=3, cost=guess(5e9, 8e6), limit=SMALL, free=pl.ANY,
        aliases={6 + n: n for n in range(len(shared))},
    )(place, bucket, lengths, x, own, other, *shared)


def attend_back_one_kernel(
    away, place, bucket, lengths, x_t_far, kept, grad_context, lse, delta, gow_far, inner, outer, gub,
    send, keep, grads_out,
    queries_ext, keys_ext, grads, found, sums, x_t, gow, sems,
):
    depth, height, width = send.shape
    tall = height - 16
    step, steps = pl.program_id(0), pl.num_programs(0)
    fsdp = w_out_fsdp(place, depth)
    core, j = core_of(place, depth, fsdp), neighbour_of(place, away, depth, fsdp)
    copies = [
        pltpu.make_async_copy(source, target, sems.at[n])
        for n, (source, target) in enumerate(((x_t_far, x_t), (gow_far.at[j], gow)))
    ]

    @pl.when(step == 0)
    def _():
        for copy in copies:
            copy.start()
        segment_lanes(bucket, lengths, queries_ext, keys_ext)
        sums[...] = jnp.zeros_like(sums)

    lane = lax.broadcasted_iota(jnp.int32, (PLEN, PAIR), 1)
    low_half = lane < HD
    scale = HD ** (-0.5)

    rows = pl.ds(pl.multiple_of(step * PLEN, PLEN), PLEN)
    queries, keys, values, both, values_two = (kept[:, n * PAIR:(n + 1) * PAIR] for n in range(5))
    keys_two = pltpu.roll(both.astype(f32), HD, 1).astype(bf16)
    q_ext, k_ext = queries_ext[rows, :], keys_ext[rows, :]
    nothing = jnp.zeros_like(values)
    grad_two = jnp.concatenate([grad_context[0, :, PAIR:]] * 2, axis=1)

    def one(a, mine, q, k, v, grad_ctx):
        scores = dot_nt(jnp.where(mine, k, k_ext), jnp.where(mine, q, q_ext))
        probs = jnp.exp(scores - lse[a:a + 1, :])
        grad_probs = dot_nt(jnp.where(mine, v, nothing), grad_ctx)
        grad_scores = (probs * (grad_probs - delta[0, a:a + 1, :])).astype(bf16)
        grad_v = dot(probs.astype(bf16), grad_ctx)
        grad_k = dot(grad_scores, q)
        grad_q = dot_tn(grad_scores, k) * scale
        return grad_q, grad_k, grad_v

    grad_pair = grad_context[0, :, :PAIR]
    q_a, k_a, v_a = one(0, low_half, queries, keys, values, grad_pair)
    q_b, k_b, v_b = one(1, ~low_half, queries, keys, values, grad_pair)
    q_c, k_c, v_c = one(2, low_half, both, keys_two, values_two, grad_two)
    made = [
        jnp.where(low_half, q_a, q_b), jnp.where(low_half, k_a, k_b), jnp.where(low_half, v_a, v_b),
        jnp.where(low_half, q_c, pltpu.roll(k_c, HD, 1)), jnp.where(low_half, v_c, 0.0),
    ]
    for n in range(5):
        low = made[n].astype(bf16)
        lanes = slice(n * PAIR, (n + 1) * PAIR)
        grads[rows, lanes] = low
        grads_out[:, lanes] = low
        sums[0:1, lanes] += jnp.sum(low.astype(f32), axis=0, keepdims=True)

    @pl.when(step == steps - 1)
    def _():
        for copy in copies:
            copy.wait()
        columns = grads[...]
        product = dot(x_t[...], columns)
        found[:, :4 * PAIR] = product[:, :4 * PAIR].astype(bf16)
        found[:, 4 * PAIR:] = jnp.concatenate(
            [product[:, 4 * PAIR:4 * PAIR + HD], gow[...].astype(f32)], axis=1
        ).astype(bf16)
        narrow = width // 4
        none = jnp.zeros((1, 3 * narrow), f32)
        inner_rows, outer_rows = inner[0], outer[0]
        first = jnp.concatenate([sums[0:1, :4 * PAIR + HD], inner_rows[2:3]], axis=1)
        second = jnp.concatenate([inner_rows[0:1], inner_rows[1:2], outer_rows[0:1], outer_rows[1:2]], axis=1)
        third = jnp.concatenate([outer_rows[2:3], none], axis=1)
        row = lax.broadcasted_iota(jnp.int32, (16, width), 0)
        rest = jnp.where(row == 1, second, jnp.where(row == 2, third, jnp.where(row == 3, gub[0], 0.0)))
        below = jnp.where(row == 0, first, rest).astype(bf16)
        for n, target in ((1, send), (0, keep)):
            for z in range(depth):
                i = 2 * z + lax.rem(core + n, 2)
                target[z, :tall, :] = found[pl.ds(pl.multiple_of(i * tall, 16), tall), :]
                target[z, tall:, :] = below


def attend_back_one(
    away, fsdp, depth, place, bucket, lengths, x_t, kept, grad_context, lse, delta, gow, inner, outer, gub
):
    d, t = x_t.shape
    tall, narrow, width = d // (2 * depth), d // fsdp, 4 * d // fsdp
    j = lambda place: neighbour_of(place, away, depth, fsdp)
    any_space = pl.BlockSpec(memory_space=pl.ANY)
    small = lambda *shape: pl.BlockSpec((1, *shape), lambda s, place, *_: (j(place), 0, 0))
    sent = (depth, tall + 16, width)
    rows = pl.BlockSpec((PLEN, USED), lambda s, *_: (s, 0))
    return call(
        functools.partial(attend_back_one_kernel, away), "attend_back", (t // PLEN,),
        [any_space, rows, pl.BlockSpec((1, PLEN, narrow), lambda s, place, *_: (j(place), s, 0)),
         pl.BlockSpec((8, PLEN), lambda s, *_: (0, s)),
         pl.BlockSpec((1, 8, PLEN), lambda s, place, *_: (j(place), 0, s)), any_space,
         small(8, narrow), small(8, narrow), small(1, width)],
        [whole(sent), whole(sent), rows],
        [sds(sent, bf16)] * 2 + [sds((t, USED), bf16)],
        [pltpu.VMEM((t, PAIR), bf16), pltpu.VMEM((t, PAIR), bf16), pltpu.VMEM((t, USED), bf16),
         pltpu.VMEM((d, width), bf16), pltpu.VMEM((8, USED), f32), pltpu.VMEM((d, t), bf16),
         pltpu.VMEM((d, narrow), bf16), pltpu.SemaphoreType.DMA((2,))],
        prefetch=3, cost=guess(10e9, 12e6), limit=SMALL,
    )(place, bucket, lengths, x_t, kept, grad_context, lse, delta, gow, inner, outer, gub)


def input_grad_kernel(place, inner, *refs):
    grads, weights, out = refs[:-2], refs[-2], refs[-1]
    fsdp, depth, _, tall, _ = weights.shape
    total = inner[...]
    for away, columns in enumerate(grads):
        held_weights = weights[neighbour_of(place, away, depth, fsdp)][:, :, :, :USED]
        total += dot_nt(columns[...], held_weights.reshape(2 * depth * tall, USED))
    out[...] = total


def make_input_grad(place, inner, grads, weights):
    t, d = inner.shape
    rows = pl.BlockSpec((ROWS, d), lambda r, *_: (r, 0))
    return [call(
        input_grad_kernel, "input_grad", (t // ROWS,),
        [rows] + [pl.BlockSpec((ROWS, USED), lambda r, *_: (r, 0))] * len(grads) + [whole(weights.shape)],
        rows, sds((t, d), f32), prefetch=1, cost=guess(5e9, 15e6), limit=SMALL,
    )(place, inner, *grads, weights)]


def attend_back_kernel(
    bucket, lengths, x_t, q, k, v, grad_context, lse, delta, qw, kw, vw, grad_inner,
    gqw, gkw, gvw, gqb, gvb, input_grad,
    queries_ext, keys_ext, grads,
):
    pair = pl.program_id(0)
    row_count = q.shape[0]

    @pl.when(pair == 0)
    def _():
        segment_lanes(bucket, lengths, queries_ext, keys_ext)

    low_half = lax.broadcasted_iota(jnp.int32, (PLEN, PAIR), 1) < HD

    def block(b, carry):
        rows = pl.ds(pl.multiple_of(b * PLEN, PLEN), PLEN)
        queries, keys, values, grad_ctx = q[rows, :], k[rows, :], v[rows, :], grad_context[rows, :]
        q_ext, k_ext = queries_ext[rows, :], keys_ext[rows, :]
        nothing = jnp.zeros_like(values)
        got = []
        for half in range(2):
            mine = low_half if half == 0 else ~low_half
            lse_row = lse[pl.ds(half * HD + pair, 1), rows]
            delta_row = delta[pl.ds(half * HD + pair, 1), rows]
            scores = dot_nt(jnp.where(mine, keys, k_ext), jnp.where(mine, queries, q_ext))
            probs = jnp.exp(scores - lse_row)
            grad_probs = dot_nt(jnp.where(mine, values, nothing), grad_ctx)
            grad_scores = (probs * (grad_probs - delta_row)).astype(bf16)
            grad_v = dot(probs.astype(bf16), grad_ctx)
            grad_k = dot(grad_scores, queries)
            grad_q = dot_tn(grad_scores, keys)
            got.append((grad_q, grad_k, grad_v))
        gq = (jnp.where(low_half, got[0][0], got[1][0]) * HD ** (-0.5)).astype(bf16)
        gk = jnp.where(low_half, got[0][1], got[1][1]).astype(bf16)
        gv = jnp.where(low_half, got[0][2], got[1][2]).astype(bf16)
        grads[rows, :PAIR] = gq
        grads[rows, PAIR:2 * PAIR] = gk
        grads[rows, 2 * PAIR:] = gv
        sum_q = jnp.sum(gq.astype(f32), axis=0, keepdims=True)
        sum_v = jnp.sum(gv.astype(f32), axis=0, keepdims=True)
        return (carry[0] + sum_q, carry[1] + sum_v)

    start = jnp.zeros((1, PAIR), f32)
    gqb[...], gvb[...] = lax.fori_loop(0, row_count // PLEN, block, (start, start))

    columns = grads[...]
    weight_grads = dot(x_t[...], columns)
    gqw[...] = weight_grads[:, :PAIR].astype(gqw.dtype)
    gkw[...] = weight_grads[:, PAIR:2 * PAIR].astype(gkw.dtype)
    gvw[...] = weight_grads[:, 2 * PAIR:].astype(gvw.dtype)

    @pl.when(pair == 0)
    def _():
        input_grad[...] = grad_inner[...]

    weights = jnp.concatenate([qw[0], kw[0], vw[0]], axis=1)
    input_grad[...] += dot_nt(columns, weights)


def attend_back(bucket, lengths, x_t, q, k, v, grad_context, lse, delta, weights, grad_inner):
    t, d = q.shape
    pairs = d // PAIR
    column = lambda m: pl.BlockSpec((1, d, PAIR), lambda p, *_: (m, 0, p))
    vector = pl.BlockSpec((1, PAIR), lambda p, *_: (0, p))
    tall = pl.BlockSpec((t, PAIR), lambda p, *_: (0, p))
    made = pl.BlockSpec((d, PAIR), lambda p, *_: (0, p))
    return call(
        attend_back_kernel, "attend_back", (pairs,),
        [whole((d, t)), tall, tall, tall, tall, whole((PAIR, t)), whole((PAIR, t)),
         column(0), column(1), column(2), whole((t, d))],
        [made, made, made, vector, vector, whole((t, d))],
        [sds((d, d), bf16)] * 3 + [sds((1, d), f32)] * 2 + [sds((t, d), f32)],
        [pltpu.VMEM((t, PAIR), bf16), pltpu.VMEM((t, PAIR), bf16), pltpu.VMEM((t, 3 * PAIR), bf16)],
        prefetch=2, cost=guess(30e9, 25e6),
    )(bucket, lengths, x_t, q, k, v, grad_context, lse, delta, weights, weights, weights, grad_inner)


def normed(v):
    centred = v - jnp.mean(v, axis=-1, keepdims=True)
    r = lax.rsqrt(jnp.mean(centred * centred, axis=-1, keepdims=True) + epsilon)
    return centred * r, r


def norm_back(dy, n, r, gain):
    dn = dy * gain
    return r * (dn - jnp.mean(dn, axis=-1, keepdims=True) - n * jnp.mean(dn * n, axis=-1, keepdims=True))


def gelu_parts(u):
    phi = 0.5 + 0.5 * lax.erf(u * 0.5 ** 0.5)
    bell = jnp.exp2(u * u * -0.7213475204444817)
    return u * phi, phi + u * (bell * 0.3989422804014327)


VECTORS = ((0, 2), (0, 3), (1, 0), (1, 1), (1, 2), (1, 3))


def attended_kernel(x, context, ow, slabs, n1_out, r1_out, low_out, low_t, ow_out, vectors):
    rows = pl.ds(pl.multiple_of(pl.program_id(0) * ROWS, ROWS), ROWS)
    parts, _, narrow = context.shape

    @pl.when(pl.program_id(0) == 0)
    def _():
        ow_out[...] = jnp.concatenate([ow[j][:, ow.shape[2] - narrow:] for j in range(parts)], axis=1)
        cuts, _, width = slabs.shape
        piece = width // 4
        held_slabs = [slabs[j].astype(f32) for j in range(cuts)]
        for n, (r, m) in enumerate(VECTORS):
            vectors[n:n + 1, :] = jnp.concatenate(
                [v[r:r + 1, m * piece:(m + 1) * piece] for v in held_slabs], axis=1
            )

    joined = jnp.concatenate([context[j] for j in range(parts)], axis=1)
    ob, g1, b1 = (vectors[n:n + 1, :] for n in range(3))
    attended = dot(joined, ow_out[...]) + ob
    n1, r1 = normed(x[...].astype(f32) + attended)
    n1_out[rows, :] = n1
    r1_out[rows, :] = jnp.broadcast_to(r1, (ROWS, r1_out.shape[1]))
    low = (n1 * g1 + b1).astype(bf16)
    low_out[rows, :] = low
    low_t[:, rows] = low.T


def attended(x, context, ow, last, slabs):
    t, d = x.shape
    parts, _, narrow = context.shape
    wide = ow.shape[2] // (last + 1)
    rows = pl.BlockSpec((ROWS, d), lambda r: (r, 0))
    return call(
        attended_kernel, "attended", (t // ROWS,),
        [rows, pl.BlockSpec((parts, ROWS, narrow), lambda r: (0, r, 0)),
         pl.BlockSpec((parts, d, wide), lambda r: (0, 0, last)), whole(slabs.shape)],
        [held()] * 5 + [whole((8, d))],
        [pltpu.VMEM((t, d), f32), pltpu.VMEM((t, 128), f32), pltpu.VMEM((t, d), bf16), pltpu.VMEM((d, t), bf16),
         pltpu.VMEM((d, d), bf16), sds((8, d), f32)],
        cost=guess(3e9, 10e6), limit=SMALL,
    )(x, context, ow, slabs)


def up_tiles(tile, uw, slabs, act_out, slope_out):
    count, depth, _, tall, columns = uw.shape
    for j in range(act_out.shape[0]):
        hidden = dot(tile, uw[j].reshape(2 * depth * tall, columns)) + slabs[j, 2:3, :].astype(f32)
        active, slope = gelu_parts(hidden)
        act_out[j] = active.astype(bf16)
        slope_out[j] = slope.astype(bf16)


def up_kernel(place, low, slabs, u0, u1, u2, u3, act_out, slope_out, uw, sems):
    rows = pl.ds(pl.multiple_of(pl.program_id(0) * ROWS, ROWS), ROWS)
    copies = block_copies(place, (u0, u1, u2, u3), lambda core, j: uw.at[j, :, core], sems)

    @pl.when(pl.program_id(0) == 0)
    def _():
        for copy in copies:
            copy.start()
        for copy in copies:
            copy.wait()

    up_tiles(low[rows, :], uw, slabs, act_out, slope_out)


def up_rest_kernel(place, low, slabs, uw, act_in, slope_in, act_out, slope_out):
    rows = pl.ds(pl.multiple_of(pl.program_id(0) * ROWS, ROWS), ROWS)
    up_tiles(low[rows, :], uw, slabs, act_out, slope_out)


def up(place, low, slabs, blocks):
    t, d = low.shape
    half, depth, tall, wide = blocks[0].shape
    f = 2 * half
    high = pl.BlockSpec((half, ROWS, wide), lambda r, *_: (0, r, 0))
    return call(
        up_kernel, "up", (t // ROWS,),
        [held(), whole((half, 16, wide))] + [pl.BlockSpec(memory_space=pl.ANY)] * 4,
        [high, high, whole((f, depth, 2, tall, wide))],
        [sds((f, t, wide), bf16), sds((f, t, wide), bf16), sds((f, depth, 2, tall, wide), bf16)],
        [pltpu.SemaphoreType.DMA((2 * f,))],
        prefetch=1, cost=guess(6e9, 20e6), limit=SMALL, free=pl.ANY,
    )(place, low, slabs, *blocks)


def up_rest(place, low, slabs, uw, act, slope):
    t, d = low.shape
    f, depth, _, tall, wide = uw.shape
    half = f // 2
    high = pl.BlockSpec((half, ROWS, wide), lambda r, *_: (1, r, 0))
    any_space = pl.BlockSpec(memory_space=pl.ANY)
    return call(
        up_rest_kernel, "up_rest", (t // ROWS,),
        [held(), pl.BlockSpec((half, 16, wide), lambda r, *_: (1, 0, 0)),
         pl.BlockSpec((half, depth, 2, tall, wide), lambda r, *_: (1, 0, 0, 0, 0)),
         any_space, any_space],
        [high, high],
        [sds((f, t, wide), bf16), sds((f, t, wide), bf16)],
        prefetch=1, cost=guess(6e9, 16e6), limit=SMALL, aliases={4: 0, 5: 1},
    )(place, low, slabs, uw, act, slope)


def down_kernel(
    place, bucket, lengths, act_rows, n1, given, cotangent, act_part, d0, d1, d2, d3,
    out, pooled, mixed_out, branch_out, vectors, send, keep, dw,
    branch_t, counts, sums, found, sems,
):
    step = pl.program_id(0)
    tiles = branch_t.shape[1] // ROWS
    f, _, tall, narrow = send.shape
    depth = (place.shape[0] - 1 - 5 * f) // 2
    shared = f == depth

    def target(core, j):
        rows = pl.ds(pl.multiple_of(j * tall, 16), tall)
        if shared:
            return dw.at[:, rows, pl.ds(pl.multiple_of(core * narrow, narrow), narrow)]
        return dw.at[:, core, rows, :]

    copies = block_copies(place, (d0, d1, d2, d3), target, sems)

    @pl.when(step == 0)
    def _():
        for copy in copies:
            copy.start()
        pooled[...] = jnp.zeros_like(pooled)
        counts[...] = jnp.zeros_like(counts)
        sums[...] = jnp.zeros_like(sums)
        for copy in copies:
            copy.wait()

    @pl.when(step < tiles)
    def _():
        rows = pl.ds(pl.multiple_of(step * ROWS, ROWS), ROWS)
        if shared:
            parts = [dot_nt(act_rows[row_of(place, 0, s, depth) // 2], dw[s]) for s in range(f)]
        else:
            parts = [dot_nt(act_rows[i], dw[i // 2, i % 2]) for i in range(f)]
        branch = sum(parts[1:], parts[0])
        g1, b1, db, g2, b2 = (given[n:n + 1, :] for n in range(1, 6))
        residual = n1[rows, :] * g1 + b1 + (branch + db)
        n2, r2 = normed(residual)
        result = n2 * g2 + b2
        out[...] = result.astype(bf16)
        passage = bucket[0] == 1
        for part in range(ROWS // QLEN):
            start = step * ROWS + part * QLEN
            segment = jnp.where(passage, start // PLEN, start // QLEN)
            position = jnp.where(passage, lax.rem(start, PLEN), 0)
            alive = jnp.clip(lengths[segment] - position, 0, QLEN)
            row = lax.broadcasted_iota(jnp.int32, (QLEN, 1), 0)
            picked = jnp.where(row < alive, result[part * QLEN:(part + 1) * QLEN], 0.0)
            pooled[pl.ds(segment, 1), :] += jnp.sum(picked, axis=0, keepdims=True)
            counts[pl.ds(segment, 1), :] += jnp.full((1, 128), 1.0, f32) * alive.astype(f32)
        dy = cotangent[...].astype(f32)
        sums[1:2, :] += jnp.sum(dy * n2, axis=0, keepdims=True)
        sums[2:3, :] += jnp.sum(dy, axis=0, keepdims=True)
        mixed = norm_back(dy, n2, r2, g2)
        mixed_out[rows, :] = mixed
        low = mixed.astype(bf16)
        branch_out[rows, :] = low
        sums[0:1, :] += jnp.sum(low.astype(f32), axis=0, keepdims=True)
        branch_t[:, rows] = low.T

    @pl.when(step == tiles - 1)
    def _():
        pooled[...] = pooled[...] / jnp.maximum(counts[...], 1.0)[:, :1]
        for j in range(vectors.shape[0]):
            vectors[j] = sums[:, j * vectors.shape[2]:(j + 1) * vectors.shape[2]]

    if shared:
        @pl.when(step >= tiles)
        def _():
            core = core_of(place, depth, f)
            found[...] = dot(branch_t[...], act_part[0]).astype(bf16)
            for n, made in ((1, send), (0, keep)):
                lanes = pl.ds(pl.multiple_of(lax.rem(core + n, 2) * narrow, narrow), narrow)
                for j in range(f):
                    made[slot_of(place, n, j, depth, f), 0] = found[j * tall:(j + 1) * tall, lanes]
    else:
        def part(n, made):
            part_found = dot(branch_t[...], act_part[0]).astype(bf16)
            for j in range(f):
                made[slot_of(place, n, j, depth, f), 0] = part_found[j * tall:(j + 1) * tall]

        @pl.when((step >= tiles) & (step < tiles + depth))
        def _():
            part(1, send)

        @pl.when(step >= tiles + depth)
        def _():
            part(0, keep)


def down(cuts, place, bucket, lengths, active, n1, given, cotangent, blocks):
    f, t, wide = active.shape
    d = n1.shape[1]
    tiles = t // ROWS
    slots = lengths.shape[0]
    _, depth, tall, narrow = blocks[0].shape
    shared = f == depth
    parts = f
    weights = (f, d, wide) if shared else (depth, 2, d, narrow)
    early = lambda s: jnp.minimum(s, tiles - 1)
    if shared:
        late = lambda s, place: place[jnp.maximum(s - tiles, 0)] // 2
    else:
        late = lambda s, place: place[(jnp.maximum(s - tiles, 0) + depth) % parts]
    made = lambda first: pl.BlockSpec(
        (f, 1, tall, narrow), lambda s, *_: (0, jnp.clip(s - tiles - first, 0, depth - 1), 0, 0)
    )
    rows = pl.BlockSpec((ROWS, d), lambda s, *_: (early(s), 0))
    return call(
        down_kernel, "down", (tiles + parts,),
        [pl.BlockSpec((f, ROWS, wide), lambda s, *_: (0, early(s), 0)), held(), whole((8, d)), rows, pl.BlockSpec((1, t, wide), lambda s, place, *_: (late(s, place), 0, 0))]
        + [pl.BlockSpec(memory_space=pl.ANY)] * 4,
        [rows, whole((slots, d)), held(), held(), whole((cuts, 8, d // cuts)), made(0), made(0 if shared else depth),
         whole(weights)],
        [sds((t, d), bf16), sds((slots, d), f32), pltpu.VMEM((t, d), f32), pltpu.VMEM((t, d), bf16)]
        + [sds((cuts, 8, d // cuts), f32)] + [sds((f, depth, tall, narrow), bf16)] * 2
        + [sds(weights, bf16)],
        [pltpu.VMEM((d, t), bf16), pltpu.VMEM((slots, 128), f32), pltpu.VMEM((8, d), f32),
         pltpu.VMEM((d, wide), bf16), pltpu.SemaphoreType.DMA((2 * f,))],
        prefetch=3, cost=guess(12e9, 35e6), limit=SMALL, free=pl.ANY,
    )(place, bucket, lengths, active, n1, given, cotangent, active, *blocks)


def feed_back_kernel(
    place, branch, slope, dw, uw, low_t, mixed, *refs,
):
    send, keep, gub, grad_normed, hidden, found = refs[-6:]
    j = pl.program_id(0)
    _, depth, tall, _ = send.shape
    _, t, wide = slope.shape
    tiles = t // FEED_ROWS

    def gelu_rows(r, sums):
        rows = pl.ds(pl.multiple_of(r * FEED_ROWS, FEED_ROWS), FEED_ROWS)
        grad = (slope[0, rows, :].astype(f32) * dot(branch[rows, :], dw[0])).astype(bf16)
        hidden[rows, :] = grad
        return sums + jnp.sum(grad.astype(f32), axis=0, keepdims=True)

    gub[0] = lax.fori_loop(0, tiles, gelu_rows, jnp.zeros((1, wide), f32))
    found[...] = dot(low_t[...], hidden[...]).astype(bf16)
    for n, target in ((1, send), (0, keep)):
        for slot in range(depth):
            i = row_of(place, n, slot, depth)
            target[0, slot] = found[pl.ds(pl.multiple_of(i * tall, 16), tall), :]

    @pl.when(j == 0)
    def _():
        grad_normed[...] = mixed[...]

    def normed_rows(r, carry):
        rows = pl.ds(pl.multiple_of(r * FEED_ROWS, FEED_ROWS), FEED_ROWS)
        grad_normed[rows, :] += dot_nt(hidden[rows, :], uw[0])
        return carry

    lax.fori_loop(0, tiles, normed_rows, 0)


def feed_back(first, count, place, branch, slope, dw, uw, low_t, mixed, shared):
    t = slope.shape[1]
    f, d, wide = uw.shape
    dp, _, depth, _ = axis_facts()
    tall = d // dp
    made = lambda n: pl.BlockSpec(
        (1, depth, tall, wide), lambda j, place: (slot_of(place, n, first + j, depth, f), 0, 0, 0)
    )
    part = lambda *shape: pl.BlockSpec((1, *shape), lambda j, *_: (first + j, 0, 0))
    slot = lambda j, place: row_of(place, 0, first + j, depth) // 2 if f == depth else first + j
    any_space = pl.BlockSpec(memory_space=pl.ANY)
    return call(
        feed_back_kernel, "feed_back", (count,),
        [held(), part(t, wide), pl.BlockSpec((1, d, wide), lambda j, place: (slot(j, place), 0, 0)), part(d, wide),
         held(), held()] + [any_space] * len(shared),
        [made(1), made(0), part(1, wide), held()],
        [sds((f, depth, tall, wide), bf16)] * 2 + [pltpu.HBM((f, 1, wide), f32), pltpu.VMEM((t, d), f32)],
        [pltpu.VMEM((t, wide), bf16), pltpu.VMEM((d, wide), bf16)],
        prefetch=1, cost=guess(15e9, 35e6), limit=SMALL, least=0, aliases={7 + n: n for n in range(len(shared))},
    )(place, branch, slope, dw, uw, low_t, mixed, *shared)


def inner_kernel(
    head_of, grad_normed, n1, r1, given, context, ow,
    inner_out, vectors, gow, grad_context, delta_out,
    weight_grad, sums,
):
    step = pl.program_id(0)
    d = n1.shape[1]
    parts, _, narrow = context.shape

    @pl.when(step == 0)
    def _():
        weight_grad[...] = jnp.zeros_like(weight_grad)
        sums[...] = jnp.zeros_like(sums)

    shape = (delta_out.shape[0], d)
    head = head_of(lax.broadcasted_iota(jnp.int32, shape, 0))
    pick = jnp.where(lax.broadcasted_iota(jnp.int32, shape, 1) // HD == head, 1.0, 0.0).astype(bf16)
    rows = pl.ds(pl.multiple_of(step * ROWS, ROWS), ROWS)
    dy, n = grad_normed[rows, :], n1[rows, :]
    inner = norm_back(dy, n, r1[rows, :1], given[1:2, :])
    inner_out[...] = inner
    low = inner.astype(bf16)
    grad_ctx = dot_nt(low, ow[...]).astype(bf16)
    for j in range(parts):
        grad_context[j] = grad_ctx[:, j * narrow:(j + 1) * narrow]
    joined = jnp.concatenate([context[j] for j in range(parts)], axis=1)
    both = grad_ctx.astype(f32) * joined.astype(f32)
    high = both.astype(bf16)
    rest = (both - high.astype(f32)).astype(bf16)
    delta_out[...] = dot_nt(pick, high) + dot_nt(pick, rest)
    sums[0:1, :] += jnp.sum(dy * n, axis=0, keepdims=True)
    sums[1:2, :] += jnp.sum(dy, axis=0, keepdims=True)
    sums[2:3, :] += jnp.sum(low.astype(f32), axis=0, keepdims=True)
    weight_grad[...] += dot_tn(joined, low)

    @pl.when(step == pl.num_programs(0) - 1)
    def _():
        for j in range(parts):
            columns = slice(j * narrow, (j + 1) * narrow)
            gow[j] = weight_grad[:, columns].astype(bf16)
            vectors[j] = sums[:, columns]


def inner_back(count, head_of, grad_normed, n1, r1, given, context, ow):
    t, d = n1.shape
    parts, _, narrow = context.shape
    tile = pl.BlockSpec((parts, ROWS, narrow), lambda r: (0, r, 0))
    return call(
        functools.partial(inner_kernel, head_of), "inner_back", (t // ROWS,),
        [held(), held(), held(), whole((8, d)), tile, held()],
        [pl.BlockSpec((ROWS, d), lambda r: (r, 0)), whole((parts, 8, narrow)), whole((parts, d, narrow)), tile,
         pl.BlockSpec((count, ROWS), lambda r: (0, r))],
        [sds((t, d), f32), sds((parts, 8, narrow), f32), sds((parts, d, narrow), bf16), sds((parts, t, narrow), bf16),
         sds((count, t), f32)],
        [pltpu.VMEM((d, d), f32), pltpu.VMEM((8, d), f32)],
        cost=guess(4e9, 10e6), limit=SMALL,
    )(grad_normed, n1, r1, given, context, ow)


def shards(
    tokens, bucket, lengths, cotangent,
    query_weight, query_bias, key_weight, value_weight, value_bias, out_weight, out_bias,
    norm1_gain, norm1_bias, up_weight, up_bias, down_weight, down_bias, norm2_gain, norm2_bias,
):
    t, d = tokens.shape
    dp, fsdp = lax.axis_size("dp"), lax.axis_size("fsdp")
    lengths = lengths[0]

    place = places()
    depth = dp // 2
    tall, narrow = d // dp, d // fsdp
    width = 4 * narrow
    by_head = narrow == HEADS * HD and fsdp == 4
    down_t = down_weight.T

    if by_head:
        block = make_block(
            query_weight, key_weight, value_weight, out_weight, query_bias, value_bias, out_bias, norm1_gain,
            norm1_bias, down_bias, norm2_gain, norm2_bias, up_bias,
        )
        along = Once([(block, "dp", along_z(s)) for s in range(1, depth)])
        x_t, = beside([along], lambda x: (x.T,), (tokens,))
        own = [block] + along.got
        own = line_up(place, own)
        swap = lambda v: (v, "dp", across_cores())
        in_plane = lambda v, s: (v, "fsdp", [(f, f ^ s) for f in range(fsdp)])
        paired = Once([swap(own)])
        beside([paired])
        pair_0 = paired.got[0]
        ups = Once([(up_weight, "dp", along_z(s)) for s in range(1, depth)])
        sides = Once([in_plane(own, 1), in_plane(own, 2)])
        one = lambda away: functools.partial(attend_one, away, fsdp)
        run = (bucket, lengths, tokens)
        *shared, kept_0, lse_0 = beside([sides, ups], one(0), (place, *run, own, pair_0, []), out=3)
        own_x, own_y = sides.got
        to_u = Gather(line_up(place, [up_weight] + ups.got))
        paired = Once([swap(own_x), swap(own_y)])
        corner = Once([(select_core(own_y, own_x), ("dp", "fsdp"), along_bit(0))])
        beside([paired])
        pair_x, pair_y = paired.got
        downs = Once([(down_t, "dp", along_z(s)) for s in range(1, depth)])
        *shared, kept_1, lse_1 = beside([corner, to_u, downs], one(1), (place, *run, own_x, pair_x, shared), out=3)
        own_c = corner.got[0]
        to_d = Gather(jnp.stack([down_t] + downs.got))
        paired = Once([swap(own_c)])
        *shared, kept_2, lse_2 = beside([paired, to_u], one(2), (place, *run, own_y, pair_y, shared), out=3)
        *shared, kept_3, lse_3 = beside([to_u, to_d], one(3), (place, *run, own_c, paired.got[0], shared), out=3)
        context, weights, slabs = shared
        ow, last = weights.reshape(fsdp, d, width), 2
        count, head_of = 8 * fsdp, lambda r: jnp.where(r % 8 < HEADS, r // 8 * HEADS + r % 8, -1)
    else:
        block = jnp.concatenate([
            jnp.concatenate([query_weight, key_weight, value_weight, out_weight], axis=1),
            jnp.concatenate([query_bias, value_bias, out_bias, norm1_gain])[None],
            jnp.concatenate([norm1_bias, down_bias, norm2_gain, norm2_bias])[None],
            up_bias[None],
            jnp.zeros((13, width), bf16),
        ])
        to_a, to_u, to_d = Gather(gather_z(block)), Gather(gather_z(up_weight)), Gather(gather_z(down_t))
        finish(to_a)
        weights, vectors, slabs = assemble(place, to_a.blocks)
        qb, vb = (vectors[m, 0:1] for m in range(2))
        q, k, v, context, lse = attend(bucket, lengths, tokens, weights, qb, vb)
        context, ow, last = context[None], weights[3:], 0
        count, head_of = PAIR, lambda r: 2 * (r % HD) + r // HD

    finish(to_u)

    def attended_up(place, *args):
        normal = attended(*args)
        return [*normal, *up(place, normal[2], slabs, to_u.blocks)]

    n1, r1, low, low_t, ow, given, active, slope, uw = beside(
        [to_d], attended_up, (place, tokens, context, ow, last, slabs), key=5, out=6
    )
    active, slope = beside([to_d], up_rest, (place, low, slabs, uw, active, slope))
    finish(to_d)
    cuts = context.shape[0]
    out, pooled, mixed, branch, down_vectors, send_d, keep_d, dw = down(
        cuts, place, bucket, lengths, active, n1, given, cotangent, to_d.blocks
    )
    of_d = Scatter(keep_d, send_d)
    dw, uw = dw.reshape(fsdp, d, -1), uw.reshape(fsdp, d, -1)
    part = fsdp // 2
    *shared, so_far = beside(
        [of_d], functools.partial(feed_back, 0, part), (place, branch, slope, dw, uw, low_t, mixed, [])
    )
    send_u, keep_u, gub, grad_normed = beside(
        [of_d], functools.partial(feed_back, part, fsdp - part),
        (place, branch, slope, dw, uw, low_t, so_far, shared),
    )
    of_u = Scatter(keep_u, send_u)
    inner, inner_vectors, gow, grad_context, delta = beside(
        [of_d, of_u], functools.partial(inner_back, count, head_of), (grad_normed, n1, r1, given, context, ow),
        key=3, out=2
    )

    if by_head:
        delta = delta.reshape(fsdp, 8, t)

        def back(away, moves, kept, lse):
            args = (place, bucket, lengths, x_t, kept, grad_context, lse, delta, gow, inner_vectors, down_vectors, gub)
            return beside(moves, functools.partial(attend_back_one, away, fsdp, depth), args)

        send_3, keep_3, grads_3 = back(3, [of_d, of_u], kept_3, lse_3)
        swap_3 = Once([swap(send_3)])
        send_1, keep_1, grads_1 = back(1, [swap_3, of_u], kept_1, lse_1)
        corner = Once([(add(keep_3, swap_3.got[0]), ("dp", "fsdp"), along_bit(0))])
        send_2, keep_2, grads_2 = back(2, [corner, of_u], kept_2, lse_2)
        sums = Once([swap(send_1), swap(send_2)])
        beside([sums])
        add_both = lambda *v: sum(u.astype(f32) for u in v)
        through = corner.got[0]
        sum_1 = add_both(keep_1, sums.got[0]) + select_core(jnp.zeros_like(through), through).astype(f32)
        sum_2 = add_both(keep_2, sums.got[1]) + select_core(through, jnp.zeros_like(through)).astype(f32)
        sides = Once([in_plane(sum_1.astype(bf16), 1), in_plane(sum_2.astype(bf16), 2)])
        send_0, keep_0, grads_0 = back(0, [sides, of_u], kept_0, lse_0)
        sums = Once([swap(send_0)])
        beside([sums, of_u])
        total = add_both(keep_0, sums.got[0], *sides.got)
        z = lax.axis_index("dp") // 2
        at = lambda s: lax.dynamic_index_in_dim(total, (z - s) % depth, 0, keepdims=False)
        along = Once([(at(s).astype(bf16), "dp", along_z(-s)) for s in range(1, depth)])
        input_grad, = beside(
            [along, of_u], make_input_grad, (place, inner, (grads_0, grads_1, grads_2, grads_3), weights)
        )
        *made, gqb, gvb, gob, gg1, gb1, gdb, gg2, gb2, gub = unblock(at(0), along.got)
        vectors = (gqb, gvb, gob, gg1, gb1, gdb, gg2, gb2)
        finish(of_d)
        finish(of_u)
    else:
        gg1, gb1, gob = (inner_vectors[0, n:n + 1] for n in range(3))
        gdb, gg2, gb2 = (down_vectors[0, n:n + 1] for n in range(3))
        gqw, gkw, gvw, gqb, gvb, input_grad = attend_back(
            bucket, lengths, tokens.T, q, k, v, grad_context[0], lse, delta, weights, inner
        )
        firsts = jnp.stack([gqb, gvb, gob, gg1])
        seconds = jnp.stack([gb1, gdb, gg2, gb2])
        vectors = jnp.concatenate([firsts, seconds, jnp.zeros((4, 14, d), f32)], axis=1)
        of_a = Scatter(*reversed(pack(place, (gqw, gkw, gvw, gow[0]), vectors, gub)))
        while not (of_a.done() and of_u.done() and of_d.done()):
            beside([of_a, of_u, of_d])
        made_a = of_a.total
        made = [made_a[:tall, m * narrow:(m + 1) * narrow] for m in range(4)]
        vectors = [made_a[tall + n, m * narrow:(m + 1) * narrow] for n in range(2) for m in range(4)]
        gub = made_a[tall + 2]
    return (
        out, pooled, input_grad, made[0], vectors[0], made[1], made[2], vectors[1], made[3], vectors[2], vectors[3],
        vectors[4], of_u.total, gub, of_d.total.T, vectors[5], vectors[6], vectors[7],
    )


def solution(mesh):
    tall, square, vector = P(("dp", "fsdp"), None), P("dp", "fsdp"), P("fsdp")
    in_specs = (
        tall, P(("dp", "fsdp")), tall, tall, square, vector, square, square, vector, square, vector,
        vector, vector, square, vector, square, vector, vector, vector,
    )
    out_specs = (
        tall, tall, tall, square, vector, square, square, vector, square, vector, vector, vector,
        square, vector, square, vector, vector, vector,
    )
    return jax.shard_map(shards, mesh=mesh, in_specs=in_specs, out_specs=out_specs, check_vma=False)
```

```python
import functools

import jax
import jax.numpy as jnp
from jax import lax
from jax.experimental import pallas as pl
from jax.experimental.pallas import tpu as pltpu
from jax.sharding import PartitionSpec as P

H = 12
HD = 64
PLEN = 512
QLEN = 128
PAIR = 2 * HD
ROWS = 256
FEED_ROWS = 512

epsilon = 1e-06
masked_score = -1e30
f32 = jnp.float32
bf16 = jnp.bfloat16
LIMIT = 60 * 1024 * 1024
SMALL = 24 * 1024 * 1024


def dot(left, right):
    return jnp.dot(left, right, preferred_element_type=f32)


def dot_nt(left, right):
    return lax.dot_general(left, right, (((1,), (1,)), ((), ())), preferred_element_type=f32)


def dot_tn(left, right):
    return lax.dot_general(left, right, (((0,), (0,)), ((), ())), preferred_element_type=f32)


BIG = 16 * 1024


def far(v, least):
    if v.size * v.dtype.itemsize < least:
        return v
    return pltpu.with_memory_space_constraint(v, pltpu.HBM)


def call(
    kernel, name, grid, in_specs, out_specs, out_shape, scratch=(), prefetch=0, cost=None, limit=LIMIT, aliases={},
    least=BIG, free=pltpu.VMEM,
):
    several = isinstance(out_shape, list)
    shapes = [
        pltpu.HBM(v.shape, v.dtype)
        if isinstance(v, jax.ShapeDtypeStruct) and v.size * v.dtype.itemsize >= BIG else v
        for v in (out_shape if several else [out_shape])
    ]
    run = pl.pallas_call(
        kernel,
        name=name,
        grid_spec=pltpu.PrefetchScalarGridSpec(
            num_scalar_prefetch=prefetch,
            grid=grid,
            in_specs=in_specs,
            out_specs=out_specs,
            scratch_shapes=list(scratch),
        ),
        out_shape=shapes if several else shapes[0],
        input_output_aliases=aliases,
        compiler_params=pltpu.CompilerParams(
            vmem_limit_bytes=limit, dimension_semantics=("arbitrary",) * len(grid)
        ),
        cost_estimate=cost,
    )

    def run_far(*args):
        given = [
            v if spec.memory_space in (pltpu.VMEM, free) else far(v, least) for v, spec in zip(args[prefetch:], in_specs)
        ]
        return run(*args[:prefetch], *given)

    return run_far


def whole(shape):
    return pl.BlockSpec(shape, lambda *_: (0,) * len(shape))


def sds(shape, dtype):
    return jax.ShapeDtypeStruct(shape, dtype)


def held():
    return pl.BlockSpec(memory_space=pltpu.VMEM)


def guess(flops, nbytes):
    return pl.CostEstimate(flops=int(flops), bytes_accessed=int(nbytes), transcendentals=0)


def reverse(s, bits):
    return sum(((s >> b) & 1) << (bits - 1 - b) for b in range(bits))


def axis_facts():
    dp, fsdp = lax.axis_size("dp"), lax.axis_size("fsdp")
    return dp, fsdp, dp // 2, fsdp.bit_length() - 1


def along_z(hop):
    dp = lax.axis_size("dp")
    return [(d, (d + 2 * hop) % dp) for d in range(dp)]


def across_cores():
    return [(d, d ^ 1) for d in range(lax.axis_size("dp"))]


def along_bit(r):
    dp, fsdp, _, bits = axis_facts()
    pairs = []
    for d in range(dp):
        flip = 1 << (r if d % 2 == 0 else bits - 1 - r)
        pairs += [(d * fsdp + f, d * fsdp + (f ^ flip)) for f in range(fsdp)]
    return pairs


def select_core(even, odd):
    return jnp.where(lax.axis_index("dp") % 2 == 0, even, odd)


def gather_z(block):
    dp = lax.axis_size("dp")
    groups = [list(range(core, dp, 2)) for core in range(2)]
    return lax.all_gather(block, "dp", axis=0, axis_index_groups=groups)


class Gather:
    def __init__(self, along):
        self.held, self.round, self.blocks = along[None], 0, None

    def stage(self):
        bits = axis_facts()[3]
        if self.round < bits:
            return [(self.held, ("dp", "fsdp"), along_bit(self.round))]
        return [(v, "dp", across_cores()) for v in self.own]

    def take(self, got):
        bits = axis_facts()[3]
        if self.round < bits - 1:
            self.held = jnp.concatenate([self.held] + got)
        elif self.round < bits:
            self.own = [self.held] + got
        else:
            self.blocks = self.own + got
        self.round += 1

    def done(self):
        return self.blocks is not None


class Once:
    def __init__(self, sends):
        self.sends, self.got = sends, None

    def stage(self):
        return self.sends

    def take(self, got):
        self.got = got

    def done(self):
        return self.got is not None


def add(left, right):
    return (left.astype(f32) + right.astype(f32)).astype(bf16)


class Scatter:
    def __init__(self, keep, send):
        self.keep, self.send, self.round, self.total = keep, [send], axis_facts()[3], None
        self.joined = False

    def stage(self):
        _, _, depth, bits = axis_facts()
        if self.round == bits:
            return [(self.send[0], "dp", across_cores())]
        if self.round >= 0:
            return [(self.send[0], ("dp", "fsdp"), along_bit(self.round))]
        return [(self.send[s - 1], "dp", along_z(-s)) for s in range(1, depth)]

    def take(self, got):
        depth = axis_facts()[2]
        keep = self.keep
        if self.round > 0:
            half = keep.shape[0] // 2
            self.send = [add(keep[half:], got[0][half:])]
            self.keep = add(keep[:half], got[0][:half])
        elif self.round == 0:
            self.send = [add(keep[0, s], got[0][0, s]) for s in range(1, depth)]
            self.keep = keep[0, 0].astype(f32) + got[0][0, 0].astype(f32)
        else:
            for part in got:
                keep = keep + part.astype(f32)
            self.total = keep
        self.round -= 1

    def done(self):
        return self.total is not None or (self.joined and self.round < 0)


def beside(moves, compute=None, args=(), key=0, out=0):
    moves = [move for move in moves if not move.done()]
    stages = [move.stage() for move in moves]
    arrays = [[v for v, _, _ in stage] for stage in stages]
    args = list(args)
    results = ()
    if compute:
        args[key], arrays = lax.optimization_barrier((args[key], arrays))
        results = list(compute(*args))
    else:
        arrays = lax.optimization_barrier(arrays)
    got = [
        [lax.ppermute(v, axis, perm) for v, (_, axis, perm) in zip(sent, stage)]
        for sent, stage in zip(arrays, stages)
    ]
    if compute:
        results[out], got = lax.optimization_barrier((results[out], got))
    else:
        got = lax.optimization_barrier(got)
    for move, parts in zip(moves, got):
        move.take(parts)
    return results


def finish(move):
    while not move.done():
        beside([move])


def places():
    dp, fsdp, depth, bits = axis_facts()
    d, f = lax.axis_index("dp"), lax.axis_index("fsdp")
    z, core = d // 2, d % 2
    slot = jnp.arange(depth, dtype=jnp.int32)
    index = jnp.arange(fsdp, dtype=jnp.int32)
    mirror = sum((((index >> b) & 1) << (bits - 1 - b) for b in range(bits)), jnp.zeros_like(index))
    rows, slots, columns = [], [], []
    for n in range(2):
        there = core ^ n
        rows.append(2 * ((z - slot) % depth) + there)
        away = index ^ f
        mirrored = sum((((away >> b) & 1) << (bits - 1 - b) for b in range(bits)), jnp.zeros_like(index))
        slots.append(jnp.where(there == 0, away, mirrored))
        columns.append(f ^ jnp.where(there == 0, index, mirror))
    neighbours = [(f ^ s)[None] for s in range(fsdp)]
    return jnp.concatenate(rows + slots + columns + [core[None]] + neighbours).astype(jnp.int32)


def row_of(place, n, slot, depth):
    return place[n * depth + slot]


def slot_of(place, n, j, depth, fsdp):
    return place[2 * depth + n * fsdp + j]


def column_of(place, n, s, depth, fsdp):
    return place[2 * depth + 2 * fsdp + n * fsdp + s]


def core_of(place, depth, fsdp):
    return place[2 * depth + 4 * fsdp]


def neighbour_of(place, s, depth, fsdp):
    return place[2 * depth + 4 * fsdp + 1 + s]


def block_copies(place, arrays, target, sems):
    half, depth = arrays[0].shape[:2]
    fsdp = 2 * half
    copies = []
    for a, array in enumerate(arrays):
        core = lax.rem(core_of(place, depth, fsdp) + a // 2, 2)
        for q in range(half):
            j = column_of(place, a // 2, (a % 2) * half + q, depth, fsdp)
            copies.append(pltpu.make_async_copy(array.at[q], target(core, j), sems.at[len(copies)]))
    return copies


def assemble_kernel(place, own_low, own_high, other_low, other_high, weights, vectors, ub):
    step = pl.program_id(0)
    half, _, height, width = own_low.shape
    fsdp, depth, tall = 2 * half, pl.num_programs(0) // 2, height - 16
    narrow = width // 4

    def fill(n, low, high):
        pieces = []
        for j in range(fsdp):
            slot = slot_of(place, n, j, depth, fsdp)
            upper, q = slot >= half, lax.rem(slot, half)
            pieces.append(jnp.where(upper, high[q, 0].astype(f32), low[q, 0].astype(f32)))
        for m in range(4):
            row = jnp.concatenate([p[:, m * narrow:(m + 1) * narrow] for p in pieces], axis=1)
            weights[m] = row[:tall].astype(bf16)
            vectors[m] = row[tall:]
        for j in range(fsdp):
            ub[j] = pieces[j][tall:]

    @pl.when(step < depth)
    def _():
        fill(0, own_low, own_high)

    @pl.when(step >= depth)
    def _():
        fill(1, other_low, other_high)


def row_at(place, s, depth, fsdp):
    core = core_of(place, depth, fsdp)
    return 2 * lax.rem(s, depth) + lax.rem(core + s // depth, 2)


def assemble(place, arrays):
    half, depth, height, width = arrays[0].shape
    fsdp, tall, d = 2 * half, height - 16, half * width // 2
    own = pl.BlockSpec((half, 1, height, width), lambda s, place: (0, jnp.minimum(s, depth - 1), 0, 0))
    other = pl.BlockSpec((half, 1, height, width), lambda s, place: (0, jnp.maximum(s - depth, 0), 0, 0))
    return call(
        assemble_kernel, "assemble", (2 * depth,),
        [own, own, other, other],
        [pl.BlockSpec((4, tall, d), lambda s, place: (0, row_at(place, s, depth, fsdp), 0)), whole((4, 16, d)),
         whole((fsdp, 16, width))],
        [sds((4, 2 * depth * tall, d), bf16), sds((4, 16, d), f32), sds((fsdp, 16, width), f32)],
        prefetch=1, cost=guess(1e9, 11e6),
    )(place, *arrays)


def pack_kernel(place, gq, gk, gv, go, vectors, gub, send, keep):
    step = pl.program_id(0)
    fsdp, _, height, width = send.shape
    depth, tall, narrow = pl.num_programs(0) // 2, height - 16, width // 4

    def fill(n, out):
        for j in range(fsdp):
            slot = slot_of(place, n, j, depth, fsdp)
            columns = slice(j * narrow, (j + 1) * narrow)
            out[slot, 0, :tall, :] = jnp.concatenate(
                [g[:, columns].astype(f32) for g in (gq, gk, gv, go)], axis=1
            ).astype(bf16)
            slab = jnp.concatenate([vectors[m, :, columns] for m in range(4)], axis=1)
            third = lax.broadcasted_iota(jnp.int32, slab.shape, 0) == 2
            out[slot, 0, tall:, :] = jnp.where(third, gub[j], slab).astype(bf16)

    @pl.when(step < depth)
    def _():
        fill(1, send)

    @pl.when(step >= depth)
    def _():
        fill(0, keep)


def pack(place, grads, vectors, gub):
    d = grads[0].shape[0]
    dp, fsdp, depth, _ = axis_facts()
    tall, width = d // dp, 4 * d // fsdp
    rows = pl.BlockSpec((tall, d), lambda s, place: (place[(s + depth) % (2 * depth)], 0))
    sent = pl.BlockSpec((fsdp, 1, tall + 16, width), lambda s, place: (0, jnp.minimum(s, depth - 1), 0, 0))
    kept = pl.BlockSpec((fsdp, 1, tall + 16, width), lambda s, place: (0, jnp.maximum(s - depth, 0), 0, 0))
    return call(
        pack_kernel, "pack", (2 * depth,),
        [rows, rows, rows, rows, whole((4, 16, d)), whole((fsdp, 1, width))],
        [sent, kept],
        [sds((fsdp, depth, tall + 16, width), bf16)] * 2,
        prefetch=1, cost=guess(1e9, 11e6),
    )(place, *grads, vectors, gub)


def segment_lanes(bucket, lengths, queries_ext, keys_ext):
    row_count = queries_ext.shape[0]
    slots = lengths.shape[0]
    shape = (row_count, PAIR)
    row = lax.broadcasted_iota(jnp.int32, shape, 0)
    lane = lax.broadcasted_iota(jnp.int32, shape, 1) % HD
    passage = bucket[0] == 1
    segment = jnp.where(passage, row // PLEN, row // QLEN)
    position = jnp.where(passage, row % PLEN, row % QLEN)
    limit = jnp.zeros(shape, jnp.int32)
    for s in range(slots):
        limit = jnp.where(segment == s, lengths[s], limit)
    alive = position < limit
    same = segment == lane
    queries_ext[...] = jnp.where(same, 1.0, 0.0).astype(bf16)
    keys_ext[...] = jnp.where((lane < slots) & ~(same & alive), masked_score, 0.0).astype(bf16)


def attend_kernel(
    bucket, lengths, x, qw, kw, vw, qb, vb,
    q_out, k_out, v_out, context_out, lse_out,
    queries_ext, keys_ext, lse_all,
):
    pair = pl.program_id(0)
    row_count = x.shape[0]

    @pl.when(pair == 0)
    def _():
        segment_lanes(bucket, lengths, queries_ext, keys_ext)
        lse_all[...] = jnp.zeros_like(lse_all)

    weights = jnp.concatenate([qw[0], kw[0], vw[0]], axis=1)
    qb_row = qb[...]
    vb_row = vb[...]
    low_half = lax.broadcasted_iota(jnp.int32, (PLEN, PAIR), 1) < HD
    lane = lax.broadcasted_iota(jnp.int32, (PLEN, PAIR), 1)

    def block(b, carry):
        rows = pl.ds(pl.multiple_of(b * PLEN, PLEN), PLEN)
        qkv = dot(x[rows, :], weights)
        queries = ((qkv[:, :PAIR] + qb_row).astype(bf16).astype(f32) * HD ** (-0.5)).astype(bf16)
        keys = qkv[:, PAIR:2 * PAIR].astype(bf16)
        values = (qkv[:, 2 * PAIR:] + vb_row).astype(bf16)
        q_out[rows, :] = queries
        k_out[rows, :] = keys
        v_out[rows, :] = values
        q_ext = queries_ext[rows, :]
        k_ext = keys_ext[rows, :]
        ones = jnp.ones_like(values)
        sums, tops = [], []
        for half in range(2):
            mine = low_half if half == 0 else ~low_half
            scores = dot_nt(jnp.where(mine, queries, q_ext), jnp.where(mine, keys, k_ext))
            top = jnp.max(scores, axis=-1, keepdims=True)
            weight = jnp.exp(scores - top).astype(bf16)
            sums.append(dot(weight, jnp.where(mine, values, ones)))
            tops.append(top)
        numer = jnp.where(low_half, sums[0], sums[1])
        denom = pltpu.roll(jnp.where(low_half, sums[1], sums[0]), HD, 1)
        context_out[rows, :] = (numer / denom).astype(bf16)
        lse = jnp.where(low_half, tops[0], tops[1]) + jnp.log(denom)
        mine = (lane % HD) == pair
        lse_all[rows, :] = jnp.where(mine, lse, lse_all[rows, :])
        return carry

    lax.fori_loop(0, row_count // PLEN, block, 0)

    @pl.when(pair == pl.num_programs(0) - 1)
    def _():
        lse_out[...] = lse_all[...].T


def attend(bucket, lengths, x, weights, qb, vb):
    t, d = x.shape
    pairs = d // PAIR
    column = lambda m: pl.BlockSpec((1, d, PAIR), lambda p, *_: (m, 0, p))
    vector = pl.BlockSpec((1, PAIR), lambda p, *_: (0, p))
    tall = pl.BlockSpec((t, PAIR), lambda p, *_: (0, p))
    return call(
        attend_kernel, "attend", (pairs,),
        [whole((t, d)), column(0), column(1), column(2), vector, vector],
        [tall, tall, tall, tall, whole((PAIR, t))],
        [sds((t, d), bf16)] * 4 + [sds((PAIR, t), f32)],
        [pltpu.VMEM((t, PAIR), bf16), pltpu.VMEM((t, PAIR), bf16), pltpu.VMEM((t, PAIR), f32)],
        prefetch=2, cost=guess(15e9, 12e6),
    )(bucket, lengths, x, weights, weights, weights, qb, vb)


HEADS = 3
USED = 5 * PAIR


def block_kernel(q, k, v, o, *refs):
    *vectors, ub, out, slab = refs
    out[...] = jnp.concatenate(
        [part.astype(f32) for part in (
            q[:, :PAIR], k[:, :PAIR], v[:, :PAIR], q[:, PAIR:], k[:, PAIR:], v[:, PAIR:], o[...]
        )], axis=1
    ).astype(bf16)
    each = [v[...].astype(f32)[None, :] for v in vectors]
    first, second = jnp.concatenate(each[:4], axis=1), jnp.concatenate(each[4:], axis=1)
    third = ub[...].astype(f32)[None, :]
    row = lax.broadcasted_iota(jnp.int32, (16, out.shape[1]), 0)
    slab[...] = jnp.where(
        row == 0, first, jnp.where(row == 1, second, jnp.where(row == 2, third, 0.0))
    ).astype(bf16)


def make_block(q, k, v, o, *vectors):
    tall, narrow = q.shape
    shapes = [(tall, 4 * narrow), (16, 4 * narrow)]
    return call(
        block_kernel, "block", (1,), [whole(q.shape)] * 4 + [whole(u.shape) for u in vectors],
        [whole(v) for v in shapes], [sds(v, bf16) for v in shapes], cost=guess(1e6, 1e6), limit=SMALL, least=0,
    )(q, k, v, o, *vectors)


def total_kernel(place, *refs):
    parts, first, others = refs[:4], refs[4], refs[5:]
    depth = parts[0].shape[0]
    for s in range(depth):
        z = row_of(place, 0, s, depth) // 2
        total = sum((part[z].astype(f32) for part in parts[1:]), parts[0][z].astype(f32))
        if s:
            others[s - 1][...] = total.astype(bf16)
        else:
            first[...] = total


def make_total(place, parts):
    depth, height, width = parts[0].shape
    out = (height, width)
    return call(
        total_kernel, "total", (1,), [whole(parts[0].shape)] * 4, [whole(out)] * depth,
        [sds(out, f32)] + [sds(out, bf16)] * (depth - 1), prefetch=1, cost=guess(1e6, 4e6), limit=SMALL,
    )(place, *parts)


def unblock_kernel(total, *refs):
    got, (gq, gk, gv, go, *vectors) = refs[:-13], refs[-13:]
    tall, narrow = gq.shape
    block = total[...]
    for part in got:
        block = block + part[...].astype(f32)

    def split(v):
        return (
            jnp.concatenate([v[:, :PAIR], v[:, 3 * PAIR:3 * PAIR + HD]], axis=1),
            jnp.concatenate([v[:, PAIR:2 * PAIR], v[:, 3 * PAIR + HD:4 * PAIR]], axis=1),
            jnp.concatenate([v[:, 2 * PAIR:3 * PAIR], v[:, 4 * PAIR:4 * PAIR + HD]], axis=1),
            v[:, 4 * PAIR + HD:],
        )

    gq[...], gk[...], gv[...], go[...] = split(block[:tall])
    qb, _, vb, ob = split(block[tall:tall + 1])
    rest = [block[tall + r:tall + r + 1, m * narrow:(m + 1) * narrow] for r, m in ((1, 0), (1, 1), (1, 2), (1, 3), (2, 0))]
    for ref, row in zip(vectors, (qb, vb, ob, *rest, block[tall + 3:tall + 4])):
        ref[...] = row[0]


def unblock(total, got):
    height, width = total.shape
    tall, narrow = height - 16, width // 4
    shapes = [(tall, narrow)] * 4 + [(narrow,)] * 8 + [(width,)]
    return call(
        unblock_kernel, "unblock", (1,), [whole(total.shape)] * (1 + len(got)), [whole(v) for v in shapes],
        [sds(v, f32) for v in shapes], cost=guess(1e6, 1e6), limit=SMALL,
    )(total, *got)


def line_up_kernel(place, *refs):
    out = refs[-1]
    depth = len(refs) - 1
    for s in range(depth):
        out[row_of(place, 0, s, depth) // 2] = refs[s][...]


def line_up(place, parts):
    shape = parts[0].shape
    out = (len(parts), *shape)
    return call(
        line_up_kernel, "line_up", (1,), [whole(shape)] * len(parts), whole(out), sds(out, parts[0].dtype),
        prefetch=1, cost=guess(1e6, 1e6), limit=SMALL,
    )(place, *parts)


def line_up_rows_kernel(place, *refs):
    *parts, slab, out = refs
    depth, tall = len(parts), parts[0].shape[0]
    for s in range(depth):
        z = row_of(place, 0, s, depth) // 2
        out[pl.ds(pl.multiple_of(z * tall, 16), tall), :] = parts[s][...]
    out[depth * tall:, :] = slab[...]


def line_up_rows(place, parts, slab):
    tall, width = parts[0].shape
    out = (len(parts) * tall + 16, width)
    return call(
        line_up_rows_kernel, "line_up_rows", (1,), [whole((tall, width))] * len(parts) + [whole(slab.shape)],
        whole(out), sds(out, bf16), prefetch=1, cost=guess(1e6, 1e6), limit=SMALL,
    )(place, *parts, slab)


def attend_one_kernel(
    away, place, bucket, lengths, x, own, other, *refs,
):
    *given, context_out, w_out, slab_out, kept, lse_out, queries_ext, keys_ext, weights_here, sems = refs
    if away:
        queries_ext, keys_ext = given[:2]
    depth, _, tall, width = weights_here.shape
    step, fsdp = pl.program_id(0), w_out_fsdp(place, depth)
    core = core_of(place, depth, fsdp)
    j = neighbour_of(place, away, depth, fsdp)
    copies = [
        pltpu.make_async_copy(
            ref.at[pl.ds(0, depth * tall), :].reshape(depth, tall, width), weights_here.at[:, lax.rem(core + n, 2)],
            sems.at[n],
        )
        for n, ref in enumerate((own, other))
    ]
    copies.append(pltpu.make_async_copy(own.at[pl.ds(depth * tall, 16), :], slab_out.at[0], sems.at[2]))
    onward = pltpu.make_async_copy(weights_here, w_out.at[j], sems.at[3])

    @pl.when(step == 0)
    def _():
        for copy in copies:
            copy.start()
        if not away:
            segment_lanes(bucket, lengths, queries_ext, keys_ext)
        for copy in copies:
            copy.wait()
        onward.start()

    narrow = width // 4
    row = slab_out[0, 0:1, :].astype(f32)
    qb, vb = row[:, :narrow], row[:, narrow:2 * narrow]
    none = jnp.zeros((1, PAIR), f32)
    bias = jnp.concatenate(
        [qb[:, :PAIR], none, vb[:, :PAIR], qb[:, PAIR:], none[:, :HD], vb[:, PAIR:], none[:, :HD]], axis=1
    )
    lane = lax.broadcasted_iota(jnp.int32, (PLEN, PAIR), 1)
    low_half = lane < HD
    scale = HD ** (-0.5)

    rows = pl.ds(pl.multiple_of(step * PLEN, PLEN), PLEN)
    weights = weights_here[:, :, :, :USED].reshape(2 * depth * tall, USED)
    qkv = dot(x[...], weights) + bias
    tiles = [qkv[:, n * PAIR:(n + 1) * PAIR].astype(bf16) for n in range(5)]
    tiles[0] = tiles[0] * jnp.array(scale, bf16)
    tiles[3] = jnp.where(low_half, tiles[3] * jnp.array(scale, bf16), tiles[3])
    for n in range(5):
        kept[:, n * PAIR:(n + 1) * PAIR] = tiles[n]
    queries, keys, values, both, values_two = tiles
    keys_two = pltpu.roll(both.astype(f32), HD, 1).astype(bf16)
    q_ext, k_ext = queries_ext[rows, :], keys_ext[rows, :]
    ones = jnp.ones_like(values)

    def one(mine, q, k, v):
        scores = dot_nt(jnp.where(mine, q, q_ext), jnp.where(mine, k, k_ext))
        top = jnp.max(scores, axis=-1, keepdims=True)
        weight = jnp.exp(scores - top).astype(bf16)
        return top, dot(weight, jnp.where(mine, v, ones))

    top_a, sum_a = one(low_half, queries, keys, values)
    top_b, sum_b = one(~low_half, queries, keys, values)
    top_c, sum_c = one(low_half, both, keys_two, values_two)
    denom = pltpu.roll(jnp.where(low_half, sum_b, sum_a), HD, 1)
    denom_c = pltpu.roll(sum_c, HD, 1)
    context_out[0, :, :PAIR] = (jnp.where(low_half, sum_a, sum_b) / denom).astype(bf16)
    context_out[0, :, PAIR:] = (sum_c / denom_c)[:, :HD].astype(bf16)
    lse_ab = jnp.where(low_half, top_a, top_b) + jnp.log(denom)
    lse_c = top_c + jnp.log(denom_c)
    every = jnp.where((lane >= 32) & low_half, lse_c, lse_ab).T
    lse_out[0:1, :] = every[0:1]
    lse_out[1:2, :] = every[HD:HD + 1]
    lse_out[2:3, :] = every[32:33]

    @pl.when(step == pl.num_programs(0) - 1)
    def _():
        onward.wait()


def w_out_fsdp(place, depth):
    return (place.shape[0] - 2 * depth - 1) // 5


def attend_one(away, fsdp, place, bucket, lengths, x, own, other, ext, shared):
    t, d = x.shape
    depth = axis_facts()[2]
    height, width = own.shape
    tall, narrow = (height - 16) // depth, d // fsdp
    shapes = [(fsdp, t, narrow), (fsdp, depth, 2, tall, width), (fsdp, 16, width)]
    j = lambda place: neighbour_of(place, away, depth, fsdp)
    any_space = pl.BlockSpec(memory_space=pl.ANY)
    return call(
        functools.partial(attend_one_kernel, away), "attend", (t // PLEN,),
        [pl.BlockSpec((PLEN, d), lambda s, *_: (s, 0)), any_space, any_space] + [held()] * len(ext)
        + [any_space] * len(shared),
        [
            pl.BlockSpec((1, PLEN, narrow), lambda s, place, *_: (j(place), s, 0)), any_space,
            pl.BlockSpec((1, 16, width), lambda s, place, *_: (j(place), 0, 0)),
            pl.BlockSpec((PLEN, USED), lambda s, *_: (s, 0)), pl.BlockSpec((8, PLEN), lambda s, *_: (0, s)),
        ] + ([] if away else [held()] * 2),
        [sds(shape, bf16) for shape in shapes] + [sds((t, USED), bf16), sds((8, t), f32)]
        + ([] if away else [pltpu.VMEM((t, PAIR), bf16)] * 2),
        ([pltpu.VMEM((8, PAIR), bf16)] * 2 if away else [])
        + [pltpu.VMEM((depth, 2, tall, width), bf16), pltpu.SemaphoreType.DMA((4,))],
        prefetch=3, cost=guess(5e9, 8e6), limit=SMALL, free=pl.ANY,
        aliases={6 + len(ext) + n: n for n in range(len(shared))},
    )(place, bucket, lengths, x, own, other, *ext, *shared)


def attend_back_one_kernel(
    away, place, x_t_far, kept, grad_context, lse, delta, gow_far, inner, outer, gub, queries_ext, keys_ext,
    send, keep, grads_out,
    grads, found, sums, x_t, gow, sems,
):
    depth, height, width = send.shape
    tall = height - 16
    step, steps = pl.program_id(0), pl.num_programs(0)
    fsdp = w_out_fsdp(place, depth)
    core, j = core_of(place, depth, fsdp), neighbour_of(place, away, depth, fsdp)
    copies = [
        pltpu.make_async_copy(source, target, sems.at[n])
        for n, (source, target) in enumerate(((x_t_far, x_t), (gow_far.at[j], gow)))
    ]

    @pl.when(step == 0)
    def _():
        for copy in copies:
            copy.start()
        sums[...] = jnp.zeros_like(sums)

    lane = lax.broadcasted_iota(jnp.int32, (PLEN, PAIR), 1)
    low_half = lane < HD
    scale = HD ** (-0.5)

    rows = pl.ds(pl.multiple_of(step * PLEN, PLEN), PLEN)
    queries, keys, values, both, values_two = (kept[:, n * PAIR:(n + 1) * PAIR] for n in range(5))
    keys_two = pltpu.roll(both.astype(f32), HD, 1).astype(bf16)
    q_ext, k_ext = queries_ext[rows, :], keys_ext[rows, :]
    nothing = jnp.zeros_like(values)
    grad_two = jnp.concatenate([grad_context[0, :, PAIR:]] * 2, axis=1)

    def one(a, mine, q, k, v, grad_ctx):
        scores = dot_nt(jnp.where(mine, k, k_ext), jnp.where(mine, q, q_ext))
        probs = jnp.exp(scores - lse[a:a + 1, :])
        grad_probs = dot_nt(jnp.where(mine, v, nothing), grad_ctx)
        grad_scores = (probs * (grad_probs - delta[0, a:a + 1, :])).astype(bf16)
        grad_v = dot(probs.astype(bf16), grad_ctx)
        grad_k = dot(grad_scores, q)
        grad_q = dot_tn(grad_scores, k) * scale
        return grad_q, grad_k, grad_v

    grad_pair = grad_context[0, :, :PAIR]
    q_a, k_a, v_a = one(0, low_half, queries, keys, values, grad_pair)
    q_b, k_b, v_b = one(1, ~low_half, queries, keys, values, grad_pair)
    q_c, k_c, v_c = one(2, low_half, both, keys_two, values_two, grad_two)
    made = [
        jnp.where(low_half, q_a, q_b), jnp.where(low_half, k_a, k_b), jnp.where(low_half, v_a, v_b),
        jnp.where(low_half, q_c, pltpu.roll(k_c, HD, 1)), jnp.where(low_half, v_c, 0.0),
    ]
    for n in range(5):
        low = made[n].astype(bf16)
        lanes = slice(n * PAIR, (n + 1) * PAIR)
        grads[rows, lanes] = low
        grads_out[:, lanes] = low
        sums[0:1, lanes] += jnp.sum(low.astype(f32), axis=0, keepdims=True)

    @pl.when(step == steps - 1)
    def _():
        for copy in copies:
            copy.wait()
        columns = grads[...]
        product = dot(x_t[...], columns)
        found[:, :4 * PAIR] = product[:, :4 * PAIR].astype(bf16)
        found[:, 4 * PAIR:] = jnp.concatenate(
            [product[:, 4 * PAIR:4 * PAIR + HD], gow[...].astype(f32)], axis=1
        ).astype(bf16)
        narrow = width // 4
        none = jnp.zeros((1, 3 * narrow), f32)
        inner_rows, outer_rows = inner[0], outer[0]
        first = jnp.concatenate([sums[0:1, :4 * PAIR + HD], inner_rows[2:3]], axis=1)
        second = jnp.concatenate([inner_rows[0:1], inner_rows[1:2], outer_rows[0:1], outer_rows[1:2]], axis=1)
        third = jnp.concatenate([outer_rows[2:3], none], axis=1)
        row = lax.broadcasted_iota(jnp.int32, (16, width), 0)
        rest = jnp.where(row == 1, second, jnp.where(row == 2, third, jnp.where(row == 3, gub[0], 0.0)))
        below = jnp.where(row == 0, first, rest).astype(bf16)
        for n, target in ((1, send), (0, keep)):
            for z in range(depth):
                i = 2 * z + lax.rem(core + n, 2)
                target[z, :tall, :] = found[pl.ds(pl.multiple_of(i * tall, 16), tall), :]
                target[z, tall:, :] = below


def attend_back_one(
    away, fsdp, depth, place, x_t, kept, grad_context, lse, delta, gow, inner, outer, gub, q_ext, k_ext
):
    d, t = x_t.shape
    tall, narrow, width = d // (2 * depth), d // fsdp, 4 * d // fsdp
    j = lambda place: neighbour_of(place, away, depth, fsdp)
    any_space = pl.BlockSpec(memory_space=pl.ANY)
    small = lambda *shape: pl.BlockSpec((1, *shape), lambda s, place, *_: (j(place), 0, 0))
    sent = (depth, tall + 16, width)
    rows = pl.BlockSpec((PLEN, USED), lambda s, *_: (s, 0))
    return call(
        functools.partial(attend_back_one_kernel, away), "attend_back", (t // PLEN,),
        [any_space, rows, pl.BlockSpec((1, PLEN, narrow), lambda s, place, *_: (j(place), s, 0)),
         pl.BlockSpec((8, PLEN), lambda s, *_: (0, s)),
         pl.BlockSpec((1, 8, PLEN), lambda s, place, *_: (j(place), 0, s)), any_space,
         small(8, narrow), small(8, narrow), small(1, width), held(), held()],
        [whole(sent), whole(sent), rows],
        [sds(sent, bf16)] * 2 + [sds((t, USED), bf16)],
        [pltpu.VMEM((t, USED), bf16), pltpu.VMEM((d, width), bf16), pltpu.VMEM((8, USED), f32), pltpu.VMEM((d, t), bf16),
         pltpu.VMEM((d, narrow), bf16), pltpu.SemaphoreType.DMA((2,))],
        prefetch=1, cost=guess(10e9, 12e6), limit=SMALL,
    )(place, x_t, kept, grad_context, lse, delta, gow, inner, outer, gub, q_ext, k_ext)


def input_grad_kernel(place, inner, *refs):
    grads, weights, out = refs[:-2], refs[-2], refs[-1]
    fsdp, depth, _, tall, _ = weights.shape
    total = inner[...]
    for away, columns in enumerate(grads):
        held_weights = weights[neighbour_of(place, away, depth, fsdp)][:, :, :, :USED]
        total += dot_nt(columns[...], held_weights.reshape(2 * depth * tall, USED))
    out[...] = total


def make_input_grad(place, inner, grads, weights):
    t, d = inner.shape
    rows = pl.BlockSpec((ROWS, d), lambda r, *_: (r, 0))
    return [call(
        input_grad_kernel, "input_grad", (t // ROWS,),
        [rows] + [pl.BlockSpec((ROWS, USED), lambda r, *_: (r, 0))] * len(grads) + [whole(weights.shape)],
        rows, sds((t, d), f32), prefetch=1, cost=guess(5e9, 15e6), limit=SMALL,
    )(place, inner, *grads, weights)]


def attend_back_kernel(
    bucket, lengths, x_t, q, k, v, grad_context, lse, delta, qw, kw, vw, grad_inner,
    gqw, gkw, gvw, gqb, gvb, input_grad,
    queries_ext, keys_ext, grads,
):
    pair = pl.program_id(0)
    row_count = q.shape[0]

    @pl.when(pair == 0)
    def _():
        segment_lanes(bucket, lengths, queries_ext, keys_ext)

    low_half = lax.broadcasted_iota(jnp.int32, (PLEN, PAIR), 1) < HD

    def block(b, carry):
        rows = pl.ds(pl.multiple_of(b * PLEN, PLEN), PLEN)
        queries, keys, values, grad_ctx = q[rows, :], k[rows, :], v[rows, :], grad_context[rows, :]
        q_ext, k_ext = queries_ext[rows, :], keys_ext[rows, :]
        nothing = jnp.zeros_like(values)
        got = []
        for half in range(2):
            mine = low_half if half == 0 else ~low_half
            lse_row = lse[pl.ds(half * HD + pair, 1), rows]
            delta_row = delta[pl.ds(half * HD + pair, 1), rows]
            scores = dot_nt(jnp.where(mine, keys, k_ext), jnp.where(mine, queries, q_ext))
            probs = jnp.exp(scores - lse_row)
            grad_probs = dot_nt(jnp.where(mine, values, nothing), grad_ctx)
            grad_scores = (probs * (grad_probs - delta_row)).astype(bf16)
            grad_v = dot(probs.astype(bf16), grad_ctx)
            grad_k = dot(grad_scores, queries)
            grad_q = dot_tn(grad_scores, keys)
            got.append((grad_q, grad_k, grad_v))
        gq = (jnp.where(low_half, got[0][0], got[1][0]) * HD ** (-0.5)).astype(bf16)
        gk = jnp.where(low_half, got[0][1], got[1][1]).astype(bf16)
        gv = jnp.where(low_half, got[0][2], got[1][2]).astype(bf16)
        grads[rows, :PAIR] = gq
        grads[rows, PAIR:2 * PAIR] = gk
        grads[rows, 2 * PAIR:] = gv
        sum_q = jnp.sum(gq.astype(f32), axis=0, keepdims=True)
        sum_v = jnp.sum(gv.astype(f32), axis=0, keepdims=True)
        return (carry[0] + sum_q, carry[1] + sum_v)

    start = jnp.zeros((1, PAIR), f32)
    gqb[...], gvb[...] = lax.fori_loop(0, row_count // PLEN, block, (start, start))

    columns = grads[...]
    weight_grads = dot(x_t[...], columns)
    gqw[...] = weight_grads[:, :PAIR].astype(gqw.dtype)
    gkw[...] = weight_grads[:, PAIR:2 * PAIR].astype(gkw.dtype)
    gvw[...] = weight_grads[:, 2 * PAIR:].astype(gvw.dtype)

    @pl.when(pair == 0)
    def _():
        input_grad[...] = grad_inner[...]

    weights = jnp.concatenate([qw[0], kw[0], vw[0]], axis=1)
    input_grad[...] += dot_nt(columns, weights)


def attend_back(bucket, lengths, x_t, q, k, v, grad_context, lse, delta, weights, grad_inner):
    t, d = q.shape
    pairs = d // PAIR
    column = lambda m: pl.BlockSpec((1, d, PAIR), lambda p, *_: (m, 0, p))
    vector = pl.BlockSpec((1, PAIR), lambda p, *_: (0, p))
    tall = pl.BlockSpec((t, PAIR), lambda p, *_: (0, p))
    made = pl.BlockSpec((d, PAIR), lambda p, *_: (0, p))
    return call(
        attend_back_kernel, "attend_back", (pairs,),
        [whole((d, t)), tall, tall, tall, tall, whole((PAIR, t)), whole((PAIR, t)),
         column(0), column(1), column(2), whole((t, d))],
        [made, made, made, vector, vector, whole((t, d))],
        [sds((d, d), bf16)] * 3 + [sds((1, d), f32)] * 2 + [sds((t, d), f32)],
        [pltpu.VMEM((t, PAIR), bf16), pltpu.VMEM((t, PAIR), bf16), pltpu.VMEM((t, 3 * PAIR), bf16)],
        prefetch=2, cost=guess(30e9, 25e6),
    )(bucket, lengths, x_t, q, k, v, grad_context, lse, delta, weights, weights, weights, grad_inner)


def normed(v):
    centred = v - jnp.mean(v, axis=-1, keepdims=True)
    r = lax.rsqrt(jnp.mean(centred * centred, axis=-1, keepdims=True) + epsilon)
    return centred * r, r


def norm_back(dy, n, r, gain):
    dn = dy * gain
    return r * (dn - jnp.mean(dn, axis=-1, keepdims=True) - n * jnp.mean(dn * n, axis=-1, keepdims=True))


def gelu_parts(u):
    phi = 0.5 + 0.5 * lax.erf(u * 0.5 ** 0.5)
    bell = jnp.exp2(u * u * -0.7213475204444817)
    return u * phi, phi + u * (bell * 0.3989422804014327)


VECTORS = ((0, 2), (0, 3), (1, 0), (1, 1), (1, 2), (1, 3))


def attended_kernel(x, context, ow, slabs, n1_out, r1_out, low_out, low_t, ow_out, vectors):
    rows = pl.ds(pl.multiple_of(pl.program_id(0) * ROWS, ROWS), ROWS)
    parts, _, narrow = context.shape

    @pl.when(pl.program_id(0) == 0)
    def _():
        ow_out[...] = jnp.concatenate([ow[j][:, ow.shape[2] - narrow:] for j in range(parts)], axis=1)
        cuts, _, width = slabs.shape
        piece = width // 4
        held_slabs = [slabs[j].astype(f32) for j in range(cuts)]
        for n, (r, m) in enumerate(VECTORS):
            vectors[n:n + 1, :] = jnp.concatenate(
                [v[r:r + 1, m * piece:(m + 1) * piece] for v in held_slabs], axis=1
            )

    joined = jnp.concatenate([context[j] for j in range(parts)], axis=1)
    ob, g1, b1 = (vectors[n:n + 1, :] for n in range(3))
    attended = dot(joined, ow_out[...]) + ob
    n1, r1 = normed(x[...].astype(f32) + attended)
    n1_out[rows, :] = n1
    r1_out[rows, :] = jnp.broadcast_to(r1, (ROWS, r1_out.shape[1]))
    low = (n1 * g1 + b1).astype(bf16)
    low_out[rows, :] = low
    low_t[:, rows] = low.T


def attended(x, context, ow, last, slabs):
    t, d = x.shape
    parts, _, narrow = context.shape
    wide = ow.shape[2] // (last + 1)
    rows = pl.BlockSpec((ROWS, d), lambda r: (r, 0))
    return call(
        attended_kernel, "attended", (t // ROWS,),
        [rows, pl.BlockSpec((parts, ROWS, narrow), lambda r: (0, r, 0)),
         pl.BlockSpec((parts, d, wide), lambda r: (0, 0, last)), whole(slabs.shape)],
        [held()] * 5 + [whole((8, d))],
        [pltpu.VMEM((t, d), f32), pltpu.VMEM((t, 128), f32), pltpu.VMEM((t, d), bf16), pltpu.VMEM((d, t), bf16),
         pltpu.VMEM((d, d), bf16), sds((8, d), f32)],
        cost=guess(3e9, 10e6), limit=SMALL,
    )(x, context, ow, slabs)


def up_tiles(tile, uw, slabs, act_out, slope_out):
    count, depth, _, tall, columns = uw.shape
    for j in range(act_out.shape[0]):
        hidden = dot(tile, uw[j].reshape(2 * depth * tall, columns)) + slabs[j, 2:3, :].astype(f32)
        active, slope = gelu_parts(hidden)
        act_out[j] = active.astype(bf16)
        slope_out[j] = slope.astype(bf16)


def up_kernel(place, low, slabs, u0, u1, u2, u3, act_out, slope_out, uw, sems):
    rows = pl.ds(pl.multiple_of(pl.program_id(0) * ROWS, ROWS), ROWS)
    copies = block_copies(place, (u0, u1, u2, u3), lambda core, j: uw.at[j, :, core], sems)

    @pl.when(pl.program_id(0) == 0)
    def _():
        for copy in copies:
            copy.start()
        for copy in copies:
            copy.wait()

    up_tiles(low[rows, :], uw, slabs, act_out, slope_out)


def up_rest_kernel(place, low, slabs, uw, act_in, slope_in, act_out, slope_out):
    rows = pl.ds(pl.multiple_of(pl.program_id(0) * ROWS, ROWS), ROWS)
    up_tiles(low[rows, :], uw, slabs, act_out, slope_out)


def up(place, low, slabs, blocks):
    t, d = low.shape
    half, depth, tall, wide = blocks[0].shape
    f = 2 * half
    high = pl.BlockSpec((half, ROWS, wide), lambda r, *_: (0, r, 0))
    return call(
        up_kernel, "up", (t // ROWS,),
        [held(), whole((half, 16, wide))] + [pl.BlockSpec(memory_space=pl.ANY)] * 4,
        [high, high, whole((f, depth, 2, tall, wide))],
        [sds((f, t, wide), bf16), sds((f, t, wide), bf16), sds((f, depth, 2, tall, wide), bf16)],
        [pltpu.SemaphoreType.DMA((2 * f,))],
        prefetch=1, cost=guess(6e9, 20e6), limit=SMALL, free=pl.ANY,
    )(place, low, slabs, *blocks)


def up_rest(place, low, slabs, uw, act, slope):
    t, d = low.shape
    f, depth, _, tall, wide = uw.shape
    half = f // 2
    high = pl.BlockSpec((half, ROWS, wide), lambda r, *_: (1, r, 0))
    any_space = pl.BlockSpec(memory_space=pl.ANY)
    return call(
        up_rest_kernel, "up_rest", (t // ROWS,),
        [held(), pl.BlockSpec((half, 16, wide), lambda r, *_: (1, 0, 0)),
         pl.BlockSpec((half, depth, 2, tall, wide), lambda r, *_: (1, 0, 0, 0, 0)),
         any_space, any_space],
        [high, high],
        [sds((f, t, wide), bf16), sds((f, t, wide), bf16)],
        prefetch=1, cost=guess(6e9, 16e6), limit=SMALL, aliases={4: 0, 5: 1},
    )(place, low, slabs, uw, act, slope)


def down_kernel(
    place, bucket, lengths, act_rows, n1, given, cotangent, act_part, d0, d1, d2, d3,
    out, pooled, mixed_out, branch_out, vectors, send, keep, dw,
    branch_t, counts, sums, found, sems,
):
    step = pl.program_id(0)
    tiles = branch_t.shape[1] // ROWS
    f, _, height, width = send.shape
    each = d0.shape[2] // height
    tall, narrow = height * each, width // each
    depth = (place.shape[0] - 1 - 5 * f) // 2
    shared = f == depth

    def target(core, j):
        rows = pl.ds(pl.multiple_of(j * tall, 16), tall)
        if shared:
            return dw.at[:, rows, pl.ds(pl.multiple_of(core * narrow, narrow), narrow)]
        return dw.at[:, core, rows, :]

    copies = block_copies(place, (d0, d1, d2, d3), target, sems)

    @pl.when(step == 0)
    def _():
        for copy in copies:
            copy.start()
        pooled[...] = jnp.zeros_like(pooled)
        counts[...] = jnp.zeros_like(counts)
        sums[...] = jnp.zeros_like(sums)
        for copy in copies:
            copy.wait()

    @pl.when(step < tiles)
    def _():
        rows = pl.ds(pl.multiple_of(step * ROWS, ROWS), ROWS)
        if shared:
            parts = [dot_nt(act_rows[row_of(place, 0, s, depth) // 2], dw[s]) for s in range(f)]
        else:
            parts = [dot_nt(act_rows[i], dw[i // 2, i % 2]) for i in range(f)]
        branch = sum(parts[1:], parts[0])
        g1, b1, db, g2, b2 = (given[n:n + 1, :] for n in range(1, 6))
        residual = n1[rows, :] * g1 + b1 + (branch + db)
        n2, r2 = normed(residual)
        result = n2 * g2 + b2
        out[...] = result.astype(bf16)
        passage = bucket[0] == 1
        for part in range(ROWS // QLEN):
            start = step * ROWS + part * QLEN
            segment = jnp.where(passage, start // PLEN, start // QLEN)
            position = jnp.where(passage, lax.rem(start, PLEN), 0)
            alive = jnp.clip(lengths[segment] - position, 0, QLEN)
            row = lax.broadcasted_iota(jnp.int32, (QLEN, 1), 0)
            picked = jnp.where(row < alive, result[part * QLEN:(part + 1) * QLEN], 0.0)
            pooled[pl.ds(segment, 1), :] += jnp.sum(picked, axis=0, keepdims=True)
            counts[pl.ds(segment, 1), :] += jnp.full((1, 128), 1.0, f32) * alive.astype(f32)
        dy = cotangent[...].astype(f32)
        sums[1:2, :] += jnp.sum(dy * n2, axis=0, keepdims=True)
        sums[2:3, :] += jnp.sum(dy, axis=0, keepdims=True)
        mixed = norm_back(dy, n2, r2, g2)
        mixed_out[rows, :] = mixed
        low = mixed.astype(bf16)
        branch_out[rows, :] = low
        sums[0:1, :] += jnp.sum(low.astype(f32), axis=0, keepdims=True)
        branch_t[:, rows] = low.T

    @pl.when(step == tiles - 1)
    def _():
        pooled[...] = pooled[...] / jnp.maximum(counts[...], 1.0)[:, :1]
        for j in range(vectors.shape[0]):
            vectors[j] = sums[:, j * vectors.shape[2]:(j + 1) * vectors.shape[2]]

    if shared:
        @pl.when(step >= tiles)
        def _():
            core = core_of(place, depth, f)
            found[...] = dot(branch_t[...], act_part[0]).astype(bf16)
            for n, made in ((1, send), (0, keep)):
                lanes = pl.ds(pl.multiple_of(lax.rem(core + n, 2) * narrow, narrow), narrow)
                for j in range(f):
                    slot = slot_of(place, n, j, depth, f)
                    for r in range(each):
                        top = j * tall + r * height
                        made[slot, 0, :, r * narrow:(r + 1) * narrow] = found[top:top + height, lanes]
    else:
        def part(n, made):
            part_found = dot(branch_t[...], act_part[0]).astype(bf16)
            for j in range(f):
                made[slot_of(place, n, j, depth, f), 0] = part_found[j * tall:(j + 1) * tall]

        @pl.when((step >= tiles) & (step < tiles + depth))
        def _():
            part(1, send)

        @pl.when(step >= tiles + depth)
        def _():
            part(0, keep)


def down(cuts, place, bucket, lengths, active, n1, given, cotangent, blocks):
    f, t, wide = active.shape
    d = n1.shape[1]
    tiles = t // ROWS
    slots = lengths.shape[0]
    _, depth, tall, narrow = blocks[0].shape
    shared = f == depth
    parts = f
    weights = (f, d, wide) if shared else (depth, 2, d, narrow)
    each = wide // narrow
    early = lambda s: jnp.minimum(s, tiles - 1)
    if shared:
        late = lambda s, place: place[jnp.maximum(s - tiles, 0)] // 2
    else:
        late = lambda s, place: place[(jnp.maximum(s - tiles, 0) + depth) % parts]
    made = lambda first: pl.BlockSpec(
        (f, 1, tall // each, narrow * each), lambda s, *_: (0, jnp.clip(s - tiles - first, 0, depth - 1), 0, 0)
    )
    rows = pl.BlockSpec((ROWS, d), lambda s, *_: (early(s), 0))
    return call(
        down_kernel, "down", (tiles + parts,),
        [pl.BlockSpec((f, ROWS, wide), lambda s, *_: (0, early(s), 0)), held(), whole((8, d)), rows, pl.BlockSpec((1, t, wide), lambda s, place, *_: (late(s, place), 0, 0))]
        + [pl.BlockSpec(memory_space=pl.ANY)] * 4,
        [rows, whole((slots, d)), held(), held(), whole((cuts, 8, d // cuts)), made(0), made(0 if shared else depth),
         whole(weights)],
        [sds((t, d), bf16), sds((slots, d), f32), pltpu.VMEM((t, d), f32), pltpu.VMEM((t, d), bf16)]
        + [sds((cuts, 8, d // cuts), f32)] + [sds((f, depth, tall // each, narrow * each), bf16)] * 2
        + [sds(weights, bf16)],
        [pltpu.VMEM((d, t), bf16), pltpu.VMEM((slots, 128), f32), pltpu.VMEM((8, d), f32),
         pltpu.VMEM((d, wide), bf16), pltpu.SemaphoreType.DMA((2 * f,))],
        prefetch=3, cost=guess(12e9, 35e6), limit=SMALL, free=pl.ANY,
    )(place, bucket, lengths, active, n1, given, cotangent, active, *blocks)


def feed_back_kernel(
    place, branch, slope, dw, uw, low_t, mixed, *refs,
):
    send, keep, gub, grad_normed, hidden, found = refs[-6:]
    j = pl.program_id(0)
    _, depth, tall, _ = send.shape
    _, t, wide = slope.shape
    tiles = t // FEED_ROWS

    def gelu_rows(r, sums):
        rows = pl.ds(pl.multiple_of(r * FEED_ROWS, FEED_ROWS), FEED_ROWS)
        grad = (slope[0, rows, :].astype(f32) * dot(branch[rows, :], dw[0])).astype(bf16)
        hidden[rows, :] = grad
        return sums + jnp.sum(grad.astype(f32), axis=0, keepdims=True)

    gub[0] = lax.fori_loop(0, tiles, gelu_rows, jnp.zeros((1, wide), f32))
    found[...] = dot(low_t[...], hidden[...]).astype(bf16)
    for n, target in ((1, send), (0, keep)):
        for slot in range(depth):
            i = row_of(place, n, slot, depth)
            target[0, slot] = found[pl.ds(pl.multiple_of(i * tall, 16), tall), :]

    @pl.when(j == 0)
    def _():
        grad_normed[...] = mixed[...]

    def normed_rows(r, carry):
        rows = pl.ds(pl.multiple_of(r * FEED_ROWS, FEED_ROWS), FEED_ROWS)
        grad_normed[rows, :] += dot_nt(hidden[rows, :], uw[0])
        return carry

    lax.fori_loop(0, tiles, normed_rows, 0)


def feed_back(first, count, place, branch, slope, dw, uw, low_t, mixed, shared):
    t = slope.shape[1]
    f, d, wide = uw.shape
    dp, _, depth, _ = axis_facts()
    tall = d // dp
    made = lambda n: pl.BlockSpec(
        (1, depth, tall, wide), lambda j, place: (slot_of(place, n, first + j, depth, f), 0, 0, 0)
    )
    part = lambda *shape: pl.BlockSpec((1, *shape), lambda j, *_: (first + j, 0, 0))
    slot = lambda j, place: row_of(place, 0, first + j, depth) // 2 if f == depth else first + j
    any_space = pl.BlockSpec(memory_space=pl.ANY)
    return call(
        feed_back_kernel, "feed_back", (count,),
        [held(), part(t, wide), pl.BlockSpec((1, d, wide), lambda j, place: (slot(j, place), 0, 0)), part(d, wide),
         held(), held()] + [any_space] * len(shared),
        [made(1), made(0), part(1, wide), held()],
        [sds((f, depth, tall, wide), bf16)] * 2 + [pltpu.HBM((f, 1, wide), f32), pltpu.VMEM((t, d), f32)],
        [pltpu.VMEM((t, wide), bf16), pltpu.VMEM((d, wide), bf16)],
        prefetch=1, cost=guess(15e9, 35e6), limit=SMALL, least=0, aliases={7 + n: n for n in range(len(shared))},
    )(place, branch, slope, dw, uw, low_t, mixed, *shared)


def inner_kernel(
    head_of, grad_normed, n1, r1, given, context, ow,
    inner_out, vectors, gow, grad_context, delta_out,
    weight_grad, sums,
):
    step = pl.program_id(0)
    d = n1.shape[1]
    parts, _, narrow = context.shape

    @pl.when(step == 0)
    def _():
        weight_grad[...] = jnp.zeros_like(weight_grad)
        sums[...] = jnp.zeros_like(sums)

    shape = (delta_out.shape[0], d)
    head = head_of(lax.broadcasted_iota(jnp.int32, shape, 0))
    pick = jnp.where(lax.broadcasted_iota(jnp.int32, shape, 1) // HD == head, 1.0, 0.0).astype(bf16)
    rows = pl.ds(pl.multiple_of(step * ROWS, ROWS), ROWS)
    dy, n = grad_normed[rows, :], n1[rows, :]
    inner = norm_back(dy, n, r1[rows, :1], given[1:2, :])
    inner_out[...] = inner
    low = inner.astype(bf16)
    grad_ctx = dot_nt(low, ow[...]).astype(bf16)
    for j in range(parts):
        grad_context[j] = grad_ctx[:, j * narrow:(j + 1) * narrow]
    joined = jnp.concatenate([context[j] for j in range(parts)], axis=1)
    both = grad_ctx.astype(f32) * joined.astype(f32)
    high = both.astype(bf16)
    rest = (both - high.astype(f32)).astype(bf16)
    delta_out[...] = dot_nt(pick, high) + dot_nt(pick, rest)
    sums[0:1, :] += jnp.sum(dy * n, axis=0, keepdims=True)
    sums[1:2, :] += jnp.sum(dy, axis=0, keepdims=True)
    sums[2:3, :] += jnp.sum(low.astype(f32), axis=0, keepdims=True)
    weight_grad[...] += dot_tn(joined, low)

    @pl.when(step == pl.num_programs(0) - 1)
    def _():
        for j in range(parts):
            columns = slice(j * narrow, (j + 1) * narrow)
            gow[j] = weight_grad[:, columns].astype(bf16)
            vectors[j] = sums[:, columns]


def inner_back(count, head_of, grad_normed, n1, r1, given, context, ow):
    t, d = n1.shape
    parts, _, narrow = context.shape
    tile = pl.BlockSpec((parts, ROWS, narrow), lambda r: (0, r, 0))
    return call(
        functools.partial(inner_kernel, head_of), "inner_back", (t // ROWS,),
        [held(), held(), held(), whole((8, d)), tile, held()],
        [pl.BlockSpec((ROWS, d), lambda r: (r, 0)), whole((parts, 8, narrow)), whole((parts, d, narrow)), tile,
         pl.BlockSpec((count, ROWS), lambda r: (0, r))],
        [sds((t, d), f32), sds((parts, 8, narrow), f32), sds((parts, d, narrow), bf16), sds((parts, t, narrow), bf16),
         sds((count, t), f32)],
        [pltpu.VMEM((d, d), f32), pltpu.VMEM((8, d), f32)],
        cost=guess(4e9, 10e6), limit=SMALL,
    )(grad_normed, n1, r1, given, context, ow)


def shards(
    tokens, bucket, lengths, cotangent,
    query_weight, query_bias, key_weight, value_weight, value_bias, out_weight, out_bias,
    norm1_gain, norm1_bias, up_weight, up_bias, down_weight, down_bias, norm2_gain, norm2_bias,
):
    t, d = tokens.shape
    dp, fsdp = lax.axis_size("dp"), lax.axis_size("fsdp")
    lengths = lengths[0]

    place = places()
    depth = dp // 2
    tall, narrow = d // dp, d // fsdp
    width = 4 * narrow
    by_head = narrow == HEADS * HD and fsdp == 4
    down_t = down_weight.T

    if by_head:
        block, slab = make_block(
            query_weight, key_weight, value_weight, out_weight, query_bias, value_bias, out_bias, norm1_gain,
            norm1_bias, down_bias, norm2_gain, norm2_bias, up_bias,
        )
        along = Once([(block, "dp", along_z(s)) for s in range(1, depth)])
        x_t, = beside([along], lambda x: (x.T,), (tokens,))
        own = [block] + along.got
        own = line_up_rows(place, own, slab)
        swap = lambda v: (v, "dp", across_cores())
        in_plane = lambda v, s: (v, "fsdp", [(f, f ^ s) for f in range(fsdp)])
        paired = Once([swap(own)])
        beside([paired])
        pair_0 = paired.got[0]
        ups = Once([(up_weight, "dp", along_z(s)) for s in range(1, depth)])
        sides = Once([in_plane(own, 1), in_plane(own, 2)])
        one = lambda away: functools.partial(attend_one, away, fsdp)
        run = (bucket, lengths, tokens)
        *shared, kept_0, lse_0, q_ext, k_ext = beside(
            [sides, ups], one(0), (place, *run, own, pair_0, [], []), out=3
        )
        ext = [q_ext, k_ext]
        own_x, own_y = sides.got
        to_u = Gather(line_up(place, [up_weight] + ups.got))
        paired = Once([swap(own_x), swap(own_y)])
        corner = Once([(select_core(own_y, own_x), ("dp", "fsdp"), along_bit(0))])
        beside([paired])
        pair_x, pair_y = paired.got
        downs = Once([(down_t, "dp", along_z(s)) for s in range(1, depth)])
        *shared, kept_1, lse_1 = beside([corner, to_u, downs], one(1), (place, *run, own_x, pair_x, ext, shared), out=3)
        own_c = corner.got[0]
        to_d = Gather(jnp.stack([down_t] + downs.got))

        def last_two(place, own_c):
            pair_c = lax.ppermute(own_c, "dp", across_cores())
            *part, kept_2, lse_2 = one(2)(place, *run, own_y, pair_y, ext, shared)
            *part, kept_3, lse_3 = one(3)(place, *run, own_c, pair_c, ext, part)
            return [*part, kept_2, lse_2, kept_3, lse_3]

        *shared, kept_2, lse_2, kept_3, lse_3 = beside([to_u], last_two, (place, own_c), out=5)
        context, weights, slabs = shared
        ow, last = weights.reshape(fsdp, d, width), 2
        count, head_of = 8 * fsdp, lambda r: jnp.where(r % 8 < HEADS, r // 8 * HEADS + r % 8, -1)
    else:
        block = jnp.concatenate([
            jnp.concatenate([query_weight, key_weight, value_weight, out_weight], axis=1),
            jnp.concatenate([query_bias, value_bias, out_bias, norm1_gain])[None],
            jnp.concatenate([norm1_bias, down_bias, norm2_gain, norm2_bias])[None],
            up_bias[None],
            jnp.zeros((13, width), bf16),
        ])
        to_a, to_u, to_d = Gather(gather_z(block)), Gather(gather_z(up_weight)), Gather(gather_z(down_t))
        finish(to_a)
        weights, vectors, slabs = assemble(place, to_a.blocks)
        qb, vb = (vectors[m, 0:1] for m in range(2))
        q, k, v, context, lse = attend(bucket, lengths, tokens, weights, qb, vb)
        context, ow, last = context[None], weights[3:], 0
        count, head_of = PAIR, lambda r: 2 * (r % HD) + r // HD

    n1, r1, low, low_t, ow, given = beside(
        [to_u, to_d], attended, (tokens, context, ow, last, slabs), key=4, out=5
    )
    finish(to_u)
    active, slope, uw = beside([to_d], up, (place, low, slabs, to_u.blocks))
    active, slope = beside([to_d], up_rest, (place, low, slabs, uw, active, slope))
    finish(to_d)
    cuts = context.shape[0]
    out, pooled, mixed, branch, down_vectors, send_d, keep_d, dw = down(
        cuts, place, bucket, lengths, active, n1, given, cotangent, to_d.blocks
    )
    of_d = Scatter(keep_d, send_d)
    dw, uw = dw.reshape(fsdp, d, -1), uw.reshape(fsdp, d, -1)
    part = fsdp // 2
    *shared, so_far = beside(
        [of_d], functools.partial(feed_back, 0, part), (place, branch, slope, dw, uw, low_t, mixed, [])
    )
    send_u, keep_u, gub, grad_normed = beside(
        [of_d], functools.partial(feed_back, part, fsdp - part),
        (place, branch, slope, dw, uw, low_t, so_far, shared),
    )
    of_u = Scatter(keep_u, send_u)
    of_d.joined = of_u.joined = by_head
    inner, inner_vectors, gow, grad_context, delta = beside(
        [of_d, of_u], functools.partial(inner_back, count, head_of), (grad_normed, n1, r1, given, context, ow),
        key=3, out=2
    )

    if by_head:
        delta = delta.reshape(fsdp, 8, t)

        def back(away, moves, kept, lse):
            args = (place, x_t, kept, grad_context, lse, delta, gow, inner_vectors, down_vectors, gub, q_ext, k_ext)
            return beside(moves, functools.partial(attend_back_one, away, fsdp, depth), args)

        send_3, keep_3, grads_3 = back(3, [of_d, of_u], kept_3, lse_3)
        swap_3 = Once([swap(send_3)])
        send_1, keep_1, grads_1 = back(1, [swap_3, of_u], kept_1, lse_1)
        corner = Once([(add(keep_3, swap_3.got[0]), ("dp", "fsdp"), along_bit(0))])
        both = [
            (jnp.concatenate([u, v]), "dp", along_z(-s - 1)) for s, (u, v) in enumerate(zip(of_u.send, of_d.send))
        ]
        near, rest = Once(both[:1]), Once(both[1:])
        swap_1 = Once([swap(send_1)])
        send_2, keep_2, grads_2 = back(2, [corner, near, swap_1], kept_2, lse_2)
        swap_2 = Once([swap(send_2)])
        beside([swap_2])
        add_both = lambda *v: sum(u.astype(f32) for u in v)
        through = corner.got[0]
        sum_1 = add_both(keep_1, swap_1.got[0]) + select_core(jnp.zeros_like(through), through).astype(f32)
        sum_2 = add_both(keep_2, swap_2.got[0]) + select_core(through, jnp.zeros_like(through)).astype(f32)
        sides = Once([in_plane(sum_1.astype(bf16), 1), in_plane(sum_2.astype(bf16), 2)])
        send_0, keep_0, grads_0 = back(0, [sides, rest], kept_0, lse_0)
        sums = Once([swap(send_0)])
        beside([sums, of_u])
        mine, *away = make_total(place, [keep_0, sums.got[0], *sides.got])
        along = Once([(v, "dp", along_z(-s - 1)) for s, v in enumerate(away)])
        input_grad, = beside(
            [along, of_u], make_input_grad, (place, inner, (grads_0, grads_1, grads_2, grads_3), weights)
        )
        *made, gqb, gvb, gob, gg1, gb1, gdb, gg2, gb2, gub = unblock(mine, along.got)
        vectors = (gqb, gvb, gob, gg1, gb1, gdb, gg2, gb2)
        got, input_grad = lax.optimization_barrier((near.got + rest.got, input_grad))
        sum_u = add_both(of_u.keep, *(v[:tall] for v in got))
        sum_d = add_both(of_d.keep, *(v[tall:] for v in got))
    else:
        gg1, gb1, gob = (inner_vectors[0, n:n + 1] for n in range(3))
        gdb, gg2, gb2 = (down_vectors[0, n:n + 1] for n in range(3))
        gqw, gkw, gvw, gqb, gvb, input_grad = attend_back(
            bucket, lengths, tokens.T, q, k, v, grad_context[0], lse, delta, weights, inner
        )
        firsts = jnp.stack([gqb, gvb, gob, gg1])
        seconds = jnp.stack([gb1, gdb, gg2, gb2])
        vectors = jnp.concatenate([firsts, seconds, jnp.zeros((4, 14, d), f32)], axis=1)
        of_a = Scatter(*reversed(pack(place, (gqw, gkw, gvw, gow[0]), vectors, gub)))
        while not (of_a.done() and of_u.done() and of_d.done()):
            beside([of_a, of_u, of_d])
        made_a = of_a.total
        made = [made_a[:tall, m * narrow:(m + 1) * narrow] for m in range(4)]
        vectors = [made_a[tall + n, m * narrow:(m + 1) * narrow] for n in range(2) for m in range(4)]
        gub = made_a[tall + 2]
    if not by_head:
        sum_u, sum_d = of_u.total, of_d.total
    columns = down_weight.shape[0]
    made_u = sum_u
    made_d = jnp.concatenate([sum_d[:, c:c + columns] for c in range(0, width, columns)])
    return (
        out, pooled, input_grad, made[0], vectors[0], made[1], made[2], vectors[1], made[3], vectors[2], vectors[3],
        vectors[4], made_u, gub, made_d.T, vectors[5], vectors[6], vectors[7],
    )


def solution(mesh):
    tall, square, vector = P(("dp", "fsdp"), None), P("dp", "fsdp"), P("fsdp")
    in_specs = (
        tall, P(("dp", "fsdp")), tall, tall, square, vector, square, square, vector, square, vector,
        vector, vector, square, vector, square, vector, vector, vector,
    )
    out_specs = (
        tall, tall, tall, square, vector, square, square, vector, square, vector, vector, vector,
        square, vector, square, vector, vector, vector,
    )
    return jax.shard_map(shards, mesh=mesh, in_specs=in_specs, out_specs=out_specs, check_vma=False)
```

```python
import functools

import jax
import jax.numpy as jnp
from jax import lax
from jax.experimental import pallas as pl
from jax.experimental.pallas import tpu as pltpu
from jax.sharding import PartitionSpec as P

H = 12
HD = 64
PLEN = 512
QLEN = 128
PAIR = 2 * HD
ROWS = 256
FEED_ROWS = 512

epsilon = 1e-06
masked_score = -1e30
f32 = jnp.float32
bf16 = jnp.bfloat16
LIMIT = 60 * 1024 * 1024
SMALL = 24 * 1024 * 1024


def dot(left, right):
    return jnp.dot(left, right, preferred_element_type=f32)


def dot_nt(left, right):
    return lax.dot_general(left, right, (((1,), (1,)), ((), ())), preferred_element_type=f32)


def dot_tn(left, right):
    return lax.dot_general(left, right, (((0,), (0,)), ((), ())), preferred_element_type=f32)


BIG = 16 * 1024


def far(v, least):
    if v.size * v.dtype.itemsize < least:
        return v
    return pltpu.with_memory_space_constraint(v, pltpu.HBM)


def call(
    kernel, name, grid, in_specs, out_specs, out_shape, scratch=(), prefetch=0, cost=None, limit=LIMIT, aliases={},
    least=BIG, free=pltpu.VMEM,
):
    several = isinstance(out_shape, list)
    shapes = [
        pltpu.HBM(v.shape, v.dtype)
        if isinstance(v, jax.ShapeDtypeStruct) and v.size * v.dtype.itemsize >= BIG else v
        for v in (out_shape if several else [out_shape])
    ]
    run = pl.pallas_call(
        kernel,
        name=name,
        grid_spec=pltpu.PrefetchScalarGridSpec(
            num_scalar_prefetch=prefetch,
            grid=grid,
            in_specs=in_specs,
            out_specs=out_specs,
            scratch_shapes=list(scratch),
        ),
        out_shape=shapes if several else shapes[0],
        input_output_aliases=aliases,
        compiler_params=pltpu.CompilerParams(
            vmem_limit_bytes=limit, dimension_semantics=("arbitrary",) * len(grid)
        ),
        cost_estimate=cost,
    )

    def run_far(*args):
        given = [
            v if spec.memory_space in (pltpu.VMEM, free) else far(v, least) for v, spec in zip(args[prefetch:], in_specs)
        ]
        return run(*args[:prefetch], *given)

    return run_far


def whole(shape):
    return pl.BlockSpec(shape, lambda *_: (0,) * len(shape))


def sds(shape, dtype):
    return jax.ShapeDtypeStruct(shape, dtype)


def held():
    return pl.BlockSpec(memory_space=pltpu.VMEM)


def guess(flops, nbytes):
    return pl.CostEstimate(flops=int(flops), bytes_accessed=int(nbytes), transcendentals=0)


def reverse(s, bits):
    return sum(((s >> b) & 1) << (bits - 1 - b) for b in range(bits))


def axis_facts():
    dp, fsdp = lax.axis_size("dp"), lax.axis_size("fsdp")
    return dp, fsdp, dp // 2, fsdp.bit_length() - 1


def along_z(hop):
    dp = lax.axis_size("dp")
    return [(d, (d + 2 * hop) % dp) for d in range(dp)]


def across_cores():
    return [(d, d ^ 1) for d in range(lax.axis_size("dp"))]


def along_bit(r):
    dp, fsdp, _, bits = axis_facts()
    pairs = []
    for d in range(dp):
        flip = 1 << (r if d % 2 == 0 else bits - 1 - r)
        pairs += [(d * fsdp + f, d * fsdp + (f ^ flip)) for f in range(fsdp)]
    return pairs


def select_core(even, odd):
    return jnp.where(lax.axis_index("dp") % 2 == 0, even, odd)


def gather_z(block):
    dp = lax.axis_size("dp")
    groups = [list(range(core, dp, 2)) for core in range(2)]
    return lax.all_gather(block, "dp", axis=0, axis_index_groups=groups)


class Gather:
    def __init__(self, along):
        self.held, self.round, self.blocks = along[None], 0, None

    def stage(self):
        bits = axis_facts()[3]
        if self.round < bits - 1:
            return [(self.held, ("dp", "fsdp"), along_bit(self.round))]
        if self.round < bits:
            return [(self.held, ("dp", "fsdp"), along_bit(self.round)), (self.held, "dp", across_cores())]
        return [(self.own[1], "dp", across_cores())]

    def take(self, got):
        bits = axis_facts()[3]
        if self.round < bits - 1:
            self.held = jnp.concatenate([self.held] + got)
        elif self.round < bits:
            self.own, self.other = [self.held, got[0]], got[1]
        else:
            self.blocks = self.own + [self.other] + got
        self.round += 1

    def done(self):
        return self.blocks is not None


class Once:
    def __init__(self, sends):
        self.sends, self.got = sends, None

    def stage(self):
        return self.sends

    def take(self, got):
        self.got = got

    def done(self):
        return self.got is not None


def add(left, right):
    return (left.astype(f32) + right.astype(f32)).astype(bf16)


class Scatter:
    def __init__(self, keep, send):
        self.keep, self.send, self.round, self.total = keep, [send], axis_facts()[3], None
        self.joined = False

    def stage(self):
        _, _, depth, bits = axis_facts()
        if self.round == bits:
            return [(self.send[0], "dp", across_cores())]
        if self.round >= 0:
            return [(self.send[0], ("dp", "fsdp"), along_bit(self.round))]
        return [(self.send[s - 1], "dp", along_z(-s)) for s in range(1, depth)]

    def take(self, got):
        depth = axis_facts()[2]
        keep = self.keep
        if self.round > 0:
            half = keep.shape[0] // 2
            self.send = [add(keep[half:], got[0][half:])]
            self.keep = add(keep[:half], got[0][:half])
        elif self.round == 0:
            self.send = [add(keep[0, s], got[0][0, s]) for s in range(1, depth)]
            self.keep = keep[0, 0].astype(f32) + got[0][0, 0].astype(f32)
        else:
            for part in got:
                keep = keep + part.astype(f32)
            self.total = keep
        self.round -= 1

    def done(self):
        return self.total is not None or (self.joined and self.round < 0)


def beside(moves, compute=None, args=(), key=0, out=0):
    moves = [move for move in moves if not move.done()]
    stages = [move.stage() for move in moves]
    arrays = [[v for v, _, _ in stage] for stage in stages]
    args = list(args)
    results = ()
    if compute:
        args[key], arrays = lax.optimization_barrier((args[key], arrays))
        results = list(compute(*args))
    else:
        arrays = lax.optimization_barrier(arrays)
    got = [
        [lax.ppermute(v, axis, perm) for v, (_, axis, perm) in zip(sent, stage)]
        for sent, stage in zip(arrays, stages)
    ]
    if compute:
        results[out], got = lax.optimization_barrier((results[out], got))
    else:
        got = lax.optimization_barrier(got)
    for move, parts in zip(moves, got):
        move.take(parts)
    return results


def finish(move):
    while not move.done():
        beside([move])


def places():
    dp, fsdp, depth, bits = axis_facts()
    d, f = lax.axis_index("dp"), lax.axis_index("fsdp")
    z, core = d // 2, d % 2
    slot = jnp.arange(depth, dtype=jnp.int32)
    index = jnp.arange(fsdp, dtype=jnp.int32)
    mirror = sum((((index >> b) & 1) << (bits - 1 - b) for b in range(bits)), jnp.zeros_like(index))
    rows, slots, columns = [], [], []
    for n in range(2):
        there = core ^ n
        rows.append(2 * ((z - slot) % depth) + there)
        away = index ^ f
        mirrored = sum((((away >> b) & 1) << (bits - 1 - b) for b in range(bits)), jnp.zeros_like(index))
        slots.append(jnp.where(there == 0, away, mirrored))
        columns.append(f ^ jnp.where(there == 0, index, mirror))
    neighbours = [(f ^ s)[None] for s in range(fsdp)]
    return jnp.concatenate(rows + slots + columns + [core[None]] + neighbours).astype(jnp.int32)


def row_of(place, n, slot, depth):
    return place[n * depth + slot]


def slot_of(place, n, j, depth, fsdp):
    return place[2 * depth + n * fsdp + j]


def column_of(place, n, s, depth, fsdp):
    return place[2 * depth + 2 * fsdp + n * fsdp + s]


def core_of(place, depth, fsdp):
    return place[2 * depth + 4 * fsdp]


def neighbour_of(place, s, depth, fsdp):
    return place[2 * depth + 4 * fsdp + 1 + s]


def block_copies(place, arrays, target, sems):
    half, depth = arrays[0].shape[:2]
    fsdp = 2 * half
    copies = []
    for a, array in enumerate(arrays):
        core = lax.rem(core_of(place, depth, fsdp) + a // 2, 2)
        for q in range(half):
            j = column_of(place, a // 2, (a % 2) * half + q, depth, fsdp)
            copies.append(pltpu.make_async_copy(array.at[q], target(core, j), sems.at[len(copies)]))
    return copies


def assemble_kernel(place, own_low, own_high, other_low, other_high, weights, vectors, ub):
    step = pl.program_id(0)
    half, _, height, width = own_low.shape
    fsdp, depth, tall = 2 * half, pl.num_programs(0) // 2, height - 16
    narrow = width // 4

    def fill(n, low, high):
        pieces = []
        for j in range(fsdp):
            slot = slot_of(place, n, j, depth, fsdp)
            upper, q = slot >= half, lax.rem(slot, half)
            pieces.append(jnp.where(upper, high[q, 0].astype(f32), low[q, 0].astype(f32)))
        for m in range(4):
            row = jnp.concatenate([p[:, m * narrow:(m + 1) * narrow] for p in pieces], axis=1)
            weights[m] = row[:tall].astype(bf16)
            vectors[m] = row[tall:]
        for j in range(fsdp):
            ub[j] = pieces[j][tall:]

    @pl.when(step < depth)
    def _():
        fill(0, own_low, own_high)

    @pl.when(step >= depth)
    def _():
        fill(1, other_low, other_high)


def row_at(place, s, depth, fsdp):
    core = core_of(place, depth, fsdp)
    return 2 * lax.rem(s, depth) + lax.rem(core + s // depth, 2)


def assemble(place, arrays):
    half, depth, height, width = arrays[0].shape
    fsdp, tall, d = 2 * half, height - 16, half * width // 2
    own = pl.BlockSpec((half, 1, height, width), lambda s, place: (0, jnp.minimum(s, depth - 1), 0, 0))
    other = pl.BlockSpec((half, 1, height, width), lambda s, place: (0, jnp.maximum(s - depth, 0), 0, 0))
    return call(
        assemble_kernel, "assemble", (2 * depth,),
        [own, own, other, other],
        [pl.BlockSpec((4, tall, d), lambda s, place: (0, row_at(place, s, depth, fsdp), 0)), whole((4, 16, d)),
         whole((fsdp, 16, width))],
        [sds((4, 2 * depth * tall, d), bf16), sds((4, 16, d), f32), sds((fsdp, 16, width), f32)],
        prefetch=1, cost=guess(1e9, 11e6),
    )(place, *arrays)


def pack_kernel(place, gq, gk, gv, go, vectors, gub, send, keep):
    step = pl.program_id(0)
    fsdp, _, height, width = send.shape
    depth, tall, narrow = pl.num_programs(0) // 2, height - 16, width // 4

    def fill(n, out):
        for j in range(fsdp):
            slot = slot_of(place, n, j, depth, fsdp)
            columns = slice(j * narrow, (j + 1) * narrow)
            out[slot, 0, :tall, :] = jnp.concatenate(
                [g[:, columns].astype(f32) for g in (gq, gk, gv, go)], axis=1
            ).astype(bf16)
            slab = jnp.concatenate([vectors[m, :, columns] for m in range(4)], axis=1)
            third = lax.broadcasted_iota(jnp.int32, slab.shape, 0) == 2
            out[slot, 0, tall:, :] = jnp.where(third, gub[j], slab).astype(bf16)

    @pl.when(step < depth)
    def _():
        fill(1, send)

    @pl.when(step >= depth)
    def _():
        fill(0, keep)


def pack(place, grads, vectors, gub):
    d = grads[0].shape[0]
    dp, fsdp, depth, _ = axis_facts()
    tall, width = d // dp, 4 * d // fsdp
    rows = pl.BlockSpec((tall, d), lambda s, place: (place[(s + depth) % (2 * depth)], 0))
    sent = pl.BlockSpec((fsdp, 1, tall + 16, width), lambda s, place: (0, jnp.minimum(s, depth - 1), 0, 0))
    kept = pl.BlockSpec((fsdp, 1, tall + 16, width), lambda s, place: (0, jnp.maximum(s - depth, 0), 0, 0))
    return call(
        pack_kernel, "pack", (2 * depth,),
        [rows, rows, rows, rows, whole((4, 16, d)), whole((fsdp, 1, width))],
        [sent, kept],
        [sds((fsdp, depth, tall + 16, width), bf16)] * 2,
        prefetch=1, cost=guess(1e9, 11e6),
    )(place, *grads, vectors, gub)


def segment_lanes(bucket, lengths, queries_ext, keys_ext):
    row_count = queries_ext.shape[0]
    slots = lengths.shape[0]
    shape = (row_count, PAIR)
    row = lax.broadcasted_iota(jnp.int32, shape, 0)
    lane = lax.broadcasted_iota(jnp.int32, shape, 1) % HD
    passage = bucket[0] == 1
    segment = jnp.where(passage, row // PLEN, row // QLEN)
    position = jnp.where(passage, row % PLEN, row % QLEN)
    limit = jnp.zeros(shape, jnp.int32)
    for s in range(slots):
        limit = jnp.where(segment == s, lengths[s], limit)
    alive = position < limit
    same = segment == lane
    queries_ext[...] = jnp.where(same, 1.0, 0.0).astype(bf16)
    keys_ext[...] = jnp.where((lane < slots) & ~(same & alive), masked_score, 0.0).astype(bf16)


def attend_kernel(
    bucket, lengths, x, qw, kw, vw, qb, vb,
    q_out, k_out, v_out, context_out, lse_out,
    queries_ext, keys_ext, lse_all,
):
    pair = pl.program_id(0)
    row_count = x.shape[0]

    @pl.when(pair == 0)
    def _():
        segment_lanes(bucket, lengths, queries_ext, keys_ext)
        lse_all[...] = jnp.zeros_like(lse_all)

    weights = jnp.concatenate([qw[0], kw[0], vw[0]], axis=1)
    qb_row = qb[...]
    vb_row = vb[...]
    low_half = lax.broadcasted_iota(jnp.int32, (PLEN, PAIR), 1) < HD
    lane = lax.broadcasted_iota(jnp.int32, (PLEN, PAIR), 1)

    def block(b, carry):
        rows = pl.ds(pl.multiple_of(b * PLEN, PLEN), PLEN)
        qkv = dot(x[rows, :], weights)
        queries = ((qkv[:, :PAIR] + qb_row).astype(bf16).astype(f32) * HD ** (-0.5)).astype(bf16)
        keys = qkv[:, PAIR:2 * PAIR].astype(bf16)
        values = (qkv[:, 2 * PAIR:] + vb_row).astype(bf16)
        q_out[rows, :] = queries
        k_out[rows, :] = keys
        v_out[rows, :] = values
        q_ext = queries_ext[rows, :]
        k_ext = keys_ext[rows, :]
        ones = jnp.ones_like(values)
        sums, tops = [], []
        for half in range(2):
            mine = low_half if half == 0 else ~low_half
            scores = dot_nt(jnp.where(mine, queries, q_ext), jnp.where(mine, keys, k_ext))
            top = jnp.max(scores, axis=-1, keepdims=True)
            weight = jnp.exp(scores - top).astype(bf16)
            sums.append(dot(weight, jnp.where(mine, values, ones)))
            tops.append(top)
        numer = jnp.where(low_half, sums[0], sums[1])
        denom = pltpu.roll(jnp.where(low_half, sums[1], sums[0]), HD, 1)
        context_out[rows, :] = (numer / denom).astype(bf16)
        lse = jnp.where(low_half, tops[0], tops[1]) + jnp.log(denom)
        mine = (lane % HD) == pair
        lse_all[rows, :] = jnp.where(mine, lse, lse_all[rows, :])
        return carry

    lax.fori_loop(0, row_count // PLEN, block, 0)

    @pl.when(pair == pl.num_programs(0) - 1)
    def _():
        lse_out[...] = lse_all[...].T


def attend(bucket, lengths, x, weights, qb, vb):
    t, d = x.shape
    pairs = d // PAIR
    column = lambda m: pl.BlockSpec((1, d, PAIR), lambda p, *_: (m, 0, p))
    vector = pl.BlockSpec((1, PAIR), lambda p, *_: (0, p))
    tall = pl.BlockSpec((t, PAIR), lambda p, *_: (0, p))
    return call(
        attend_kernel, "attend", (pairs,),
        [whole((t, d)), column(0), column(1), column(2), vector, vector],
        [tall, tall, tall, tall, whole((PAIR, t))],
        [sds((t, d), bf16)] * 4 + [sds((PAIR, t), f32)],
        [pltpu.VMEM((t, PAIR), bf16), pltpu.VMEM((t, PAIR), bf16), pltpu.VMEM((t, PAIR), f32)],
        prefetch=2, cost=guess(15e9, 12e6),
    )(bucket, lengths, x, weights, weights, weights, qb, vb)


HEADS = 3
USED = 5 * PAIR


def block_kernel(q, k, v, o, *refs):
    *vectors, ub, out, slab = refs
    out[...] = jnp.concatenate(
        [part.astype(f32) for part in (
            q[:, :PAIR], k[:, :PAIR], v[:, :PAIR], q[:, PAIR:], k[:, PAIR:], v[:, PAIR:], o[...]
        )], axis=1
    ).astype(bf16)
    each = [v[...].astype(f32)[None, :] for v in vectors]
    first, second = jnp.concatenate(each[:4], axis=1), jnp.concatenate(each[4:], axis=1)
    third = ub[...].astype(f32)[None, :]
    row = lax.broadcasted_iota(jnp.int32, (16, out.shape[1]), 0)
    slab[...] = jnp.where(
        row == 0, first, jnp.where(row == 1, second, jnp.where(row == 2, third, 0.0))
    ).astype(bf16)


def make_block(q, k, v, o, *vectors):
    tall, narrow = q.shape
    shapes = [(tall, 4 * narrow), (16, 4 * narrow)]
    return call(
        block_kernel, "block", (1,), [whole(q.shape)] * 4 + [whole(u.shape) for u in vectors],
        [whole(v) for v in shapes], [sds(v, bf16) for v in shapes], cost=guess(1e6, 1e6), limit=SMALL, least=0,
    )(q, k, v, o, *vectors)


def total_kernel(place, *refs):
    parts, first, others = refs[:4], refs[4], refs[5:]
    depth = 1 + len(others)
    tall = (parts[0].shape[0] - 16) // depth

    def summed(rows):
        return sum((part[rows, :].astype(f32) for part in parts[1:]), parts[0][rows, :].astype(f32))

    below = summed(pl.ds(depth * tall, 16))
    for s in range(depth):
        z = row_of(place, 0, s, depth) // 2
        total = jnp.concatenate([summed(pl.ds(pl.multiple_of(z * tall, 16), tall)), below])
        if s:
            others[s - 1][...] = total.astype(bf16)
        else:
            first[...] = total


def make_total(place, parts):
    depth = axis_facts()[2]
    height, width = parts[0].shape
    out = ((height - 16) // depth + 16, width)
    return call(
        total_kernel, "total", (1,), [whole(parts[0].shape)] * 4, [whole(out)] * depth,
        [sds(out, f32)] + [sds(out, bf16)] * (depth - 1), prefetch=1, cost=guess(1e6, 4e6), limit=SMALL,
    )(place, *parts)


def unblock_kernel(total, *refs):
    got, (gq, gk, gv, go, *vectors) = refs[:-13], refs[-13:]
    tall, narrow = gq.shape
    block = total[...]
    for part in got:
        block = block + part[...].astype(f32)

    def split(v):
        return (
            jnp.concatenate([v[:, :PAIR], v[:, 3 * PAIR:3 * PAIR + HD]], axis=1),
            jnp.concatenate([v[:, PAIR:2 * PAIR], v[:, 3 * PAIR + HD:4 * PAIR]], axis=1),
            jnp.concatenate([v[:, 2 * PAIR:3 * PAIR], v[:, 4 * PAIR:4 * PAIR + HD]], axis=1),
            v[:, 4 * PAIR + HD:],
        )

    gq[...], gk[...], gv[...], go[...] = split(block[:tall])
    qb, _, vb, ob = split(block[tall:tall + 1])
    rest = [block[tall + r:tall + r + 1, m * narrow:(m + 1) * narrow] for r, m in ((1, 0), (1, 1), (1, 2), (1, 3), (2, 0))]
    for ref, row in zip(vectors, (qb, vb, ob, *rest, block[tall + 3:tall + 4])):
        ref[...] = row[0]


def unblock(total, got):
    height, width = total.shape
    tall, narrow = height - 16, width // 4
    shapes = [(tall, narrow)] * 4 + [(narrow,)] * 8 + [(width,)]
    return call(
        unblock_kernel, "unblock", (1,), [whole(total.shape)] * (1 + len(got)), [whole(v) for v in shapes],
        [sds(v, f32) for v in shapes], cost=guess(1e6, 1e6), limit=SMALL,
    )(total, *got)


def line_up_kernel(place, *refs):
    out = refs[-1]
    depth = len(refs) - 1
    for s in range(depth):
        out[row_of(place, 0, s, depth) // 2] = refs[s][...]


def line_up(place, parts):
    shape = parts[0].shape
    out = (len(parts), *shape)
    return call(
        line_up_kernel, "line_up", (1,), [whole(shape)] * len(parts), whole(out), sds(out, parts[0].dtype),
        prefetch=1, cost=guess(1e6, 1e6), limit=SMALL,
    )(place, *parts)


def line_up_rows_kernel(place, *refs):
    *parts, slab, out = refs
    depth, tall = len(parts), parts[0].shape[0]
    for s in range(depth):
        z = row_of(place, 0, s, depth) // 2
        out[pl.ds(pl.multiple_of(z * tall, 16), tall), :] = parts[s][...]
    out[depth * tall:, :] = slab[...]


def line_up_rows(place, parts, slab):
    tall, width = parts[0].shape
    out = (len(parts) * tall + 16, width)
    return call(
        line_up_rows_kernel, "line_up_rows", (1,), [whole((tall, width))] * len(parts) + [whole(slab.shape)],
        whole(out), sds(out, bf16), prefetch=1, cost=guess(1e6, 1e6), limit=SMALL,
    )(place, *parts, slab)


def attend_one_kernel(
    away, place, bucket, lengths, x, own, other, *refs,
):
    *given, context_out, w_out, slab_out, kept, lse_out, queries_ext, keys_ext, weights_here, sems = refs
    if away:
        queries_ext, keys_ext = given[:2]
    depth, _, tall, width = weights_here.shape
    step, fsdp = pl.program_id(0), w_out_fsdp(place, depth)
    core = core_of(place, depth, fsdp)
    j = neighbour_of(place, away, depth, fsdp)
    copies = [
        pltpu.make_async_copy(
            ref.at[pl.ds(0, depth * tall), :].reshape(depth, tall, width), weights_here.at[:, lax.rem(core + n, 2)],
            sems.at[n],
        )
        for n, ref in enumerate((own, other))
    ]
    copies.append(pltpu.make_async_copy(own.at[pl.ds(depth * tall, 16), :], slab_out.at[0], sems.at[2]))
    onward = pltpu.make_async_copy(weights_here, w_out.at[j], sems.at[3])

    @pl.when(step == 0)
    def _():
        for copy in copies:
            copy.start()
        if not away:
            segment_lanes(bucket, lengths, queries_ext, keys_ext)
        for copy in copies:
            copy.wait()
        onward.start()

    narrow = width // 4
    row = slab_out[0, 0:1, :].astype(f32)
    qb, vb = row[:, :narrow], row[:, narrow:2 * narrow]
    none = jnp.zeros((1, PAIR), f32)
    bias = jnp.concatenate(
        [qb[:, :PAIR], none, vb[:, :PAIR], qb[:, PAIR:], none[:, :HD], vb[:, PAIR:], none[:, :HD]], axis=1
    )
    lane = lax.broadcasted_iota(jnp.int32, (PLEN, PAIR), 1)
    low_half = lane < HD
    scale = HD ** (-0.5)

    rows = pl.ds(pl.multiple_of(step * PLEN, PLEN), PLEN)
    weights = weights_here[:, :, :, :USED].reshape(2 * depth * tall, USED)
    qkv = dot(x[...], weights) + bias
    tiles = [qkv[:, n * PAIR:(n + 1) * PAIR].astype(bf16) for n in range(5)]
    tiles[0] = tiles[0] * jnp.array(scale, bf16)
    tiles[3] = jnp.where(low_half, tiles[3] * jnp.array(scale, bf16), tiles[3])
    for n in range(5):
        kept[:, n * PAIR:(n + 1) * PAIR] = tiles[n]
    queries, keys, values, both, values_two = tiles
    keys_two = pltpu.roll(both.astype(f32), HD, 1).astype(bf16)
    q_ext, k_ext = queries_ext[rows, :], keys_ext[rows, :]
    ones = jnp.ones_like(values)

    def one(mine, q, k, v):
        scores = dot_nt(jnp.where(mine, q, q_ext), jnp.where(mine, k, k_ext))
        top = jnp.max(scores, axis=-1, keepdims=True)
        weight = jnp.exp(scores - top).astype(bf16)
        return top, dot(weight, jnp.where(mine, v, ones))

    top_a, sum_a = one(low_half, queries, keys, values)
    top_b, sum_b = one(~low_half, queries, keys, values)
    top_c, sum_c = one(low_half, both, keys_two, values_two)
    denom = pltpu.roll(jnp.where(low_half, sum_b, sum_a), HD, 1)
    denom_c = pltpu.roll(sum_c, HD, 1)
    context_out[0, :, :PAIR] = (jnp.where(low_half, sum_a, sum_b) / denom).astype(bf16)
    context_out[0, :, PAIR:] = (sum_c / denom_c)[:, :HD].astype(bf16)
    lse_ab = jnp.where(low_half, top_a, top_b) + jnp.log(denom)
    lse_c = top_c + jnp.log(denom_c)
    every = jnp.where((lane >= 32) & low_half, lse_c, lse_ab).T
    lse_out[0:1, :] = every[0:1]
    lse_out[1:2, :] = every[HD:HD + 1]
    lse_out[2:3, :] = every[32:33]

    @pl.when(step == pl.num_programs(0) - 1)
    def _():
        onward.wait()


def w_out_fsdp(place, depth):
    return (place.shape[0] - 2 * depth - 1) // 5


def attend_one(away, fsdp, place, bucket, lengths, x, own, other, ext, shared):
    t, d = x.shape
    depth = axis_facts()[2]
    height, width = own.shape
    tall, narrow = (height - 16) // depth, d // fsdp
    shapes = [(fsdp, t, narrow), (fsdp, depth, 2, tall, width), (fsdp, 16, width)]
    j = lambda place: neighbour_of(place, away, depth, fsdp)
    any_space = pl.BlockSpec(memory_space=pl.ANY)
    return call(
        functools.partial(attend_one_kernel, away), "attend", (t // PLEN,),
        [pl.BlockSpec((PLEN, d), lambda s, *_: (s, 0)), any_space, any_space] + [held()] * len(ext)
        + [any_space] * len(shared),
        [
            pl.BlockSpec((1, PLEN, narrow), lambda s, place, *_: (j(place), s, 0)), any_space,
            pl.BlockSpec((1, 16, width), lambda s, place, *_: (j(place), 0, 0)),
            pl.BlockSpec((PLEN, USED), lambda s, *_: (s, 0)), pl.BlockSpec((8, PLEN), lambda s, *_: (0, s)),
        ] + ([] if away else [held()] * 2),
        [sds(shape, bf16) for shape in shapes] + [sds((t, USED), bf16), sds((8, t), f32)]
        + ([] if away else [pltpu.VMEM((t, PAIR), bf16)] * 2),
        ([pltpu.VMEM((8, PAIR), bf16)] * 2 if away else [])
        + [pltpu.VMEM((depth, 2, tall, width), bf16), pltpu.SemaphoreType.DMA((4,))],
        prefetch=3, cost=guess(5e9, 8e6), limit=SMALL, free=pl.ANY,
        aliases={6 + len(ext) + n: n for n in range(len(shared))},
    )(place, bucket, lengths, x, own, other, *ext, *shared)


def attend_back_one_kernel(
    away, depth, place, x_t_far, kept, grad_context, lse, delta, gow_far, inner, outer, gub, queries_ext, keys_ext,
    send, keep, grads_out,
    grads, found, sums, x_t, gow, sems,
):
    height, width = send.shape
    tall = (height - 16) // depth
    step, steps = pl.program_id(0), pl.num_programs(0)
    fsdp = w_out_fsdp(place, depth)
    core, j = core_of(place, depth, fsdp), neighbour_of(place, away, depth, fsdp)
    copies = [
        pltpu.make_async_copy(source, target, sems.at[n])
        for n, (source, target) in enumerate(((x_t_far, x_t), (gow_far.at[j], gow)))
    ]

    @pl.when(step == 0)
    def _():
        for copy in copies:
            copy.start()
        sums[...] = jnp.zeros_like(sums)

    lane = lax.broadcasted_iota(jnp.int32, (PLEN, PAIR), 1)
    low_half = lane < HD
    scale = HD ** (-0.5)

    rows = pl.ds(pl.multiple_of(step * PLEN, PLEN), PLEN)
    queries, keys, values, both, values_two = (kept[:, n * PAIR:(n + 1) * PAIR] for n in range(5))
    keys_two = pltpu.roll(both.astype(f32), HD, 1).astype(bf16)
    q_ext, k_ext = queries_ext[rows, :], keys_ext[rows, :]
    nothing = jnp.zeros_like(values)
    grad_two = jnp.concatenate([grad_context[0, :, PAIR:]] * 2, axis=1)

    def one(a, mine, q, k, v, grad_ctx):
        scores = dot_nt(jnp.where(mine, k, k_ext), jnp.where(mine, q, q_ext))
        probs = jnp.exp(scores - lse[a:a + 1, :])
        grad_probs = dot_nt(jnp.where(mine, v, nothing), grad_ctx)
        grad_scores = (probs * (grad_probs - delta[0, a:a + 1, :])).astype(bf16)
        grad_v = dot(probs.astype(bf16), grad_ctx)
        grad_k = dot(grad_scores, q)
        grad_q = dot_tn(grad_scores, k) * scale
        return grad_q, grad_k, grad_v

    grad_pair = grad_context[0, :, :PAIR]
    q_a, k_a, v_a = one(0, low_half, queries, keys, values, grad_pair)
    q_b, k_b, v_b = one(1, ~low_half, queries, keys, values, grad_pair)
    q_c, k_c, v_c = one(2, low_half, both, keys_two, values_two, grad_two)
    made = [
        jnp.where(low_half, q_a, q_b), jnp.where(low_half, k_a, k_b), jnp.where(low_half, v_a, v_b),
        jnp.where(low_half, q_c, pltpu.roll(k_c, HD, 1)), jnp.where(low_half, v_c, 0.0),
    ]
    for n in range(5):
        low = made[n].astype(bf16)
        lanes = slice(n * PAIR, (n + 1) * PAIR)
        grads[rows, lanes] = low
        grads_out[:, lanes] = low
        sums[0:1, lanes] += jnp.sum(low.astype(f32), axis=0, keepdims=True)

    @pl.when(step == steps - 1)
    def _():
        for copy in copies:
            copy.wait()
        columns = grads[...]
        product = dot(x_t[...], columns)
        found[:, :4 * PAIR] = product[:, :4 * PAIR].astype(bf16)
        found[:, 4 * PAIR:] = jnp.concatenate(
            [product[:, 4 * PAIR:4 * PAIR + HD], gow[...].astype(f32)], axis=1
        ).astype(bf16)
        narrow = width // 4
        none = jnp.zeros((1, 3 * narrow), f32)
        inner_rows, outer_rows = inner[0], outer[0]
        first = jnp.concatenate([sums[0:1, :4 * PAIR + HD], inner_rows[2:3]], axis=1)
        second = jnp.concatenate([inner_rows[0:1], inner_rows[1:2], outer_rows[0:1], outer_rows[1:2]], axis=1)
        third = jnp.concatenate([outer_rows[2:3], none], axis=1)
        row = lax.broadcasted_iota(jnp.int32, (16, width), 0)
        rest = jnp.where(row == 1, second, jnp.where(row == 2, third, jnp.where(row == 3, gub[0], 0.0)))
        below = jnp.where(row == 0, first, rest).astype(bf16)
        for n, target in ((1, send), (0, keep)):
            for z in range(depth):
                i = 2 * z + lax.rem(core + n, 2)
                target[z * tall:(z + 1) * tall, :] = found[pl.ds(pl.multiple_of(i * tall, 16), tall), :]
            target[depth * tall:, :] = below


def attend_back_one(
    away, fsdp, depth, place, x_t, kept, grad_context, lse, delta, gow, inner, outer, gub, q_ext, k_ext
):
    d, t = x_t.shape
    tall, narrow, width = d // (2 * depth), d // fsdp, 4 * d // fsdp
    j = lambda place: neighbour_of(place, away, depth, fsdp)
    any_space = pl.BlockSpec(memory_space=pl.ANY)
    small = lambda *shape: pl.BlockSpec((1, *shape), lambda s, place, *_: (j(place), 0, 0))
    sent = (depth * tall + 16, width)
    rows = pl.BlockSpec((PLEN, USED), lambda s, *_: (s, 0))
    return call(
        functools.partial(attend_back_one_kernel, away, depth), "attend_back", (t // PLEN,),
        [any_space, rows, pl.BlockSpec((1, PLEN, narrow), lambda s, place, *_: (j(place), s, 0)),
         pl.BlockSpec((8, PLEN), lambda s, *_: (0, s)),
         pl.BlockSpec((1, 8, PLEN), lambda s, place, *_: (j(place), 0, s)), any_space,
         small(8, narrow), small(8, narrow), small(1, width), held(), held()],
        [whole(sent), whole(sent), rows],
        [sds(sent, bf16)] * 2 + [sds((t, USED), bf16)],
        [pltpu.VMEM((t, USED), bf16), pltpu.VMEM((d, width), bf16), pltpu.VMEM((8, USED), f32), pltpu.VMEM((d, t), bf16),
         pltpu.VMEM((d, narrow), bf16), pltpu.SemaphoreType.DMA((2,))],
        prefetch=1, cost=guess(10e9, 12e6), limit=SMALL,
    )(place, x_t, kept, grad_context, lse, delta, gow, inner, outer, gub, q_ext, k_ext)


def input_grad_kernel(place, inner, *refs):
    grads, weights, out = refs[:-2], refs[-2], refs[-1]
    fsdp, depth, _, tall, _ = weights.shape
    total = inner[...]
    for away, columns in enumerate(grads):
        held_weights = weights[neighbour_of(place, away, depth, fsdp)][:, :, :, :USED]
        total += dot_nt(columns[...], held_weights.reshape(2 * depth * tall, USED))
    out[...] = total


def make_input_grad(place, inner, grads, weights):
    t, d = inner.shape
    rows = pl.BlockSpec((ROWS, d), lambda r, *_: (r, 0))
    return [call(
        input_grad_kernel, "input_grad", (t // ROWS,),
        [rows] + [pl.BlockSpec((ROWS, USED), lambda r, *_: (r, 0))] * len(grads) + [whole(weights.shape)],
        rows, sds((t, d), f32), prefetch=1, cost=guess(5e9, 15e6), limit=SMALL,
    )(place, inner, *grads, weights)]


def attend_back_kernel(
    bucket, lengths, x_t, q, k, v, grad_context, lse, delta, qw, kw, vw, grad_inner,
    gqw, gkw, gvw, gqb, gvb, input_grad,
    queries_ext, keys_ext, grads,
):
    pair = pl.program_id(0)
    row_count = q.shape[0]

    @pl.when(pair == 0)
    def _():
        segment_lanes(bucket, lengths, queries_ext, keys_ext)

    low_half = lax.broadcasted_iota(jnp.int32, (PLEN, PAIR), 1) < HD

    def block(b, carry):
        rows = pl.ds(pl.multiple_of(b * PLEN, PLEN), PLEN)
        queries, keys, values, grad_ctx = q[rows, :], k[rows, :], v[rows, :], grad_context[rows, :]
        q_ext, k_ext = queries_ext[rows, :], keys_ext[rows, :]
        nothing = jnp.zeros_like(values)
        got = []
        for half in range(2):
            mine = low_half if half == 0 else ~low_half
            lse_row = lse[pl.ds(half * HD + pair, 1), rows]
            delta_row = delta[pl.ds(half * HD + pair, 1), rows]
            scores = dot_nt(jnp.where(mine, keys, k_ext), jnp.where(mine, queries, q_ext))
            probs = jnp.exp(scores - lse_row)
            grad_probs = dot_nt(jnp.where(mine, values, nothing), grad_ctx)
            grad_scores = (probs * (grad_probs - delta_row)).astype(bf16)
            grad_v = dot(probs.astype(bf16), grad_ctx)
            grad_k = dot(grad_scores, queries)
            grad_q = dot_tn(grad_scores, keys)
            got.append((grad_q, grad_k, grad_v))
        gq = (jnp.where(low_half, got[0][0], got[1][0]) * HD ** (-0.5)).astype(bf16)
        gk = jnp.where(low_half, got[0][1], got[1][1]).astype(bf16)
        gv = jnp.where(low_half, got[0][2], got[1][2]).astype(bf16)
        grads[rows, :PAIR] = gq
        grads[rows, PAIR:2 * PAIR] = gk
        grads[rows, 2 * PAIR:] = gv
        sum_q = jnp.sum(gq.astype(f32), axis=0, keepdims=True)
        sum_v = jnp.sum(gv.astype(f32), axis=0, keepdims=True)
        return (carry[0] + sum_q, carry[1] + sum_v)

    start = jnp.zeros((1, PAIR), f32)
    gqb[...], gvb[...] = lax.fori_loop(0, row_count // PLEN, block, (start, start))

    columns = grads[...]
    weight_grads = dot(x_t[...], columns)
    gqw[...] = weight_grads[:, :PAIR].astype(gqw.dtype)
    gkw[...] = weight_grads[:, PAIR:2 * PAIR].astype(gkw.dtype)
    gvw[...] = weight_grads[:, 2 * PAIR:].astype(gvw.dtype)

    @pl.when(pair == 0)
    def _():
        input_grad[...] = grad_inner[...]

    weights = jnp.concatenate([qw[0], kw[0], vw[0]], axis=1)
    input_grad[...] += dot_nt(columns, weights)


def attend_back(bucket, lengths, x_t, q, k, v, grad_context, lse, delta, weights, grad_inner):
    t, d = q.shape
    pairs = d // PAIR
    column = lambda m: pl.BlockSpec((1, d, PAIR), lambda p, *_: (m, 0, p))
    vector = pl.BlockSpec((1, PAIR), lambda p, *_: (0, p))
    tall = pl.BlockSpec((t, PAIR), lambda p, *_: (0, p))
    made = pl.BlockSpec((d, PAIR), lambda p, *_: (0, p))
    return call(
        attend_back_kernel, "attend_back", (pairs,),
        [whole((d, t)), tall, tall, tall, tall, whole((PAIR, t)), whole((PAIR, t)),
         column(0), column(1), column(2), whole((t, d))],
        [made, made, made, vector, vector, whole((t, d))],
        [sds((d, d), bf16)] * 3 + [sds((1, d), f32)] * 2 + [sds((t, d), f32)],
        [pltpu.VMEM((t, PAIR), bf16), pltpu.VMEM((t, PAIR), bf16), pltpu.VMEM((t, 3 * PAIR), bf16)],
        prefetch=2, cost=guess(30e9, 25e6),
    )(bucket, lengths, x_t, q, k, v, grad_context, lse, delta, weights, weights, weights, grad_inner)


def normed(v):
    centred = v - jnp.mean(v, axis=-1, keepdims=True)
    r = lax.rsqrt(jnp.mean(centred * centred, axis=-1, keepdims=True) + epsilon)
    return centred * r, r


def norm_back(dy, n, r, gain):
    dn = dy * gain
    return r * (dn - jnp.mean(dn, axis=-1, keepdims=True) - n * jnp.mean(dn * n, axis=-1, keepdims=True))


def gelu_parts(u):
    phi = 0.5 + 0.5 * lax.erf(u * 0.5 ** 0.5)
    bell = jnp.exp2(u * u * -0.7213475204444817)
    return u * phi, phi + u * (bell * 0.3989422804014327)


VECTORS = ((0, 2), (0, 3), (1, 0), (1, 1), (1, 2), (1, 3))


def attended_kernel(x, context, ow, slabs, n1_out, r1_out, low_out, low_t, ow_out, vectors):
    rows = pl.ds(pl.multiple_of(pl.program_id(0) * ROWS, ROWS), ROWS)
    parts, _, narrow = context.shape

    @pl.when(pl.program_id(0) == 0)
    def _():
        ow_out[...] = jnp.concatenate([ow[j][:, ow.shape[2] - narrow:] for j in range(parts)], axis=1)
        cuts, _, width = slabs.shape
        piece = width // 4
        held_slabs = [slabs[j].astype(f32) for j in range(cuts)]
        for n, (r, m) in enumerate(VECTORS):
            vectors[n:n + 1, :] = jnp.concatenate(
                [v[r:r + 1, m * piece:(m + 1) * piece] for v in held_slabs], axis=1
            )

    joined = jnp.concatenate([context[j] for j in range(parts)], axis=1)
    ob, g1, b1 = (vectors[n:n + 1, :] for n in range(3))
    attended = dot(joined, ow_out[...]) + ob
    n1, r1 = normed(x[...].astype(f32) + attended)
    n1_out[rows, :] = n1
    r1_out[rows, :] = jnp.broadcast_to(r1, (ROWS, r1_out.shape[1]))
    low = (n1 * g1 + b1).astype(bf16)
    low_out[rows, :] = low
    low_t[:, rows] = low.T


def attended(x, context, ow, last, slabs):
    t, d = x.shape
    parts, _, narrow = context.shape
    wide = ow.shape[2] // (last + 1)
    rows = pl.BlockSpec((ROWS, d), lambda r: (r, 0))
    return call(
        attended_kernel, "attended", (t // ROWS,),
        [rows, pl.BlockSpec((parts, ROWS, narrow), lambda r: (0, r, 0)),
         pl.BlockSpec((parts, d, wide), lambda r: (0, 0, last)), whole(slabs.shape)],
        [held()] * 5 + [whole((8, d))],
        [pltpu.VMEM((t, d), f32), pltpu.VMEM((t, 128), f32), pltpu.VMEM((t, d), bf16), pltpu.VMEM((d, t), bf16),
         pltpu.VMEM((d, d), bf16), sds((8, d), f32)],
        cost=guess(3e9, 10e6), limit=SMALL,
    )(x, context, ow, slabs)


def up_tiles(tile, uw, slabs, act_out, slope_out):
    count, depth, _, tall, columns = uw.shape
    for j in range(act_out.shape[0]):
        hidden = dot(tile, uw[j].reshape(2 * depth * tall, columns)) + slabs[j, 2:3, :].astype(f32)
        active, slope = gelu_parts(hidden)
        act_out[j] = active.astype(bf16)
        slope_out[j] = slope.astype(bf16)


def up_kernel(place, low, slabs, u0, u1, u2, u3, act_out, slope_out, uw, sems):
    rows = pl.ds(pl.multiple_of(pl.program_id(0) * ROWS, ROWS), ROWS)
    copies = block_copies(place, (u0, u1, u2, u3), lambda core, j: uw.at[j, :, core], sems)

    @pl.when(pl.program_id(0) == 0)
    def _():
        for copy in copies:
            copy.start()
        for copy in copies:
            copy.wait()

    up_tiles(low[rows, :], uw, slabs, act_out, slope_out)


def up(place, low, slabs, blocks):
    t, d = low.shape
    half, depth, tall, wide = blocks[0].shape
    f = 2 * half
    high = pl.BlockSpec((f, ROWS, wide), lambda r, *_: (0, r, 0))
    return call(
        up_kernel, "up", (t // ROWS,),
        [held(), whole((f, 16, wide))] + [pl.BlockSpec(memory_space=pl.ANY)] * 4,
        [high, high, whole((f, depth, 2, tall, wide))],
        [sds((f, t, wide), bf16), sds((f, t, wide), bf16), sds((f, depth, 2, tall, wide), bf16)],
        [pltpu.SemaphoreType.DMA((2 * f,))],
        prefetch=1, cost=guess(12e9, 30e6), limit=SMALL, free=pl.ANY,
    )(place, low, slabs, *blocks)


def down_kernel(
    place, bucket, lengths, act_rows, n1, given, cotangent, act_part, d0, d1, d2, d3,
    out, pooled, mixed_out, branch_out, vectors, send, keep, dw,
    branch_t, counts, sums, found, sems,
):
    step = pl.program_id(0)
    tiles = branch_t.shape[1] // ROWS
    f, _, height, width = send.shape
    each = d0.shape[2] // height
    tall, narrow = height * each, width // each
    depth = (place.shape[0] - 1 - 5 * f) // 2
    shared = f == depth

    def target(core, j):
        rows = pl.ds(pl.multiple_of(j * tall, 16), tall)
        if shared:
            return dw.at[:, rows, pl.ds(pl.multiple_of(core * narrow, narrow), narrow)]
        return dw.at[:, core, rows, :]

    copies = block_copies(place, (d0, d1, d2, d3), target, sems)

    @pl.when(step == 0)
    def _():
        for copy in copies:
            copy.start()
        pooled[...] = jnp.zeros_like(pooled)
        counts[...] = jnp.zeros_like(counts)
        sums[...] = jnp.zeros_like(sums)
        for copy in copies:
            copy.wait()

    @pl.when(step < tiles)
    def _():
        rows = pl.ds(pl.multiple_of(step * ROWS, ROWS), ROWS)
        if shared:
            parts = [dot_nt(act_rows[row_of(place, 0, s, depth) // 2], dw[s]) for s in range(f)]
        else:
            parts = [dot_nt(act_rows[i], dw[i // 2, i % 2]) for i in range(f)]
        branch = sum(parts[1:], parts[0])
        g1, b1, db, g2, b2 = (given[n:n + 1, :] for n in range(1, 6))
        residual = n1[rows, :] * g1 + b1 + (branch + db)
        n2, r2 = normed(residual)
        result = n2 * g2 + b2
        out[...] = result.astype(bf16)
        passage = bucket[0] == 1
        for part in range(ROWS // QLEN):
            start = step * ROWS + part * QLEN
            segment = jnp.where(passage, start // PLEN, start // QLEN)
            position = jnp.where(passage, lax.rem(start, PLEN), 0)
            alive = jnp.clip(lengths[segment] - position, 0, QLEN)
            row = lax.broadcasted_iota(jnp.int32, (QLEN, 1), 0)
            picked = jnp.where(row < alive, result[part * QLEN:(part + 1) * QLEN], 0.0)
            pooled[pl.ds(segment, 1), :] += jnp.sum(picked, axis=0, keepdims=True)
            counts[pl.ds(segment, 1), :] += jnp.full((1, 128), 1.0, f32) * alive.astype(f32)
        dy = cotangent[...].astype(f32)
        sums[1:2, :] += jnp.sum(dy * n2, axis=0, keepdims=True)
        sums[2:3, :] += jnp.sum(dy, axis=0, keepdims=True)
        mixed = norm_back(dy, n2, r2, g2)
        mixed_out[rows, :] = mixed
        low = mixed.astype(bf16)
        branch_out[rows, :] = low
        sums[0:1, :] += jnp.sum(low.astype(f32), axis=0, keepdims=True)
        branch_t[:, rows] = low.T

    @pl.when(step == tiles - 1)
    def _():
        pooled[...] = pooled[...] / jnp.maximum(counts[...], 1.0)[:, :1]
        for j in range(vectors.shape[0]):
            vectors[j] = sums[:, j * vectors.shape[2]:(j + 1) * vectors.shape[2]]

    if shared:
        @pl.when(step >= tiles)
        def _():
            core = core_of(place, depth, f)
            found[...] = dot(branch_t[...], act_part[0]).astype(bf16)
            for n, made in ((1, send), (0, keep)):
                lanes = pl.ds(pl.multiple_of(lax.rem(core + n, 2) * narrow, narrow), narrow)
                for j in range(f):
                    slot = slot_of(place, n, j, depth, f)
                    for r in range(each):
                        top = j * tall + r * height
                        made[slot, 0, :, r * narrow:(r + 1) * narrow] = found[top:top + height, lanes]
    else:
        def part(n, made):
            part_found = dot(branch_t[...], act_part[0]).astype(bf16)
            for j in range(f):
                made[slot_of(place, n, j, depth, f), 0] = part_found[j * tall:(j + 1) * tall]

        @pl.when((step >= tiles) & (step < tiles + depth))
        def _():
            part(1, send)

        @pl.when(step >= tiles + depth)
        def _():
            part(0, keep)


def down(cuts, place, bucket, lengths, active, n1, given, cotangent, blocks):
    f, t, wide = active.shape
    d = n1.shape[1]
    tiles = t // ROWS
    slots = lengths.shape[0]
    _, depth, tall, narrow = blocks[0].shape
    shared = f == depth
    parts = f
    weights = (f, d, wide) if shared else (depth, 2, d, narrow)
    each = wide // narrow
    early = lambda s: jnp.minimum(s, tiles - 1)
    if shared:
        late = lambda s, place: place[jnp.maximum(s - tiles, 0)] // 2
    else:
        late = lambda s, place: place[(jnp.maximum(s - tiles, 0) + depth) % parts]
    made = lambda first: pl.BlockSpec(
        (f, 1, tall // each, narrow * each), lambda s, *_: (0, jnp.clip(s - tiles - first, 0, depth - 1), 0, 0)
    )
    rows = pl.BlockSpec((ROWS, d), lambda s, *_: (early(s), 0))
    return call(
        down_kernel, "down", (tiles + parts,),
        [pl.BlockSpec((f, ROWS, wide), lambda s, *_: (0, early(s), 0)), held(), whole((8, d)), rows, pl.BlockSpec((1, t, wide), lambda s, place, *_: (late(s, place), 0, 0))]
        + [pl.BlockSpec(memory_space=pl.ANY)] * 4,
        [rows, whole((slots, d)), held(), held(), whole((cuts, 8, d // cuts)), made(0), made(0 if shared else depth),
         whole(weights)],
        [sds((t, d), bf16), sds((slots, d), f32), pltpu.VMEM((t, d), f32), pltpu.VMEM((t, d), bf16)]
        + [sds((cuts, 8, d // cuts), f32)] + [sds((f, depth, tall // each, narrow * each), bf16)] * 2
        + [sds(weights, bf16)],
        [pltpu.VMEM((d, t), bf16), pltpu.VMEM((slots, 128), f32), pltpu.VMEM((8, d), f32),
         pltpu.VMEM((d, wide), bf16), pltpu.SemaphoreType.DMA((2 * f,))],
        prefetch=3, cost=guess(12e9, 35e6), limit=SMALL, free=pl.ANY,
    )(place, bucket, lengths, active, n1, given, cotangent, active, *blocks)


def feed_back_kernel(
    place, branch, slope, dw, uw, low_t, mixed, *refs,
):
    send, keep, gub, grad_normed, hidden, found = refs[-6:]
    j = pl.program_id(0)
    _, depth, tall, _ = send.shape
    _, t, wide = slope.shape
    tiles = t // FEED_ROWS

    def gelu_rows(r, sums):
        rows = pl.ds(pl.multiple_of(r * FEED_ROWS, FEED_ROWS), FEED_ROWS)
        grad = (slope[0, rows, :].astype(f32) * dot(branch[rows, :], dw[0])).astype(bf16)
        hidden[rows, :] = grad
        return sums + jnp.sum(grad.astype(f32), axis=0, keepdims=True)

    gub[0] = lax.fori_loop(0, tiles, gelu_rows, jnp.zeros((1, wide), f32))
    found[...] = dot(low_t[...], hidden[...]).astype(bf16)
    for n, target in ((1, send), (0, keep)):
        for slot in range(depth):
            i = row_of(place, n, slot, depth)
            target[0, slot] = found[pl.ds(pl.multiple_of(i * tall, 16), tall), :]

    @pl.when(j == 0)
    def _():
        grad_normed[...] = mixed[...]

    def normed_rows(r, carry):
        rows = pl.ds(pl.multiple_of(r * FEED_ROWS, FEED_ROWS), FEED_ROWS)
        grad_normed[rows, :] += dot_nt(hidden[rows, :], uw[0])
        return carry

    lax.fori_loop(0, tiles, normed_rows, 0)


def feed_back(first, count, place, branch, slope, dw, uw, low_t, mixed, shared):
    t = slope.shape[1]
    f, d, wide = uw.shape
    dp, _, depth, _ = axis_facts()
    tall = d // dp
    made = lambda n: pl.BlockSpec(
        (1, depth, tall, wide), lambda j, place: (slot_of(place, n, first + j, depth, f), 0, 0, 0)
    )
    part = lambda *shape: pl.BlockSpec((1, *shape), lambda j, *_: (first + j, 0, 0))
    slot = lambda j, place: row_of(place, 0, first + j, depth) // 2 if f == depth else first + j
    any_space = pl.BlockSpec(memory_space=pl.ANY)
    return call(
        feed_back_kernel, "feed_back", (count,),
        [held(), part(t, wide), pl.BlockSpec((1, d, wide), lambda j, place: (slot(j, place), 0, 0)), part(d, wide),
         held(), held()] + [any_space] * len(shared),
        [made(1), made(0), part(1, wide), held()],
        [sds((f, depth, tall, wide), bf16)] * 2 + [pltpu.HBM((f, 1, wide), f32), pltpu.VMEM((t, d), f32)],
        [pltpu.VMEM((t, wide), bf16), pltpu.VMEM((d, wide), bf16)],
        prefetch=1, cost=guess(15e9, 35e6), limit=SMALL, least=0, aliases={7 + n: n for n in range(len(shared))},
    )(place, branch, slope, dw, uw, low_t, mixed, *shared)


def inner_kernel(
    head_of, grad_normed, n1, r1, given, context, ow,
    inner_out, vectors, gow, grad_context, delta_out,
    weight_grad, sums,
):
    step = pl.program_id(0)
    d = n1.shape[1]
    parts, _, narrow = context.shape

    @pl.when(step == 0)
    def _():
        weight_grad[...] = jnp.zeros_like(weight_grad)
        sums[...] = jnp.zeros_like(sums)

    shape = (delta_out.shape[0], d)
    head = head_of(lax.broadcasted_iota(jnp.int32, shape, 0))
    pick = jnp.where(lax.broadcasted_iota(jnp.int32, shape, 1) // HD == head, 1.0, 0.0).astype(bf16)
    rows = pl.ds(pl.multiple_of(step * ROWS, ROWS), ROWS)
    dy, n = grad_normed[rows, :], n1[rows, :]
    inner = norm_back(dy, n, r1[rows, :1], given[1:2, :])
    inner_out[...] = inner
    low = inner.astype(bf16)
    grad_ctx = dot_nt(low, ow[...]).astype(bf16)
    for j in range(parts):
        grad_context[j] = grad_ctx[:, j * narrow:(j + 1) * narrow]
    joined = jnp.concatenate([context[j] for j in range(parts)], axis=1)
    both = grad_ctx.astype(f32) * joined.astype(f32)
    high = both.astype(bf16)
    rest = (both - high.astype(f32)).astype(bf16)
    delta_out[...] = dot_nt(pick, high) + dot_nt(pick, rest)
    sums[0:1, :] += jnp.sum(dy * n, axis=0, keepdims=True)
    sums[1:2, :] += jnp.sum(dy, axis=0, keepdims=True)
    sums[2:3, :] += jnp.sum(low.astype(f32), axis=0, keepdims=True)
    weight_grad[...] += dot_tn(joined, low)

    @pl.when(step == pl.num_programs(0) - 1)
    def _():
        for j in range(parts):
            columns = slice(j * narrow, (j + 1) * narrow)
            gow[j] = weight_grad[:, columns].astype(bf16)
            vectors[j] = sums[:, columns]


def inner_back(count, head_of, grad_normed, n1, r1, given, context, ow):
    t, d = n1.shape
    parts, _, narrow = context.shape
    tile = pl.BlockSpec((parts, ROWS, narrow), lambda r: (0, r, 0))
    return call(
        functools.partial(inner_kernel, head_of), "inner_back", (t // ROWS,),
        [held(), held(), held(), whole((8, d)), tile, held()],
        [pl.BlockSpec((ROWS, d), lambda r: (r, 0)), whole((parts, 8, narrow)), whole((parts, d, narrow)), tile,
         pl.BlockSpec((count, ROWS), lambda r: (0, r))],
        [sds((t, d), f32), sds((parts, 8, narrow), f32), sds((parts, d, narrow), bf16), sds((parts, t, narrow), bf16),
         sds((count, t), f32)],
        [pltpu.VMEM((d, d), f32), pltpu.VMEM((8, d), f32)],
        cost=guess(4e9, 10e6), limit=SMALL,
    )(grad_normed, n1, r1, given, context, ow)


def shards(
    tokens, bucket, lengths, cotangent,
    query_weight, query_bias, key_weight, value_weight, value_bias, out_weight, out_bias,
    norm1_gain, norm1_bias, up_weight, up_bias, down_weight, down_bias, norm2_gain, norm2_bias,
):
    t, d = tokens.shape
    dp, fsdp = lax.axis_size("dp"), lax.axis_size("fsdp")
    lengths = lengths[0]

    place = places()
    depth = dp // 2
    tall, narrow = d // dp, d // fsdp
    width = 4 * narrow
    by_head = narrow == HEADS * HD and fsdp == 4
    down_t = down_weight.T

    if by_head:
        block, slab = make_block(
            query_weight, key_weight, value_weight, out_weight, query_bias, value_bias, out_bias, norm1_gain,
            norm1_bias, down_bias, norm2_gain, norm2_bias, up_bias,
        )
        along = Once([(block, "dp", along_z(s)) for s in range(1, depth)])
        x_t, = beside([along], lambda x: (x.T,), (tokens,))
        own = [block] + along.got
        own = line_up_rows(place, own, slab)
        swap = lambda v: (v, "dp", across_cores())
        in_plane = lambda v, s: (v, "fsdp", [(f, f ^ s) for f in range(fsdp)])
        paired = Once([swap(own)])
        beside([paired])
        pair_0 = paired.got[0]
        ups = Once([(up_weight, "dp", along_z(s)) for s in range(1, depth)])
        sides = Once([in_plane(own, 1), in_plane(own, 2)])
        one = lambda away: functools.partial(attend_one, away, fsdp)
        run = (bucket, lengths, tokens)
        *shared, kept_0, lse_0, q_ext, k_ext = beside(
            [sides, ups], one(0), (place, *run, own, pair_0, [], []), out=3
        )
        ext = [q_ext, k_ext]
        own_x, own_y = sides.got
        to_u = Gather(line_up(place, [up_weight] + ups.got))
        paired = Once([swap(own_x), swap(own_y)])
        corner = Once([(select_core(own_y, own_x), ("dp", "fsdp"), along_bit(0))])
        beside([paired])
        pair_x, pair_y = paired.got
        downs = Once([(down_t, "dp", along_z(s)) for s in range(1, depth)])
        *shared, kept_1, lse_1 = beside([corner, to_u, downs], one(1), (place, *run, own_x, pair_x, ext, shared), out=3)
        own_c = corner.got[0]
        to_d = Gather(jnp.stack([down_t] + downs.got))

        def last_two(place, own_c):
            pair_c = lax.ppermute(own_c, "dp", across_cores())
            *part, kept_2, lse_2 = one(2)(place, *run, own_y, pair_y, ext, shared)
            *part, kept_3, lse_3 = one(3)(place, *run, own_c, pair_c, ext, part)
            return [*part, kept_2, lse_2, kept_3, lse_3]

        *shared, kept_2, lse_2, kept_3, lse_3 = beside([to_u], last_two, (place, own_c), out=5)
        context, weights, slabs = shared
        ow, last = weights.reshape(fsdp, d, width), 2
        count, head_of = 8 * fsdp, lambda r: jnp.where(r % 8 < HEADS, r // 8 * HEADS + r % 8, -1)
    else:
        block = jnp.concatenate([
            jnp.concatenate([query_weight, key_weight, value_weight, out_weight], axis=1),
            jnp.concatenate([query_bias, value_bias, out_bias, norm1_gain])[None],
            jnp.concatenate([norm1_bias, down_bias, norm2_gain, norm2_bias])[None],
            up_bias[None],
            jnp.zeros((13, width), bf16),
        ])
        to_a, to_u, to_d = Gather(gather_z(block)), Gather(gather_z(up_weight)), Gather(gather_z(down_t))
        finish(to_a)
        weights, vectors, slabs = assemble(place, to_a.blocks)
        qb, vb = (vectors[m, 0:1] for m in range(2))
        q, k, v, context, lse = attend(bucket, lengths, tokens, weights, qb, vb)
        context, ow, last = context[None], weights[3:], 0
        count, head_of = PAIR, lambda r: 2 * (r % HD) + r // HD

    n1, r1, low, low_t, ow, given = beside(
        [to_u, to_d], attended, (tokens, context, ow, last, slabs), key=4, out=5
    )
    finish(to_u)
    active, slope, uw = beside([to_d], up, (place, low, slabs, to_u.blocks))
    finish(to_d)
    cuts = context.shape[0]
    out, pooled, mixed, branch, down_vectors, send_d, keep_d, dw = down(
        cuts, place, bucket, lengths, active, n1, given, cotangent, to_d.blocks
    )
    of_d = Scatter(keep_d, send_d)
    dw, uw = dw.reshape(fsdp, d, -1), uw.reshape(fsdp, d, -1)
    part = fsdp // 2
    *shared, so_far = beside(
        [of_d], functools.partial(feed_back, 0, part), (place, branch, slope, dw, uw, low_t, mixed, [])
    )
    send_u, keep_u, gub, grad_normed = beside(
        [of_d], functools.partial(feed_back, part, fsdp - part),
        (place, branch, slope, dw, uw, low_t, so_far, shared),
    )
    of_u = Scatter(keep_u, send_u)
    of_u.joined = by_head
    inner, inner_vectors, gow, grad_context, delta = beside(
        [of_d, of_u], functools.partial(inner_back, count, head_of), (grad_normed, n1, r1, given, context, ow),
        key=3, out=2
    )

    if by_head:
        delta = delta.reshape(fsdp, 8, t)

        def back(away, moves, kept, lse):
            args = (place, x_t, kept, grad_context, lse, delta, gow, inner_vectors, down_vectors, gub, q_ext, k_ext)
            return beside(moves, functools.partial(attend_back_one, away, fsdp, depth), args)

        send_3, keep_3, grads_3 = back(3, [of_u, of_d], kept_3, lse_3)
        swap_3 = Once([swap(send_3)])
        send_1, keep_1, grads_1 = back(1, [swap_3, of_u], kept_1, lse_1)
        corner = Once([(add(keep_3, swap_3.got[0]), ("dp", "fsdp"), along_bit(0))])
        both = [(u, "dp", along_z(-s - 1)) for s, u in enumerate(of_u.send)]
        near, rest = Once(both[::2]), Once(both[1::2])
        swap_1 = Once([swap(send_1)])
        send_2, keep_2, grads_2 = back(2, [corner, near, swap_1], kept_2, lse_2)
        swap_2 = Once([swap(send_2)])
        beside([swap_2])
        add_both = lambda *v: sum(u.astype(f32) for u in v)
        through = corner.got[0]
        sum_1 = add_both(keep_1, swap_1.got[0]) + select_core(jnp.zeros_like(through), through).astype(f32)
        sum_2 = add_both(keep_2, swap_2.got[0]) + select_core(through, jnp.zeros_like(through)).astype(f32)
        sides = Once([in_plane(sum_1.astype(bf16), 1), in_plane(sum_2.astype(bf16), 2)])
        send_0, keep_0, grads_0 = back(0, [sides, rest], kept_0, lse_0)
        sums = Once([swap(send_0)])
        beside([sums, of_u])
        mine, *away = make_total(place, [keep_0, sums.got[0], *sides.got])
        along = Once([(v, "dp", along_z(-s - 1)) for s, v in enumerate(away)])
        input_grad, = beside(
            [along, of_u], make_input_grad, (place, inner, (grads_0, grads_1, grads_2, grads_3), weights)
        )
        *made, gqb, gvb, gob, gg1, gb1, gdb, gg2, gb2, gub = unblock(mine, along.got)
        vectors = (gqb, gvb, gob, gg1, gb1, gdb, gg2, gb2)
        got, input_grad = lax.optimization_barrier((near.got + rest.got, input_grad))
        sum_u, sum_d = add_both(of_u.keep, *got), of_d.total
    else:
        gg1, gb1, gob = (inner_vectors[0, n:n + 1] for n in range(3))
        gdb, gg2, gb2 = (down_vectors[0, n:n + 1] for n in range(3))
        gqw, gkw, gvw, gqb, gvb, input_grad = attend_back(
            bucket, lengths, tokens.T, q, k, v, grad_context[0], lse, delta, weights, inner
        )
        firsts = jnp.stack([gqb, gvb, gob, gg1])
        seconds = jnp.stack([gb1, gdb, gg2, gb2])
        vectors = jnp.concatenate([firsts, seconds, jnp.zeros((4, 14, d), f32)], axis=1)
        of_a = Scatter(*reversed(pack(place, (gqw, gkw, gvw, gow[0]), vectors, gub)))
        while not (of_a.done() and of_u.done() and of_d.done()):
            beside([of_a, of_u, of_d])
        made_a = of_a.total
        made = [made_a[:tall, m * narrow:(m + 1) * narrow] for m in range(4)]
        vectors = [made_a[tall + n, m * narrow:(m + 1) * narrow] for n in range(2) for m in range(4)]
        gub = made_a[tall + 2]
    if not by_head:
        sum_u, sum_d = of_u.total, of_d.total
    columns = down_weight.shape[0]
    made_u = sum_u
    made_d = jnp.concatenate([sum_d[:, c:c + columns] for c in range(0, width, columns)])
    return (
        out, pooled, input_grad, made[0], vectors[0], made[1], made[2], vectors[1], made[3], vectors[2], vectors[3],
        vectors[4], made_u, gub, made_d.T, vectors[5], vectors[6], vectors[7],
    )


def solution(mesh):
    tall, square, vector = P(("dp", "fsdp"), None), P("dp", "fsdp"), P("fsdp")
    in_specs = (
        tall, P(("dp", "fsdp")), tall, tall, square, vector, square, square, vector, square, vector,
        vector, vector, square, vector, square, vector, vector, vector,
    )
    out_specs = (
        tall, tall, tall, square, vector, square, square, vector, square, vector, vector, vector,
        square, vector, square, vector, vector, vector,
    )
    return jax.shard_map(shards, mesh=mesh, in_specs=in_specs, out_specs=out_specs, check_vma=False)
```

```python
import functools

import jax
import jax.numpy as jnp
from jax import lax
from jax.experimental import pallas as pl
from jax.experimental.pallas import tpu as pltpu
from jax.sharding import PartitionSpec as P

H = 12
HD = 64
PLEN = 512
QLEN = 128
PAIR = 2 * HD
ROWS = 256
FEED_ROWS = 512

epsilon = 1e-06
masked_score = -1e30
f32 = jnp.float32
bf16 = jnp.bfloat16
LIMIT = 60 * 1024 * 1024
SMALL = 24 * 1024 * 1024


def dot(left, right):
    return jnp.dot(left, right, preferred_element_type=f32)


def dot_nt(left, right):
    return lax.dot_general(left, right, (((1,), (1,)), ((), ())), preferred_element_type=f32)


def dot_tn(left, right):
    return lax.dot_general(left, right, (((0,), (0,)), ((), ())), preferred_element_type=f32)


BIG = 16 * 1024


def far(v, least):
    if v.size * v.dtype.itemsize < least:
        return v
    return pltpu.with_memory_space_constraint(v, pltpu.HBM)


def call(
    kernel, name, grid, in_specs, out_specs, out_shape, scratch=(), prefetch=0, cost=None, limit=LIMIT, aliases={},
    least=BIG, free=pltpu.VMEM, most=BIG,
):
    several = isinstance(out_shape, list)
    shapes = [
        pltpu.HBM(v.shape, v.dtype)
        if isinstance(v, jax.ShapeDtypeStruct) and v.size * v.dtype.itemsize >= most else v
        for v in (out_shape if several else [out_shape])
    ]
    run = pl.pallas_call(
        kernel,
        name=name,
        grid_spec=pltpu.PrefetchScalarGridSpec(
            num_scalar_prefetch=prefetch,
            grid=grid,
            in_specs=in_specs,
            out_specs=out_specs,
            scratch_shapes=list(scratch),
        ),
        out_shape=shapes if several else shapes[0],
        input_output_aliases=aliases,
        compiler_params=pltpu.CompilerParams(
            vmem_limit_bytes=limit, dimension_semantics=("arbitrary",) * len(grid)
        ),
        cost_estimate=cost,
    )

    def run_far(*args):
        given = [
            v if spec.memory_space in (pltpu.VMEM, free) else far(v, least) for v, spec in zip(args[prefetch:], in_specs)
        ]
        return run(*args[:prefetch], *given)

    return run_far


def whole(shape):
    return pl.BlockSpec(shape, lambda *_: (0,) * len(shape))


def sds(shape, dtype):
    return jax.ShapeDtypeStruct(shape, dtype)


def held():
    return pl.BlockSpec(memory_space=pltpu.VMEM)


def guess(flops, nbytes):
    return pl.CostEstimate(flops=int(flops), bytes_accessed=int(nbytes), transcendentals=0)


def reverse(s, bits):
    return sum(((s >> b) & 1) << (bits - 1 - b) for b in range(bits))


def axis_facts():
    dp, fsdp = lax.axis_size("dp"), lax.axis_size("fsdp")
    return dp, fsdp, dp // 2, fsdp.bit_length() - 1


def along_z(hop):
    dp = lax.axis_size("dp")
    return [(d, (d + 2 * hop) % dp) for d in range(dp)]


def across_cores():
    return [(d, d ^ 1) for d in range(lax.axis_size("dp"))]


def along_bit(r):
    dp, fsdp, _, bits = axis_facts()
    pairs = []
    for d in range(dp):
        flip = 1 << (r if d % 2 == 0 else bits - 1 - r)
        pairs += [(d * fsdp + f, d * fsdp + (f ^ flip)) for f in range(fsdp)]
    return pairs


def select_core(even, odd):
    return jnp.where(lax.axis_index("dp") % 2 == 0, even, odd)


def gather_z(block):
    dp = lax.axis_size("dp")
    groups = [list(range(core, dp, 2)) for core in range(2)]
    return lax.all_gather(block, "dp", axis=0, axis_index_groups=groups)


class Gather:
    def __init__(self, along):
        self.held, self.round, self.blocks = along[None], 0, None

    def stage(self):
        bits = axis_facts()[3]
        if self.round < bits - 1:
            return [(self.held, ("dp", "fsdp"), along_bit(self.round))]
        if self.round < bits:
            return [(self.held, ("dp", "fsdp"), along_bit(self.round)), (self.held, "dp", across_cores())]
        return [(self.own[1], "dp", across_cores())]

    def take(self, got):
        bits = axis_facts()[3]
        if self.round < bits - 1:
            self.held = jnp.concatenate([self.held] + got)
        elif self.round < bits:
            self.own, self.other = [self.held, got[0]], got[1]
        else:
            self.blocks = self.own + [self.other] + got
        self.round += 1

    def done(self):
        return self.blocks is not None


class Once:
    def __init__(self, sends):
        self.sends, self.got = sends, None

    def stage(self):
        return self.sends

    def take(self, got):
        self.got = got

    def done(self):
        return self.got is not None


def add(left, right):
    return (left.astype(f32) + right.astype(f32)).astype(bf16)


class Scatter:
    def __init__(self, keep, send):
        self.keep, self.send, self.round, self.total = keep, [send], axis_facts()[3], None
        self.joined = False

    def stage(self):
        _, _, depth, bits = axis_facts()
        if self.round == bits:
            return [(self.send[0], "dp", across_cores())]
        if self.round >= 0:
            return [(self.send[0], ("dp", "fsdp"), along_bit(self.round))]
        return [(self.send[s - 1], "dp", along_z(-s)) for s in range(1, depth)]

    def take(self, got):
        depth = axis_facts()[2]
        keep = self.keep
        if self.round > 0:
            half = keep.shape[0] // 2
            self.send = [add(keep[half:], got[0][half:])]
            self.keep = add(keep[:half], got[0][:half])
        elif self.round == 0:
            self.send = [add(keep[0, s], got[0][0, s]) for s in range(1, depth)]
            self.keep = keep[0, 0].astype(f32) + got[0][0, 0].astype(f32)
        else:
            for part in got:
                keep = keep + part.astype(f32)
            self.total = keep
        self.round -= 1

    def done(self):
        return self.total is not None or (self.joined and self.round < 0)


def beside(moves, compute=None, args=(), key=0, out=0):
    moves = [move for move in moves if not move.done()]
    stages = [move.stage() for move in moves]
    arrays = [[v for v, _, _ in stage] for stage in stages]
    args = list(args)
    results = ()
    if compute:
        args[key], arrays = lax.optimization_barrier((args[key], arrays))
        results = list(compute(*args))
    else:
        arrays = lax.optimization_barrier(arrays)
    got = [
        [lax.ppermute(v, axis, perm) for v, (_, axis, perm) in zip(sent, stage)]
        for sent, stage in zip(arrays, stages)
    ]
    if compute:
        results[out], got = lax.optimization_barrier((results[out], got))
    else:
        got = lax.optimization_barrier(got)
    for move, parts in zip(moves, got):
        move.take(parts)
    return results


def finish(move):
    while not move.done():
        beside([move])


def places():
    dp, fsdp, depth, bits = axis_facts()
    d, f = lax.axis_index("dp"), lax.axis_index("fsdp")
    z, core = d // 2, d % 2
    slot = jnp.arange(depth, dtype=jnp.int32)
    index = jnp.arange(fsdp, dtype=jnp.int32)
    mirror = sum((((index >> b) & 1) << (bits - 1 - b) for b in range(bits)), jnp.zeros_like(index))
    rows, slots, columns = [], [], []
    for n in range(2):
        there = core ^ n
        rows.append(2 * ((z - slot) % depth) + there)
        away = index ^ f
        mirrored = sum((((away >> b) & 1) << (bits - 1 - b) for b in range(bits)), jnp.zeros_like(index))
        slots.append(jnp.where(there == 0, away, mirrored))
        columns.append(f ^ jnp.where(there == 0, index, mirror))
    neighbours = [(f ^ s)[None] for s in range(fsdp)]
    return jnp.concatenate(rows + slots + columns + [core[None]] + neighbours).astype(jnp.int32)


def row_of(place, n, slot, depth):
    return place[n * depth + slot]


def slot_of(place, n, j, depth, fsdp):
    return place[2 * depth + n * fsdp + j]


def column_of(place, n, s, depth, fsdp):
    return place[2 * depth + 2 * fsdp + n * fsdp + s]


def core_of(place, depth, fsdp):
    return place[2 * depth + 4 * fsdp]


def neighbour_of(place, s, depth, fsdp):
    return place[2 * depth + 4 * fsdp + 1 + s]


def block_copies(place, arrays, target, sems):
    half, depth = arrays[0].shape[:2]
    fsdp = 2 * half
    copies = []
    for a, array in enumerate(arrays):
        core = lax.rem(core_of(place, depth, fsdp) + a // 2, 2)
        for q in range(half):
            j = column_of(place, a // 2, (a % 2) * half + q, depth, fsdp)
            copies.append(pltpu.make_async_copy(array.at[q], target(core, j), sems.at[len(copies)]))
    return copies


def assemble_kernel(place, own_low, own_high, other_low, other_high, weights, vectors, ub):
    step = pl.program_id(0)
    half, _, height, width = own_low.shape
    fsdp, depth, tall = 2 * half, pl.num_programs(0) // 2, height - 16
    narrow = width // 4

    def fill(n, low, high):
        pieces = []
        for j in range(fsdp):
            slot = slot_of(place, n, j, depth, fsdp)
            upper, q = slot >= half, lax.rem(slot, half)
            pieces.append(jnp.where(upper, high[q, 0].astype(f32), low[q, 0].astype(f32)))
        for m in range(4):
            row = jnp.concatenate([p[:, m * narrow:(m + 1) * narrow] for p in pieces], axis=1)
            weights[m] = row[:tall].astype(bf16)
            vectors[m] = row[tall:]
        for j in range(fsdp):
            ub[j] = pieces[j][tall:]

    @pl.when(step < depth)
    def _():
        fill(0, own_low, own_high)

    @pl.when(step >= depth)
    def _():
        fill(1, other_low, other_high)


def row_at(place, s, depth, fsdp):
    core = core_of(place, depth, fsdp)
    return 2 * lax.rem(s, depth) + lax.rem(core + s // depth, 2)


def assemble(place, arrays):
    half, depth, height, width = arrays[0].shape
    fsdp, tall, d = 2 * half, height - 16, half * width // 2
    own = pl.BlockSpec((half, 1, height, width), lambda s, place: (0, jnp.minimum(s, depth - 1), 0, 0))
    other = pl.BlockSpec((half, 1, height, width), lambda s, place: (0, jnp.maximum(s - depth, 0), 0, 0))
    return call(
        assemble_kernel, "assemble", (2 * depth,),
        [own, own, other, other],
        [pl.BlockSpec((4, tall, d), lambda s, place: (0, row_at(place, s, depth, fsdp), 0)), whole((4, 16, d)),
         whole((fsdp, 16, width))],
        [sds((4, 2 * depth * tall, d), bf16), sds((4, 16, d), f32), sds((fsdp, 16, width), f32)],
        prefetch=1, cost=guess(1e9, 11e6),
    )(place, *arrays)


def pack_kernel(place, gq, gk, gv, go, vectors, gub, send, keep):
    step = pl.program_id(0)
    fsdp, _, height, width = send.shape
    depth, tall, narrow = pl.num_programs(0) // 2, height - 16, width // 4

    def fill(n, out):
        for j in range(fsdp):
            slot = slot_of(place, n, j, depth, fsdp)
            columns = slice(j * narrow, (j + 1) * narrow)
            out[slot, 0, :tall, :] = jnp.concatenate(
                [g[:, columns].astype(f32) for g in (gq, gk, gv, go)], axis=1
            ).astype(bf16)
            slab = jnp.concatenate([vectors[m, :, columns] for m in range(4)], axis=1)
            third = lax.broadcasted_iota(jnp.int32, slab.shape, 0) == 2
            out[slot, 0, tall:, :] = jnp.where(third, gub[j], slab).astype(bf16)

    @pl.when(step < depth)
    def _():
        fill(1, send)

    @pl.when(step >= depth)
    def _():
        fill(0, keep)


def pack(place, grads, vectors, gub):
    d = grads[0].shape[0]
    dp, fsdp, depth, _ = axis_facts()
    tall, width = d // dp, 4 * d // fsdp
    rows = pl.BlockSpec((tall, d), lambda s, place: (place[(s + depth) % (2 * depth)], 0))
    sent = pl.BlockSpec((fsdp, 1, tall + 16, width), lambda s, place: (0, jnp.minimum(s, depth - 1), 0, 0))
    kept = pl.BlockSpec((fsdp, 1, tall + 16, width), lambda s, place: (0, jnp.maximum(s - depth, 0), 0, 0))
    return call(
        pack_kernel, "pack", (2 * depth,),
        [rows, rows, rows, rows, whole((4, 16, d)), whole((fsdp, 1, width))],
        [sent, kept],
        [sds((fsdp, depth, tall + 16, width), bf16)] * 2,
        prefetch=1, cost=guess(1e9, 11e6),
    )(place, *grads, vectors, gub)


def segment_lanes(bucket, lengths, queries_ext, keys_ext):
    row_count = queries_ext.shape[0]
    slots = lengths.shape[0]
    shape = (row_count, PAIR)
    row = lax.broadcasted_iota(jnp.int32, shape, 0)
    lane = lax.broadcasted_iota(jnp.int32, shape, 1) % HD
    passage = bucket[0] == 1
    segment = jnp.where(passage, row // PLEN, row // QLEN)
    position = jnp.where(passage, row % PLEN, row % QLEN)
    limit = jnp.zeros(shape, jnp.int32)
    for s in range(slots):
        limit = jnp.where(segment == s, lengths[s], limit)
    alive = position < limit
    same = segment == lane
    queries_ext[...] = jnp.where(same, 1.0, 0.0).astype(bf16)
    keys_ext[...] = jnp.where((lane < slots) & ~(same & alive), masked_score, 0.0).astype(bf16)


def attend_kernel(
    bucket, lengths, x, qw, kw, vw, qb, vb,
    q_out, k_out, v_out, context_out, lse_out,
    queries_ext, keys_ext, lse_all,
):
    pair = pl.program_id(0)
    row_count = x.shape[0]

    @pl.when(pair == 0)
    def _():
        segment_lanes(bucket, lengths, queries_ext, keys_ext)
        lse_all[...] = jnp.zeros_like(lse_all)

    weights = jnp.concatenate([qw[0], kw[0], vw[0]], axis=1)
    qb_row = qb[...]
    vb_row = vb[...]
    low_half = lax.broadcasted_iota(jnp.int32, (PLEN, PAIR), 1) < HD
    lane = lax.broadcasted_iota(jnp.int32, (PLEN, PAIR), 1)

    def block(b, carry):
        rows = pl.ds(pl.multiple_of(b * PLEN, PLEN), PLEN)
        qkv = dot(x[rows, :], weights)
        queries = ((qkv[:, :PAIR] + qb_row).astype(bf16).astype(f32) * HD ** (-0.5)).astype(bf16)
        keys = qkv[:, PAIR:2 * PAIR].astype(bf16)
        values = (qkv[:, 2 * PAIR:] + vb_row).astype(bf16)
        q_out[rows, :] = queries
        k_out[rows, :] = keys
        v_out[rows, :] = values
        q_ext = queries_ext[rows, :]
        k_ext = keys_ext[rows, :]
        ones = jnp.ones_like(values)
        sums, tops = [], []
        for half in range(2):
            mine = low_half if half == 0 else ~low_half
            scores = dot_nt(jnp.where(mine, queries, q_ext), jnp.where(mine, keys, k_ext))
            top = jnp.max(scores, axis=-1, keepdims=True)
            weight = jnp.exp(scores - top).astype(bf16)
            sums.append(dot(weight, jnp.where(mine, values, ones)))
            tops.append(top)
        numer = jnp.where(low_half, sums[0], sums[1])
        denom = pltpu.roll(jnp.where(low_half, sums[1], sums[0]), HD, 1)
        context_out[rows, :] = (numer / denom).astype(bf16)
        lse = jnp.where(low_half, tops[0], tops[1]) + jnp.log(denom)
        mine = (lane % HD) == pair
        lse_all[rows, :] = jnp.where(mine, lse, lse_all[rows, :])
        return carry

    lax.fori_loop(0, row_count // PLEN, block, 0)

    @pl.when(pair == pl.num_programs(0) - 1)
    def _():
        lse_out[...] = lse_all[...].T


def attend(bucket, lengths, x, weights, qb, vb):
    t, d = x.shape
    pairs = d // PAIR
    column = lambda m: pl.BlockSpec((1, d, PAIR), lambda p, *_: (m, 0, p))
    vector = pl.BlockSpec((1, PAIR), lambda p, *_: (0, p))
    tall = pl.BlockSpec((t, PAIR), lambda p, *_: (0, p))
    return call(
        attend_kernel, "attend", (pairs,),
        [whole((t, d)), column(0), column(1), column(2), vector, vector],
        [tall, tall, tall, tall, whole((PAIR, t))],
        [sds((t, d), bf16)] * 4 + [sds((PAIR, t), f32)],
        [pltpu.VMEM((t, PAIR), bf16), pltpu.VMEM((t, PAIR), bf16), pltpu.VMEM((t, PAIR), f32)],
        prefetch=2, cost=guess(15e9, 12e6),
    )(bucket, lengths, x, weights, weights, weights, qb, vb)


HEADS = 3
USED = 5 * PAIR


def block_kernel(q, k, v, o, *refs):
    *vectors, ub, out, slab = refs
    out[...] = jnp.concatenate(
        [part.astype(f32) for part in (
            q[:, :PAIR], k[:, :PAIR], v[:, :PAIR], q[:, PAIR:], k[:, PAIR:], v[:, PAIR:], o[...]
        )], axis=1
    ).astype(bf16)
    each = [v[...].astype(f32)[None, :] for v in vectors]
    first, second = jnp.concatenate(each[:4], axis=1), jnp.concatenate(each[4:], axis=1)
    third = ub[...].astype(f32)[None, :]
    row = lax.broadcasted_iota(jnp.int32, (16, out.shape[1]), 0)
    slab[...] = jnp.where(
        row == 0, first, jnp.where(row == 1, second, jnp.where(row == 2, third, 0.0))
    ).astype(bf16)


def make_block(q, k, v, o, *vectors):
    tall, narrow = q.shape
    shapes = [(tall, 4 * narrow), (16, 4 * narrow)]
    return call(
        block_kernel, "block", (1,), [whole(q.shape)] * 4 + [whole(u.shape) for u in vectors],
        [whole(v) for v in shapes], [sds(v, bf16) for v in shapes], cost=guess(1e6, 1e6), limit=SMALL, least=0, most=1 << 40,
    )(q, k, v, o, *vectors)


def total_kernel(place, *refs):
    parts, first, others = refs[:4], refs[4], refs[5:]
    depth = 1 + len(others)
    tall = (parts[0].shape[0] - 16) // depth

    def summed(rows):
        return sum((part[rows, :].astype(f32) for part in parts[1:]), parts[0][rows, :].astype(f32))

    below = summed(pl.ds(depth * tall, 16))
    for s in range(depth):
        z = row_of(place, 0, s, depth) // 2
        total = jnp.concatenate([summed(pl.ds(pl.multiple_of(z * tall, 16), tall)), below])
        if s:
            others[s - 1][...] = total.astype(bf16)
        else:
            first[...] = total


def make_total(place, parts):
    depth = axis_facts()[2]
    height, width = parts[0].shape
    out = ((height - 16) // depth + 16, width)
    return call(
        total_kernel, "total", (1,), [held()] * 4, [whole(out)] * depth,
        [sds(out, f32)] + [sds(out, bf16)] * (depth - 1), prefetch=1, cost=guess(1e6, 4e6), limit=SMALL, most=1 << 40,
    )(place, *parts)


def unblock_kernel(total, *refs):
    got, (gq, gk, gv, go, *vectors) = refs[:-13], refs[-13:]
    tall, narrow = gq.shape
    block = total[...]
    for part in got:
        block = block + part[...].astype(f32)

    def split(v):
        return (
            jnp.concatenate([v[:, :PAIR], v[:, 3 * PAIR:3 * PAIR + HD]], axis=1),
            jnp.concatenate([v[:, PAIR:2 * PAIR], v[:, 3 * PAIR + HD:4 * PAIR]], axis=1),
            jnp.concatenate([v[:, 2 * PAIR:3 * PAIR], v[:, 4 * PAIR:4 * PAIR + HD]], axis=1),
            v[:, 4 * PAIR + HD:],
        )

    gq[...], gk[...], gv[...], go[...] = split(block[:tall])
    qb, _, vb, ob = split(block[tall:tall + 1])
    rest = [block[tall + r:tall + r + 1, m * narrow:(m + 1) * narrow] for r, m in ((1, 0), (1, 1), (1, 2), (1, 3), (2, 0))]
    for ref, row in zip(vectors, (qb, vb, ob, *rest, block[tall + 3:tall + 4])):
        ref[...] = row[0]


def unblock(total, got):
    height, width = total.shape
    tall, narrow = height - 16, width // 4
    shapes = [(tall, narrow)] * 4 + [(narrow,)] * 8 + [(width,)]
    return call(
        unblock_kernel, "unblock", (1,), [held()] * (1 + len(got)), [whole(v) for v in shapes],
        [sds(v, f32) for v in shapes], cost=guess(1e6, 1e6), limit=SMALL,
    )(total, *got)


def line_up_kernel(place, *refs):
    out = refs[-1]
    depth = len(refs) - 1
    for s in range(depth):
        out[row_of(place, 0, s, depth) // 2] = refs[s][...]


def line_up(place, parts):
    shape = parts[0].shape
    out = (len(parts), *shape)
    return call(
        line_up_kernel, "line_up", (1,), [held()] * len(parts), whole(out), sds(out, parts[0].dtype),
        prefetch=1, cost=guess(1e6, 1e6), limit=SMALL, most=1 << 40,
    )(place, *parts)


def line_up_rows_kernel(place, *refs):
    *parts, slab, out = refs
    depth, tall = len(parts), parts[0].shape[0]
    for s in range(depth):
        z = row_of(place, 0, s, depth) // 2
        out[pl.ds(pl.multiple_of(z * tall, 16), tall), :] = parts[s][...]
    out[depth * tall:, :] = slab[...]


def line_up_rows(place, parts, slab):
    tall, width = parts[0].shape
    out = (len(parts) * tall + 16, width)
    return call(
        line_up_rows_kernel, "line_up_rows", (1,), [held()] * (len(parts) + 1),
        whole(out), sds(out, bf16), prefetch=1, cost=guess(1e6, 1e6), limit=SMALL, most=1 << 40,
    )(place, *parts, slab)


def attend_one_kernel(
    away, place, bucket, lengths, x, own, other, *refs,
):
    *given, context_out, w_out, slab_out, kept, lse_out, queries_ext, keys_ext, weights_here, sems = refs
    if away:
        queries_ext, keys_ext = given[:2]
    depth, _, tall, width = weights_here.shape
    step, fsdp = pl.program_id(0), w_out_fsdp(place, depth)
    core = core_of(place, depth, fsdp)
    j = neighbour_of(place, away, depth, fsdp)
    copies = [
        pltpu.make_async_copy(
            ref.at[pl.ds(0, depth * tall), :].reshape(depth, tall, width), weights_here.at[:, lax.rem(core + n, 2)],
            sems.at[n],
        )
        for n, ref in enumerate((own, other))
    ]
    copies.append(pltpu.make_async_copy(own.at[pl.ds(depth * tall, 16), :], slab_out.at[0], sems.at[2]))
    onward = pltpu.make_async_copy(weights_here, w_out.at[j], sems.at[3])

    @pl.when(step == 0)
    def _():
        for copy in copies:
            copy.start()
        if not away:
            segment_lanes(bucket, lengths, queries_ext, keys_ext)
        for copy in copies:
            copy.wait()
        onward.start()

    narrow = width // 4
    row = slab_out[0, 0:1, :].astype(f32)
    qb, vb = row[:, :narrow], row[:, narrow:2 * narrow]
    none = jnp.zeros((1, PAIR), f32)
    bias = jnp.concatenate(
        [qb[:, :PAIR], none, vb[:, :PAIR], qb[:, PAIR:], none[:, :HD], vb[:, PAIR:], none[:, :HD]], axis=1
    )
    lane = lax.broadcasted_iota(jnp.int32, (PLEN, PAIR), 1)
    low_half = lane < HD
    scale = HD ** (-0.5)

    rows = pl.ds(pl.multiple_of(step * PLEN, PLEN), PLEN)
    weights = weights_here[:, :, :, :USED].reshape(2 * depth * tall, USED)
    qkv = dot(x[...], weights) + bias
    tiles = [qkv[:, n * PAIR:(n + 1) * PAIR].astype(bf16) for n in range(5)]
    tiles[0] = tiles[0] * jnp.array(scale, bf16)
    tiles[3] = jnp.where(low_half, tiles[3] * jnp.array(scale, bf16), tiles[3])
    for n in range(5):
        kept[:, n * PAIR:(n + 1) * PAIR] = tiles[n]
    queries, keys, values, both, values_two = tiles
    keys_two = pltpu.roll(both.astype(f32), HD, 1).astype(bf16)
    q_ext, k_ext = queries_ext[rows, :], keys_ext[rows, :]
    ones = jnp.ones_like(values)

    def one(mine, q, k, v):
        scores = dot_nt(jnp.where(mine, q, q_ext), jnp.where(mine, k, k_ext))
        top = jnp.max(scores, axis=-1, keepdims=True)
        weight = jnp.exp(scores - top).astype(bf16)
        return top, dot(weight, jnp.where(mine, v, ones))

    top_a, sum_a = one(low_half, queries, keys, values)
    top_b, sum_b = one(~low_half, queries, keys, values)
    top_c, sum_c = one(low_half, both, keys_two, values_two)
    denom = pltpu.roll(jnp.where(low_half, sum_b, sum_a), HD, 1)
    denom_c = pltpu.roll(sum_c, HD, 1)
    context_out[0, :, :PAIR] = (jnp.where(low_half, sum_a, sum_b) / denom).astype(bf16)
    context_out[0, :, PAIR:] = (sum_c / denom_c)[:, :HD].astype(bf16)
    lse_ab = jnp.where(low_half, top_a, top_b) + jnp.log(denom)
    lse_c = top_c + jnp.log(denom_c)
    every = jnp.where((lane >= 32) & low_half, lse_c, lse_ab).T
    lse_out[0:1, :] = every[0:1]
    lse_out[1:2, :] = every[HD:HD + 1]
    lse_out[2:3, :] = every[32:33]

    @pl.when(step == pl.num_programs(0) - 1)
    def _():
        onward.wait()


def w_out_fsdp(place, depth):
    return (place.shape[0] - 2 * depth - 1) // 5


def attend_one(away, fsdp, place, bucket, lengths, x, own, other, ext, shared):
    t, d = x.shape
    depth = axis_facts()[2]
    height, width = own.shape
    tall, narrow = (height - 16) // depth, d // fsdp
    shapes = [(fsdp, t, narrow), (fsdp, depth, 2, tall, width), (fsdp, 16, width)]
    j = lambda place: neighbour_of(place, away, depth, fsdp)
    any_space = pl.BlockSpec(memory_space=pl.ANY)
    return call(
        functools.partial(attend_one_kernel, away), "attend", (t // PLEN,),
        [pl.BlockSpec((PLEN, d), lambda s, *_: (s, 0)), any_space, any_space] + [held()] * len(ext)
        + [any_space] * len(shared),
        [
            pl.BlockSpec((1, PLEN, narrow), lambda s, place, *_: (j(place), s, 0)), any_space,
            pl.BlockSpec((1, 16, width), lambda s, place, *_: (j(place), 0, 0)),
            pl.BlockSpec((PLEN, USED), lambda s, *_: (s, 0)), pl.BlockSpec((8, PLEN), lambda s, *_: (0, s)),
        ] + ([] if away else [held()] * 2),
        [sds(shape, bf16) for shape in shapes] + [sds((t, USED), bf16), sds((8, t), f32)]
        + ([] if away else [pltpu.VMEM((t, PAIR), bf16)] * 2),
        ([pltpu.VMEM((8, PAIR), bf16)] * 2 if away else [])
        + [pltpu.VMEM((depth, 2, tall, width), bf16), pltpu.SemaphoreType.DMA((4,))],
        prefetch=3, cost=guess(5e9, 8e6), limit=SMALL, free=pl.ANY,
        aliases={6 + len(ext) + n: n for n in range(len(shared))},
    )(place, bucket, lengths, x, own, other, *ext, *shared)


def attend_back_one_kernel(
    away, depth, place, x_t_far, kept, grad_context, lse, delta, gow_far, inner, outer, gub, queries_ext, keys_ext,
    send, keep, grads_out,
    grads, found, sums, x_t, gow, sems,
):
    height, width = send.shape
    tall = (height - 16) // depth
    step, steps = pl.program_id(0), pl.num_programs(0)
    fsdp = w_out_fsdp(place, depth)
    core, j = core_of(place, depth, fsdp), neighbour_of(place, away, depth, fsdp)
    copies = [
        pltpu.make_async_copy(source, target, sems.at[n])
        for n, (source, target) in enumerate(((x_t_far, x_t), (gow_far.at[j], gow)))
    ]

    @pl.when(step == 0)
    def _():
        for copy in copies:
            copy.start()
        sums[...] = jnp.zeros_like(sums)

    lane = lax.broadcasted_iota(jnp.int32, (PLEN, PAIR), 1)
    low_half = lane < HD
    scale = HD ** (-0.5)

    rows = pl.ds(pl.multiple_of(step * PLEN, PLEN), PLEN)
    queries, keys, values, both, values_two = (kept[:, n * PAIR:(n + 1) * PAIR] for n in range(5))
    keys_two = pltpu.roll(both.astype(f32), HD, 1).astype(bf16)
    q_ext, k_ext = queries_ext[rows, :], keys_ext[rows, :]
    nothing = jnp.zeros_like(values)
    grad_two = jnp.concatenate([grad_context[0, :, PAIR:]] * 2, axis=1)

    def one(a, mine, q, k, v, grad_ctx):
        scores = dot_nt(jnp.where(mine, k, k_ext), jnp.where(mine, q, q_ext))
        probs = jnp.exp(scores - lse[a:a + 1, :])
        grad_probs = dot_nt(jnp.where(mine, v, nothing), grad_ctx)
        grad_scores = (probs * (grad_probs - delta[0, a:a + 1, :])).astype(bf16)
        grad_v = dot(probs.astype(bf16), grad_ctx)
        grad_k = dot(grad_scores, q)
        grad_q = dot_tn(grad_scores, k) * scale
        return grad_q, grad_k, grad_v

    grad_pair = grad_context[0, :, :PAIR]
    q_a, k_a, v_a = one(0, low_half, queries, keys, values, grad_pair)
    q_b, k_b, v_b = one(1, ~low_half, queries, keys, values, grad_pair)
    q_c, k_c, v_c = one(2, low_half, both, keys_two, values_two, grad_two)
    made = [
        jnp.where(low_half, q_a, q_b), jnp.where(low_half, k_a, k_b), jnp.where(low_half, v_a, v_b),
        jnp.where(low_half, q_c, pltpu.roll(k_c, HD, 1)), jnp.where(low_half, v_c, 0.0),
    ]
    for n in range(5):
        low = made[n].astype(bf16)
        lanes = slice(n * PAIR, (n + 1) * PAIR)
        grads[rows, lanes] = low
        grads_out[:, lanes] = low
        sums[0:1, lanes] += jnp.sum(low.astype(f32), axis=0, keepdims=True)

    @pl.when(step == steps - 1)
    def _():
        for copy in copies:
            copy.wait()
        columns = grads[...]
        product = dot(x_t[...], columns)
        found[:, :4 * PAIR] = product[:, :4 * PAIR].astype(bf16)
        found[:, 4 * PAIR:] = jnp.concatenate(
            [product[:, 4 * PAIR:4 * PAIR + HD], gow[...].astype(f32)], axis=1
        ).astype(bf16)
        narrow = width // 4
        none = jnp.zeros((1, 3 * narrow), f32)
        inner_rows, outer_rows = inner[0], outer[0]
        first = jnp.concatenate([sums[0:1, :4 * PAIR + HD], inner_rows[2:3]], axis=1)
        second = jnp.concatenate([inner_rows[0:1], inner_rows[1:2], outer_rows[0:1], outer_rows[1:2]], axis=1)
        third = jnp.concatenate([outer_rows[2:3], none], axis=1)
        row = lax.broadcasted_iota(jnp.int32, (16, width), 0)
        rest = jnp.where(row == 1, second, jnp.where(row == 2, third, jnp.where(row == 3, gub[0], 0.0)))
        below = jnp.where(row == 0, first, rest).astype(bf16)
        for n, target in ((1, send), (0, keep)):
            for z in range(depth):
                i = 2 * z + lax.rem(core + n, 2)
                target[z * tall:(z + 1) * tall, :] = found[pl.ds(pl.multiple_of(i * tall, 16), tall), :]
            target[depth * tall:, :] = below


def attend_back_one(
    away, fsdp, depth, place, x_t, kept, grad_context, lse, delta, gow, inner, outer, gub, q_ext, k_ext
):
    d, t = x_t.shape
    tall, narrow, width = d // (2 * depth), d // fsdp, 4 * d // fsdp
    j = lambda place: neighbour_of(place, away, depth, fsdp)
    any_space = pl.BlockSpec(memory_space=pl.ANY)
    small = lambda *shape: pl.BlockSpec((1, *shape), lambda s, place, *_: (j(place), 0, 0))
    sent = (depth * tall + 16, width)
    rows = pl.BlockSpec((PLEN, USED), lambda s, *_: (s, 0))
    return call(
        functools.partial(attend_back_one_kernel, away, depth), "attend_back", (t // PLEN,),
        [any_space, rows, pl.BlockSpec((1, PLEN, narrow), lambda s, place, *_: (j(place), s, 0)),
         pl.BlockSpec((8, PLEN), lambda s, *_: (0, s)),
         pl.BlockSpec((1, 8, PLEN), lambda s, place, *_: (j(place), 0, s)), any_space,
         small(8, narrow), small(8, narrow), small(1, width), held(), held()],
        [whole(sent), whole(sent), rows],
        [sds(sent, bf16)] * 2 + [sds((t, USED), bf16)],
        [pltpu.VMEM((t, USED), bf16), pltpu.VMEM((d, width), bf16), pltpu.VMEM((8, USED), f32), pltpu.VMEM((d, t), bf16),
         pltpu.VMEM((d, narrow), bf16), pltpu.SemaphoreType.DMA((2,))],
        prefetch=1, cost=guess(10e9, 12e6), limit=SMALL, most=1 << 40,
    )(place, x_t, kept, grad_context, lse, delta, gow, inner, outer, gub, q_ext, k_ext)


def input_grad_kernel(place, inner, *refs):
    grads, weights, out = refs[:-2], refs[-2], refs[-1]
    fsdp, depth, _, tall, _ = weights.shape
    total = inner[...]
    for away, columns in enumerate(grads):
        held_weights = weights[neighbour_of(place, away, depth, fsdp)][:, :, :, :USED]
        total += dot_nt(columns[...], held_weights.reshape(2 * depth * tall, USED))
    out[...] = total


def make_input_grad(place, inner, grads, weights):
    t, d = inner.shape
    rows = pl.BlockSpec((ROWS, d), lambda r, *_: (r, 0))
    return [call(
        input_grad_kernel, "input_grad", (t // ROWS,),
        [rows] + [pl.BlockSpec((ROWS, USED), lambda r, *_: (r, 0))] * len(grads) + [whole(weights.shape)],
        rows, sds((t, d), f32), prefetch=1, cost=guess(5e9, 15e6), limit=SMALL,
    )(place, inner, *grads, weights)]


def attend_back_kernel(
    bucket, lengths, x_t, q, k, v, grad_context, lse, delta, qw, kw, vw, grad_inner,
    gqw, gkw, gvw, gqb, gvb, input_grad,
    queries_ext, keys_ext, grads,
):
    pair = pl.program_id(0)
    row_count = q.shape[0]

    @pl.when(pair == 0)
    def _():
        segment_lanes(bucket, lengths, queries_ext, keys_ext)

    low_half = lax.broadcasted_iota(jnp.int32, (PLEN, PAIR), 1) < HD

    def block(b, carry):
        rows = pl.ds(pl.multiple_of(b * PLEN, PLEN), PLEN)
        queries, keys, values, grad_ctx = q[rows, :], k[rows, :], v[rows, :], grad_context[rows, :]
        q_ext, k_ext = queries_ext[rows, :], keys_ext[rows, :]
        nothing = jnp.zeros_like(values)
        got = []
        for half in range(2):
            mine = low_half if half == 0 else ~low_half
            lse_row = lse[pl.ds(half * HD + pair, 1), rows]
            delta_row = delta[pl.ds(half * HD + pair, 1), rows]
            scores = dot_nt(jnp.where(mine, keys, k_ext), jnp.where(mine, queries, q_ext))
            probs = jnp.exp(scores - lse_row)
            grad_probs = dot_nt(jnp.where(mine, values, nothing), grad_ctx)
            grad_scores = (probs * (grad_probs - delta_row)).astype(bf16)
            grad_v = dot(probs.astype(bf16), grad_ctx)
            grad_k = dot(grad_scores, queries)
            grad_q = dot_tn(grad_scores, keys)
            got.append((grad_q, grad_k, grad_v))
        gq = (jnp.where(low_half, got[0][0], got[1][0]) * HD ** (-0.5)).astype(bf16)
        gk = jnp.where(low_half, got[0][1], got[1][1]).astype(bf16)
        gv = jnp.where(low_half, got[0][2], got[1][2]).astype(bf16)
        grads[rows, :PAIR] = gq
        grads[rows, PAIR:2 * PAIR] = gk
        grads[rows, 2 * PAIR:] = gv
        sum_q = jnp.sum(gq.astype(f32), axis=0, keepdims=True)
        sum_v = jnp.sum(gv.astype(f32), axis=0, keepdims=True)
        return (carry[0] + sum_q, carry[1] + sum_v)

    start = jnp.zeros((1, PAIR), f32)
    gqb[...], gvb[...] = lax.fori_loop(0, row_count // PLEN, block, (start, start))

    columns = grads[...]
    weight_grads = dot(x_t[...], columns)
    gqw[...] = weight_grads[:, :PAIR].astype(gqw.dtype)
    gkw[...] = weight_grads[:, PAIR:2 * PAIR].astype(gkw.dtype)
    gvw[...] = weight_grads[:, 2 * PAIR:].astype(gvw.dtype)

    @pl.when(pair == 0)
    def _():
        input_grad[...] = grad_inner[...]

    weights = jnp.concatenate([qw[0], kw[0], vw[0]], axis=1)
    input_grad[...] += dot_nt(columns, weights)


def attend_back(bucket, lengths, x_t, q, k, v, grad_context, lse, delta, weights, grad_inner):
    t, d = q.shape
    pairs = d // PAIR
    column = lambda m: pl.BlockSpec((1, d, PAIR), lambda p, *_: (m, 0, p))
    vector = pl.BlockSpec((1, PAIR), lambda p, *_: (0, p))
    tall = pl.BlockSpec((t, PAIR), lambda p, *_: (0, p))
    made = pl.BlockSpec((d, PAIR), lambda p, *_: (0, p))
    return call(
        attend_back_kernel, "attend_back", (pairs,),
        [whole((d, t)), tall, tall, tall, tall, whole((PAIR, t)), whole((PAIR, t)),
         column(0), column(1), column(2), whole((t, d))],
        [made, made, made, vector, vector, whole((t, d))],
        [sds((d, d), bf16)] * 3 + [sds((1, d), f32)] * 2 + [sds((t, d), f32)],
        [pltpu.VMEM((t, PAIR), bf16), pltpu.VMEM((t, PAIR), bf16), pltpu.VMEM((t, 3 * PAIR), bf16)],
        prefetch=2, cost=guess(30e9, 25e6),
    )(bucket, lengths, x_t, q, k, v, grad_context, lse, delta, weights, weights, weights, grad_inner)


def normed(v):
    centred = v - jnp.mean(v, axis=-1, keepdims=True)
    r = lax.rsqrt(jnp.mean(centred * centred, axis=-1, keepdims=True) + epsilon)
    return centred * r, r


def norm_back(dy, n, r, gain):
    dn = dy * gain
    return r * (dn - jnp.mean(dn, axis=-1, keepdims=True) - n * jnp.mean(dn * n, axis=-1, keepdims=True))


def gelu_parts(u):
    phi = 0.5 + 0.5 * lax.erf(u * 0.5 ** 0.5)
    bell = jnp.exp2(u * u * -0.7213475204444817)
    return u * phi, phi + u * (bell * 0.3989422804014327)


VECTORS = ((0, 2), (0, 3), (1, 0), (1, 1), (1, 2), (1, 3))


def attended_kernel(x, context, ow, slabs, n1_out, r1_out, low_out, low_t, ow_out, vectors):
    rows = pl.ds(pl.multiple_of(pl.program_id(0) * ROWS, ROWS), ROWS)
    parts, _, narrow = context.shape

    @pl.when(pl.program_id(0) == 0)
    def _():
        ow_out[...] = jnp.concatenate([ow[j][:, ow.shape[2] - narrow:] for j in range(parts)], axis=1)
        cuts, _, width = slabs.shape
        piece = width // 4
        held_slabs = [slabs[j].astype(f32) for j in range(cuts)]
        for n, (r, m) in enumerate(VECTORS):
            vectors[n:n + 1, :] = jnp.concatenate(
                [v[r:r + 1, m * piece:(m + 1) * piece] for v in held_slabs], axis=1
            )

    joined = jnp.concatenate([context[j] for j in range(parts)], axis=1)
    ob, g1, b1 = (vectors[n:n + 1, :] for n in range(3))
    attended = dot(joined, ow_out[...]) + ob
    n1, r1 = normed(x[...].astype(f32) + attended)
    n1_out[rows, :] = n1
    r1_out[rows, :] = jnp.broadcast_to(r1, (ROWS, r1_out.shape[1]))
    low = (n1 * g1 + b1).astype(bf16)
    low_out[rows, :] = low
    low_t[:, rows] = low.T


def attended(x, context, ow, last, slabs):
    t, d = x.shape
    parts, _, narrow = context.shape
    wide = ow.shape[2] // (last + 1)
    rows = pl.BlockSpec((ROWS, d), lambda r: (r, 0))
    return call(
        attended_kernel, "attended", (t // ROWS,),
        [rows, pl.BlockSpec((parts, ROWS, narrow), lambda r: (0, r, 0)),
         pl.BlockSpec((parts, d, wide), lambda r: (0, 0, last)), whole(slabs.shape)],
        [held()] * 5 + [whole((8, d))],
        [pltpu.VMEM((t, d), f32), pltpu.VMEM((t, 128), f32), pltpu.VMEM((t, d), bf16), pltpu.VMEM((d, t), bf16),
         pltpu.VMEM((d, d), bf16), sds((8, d), f32)],
        cost=guess(3e9, 10e6), limit=SMALL,
    )(x, context, ow, slabs)


def up_tiles(tile, uw, slabs, act_out, slope_out):
    count, depth, _, tall, columns = uw.shape
    for j in range(act_out.shape[0]):
        hidden = dot(tile, uw[j].reshape(2 * depth * tall, columns)) + slabs[j, 2:3, :].astype(f32)
        active, slope = gelu_parts(hidden)
        act_out[j] = active.astype(bf16)
        slope_out[j] = slope.astype(bf16)


def up_kernel(place, low, slabs, u0, u1, u2, u3, act_out, slope_out, uw, sems):
    rows = pl.ds(pl.multiple_of(pl.program_id(0) * ROWS, ROWS), ROWS)
    copies = block_copies(place, (u0, u1, u2, u3), lambda core, j: uw.at[j, :, core], sems)

    @pl.when(pl.program_id(0) == 0)
    def _():
        for copy in copies:
            copy.start()
        for copy in copies:
            copy.wait()

    up_tiles(low[rows, :], uw, slabs, act_out, slope_out)


def up(place, low, slabs, blocks):
    t, d = low.shape
    half, depth, tall, wide = blocks[0].shape
    f = 2 * half
    high = pl.BlockSpec((f, ROWS, wide), lambda r, *_: (0, r, 0))
    return call(
        up_kernel, "up", (t // ROWS,),
        [held(), whole((f, 16, wide))] + [pl.BlockSpec(memory_space=pl.ANY)] * 4,
        [high, high, whole((f, depth, 2, tall, wide))],
        [sds((f, t, wide), bf16), sds((f, t, wide), bf16), sds((f, depth, 2, tall, wide), bf16)],
        [pltpu.SemaphoreType.DMA((2 * f,))],
        prefetch=1, cost=guess(12e9, 30e6), limit=SMALL, free=pl.ANY,
    )(place, low, slabs, *blocks)


def down_kernel(
    place, bucket, lengths, act_rows, n1, given, cotangent, act_part, d0, d1, d2, d3,
    out, pooled, mixed_out, branch_out, vectors, send, keep, dw,
    branch_t, counts, sums, found, sems,
):
    step = pl.program_id(0)
    tiles = branch_t.shape[1] // ROWS
    f, _, height, width = send.shape
    each = d0.shape[2] // height
    tall, narrow = height * each, width // each
    depth = (place.shape[0] - 1 - 5 * f) // 2
    shared = f == depth

    def target(core, j):
        rows = pl.ds(pl.multiple_of(j * tall, 16), tall)
        if shared:
            return dw.at[:, rows, pl.ds(pl.multiple_of(core * narrow, narrow), narrow)]
        return dw.at[:, core, rows, :]

    copies = block_copies(place, (d0, d1, d2, d3), target, sems)

    @pl.when(step == 0)
    def _():
        for copy in copies:
            copy.start()
        pooled[...] = jnp.zeros_like(pooled)
        counts[...] = jnp.zeros_like(counts)
        sums[...] = jnp.zeros_like(sums)
        for copy in copies:
            copy.wait()

    @pl.when(step < tiles)
    def _():
        rows = pl.ds(pl.multiple_of(step * ROWS, ROWS), ROWS)
        if shared:
            parts = [dot_nt(act_rows[row_of(place, 0, s, depth) // 2], dw[s]) for s in range(f)]
        else:
            parts = [dot_nt(act_rows[i], dw[i // 2, i % 2]) for i in range(f)]
        branch = sum(parts[1:], parts[0])
        g1, b1, db, g2, b2 = (given[n:n + 1, :] for n in range(1, 6))
        residual = n1[rows, :] * g1 + b1 + (branch + db)
        n2, r2 = normed(residual)
        result = n2 * g2 + b2
        out[...] = result.astype(bf16)
        passage = bucket[0] == 1
        for part in range(ROWS // QLEN):
            start = step * ROWS + part * QLEN
            segment = jnp.where(passage, start // PLEN, start // QLEN)
            position = jnp.where(passage, lax.rem(start, PLEN), 0)
            alive = jnp.clip(lengths[segment] - position, 0, QLEN)
            row = lax.broadcasted_iota(jnp.int32, (QLEN, 1), 0)
            picked = jnp.where(row < alive, result[part * QLEN:(part + 1) * QLEN], 0.0)
            pooled[pl.ds(segment, 1), :] += jnp.sum(picked, axis=0, keepdims=True)
            counts[pl.ds(segment, 1), :] += jnp.full((1, 128), 1.0, f32) * alive.astype(f32)
        dy = cotangent[...].astype(f32)
        sums[1:2, :] += jnp.sum(dy * n2, axis=0, keepdims=True)
        sums[2:3, :] += jnp.sum(dy, axis=0, keepdims=True)
        mixed = norm_back(dy, n2, r2, g2)
        mixed_out[rows, :] = mixed
        low = mixed.astype(bf16)
        branch_out[rows, :] = low
        sums[0:1, :] += jnp.sum(low.astype(f32), axis=0, keepdims=True)
        branch_t[:, rows] = low.T

    @pl.when(step == tiles - 1)
    def _():
        pooled[...] = pooled[...] / jnp.maximum(counts[...], 1.0)[:, :1]
        for j in range(vectors.shape[0]):
            vectors[j] = sums[:, j * vectors.shape[2]:(j + 1) * vectors.shape[2]]

    if shared:
        @pl.when(step >= tiles)
        def _():
            core = core_of(place, depth, f)
            found[...] = dot(branch_t[...], act_part[0]).astype(bf16)
            for n, made in ((1, send), (0, keep)):
                lanes = pl.ds(pl.multiple_of(lax.rem(core + n, 2) * narrow, narrow), narrow)
                for j in range(f):
                    slot = slot_of(place, n, j, depth, f)
                    for r in range(each):
                        top = j * tall + r * height
                        made[slot, 0, :, r * narrow:(r + 1) * narrow] = found[top:top + height, lanes]
    else:
        def part(n, made):
            part_found = dot(branch_t[...], act_part[0]).astype(bf16)
            for j in range(f):
                made[slot_of(place, n, j, depth, f), 0] = part_found[j * tall:(j + 1) * tall]

        @pl.when((step >= tiles) & (step < tiles + depth))
        def _():
            part(1, send)

        @pl.when(step >= tiles + depth)
        def _():
            part(0, keep)


def down(cuts, place, bucket, lengths, active, n1, given, cotangent, blocks):
    f, t, wide = active.shape
    d = n1.shape[1]
    tiles = t // ROWS
    slots = lengths.shape[0]
    _, depth, tall, narrow = blocks[0].shape
    shared = f == depth
    parts = f
    weights = (f, d, wide) if shared else (depth, 2, d, narrow)
    each = wide // narrow
    early = lambda s: jnp.minimum(s, tiles - 1)
    if shared:
        late = lambda s, place: place[jnp.maximum(s - tiles, 0)] // 2
    else:
        late = lambda s, place: place[(jnp.maximum(s - tiles, 0) + depth) % parts]
    made = lambda first: pl.BlockSpec(
        (f, 1, tall // each, narrow * each), lambda s, *_: (0, jnp.clip(s - tiles - first, 0, depth - 1), 0, 0)
    )
    rows = pl.BlockSpec((ROWS, d), lambda s, *_: (early(s), 0))
    return call(
        down_kernel, "down", (tiles + parts,),
        [pl.BlockSpec((f, ROWS, wide), lambda s, *_: (0, early(s), 0)), held(), whole((8, d)), rows, pl.BlockSpec((1, t, wide), lambda s, place, *_: (late(s, place), 0, 0))]
        + [pl.BlockSpec(memory_space=pl.ANY)] * 4,
        [rows, whole((slots, d)), held(), held(), whole((cuts, 8, d // cuts)), made(0), made(0 if shared else depth),
         whole(weights)],
        [sds((t, d), bf16), sds((slots, d), f32), pltpu.VMEM((t, d), f32), pltpu.VMEM((t, d), bf16)]
        + [sds((cuts, 8, d // cuts), f32)] + [sds((f, depth, tall // each, narrow * each), bf16)] * 2
        + [sds(weights, bf16)],
        [pltpu.VMEM((d, t), bf16), pltpu.VMEM((slots, 128), f32), pltpu.VMEM((8, d), f32),
         pltpu.VMEM((d, wide), bf16), pltpu.SemaphoreType.DMA((2 * f,))],
        prefetch=3, cost=guess(12e9, 35e6), limit=SMALL, free=pl.ANY,
    )(place, bucket, lengths, active, n1, given, cotangent, active, *blocks)


def feed_back_kernel(
    place, branch, slope, dw, uw, low_t, mixed, *refs,
):
    send, keep, gub, grad_normed, hidden, found = refs[-6:]
    j = pl.program_id(0)
    _, depth, tall, _ = send.shape
    _, t, wide = slope.shape
    tiles = t // FEED_ROWS

    def gelu_rows(r, sums):
        rows = pl.ds(pl.multiple_of(r * FEED_ROWS, FEED_ROWS), FEED_ROWS)
        grad = (slope[0, rows, :].astype(f32) * dot(branch[rows, :], dw[0])).astype(bf16)
        hidden[rows, :] = grad
        return sums + jnp.sum(grad.astype(f32), axis=0, keepdims=True)

    gub[0] = lax.fori_loop(0, tiles, gelu_rows, jnp.zeros((1, wide), f32))
    found[...] = dot(low_t[...], hidden[...]).astype(bf16)
    for n, target in ((1, send), (0, keep)):
        for slot in range(depth):
            i = row_of(place, n, slot, depth)
            target[0, slot] = found[pl.ds(pl.multiple_of(i * tall, 16), tall), :]

    @pl.when(j == 0)
    def _():
        grad_normed[...] = mixed[...]

    def normed_rows(r, carry):
        rows = pl.ds(pl.multiple_of(r * FEED_ROWS, FEED_ROWS), FEED_ROWS)
        grad_normed[rows, :] += dot_nt(hidden[rows, :], uw[0])
        return carry

    lax.fori_loop(0, tiles, normed_rows, 0)


def feed_back(first, count, place, branch, slope, dw, uw, low_t, mixed, shared):
    t = slope.shape[1]
    f, d, wide = uw.shape
    dp, _, depth, _ = axis_facts()
    tall = d // dp
    made = lambda n: pl.BlockSpec(
        (1, depth, tall, wide), lambda j, place: (slot_of(place, n, first + j, depth, f), 0, 0, 0)
    )
    part = lambda *shape: pl.BlockSpec((1, *shape), lambda j, *_: (first + j, 0, 0))
    slot = lambda j, place: row_of(place, 0, first + j, depth) // 2 if f == depth else first + j
    any_space = pl.BlockSpec(memory_space=pl.ANY)
    return call(
        feed_back_kernel, "feed_back", (count,),
        [held(), part(t, wide), pl.BlockSpec((1, d, wide), lambda j, place: (slot(j, place), 0, 0)), part(d, wide),
         held(), held()] + [any_space] * len(shared),
        [made(1), made(0), part(1, wide), held()],
        [sds((f, depth, tall, wide), bf16)] * 2 + [pltpu.HBM((f, 1, wide), f32), pltpu.VMEM((t, d), f32)],
        [pltpu.VMEM((t, wide), bf16), pltpu.VMEM((d, wide), bf16)],
        prefetch=1, cost=guess(15e9, 35e6), limit=SMALL, least=0, aliases={7 + n: n for n in range(len(shared))},
    )(place, branch, slope, dw, uw, low_t, mixed, *shared)


def inner_kernel(
    head_of, grad_normed, n1, r1, given, context, ow,
    inner_out, vectors, gow, grad_context, delta_out,
    weight_grad, sums,
):
    step = pl.program_id(0)
    d = n1.shape[1]
    parts, _, narrow = context.shape

    @pl.when(step == 0)
    def _():
        weight_grad[...] = jnp.zeros_like(weight_grad)
        sums[...] = jnp.zeros_like(sums)

    shape = (delta_out.shape[0], d)
    head = head_of(lax.broadcasted_iota(jnp.int32, shape, 0))
    pick = jnp.where(lax.broadcasted_iota(jnp.int32, shape, 1) // HD == head, 1.0, 0.0).astype(bf16)
    rows = pl.ds(pl.multiple_of(step * ROWS, ROWS), ROWS)
    dy, n = grad_normed[rows, :], n1[rows, :]
    inner = norm_back(dy, n, r1[rows, :1], given[1:2, :])
    inner_out[...] = inner
    low = inner.astype(bf16)
    grad_ctx = dot_nt(low, ow[...]).astype(bf16)
    for j in range(parts):
        grad_context[j] = grad_ctx[:, j * narrow:(j + 1) * narrow]
    joined = jnp.concatenate([context[j] for j in range(parts)], axis=1)
    both = grad_ctx.astype(f32) * joined.astype(f32)
    high = both.astype(bf16)
    rest = (both - high.astype(f32)).astype(bf16)
    delta_out[...] = dot_nt(pick, high) + dot_nt(pick, rest)
    sums[0:1, :] += jnp.sum(dy * n, axis=0, keepdims=True)
    sums[1:2, :] += jnp.sum(dy, axis=0, keepdims=True)
    sums[2:3, :] += jnp.sum(low.astype(f32), axis=0, keepdims=True)
    weight_grad[...] += dot_tn(joined, low)

    @pl.when(step == pl.num_programs(0) - 1)
    def _():
        for j in range(parts):
            columns = slice(j * narrow, (j + 1) * narrow)
            gow[j] = weight_grad[:, columns].astype(bf16)
            vectors[j] = sums[:, columns]


def inner_back(count, head_of, grad_normed, n1, r1, given, context, ow):
    t, d = n1.shape
    parts, _, narrow = context.shape
    tile = pl.BlockSpec((parts, ROWS, narrow), lambda r: (0, r, 0))
    return call(
        functools.partial(inner_kernel, head_of), "inner_back", (t // ROWS,),
        [held(), held(), held(), whole((8, d)), tile, held()],
        [pl.BlockSpec((ROWS, d), lambda r: (r, 0)), whole((parts, 8, narrow)), whole((parts, d, narrow)), tile,
         pl.BlockSpec((count, ROWS), lambda r: (0, r))],
        [sds((t, d), f32), sds((parts, 8, narrow), f32), sds((parts, d, narrow), bf16), sds((parts, t, narrow), bf16),
         sds((count, t), f32)],
        [pltpu.VMEM((d, d), f32), pltpu.VMEM((8, d), f32)],
        cost=guess(4e9, 10e6), limit=SMALL,
    )(grad_normed, n1, r1, given, context, ow)


def shards(
    tokens, bucket, lengths, cotangent,
    query_weight, query_bias, key_weight, value_weight, value_bias, out_weight, out_bias,
    norm1_gain, norm1_bias, up_weight, up_bias, down_weight, down_bias, norm2_gain, norm2_bias,
):
    t, d = tokens.shape
    dp, fsdp = lax.axis_size("dp"), lax.axis_size("fsdp")
    lengths = lengths[0]

    place = places()
    depth = dp // 2
    tall, narrow = d // dp, d // fsdp
    width = 4 * narrow
    by_head = narrow == HEADS * HD and fsdp == 4
    down_t = down_weight.T

    if by_head:
        block, slab = make_block(
            query_weight, key_weight, value_weight, out_weight, query_bias, value_bias, out_bias, norm1_gain,
            norm1_bias, down_bias, norm2_gain, norm2_bias, up_bias,
        )
        along = Once([(block, "dp", along_z(s)) for s in range(1, depth)])
        x_t, = beside([along], lambda x: (x.T,), (tokens,))
        own = [block] + along.got
        own = line_up_rows(place, own, slab)
        swap = lambda v: (v, "dp", across_cores())
        in_plane = lambda v, s: (v, "fsdp", [(f, f ^ s) for f in range(fsdp)])
        paired = Once([swap(own)])
        beside([paired])
        pair_0 = paired.got[0]
        ups = Once([(up_weight, "dp", along_z(s)) for s in range(1, depth)])
        sides = Once([in_plane(own, 1), in_plane(own, 2)])
        one = lambda away: functools.partial(attend_one, away, fsdp)
        run = (bucket, lengths, tokens)
        *shared, kept_0, lse_0, q_ext, k_ext = beside(
            [sides, ups], one(0), (place, *run, own, pair_0, [], []), out=3
        )
        ext = [q_ext, k_ext]
        own_x, own_y = sides.got
        to_u = Gather(line_up(place, [up_weight] + ups.got))
        paired = Once([swap(own_x), swap(own_y)])
        corner = Once([(select_core(own_y, own_x), ("dp", "fsdp"), along_bit(0))])
        beside([paired])
        pair_x, pair_y = paired.got
        downs = Once([(down_t, "dp", along_z(s)) for s in range(1, depth)])
        *shared, kept_1, lse_1 = beside([corner, to_u, downs], one(1), (place, *run, own_x, pair_x, ext, shared), out=3)
        own_c = corner.got[0]
        to_d = Gather(jnp.stack([down_t] + downs.got))

        def last_two(place, own_c):
            pair_c = lax.ppermute(own_c, "dp", across_cores())
            *part, kept_2, lse_2 = one(2)(place, *run, own_y, pair_y, ext, shared)
            *part, kept_3, lse_3 = one(3)(place, *run, own_c, pair_c, ext, part)
            return [*part, kept_2, lse_2, kept_3, lse_3]

        *shared, kept_2, lse_2, kept_3, lse_3 = beside([to_u], last_two, (place, own_c), out=5)
        context, weights, slabs = shared
        ow, last = weights.reshape(fsdp, d, width), 2
        count, head_of = 8 * fsdp, lambda r: jnp.where(r % 8 < HEADS, r // 8 * HEADS + r % 8, -1)
    else:
        block = jnp.concatenate([
            jnp.concatenate([query_weight, key_weight, value_weight, out_weight], axis=1),
            jnp.concatenate([query_bias, value_bias, out_bias, norm1_gain])[None],
            jnp.concatenate([norm1_bias, down_bias, norm2_gain, norm2_bias])[None],
            up_bias[None],
            jnp.zeros((13, width), bf16),
        ])
        to_a, to_u, to_d = Gather(gather_z(block)), Gather(gather_z(up_weight)), Gather(gather_z(down_t))
        finish(to_a)
        weights, vectors, slabs = assemble(place, to_a.blocks)
        qb, vb = (vectors[m, 0:1] for m in range(2))
        q, k, v, context, lse = attend(bucket, lengths, tokens, weights, qb, vb)
        context, ow, last = context[None], weights[3:], 0
        count, head_of = PAIR, lambda r: 2 * (r % HD) + r // HD

    n1, r1, low, low_t, ow, given = beside(
        [to_u, to_d], attended, (tokens, context, ow, last, slabs), key=4, out=5
    )
    finish(to_u)
    active, slope, uw = beside([to_d], up, (place, low, slabs, to_u.blocks))
    finish(to_d)
    cuts = context.shape[0]
    out, pooled, mixed, branch, down_vectors, send_d, keep_d, dw = down(
        cuts, place, bucket, lengths, active, n1, given, cotangent, to_d.blocks
    )
    of_d = Scatter(keep_d, send_d)
    dw, uw = dw.reshape(fsdp, d, -1), uw.reshape(fsdp, d, -1)
    part = fsdp // 2
    *shared, so_far = beside(
        [of_d], functools.partial(feed_back, 0, part), (place, branch, slope, dw, uw, low_t, mixed, [])
    )
    send_u, keep_u, gub, grad_normed = beside(
        [of_d], functools.partial(feed_back, part, fsdp - part),
        (place, branch, slope, dw, uw, low_t, so_far, shared),
    )
    of_u = Scatter(keep_u, send_u)
    of_u.joined = by_head
    inner, inner_vectors, gow, grad_context, delta = beside(
        [of_d, of_u], functools.partial(inner_back, count, head_of), (grad_normed, n1, r1, given, context, ow),
        key=3, out=2
    )

    if by_head:
        delta = delta.reshape(fsdp, 8, t)

        def back(away, moves, kept, lse):
            args = (place, x_t, kept, grad_context, lse, delta, gow, inner_vectors, down_vectors, gub, q_ext, k_ext)
            return beside(moves, functools.partial(attend_back_one, away, fsdp, depth), args)

        send_3, keep_3, grads_3 = back(3, [of_u, of_d], kept_3, lse_3)
        swap_3 = Once([swap(send_3)])
        send_1, keep_1, grads_1 = back(1, [swap_3, of_u], kept_1, lse_1)
        corner = Once([(add(keep_3, swap_3.got[0]), ("dp", "fsdp"), along_bit(0))])
        both = [(u, "dp", along_z(-s - 1)) for s, u in enumerate(of_u.send)]
        near, rest = Once(both[::2]), Once(both[1::2])
        swap_1 = Once([swap(send_1)])
        send_2, keep_2, grads_2 = back(2, [corner, near, swap_1], kept_2, lse_2)
        swap_2 = Once([swap(send_2)])
        beside([swap_2])
        add_both = lambda *v: sum(u.astype(f32) for u in v)
        through = corner.got[0]
        sum_1 = add_both(keep_1, swap_1.got[0]) + select_core(jnp.zeros_like(through), through).astype(f32)
        sum_2 = add_both(keep_2, swap_2.got[0]) + select_core(through, jnp.zeros_like(through)).astype(f32)
        sides = Once([in_plane(sum_1.astype(bf16), 1), in_plane(sum_2.astype(bf16), 2)])
        send_0, keep_0, grads_0 = back(0, [sides, rest], kept_0, lse_0)
        sums = Once([swap(send_0)])
        beside([sums, of_u])
        mine, *away = make_total(place, [keep_0, sums.got[0], *sides.got])
        along = Once([(v, "dp", along_z(-s - 1)) for s, v in enumerate(away)])
        input_grad, = beside(
            [along, of_u], make_input_grad, (place, inner, (grads_0, grads_1, grads_2, grads_3), weights)
        )
        *made, gqb, gvb, gob, gg1, gb1, gdb, gg2, gb2, gub = unblock(mine, along.got)
        vectors = (gqb, gvb, gob, gg1, gb1, gdb, gg2, gb2)
        got, input_grad = lax.optimization_barrier((near.got + rest.got, input_grad))
        sum_u, sum_d = add_both(of_u.keep, *got), of_d.total
    else:
        gg1, gb1, gob = (inner_vectors[0, n:n + 1] for n in range(3))
        gdb, gg2, gb2 = (down_vectors[0, n:n + 1] for n in range(3))
        gqw, gkw, gvw, gqb, gvb, input_grad = attend_back(
            bucket, lengths, tokens.T, q, k, v, grad_context[0], lse, delta, weights, inner
        )
        firsts = jnp.stack([gqb, gvb, gob, gg1])
        seconds = jnp.stack([gb1, gdb, gg2, gb2])
        vectors = jnp.concatenate([firsts, seconds, jnp.zeros((4, 14, d), f32)], axis=1)
        of_a = Scatter(*reversed(pack(place, (gqw, gkw, gvw, gow[0]), vectors, gub)))
        while not (of_a.done() and of_u.done() and of_d.done()):
            beside([of_a, of_u, of_d])
        made_a = of_a.total
        made = [made_a[:tall, m * narrow:(m + 1) * narrow] for m in range(4)]
        vectors = [made_a[tall + n, m * narrow:(m + 1) * narrow] for n in range(2) for m in range(4)]
        gub = made_a[tall + 2]
    if not by_head:
        sum_u, sum_d = of_u.total, of_d.total
    columns = down_weight.shape[0]
    made_u = sum_u
    made_d = jnp.concatenate([sum_d[:, c:c + columns] for c in range(0, width, columns)])
    return (
        out, pooled, input_grad, made[0], vectors[0], made[1], made[2], vectors[1], made[3], vectors[2], vectors[3],
        vectors[4], made_u, gub, made_d.T, vectors[5], vectors[6], vectors[7],
    )


def solution(mesh):
    tall, square, vector = P(("dp", "fsdp"), None), P("dp", "fsdp"), P("fsdp")
    in_specs = (
        tall, P(("dp", "fsdp")), tall, tall, square, vector, square, square, vector, square, vector,
        vector, vector, square, vector, square, vector, vector, vector,
    )
    out_specs = (
        tall, tall, tall, square, vector, square, square, vector, square, vector, vector, vector,
        square, vector, square, vector, vector, vector,
    )
    return jax.shard_map(shards, mesh=mesh, in_specs=in_specs, out_specs=out_specs, check_vma=False)
```

```python
import functools

import jax
import jax.numpy as jnp
from jax import lax
from jax.experimental import pallas as pl
from jax.experimental.pallas import tpu as pltpu
from jax.sharding import PartitionSpec as P

H = 12
HD = 64
PLEN = 512
QLEN = 128
PAIR = 2 * HD
ROWS = 256
FEED_ROWS = 512

epsilon = 1e-06
masked_score = -1e30
f32 = jnp.float32
bf16 = jnp.bfloat16
LIMIT = 60 * 1024 * 1024
SMALL = 24 * 1024 * 1024


def dot(left, right):
    return jnp.dot(left, right, preferred_element_type=f32)


def dot_nt(left, right):
    return lax.dot_general(left, right, (((1,), (1,)), ((), ())), preferred_element_type=f32)


def dot_tn(left, right):
    return lax.dot_general(left, right, (((0,), (0,)), ((), ())), preferred_element_type=f32)


BIG = 16 * 1024


def far(v, least):
    if v.size * v.dtype.itemsize < least:
        return v
    return pltpu.with_memory_space_constraint(v, pltpu.HBM)


def call(
    kernel, name, grid, in_specs, out_specs, out_shape, scratch=(), prefetch=0, cost=None, limit=LIMIT, aliases={},
    least=BIG, free=pltpu.VMEM, most=BIG,
):
    several = isinstance(out_shape, list)
    shapes = [
        pltpu.HBM(v.shape, v.dtype)
        if isinstance(v, jax.ShapeDtypeStruct) and v.size * v.dtype.itemsize >= most else v
        for v in (out_shape if several else [out_shape])
    ]
    run = pl.pallas_call(
        kernel,
        name=name,
        grid_spec=pltpu.PrefetchScalarGridSpec(
            num_scalar_prefetch=prefetch,
            grid=grid,
            in_specs=in_specs,
            out_specs=out_specs,
            scratch_shapes=list(scratch),
        ),
        out_shape=shapes if several else shapes[0],
        input_output_aliases=aliases,
        compiler_params=pltpu.CompilerParams(
            vmem_limit_bytes=limit, dimension_semantics=("arbitrary",) * len(grid)
        ),
        cost_estimate=cost,
    )

    def run_far(*args):
        given = [
            v if spec.memory_space in (pltpu.VMEM, free) else far(v, least) for v, spec in zip(args[prefetch:], in_specs)
        ]
        return run(*args[:prefetch], *given)

    return run_far


def whole(shape):
    return pl.BlockSpec(shape, lambda *_: (0,) * len(shape))


def sds(shape, dtype):
    return jax.ShapeDtypeStruct(shape, dtype)


def held():
    return pl.BlockSpec(memory_space=pltpu.VMEM)


def guess(flops, nbytes):
    return pl.CostEstimate(flops=int(flops), bytes_accessed=int(nbytes), transcendentals=0)


def reverse(s, bits):
    return sum(((s >> b) & 1) << (bits - 1 - b) for b in range(bits))


def axis_facts():
    dp, fsdp = lax.axis_size("dp"), lax.axis_size("fsdp")
    return dp, fsdp, dp // 2, fsdp.bit_length() - 1


def along_z(hop):
    dp = lax.axis_size("dp")
    return [(d, (d + 2 * hop) % dp) for d in range(dp)]


def across_cores():
    return [(d, d ^ 1) for d in range(lax.axis_size("dp"))]


def along_bit(r):
    dp, fsdp, _, bits = axis_facts()
    pairs = []
    for d in range(dp):
        flip = 1 << (r if d % 2 == 0 else bits - 1 - r)
        pairs += [(d * fsdp + f, d * fsdp + (f ^ flip)) for f in range(fsdp)]
    return pairs


def select_core(even, odd):
    return jnp.where(lax.axis_index("dp") % 2 == 0, even, odd)


def gather_z(block):
    dp = lax.axis_size("dp")
    groups = [list(range(core, dp, 2)) for core in range(2)]
    return lax.all_gather(block, "dp", axis=0, axis_index_groups=groups)


class Gather:
    def __init__(self, along):
        self.held, self.round, self.blocks = along[None], 0, None

    def stage(self):
        bits = axis_facts()[3]
        if self.round < bits - 1:
            return [(self.held, ("dp", "fsdp"), along_bit(self.round))]
        if self.round < bits:
            return [(self.held, ("dp", "fsdp"), along_bit(self.round)), (self.held, "dp", across_cores())]
        return [(self.own[1], "dp", across_cores())]

    def take(self, got):
        bits = axis_facts()[3]
        if self.round < bits - 1:
            self.held = jnp.concatenate([self.held] + got)
        elif self.round < bits:
            self.own, self.other = [self.held, got[0]], got[1]
        else:
            self.blocks = self.own + [self.other] + got
        self.round += 1

    def done(self):
        return self.blocks is not None


class Once:
    def __init__(self, sends):
        self.sends, self.got = sends, None

    def stage(self):
        return self.sends

    def take(self, got):
        self.got = got

    def done(self):
        return self.got is not None


def add(left, right):
    return (left.astype(f32) + right.astype(f32)).astype(bf16)


class Scatter:
    def __init__(self, keep, send):
        self.keep, self.send, self.round, self.total = keep, [send], axis_facts()[3], None
        self.joined = False

    def stage(self):
        _, _, depth, bits = axis_facts()
        if self.round == bits:
            return [(self.send[0], "dp", across_cores())]
        if self.round >= 0:
            return [(self.send[0], ("dp", "fsdp"), along_bit(self.round))]
        return [(self.send[s - 1], "dp", along_z(-s)) for s in range(1, depth)]

    def take(self, got):
        depth = axis_facts()[2]
        keep = self.keep
        if self.round > 0:
            half = keep.shape[0] // 2
            self.send = [add(keep[half:], got[0][half:])]
            self.keep = add(keep[:half], got[0][:half])
        elif self.round == 0:
            self.send = [add(keep[0, s], got[0][0, s]) for s in range(1, depth)]
            self.keep = keep[0, 0].astype(f32) + got[0][0, 0].astype(f32)
        else:
            for part in got:
                keep = keep + part.astype(f32)
            self.total = keep
        self.round -= 1

    def done(self):
        return self.total is not None or (self.joined and self.round < 0)


def beside(moves, compute=None, args=(), key=0, out=0):
    moves = [move for move in moves if not move.done()]
    stages = [move.stage() for move in moves]
    arrays = [[v for v, _, _ in stage] for stage in stages]
    args = list(args)
    results = ()
    if compute:
        args[key], arrays = lax.optimization_barrier((args[key], arrays))
        results = list(compute(*args))
    else:
        arrays = lax.optimization_barrier(arrays)
    got = [
        [lax.ppermute(v, axis, perm) for v, (_, axis, perm) in zip(sent, stage)]
        for sent, stage in zip(arrays, stages)
    ]
    if compute:
        results[out], got = lax.optimization_barrier((results[out], got))
    else:
        got = lax.optimization_barrier(got)
    for move, parts in zip(moves, got):
        move.take(parts)
    return results


def finish(move):
    while not move.done():
        beside([move])


def places():
    dp, fsdp, depth, bits = axis_facts()
    d, f = lax.axis_index("dp"), lax.axis_index("fsdp")
    z, core = d // 2, d % 2
    slot = jnp.arange(depth, dtype=jnp.int32)
    index = jnp.arange(fsdp, dtype=jnp.int32)
    mirror = sum((((index >> b) & 1) << (bits - 1 - b) for b in range(bits)), jnp.zeros_like(index))
    rows, slots, columns = [], [], []
    for n in range(2):
        there = core ^ n
        rows.append(2 * ((z - slot) % depth) + there)
        away = index ^ f
        mirrored = sum((((away >> b) & 1) << (bits - 1 - b) for b in range(bits)), jnp.zeros_like(index))
        slots.append(jnp.where(there == 0, away, mirrored))
        columns.append(f ^ jnp.where(there == 0, index, mirror))
    neighbours = [(f ^ s)[None] for s in range(fsdp)]
    return jnp.concatenate(rows + slots + columns + [core[None]] + neighbours).astype(jnp.int32)


def row_of(place, n, slot, depth):
    return place[n * depth + slot]


def slot_of(place, n, j, depth, fsdp):
    return place[2 * depth + n * fsdp + j]


def column_of(place, n, s, depth, fsdp):
    return place[2 * depth + 2 * fsdp + n * fsdp + s]


def core_of(place, depth, fsdp):
    return place[2 * depth + 4 * fsdp]


def neighbour_of(place, s, depth, fsdp):
    return place[2 * depth + 4 * fsdp + 1 + s]


def block_copies(place, arrays, target, sems):
    half, depth = arrays[0].shape[:2]
    fsdp = 2 * half
    copies = []
    for a, array in enumerate(arrays):
        core = lax.rem(core_of(place, depth, fsdp) + a // 2, 2)
        for q in range(half):
            j = column_of(place, a // 2, (a % 2) * half + q, depth, fsdp)
            copies.append(pltpu.make_async_copy(array.at[q], target(core, j), sems.at[len(copies)]))
    return copies


def assemble_kernel(place, own_low, own_high, other_low, other_high, weights, vectors, ub):
    step = pl.program_id(0)
    half, _, height, width = own_low.shape
    fsdp, depth, tall = 2 * half, pl.num_programs(0) // 2, height - 16
    narrow = width // 4

    def fill(n, low, high):
        pieces = []
        for j in range(fsdp):
            slot = slot_of(place, n, j, depth, fsdp)
            upper, q = slot >= half, lax.rem(slot, half)
            pieces.append(jnp.where(upper, high[q, 0].astype(f32), low[q, 0].astype(f32)))
        for m in range(4):
            row = jnp.concatenate([p[:, m * narrow:(m + 1) * narrow] for p in pieces], axis=1)
            weights[m] = row[:tall].astype(bf16)
            vectors[m] = row[tall:]
        for j in range(fsdp):
            ub[j] = pieces[j][tall:]

    @pl.when(step < depth)
    def _():
        fill(0, own_low, own_high)

    @pl.when(step >= depth)
    def _():
        fill(1, other_low, other_high)


def row_at(place, s, depth, fsdp):
    core = core_of(place, depth, fsdp)
    return 2 * lax.rem(s, depth) + lax.rem(core + s // depth, 2)


def assemble(place, arrays):
    half, depth, height, width = arrays[0].shape
    fsdp, tall, d = 2 * half, height - 16, half * width // 2
    own = pl.BlockSpec((half, 1, height, width), lambda s, place: (0, jnp.minimum(s, depth - 1), 0, 0))
    other = pl.BlockSpec((half, 1, height, width), lambda s, place: (0, jnp.maximum(s - depth, 0), 0, 0))
    return call(
        assemble_kernel, "assemble", (2 * depth,),
        [own, own, other, other],
        [pl.BlockSpec((4, tall, d), lambda s, place: (0, row_at(place, s, depth, fsdp), 0)), whole((4, 16, d)),
         whole((fsdp, 16, width))],
        [sds((4, 2 * depth * tall, d), bf16), sds((4, 16, d), f32), sds((fsdp, 16, width), f32)],
        prefetch=1, cost=guess(1e9, 11e6),
    )(place, *arrays)


def pack_kernel(place, gq, gk, gv, go, vectors, gub, send, keep):
    step = pl.program_id(0)
    fsdp, _, height, width = send.shape
    depth, tall, narrow = pl.num_programs(0) // 2, height - 16, width // 4

    def fill(n, out):
        for j in range(fsdp):
            slot = slot_of(place, n, j, depth, fsdp)
            columns = slice(j * narrow, (j + 1) * narrow)
            out[slot, 0, :tall, :] = jnp.concatenate(
                [g[:, columns].astype(f32) for g in (gq, gk, gv, go)], axis=1
            ).astype(bf16)
            slab = jnp.concatenate([vectors[m, :, columns] for m in range(4)], axis=1)
            third = lax.broadcasted_iota(jnp.int32, slab.shape, 0) == 2
            out[slot, 0, tall:, :] = jnp.where(third, gub[j], slab).astype(bf16)

    @pl.when(step < depth)
    def _():
        fill(1, send)

    @pl.when(step >= depth)
    def _():
        fill(0, keep)


def pack(place, grads, vectors, gub):
    d = grads[0].shape[0]
    dp, fsdp, depth, _ = axis_facts()
    tall, width = d // dp, 4 * d // fsdp
    rows = pl.BlockSpec((tall, d), lambda s, place: (place[(s + depth) % (2 * depth)], 0))
    sent = pl.BlockSpec((fsdp, 1, tall + 16, width), lambda s, place: (0, jnp.minimum(s, depth - 1), 0, 0))
    kept = pl.BlockSpec((fsdp, 1, tall + 16, width), lambda s, place: (0, jnp.maximum(s - depth, 0), 0, 0))
    return call(
        pack_kernel, "pack", (2 * depth,),
        [rows, rows, rows, rows, whole((4, 16, d)), whole((fsdp, 1, width))],
        [sent, kept],
        [sds((fsdp, depth, tall + 16, width), bf16)] * 2,
        prefetch=1, cost=guess(1e9, 11e6),
    )(place, *grads, vectors, gub)


def segment_lanes(bucket, lengths, queries_ext, keys_ext):
    row_count = queries_ext.shape[0]
    slots = lengths.shape[0]
    shape = (row_count, PAIR)
    row = lax.broadcasted_iota(jnp.int32, shape, 0)
    lane = lax.broadcasted_iota(jnp.int32, shape, 1) % HD
    passage = bucket[0] == 1
    segment = jnp.where(passage, row // PLEN, row // QLEN)
    position = jnp.where(passage, row % PLEN, row % QLEN)
    limit = jnp.zeros(shape, jnp.int32)
    for s in range(slots):
        limit = jnp.where(segment == s, lengths[s], limit)
    alive = position < limit
    same = segment == lane
    queries_ext[...] = jnp.where(same, 1.0, 0.0).astype(bf16)
    keys_ext[...] = jnp.where((lane < slots) & ~(same & alive), masked_score, 0.0).astype(bf16)


def attend_kernel(
    bucket, lengths, x, qw, kw, vw, qb, vb,
    q_out, k_out, v_out, context_out, lse_out,
    queries_ext, keys_ext, lse_all,
):
    pair = pl.program_id(0)
    row_count = x.shape[0]

    @pl.when(pair == 0)
    def _():
        segment_lanes(bucket, lengths, queries_ext, keys_ext)
        lse_all[...] = jnp.zeros_like(lse_all)

    weights = jnp.concatenate([qw[0], kw[0], vw[0]], axis=1)
    qb_row = qb[...]
    vb_row = vb[...]
    low_half = lax.broadcasted_iota(jnp.int32, (PLEN, PAIR), 1) < HD
    lane = lax.broadcasted_iota(jnp.int32, (PLEN, PAIR), 1)

    def block(b, carry):
        rows = pl.ds(pl.multiple_of(b * PLEN, PLEN), PLEN)
        qkv = dot(x[rows, :], weights)
        queries = ((qkv[:, :PAIR] + qb_row).astype(bf16).astype(f32) * HD ** (-0.5)).astype(bf16)
        keys = qkv[:, PAIR:2 * PAIR].astype(bf16)
        values = (qkv[:, 2 * PAIR:] + vb_row).astype(bf16)
        q_out[rows, :] = queries
        k_out[rows, :] = keys
        v_out[rows, :] = values
        q_ext = queries_ext[rows, :]
        k_ext = keys_ext[rows, :]
        ones = jnp.ones_like(values)
        sums, tops = [], []
        for half in range(2):
            mine = low_half if half == 0 else ~low_half
            scores = dot_nt(jnp.where(mine, queries, q_ext), jnp.where(mine, keys, k_ext))
            top = jnp.max(scores, axis=-1, keepdims=True)
            weight = jnp.exp(scores - top).astype(bf16)
            sums.append(dot(weight, jnp.where(mine, values, ones)))
            tops.append(top)
        numer = jnp.where(low_half, sums[0], sums[1])
        denom = pltpu.roll(jnp.where(low_half, sums[1], sums[0]), HD, 1)
        context_out[rows, :] = (numer / denom).astype(bf16)
        lse = jnp.where(low_half, tops[0], tops[1]) + jnp.log(denom)
        mine = (lane % HD) == pair
        lse_all[rows, :] = jnp.where(mine, lse, lse_all[rows, :])
        return carry

    lax.fori_loop(0, row_count // PLEN, block, 0)

    @pl.when(pair == pl.num_programs(0) - 1)
    def _():
        lse_out[...] = lse_all[...].T


def attend(bucket, lengths, x, weights, qb, vb):
    t, d = x.shape
    pairs = d // PAIR
    column = lambda m: pl.BlockSpec((1, d, PAIR), lambda p, *_: (m, 0, p))
    vector = pl.BlockSpec((1, PAIR), lambda p, *_: (0, p))
    tall = pl.BlockSpec((t, PAIR), lambda p, *_: (0, p))
    return call(
        attend_kernel, "attend", (pairs,),
        [whole((t, d)), column(0), column(1), column(2), vector, vector],
        [tall, tall, tall, tall, whole((PAIR, t))],
        [sds((t, d), bf16)] * 4 + [sds((PAIR, t), f32)],
        [pltpu.VMEM((t, PAIR), bf16), pltpu.VMEM((t, PAIR), bf16), pltpu.VMEM((t, PAIR), f32)],
        prefetch=2, cost=guess(15e9, 12e6),
    )(bucket, lengths, x, weights, weights, weights, qb, vb)


HEADS = 3
USED = 5 * PAIR


def block_kernel(q, k, v, o, *refs):
    *vectors, ub, out, slab = refs
    out[...] = jnp.concatenate(
        [part.astype(f32) for part in (
            q[:, :PAIR], k[:, :PAIR], v[:, :PAIR], q[:, PAIR:], k[:, PAIR:], v[:, PAIR:], o[...]
        )], axis=1
    ).astype(bf16)
    each = [v[...].astype(f32)[None, :] for v in vectors]
    first, second = jnp.concatenate(each[:4], axis=1), jnp.concatenate(each[4:], axis=1)
    third = ub[...].astype(f32)[None, :]
    row = lax.broadcasted_iota(jnp.int32, (16, out.shape[1]), 0)
    slab[...] = jnp.where(
        row == 0, first, jnp.where(row == 1, second, jnp.where(row == 2, third, 0.0))
    ).astype(bf16)


def make_block(q, k, v, o, *vectors):
    tall, narrow = q.shape
    shapes = [(tall, 4 * narrow), (16, 4 * narrow)]
    return call(
        block_kernel, "block", (1,), [whole(q.shape)] * 4 + [whole(u.shape) for u in vectors],
        [whole(v) for v in shapes], [sds(v, bf16) for v in shapes], cost=guess(1e6, 1e6), limit=SMALL, least=0, most=1 << 40,
    )(q, k, v, o, *vectors)


def total_kernel(place, *refs):
    parts, first, others = refs[:4], refs[4], refs[5:]
    depth = 1 + len(others)
    tall = (parts[0].shape[0] - 16) // depth

    def summed(rows):
        return sum((part[rows, :].astype(f32) for part in parts[1:]), parts[0][rows, :].astype(f32))

    below = summed(pl.ds(depth * tall, 16))
    for s in range(depth):
        z = row_of(place, 0, s, depth) // 2
        total = jnp.concatenate([summed(pl.ds(pl.multiple_of(z * tall, 16), tall)), below])
        if s:
            others[s - 1][...] = total.astype(bf16)
        else:
            first[...] = total


def make_total(place, parts):
    depth = axis_facts()[2]
    height, width = parts[0].shape
    out = ((height - 16) // depth + 16, width)
    return call(
        total_kernel, "total", (1,), [held()] * 4, [whole(out)] * depth,
        [sds(out, f32)] + [sds(out, bf16)] * (depth - 1), prefetch=1, cost=guess(1e6, 4e6), limit=SMALL, most=1 << 40,
    )(place, *parts)


def unblock_kernel(total, *refs):
    got, (gq, gk, gv, go, *vectors) = refs[:-13], refs[-13:]
    tall, narrow = gq.shape
    block = total[...]
    for part in got:
        block = block + part[...].astype(f32)

    def split(v):
        return (
            jnp.concatenate([v[:, :PAIR], v[:, 3 * PAIR:3 * PAIR + HD]], axis=1),
            jnp.concatenate([v[:, PAIR:2 * PAIR], v[:, 3 * PAIR + HD:4 * PAIR]], axis=1),
            jnp.concatenate([v[:, 2 * PAIR:3 * PAIR], v[:, 4 * PAIR:4 * PAIR + HD]], axis=1),
            v[:, 4 * PAIR + HD:],
        )

    gq[...], gk[...], gv[...], go[...] = split(block[:tall])
    qb, _, vb, ob = split(block[tall:tall + 1])
    rest = [block[tall + r:tall + r + 1, m * narrow:(m + 1) * narrow] for r, m in ((1, 0), (1, 1), (1, 2), (1, 3), (2, 0))]
    for ref, row in zip(vectors, (qb, vb, ob, *rest, block[tall + 3:tall + 4])):
        ref[...] = row[0]


def unblock(total, got):
    height, width = total.shape
    tall, narrow = height - 16, width // 4
    shapes = [(tall, narrow)] * 4 + [(narrow,)] * 8 + [(width,)]
    return call(
        unblock_kernel, "unblock", (1,), [held()] * (1 + len(got)), [whole(v) for v in shapes],
        [sds(v, f32) for v in shapes], cost=guess(1e6, 1e6), limit=SMALL,
    )(total, *got)


def line_up_kernel(place, *refs):
    out = refs[-1]
    depth = len(refs) - 1
    for s in range(depth):
        out[row_of(place, 0, s, depth) // 2] = refs[s][...]


def line_up(place, parts):
    shape = parts[0].shape
    out = (len(parts), *shape)
    return call(
        line_up_kernel, "line_up", (1,), [held()] * len(parts), whole(out), sds(out, parts[0].dtype),
        prefetch=1, cost=guess(1e6, 1e6), limit=SMALL, most=1 << 40,
    )(place, *parts)


def line_up_rows_kernel(place, *refs):
    *parts, slab, out = refs
    depth, tall = len(parts), parts[0].shape[0]
    for s in range(depth):
        z = row_of(place, 0, s, depth) // 2
        out[pl.ds(pl.multiple_of(z * tall, 16), tall), :] = parts[s][...]
    out[depth * tall:, :] = slab[...]


def line_up_rows(place, parts, slab):
    tall, width = parts[0].shape
    out = (len(parts) * tall + 16, width)
    return call(
        line_up_rows_kernel, "line_up_rows", (1,), [held()] * (len(parts) + 1),
        whole(out), sds(out, bf16), prefetch=1, cost=guess(1e6, 1e6), limit=SMALL, most=1 << 40,
    )(place, *parts, slab)


def attend_one_kernel(
    away, place, bucket, lengths, x, own, other, *refs,
):
    *given, context_out, w_out, slab_out, kept, lse_out, queries_ext, keys_ext, weights_here, sems = refs
    if away:
        queries_ext, keys_ext = given[:2]
    depth, _, tall, width = weights_here.shape
    step, fsdp = pl.program_id(0), w_out_fsdp(place, depth)
    core = core_of(place, depth, fsdp)
    j = neighbour_of(place, away, depth, fsdp)
    copies = [
        pltpu.make_async_copy(
            ref.at[pl.ds(0, depth * tall), :].reshape(depth, tall, width), weights_here.at[:, lax.rem(core + n, 2)],
            sems.at[n],
        )
        for n, ref in enumerate((own, other))
    ]
    copies.append(pltpu.make_async_copy(own.at[pl.ds(depth * tall, 16), :], slab_out.at[0], sems.at[2]))
    onward = pltpu.make_async_copy(weights_here, w_out.at[j], sems.at[3])

    @pl.when(step == 0)
    def _():
        for copy in copies:
            copy.start()
        if not away:
            segment_lanes(bucket, lengths, queries_ext, keys_ext)
        for copy in copies:
            copy.wait()
        onward.start()

    narrow = width // 4
    row = slab_out[0, 0:1, :].astype(f32)
    qb, vb = row[:, :narrow], row[:, narrow:2 * narrow]
    none = jnp.zeros((1, PAIR), f32)
    bias = jnp.concatenate(
        [qb[:, :PAIR], none, vb[:, :PAIR], qb[:, PAIR:], none[:, :HD], vb[:, PAIR:], none[:, :HD]], axis=1
    )
    lane = lax.broadcasted_iota(jnp.int32, (PLEN, PAIR), 1)
    low_half = lane < HD
    scale = HD ** (-0.5)

    rows = pl.ds(pl.multiple_of(step * PLEN, PLEN), PLEN)
    weights = weights_here[:, :, :, :USED].reshape(2 * depth * tall, USED)
    qkv = dot(x[rows, :], weights) + bias
    tiles = [qkv[:, n * PAIR:(n + 1) * PAIR].astype(bf16) for n in range(5)]
    tiles[0] = tiles[0] * jnp.array(scale, bf16)
    tiles[3] = jnp.where(low_half, tiles[3] * jnp.array(scale, bf16), tiles[3])
    for n in range(5):
        kept[:, n * PAIR:(n + 1) * PAIR] = tiles[n]
    queries, keys, values, both, values_two = tiles
    keys_two = pltpu.roll(both.astype(f32), HD, 1).astype(bf16)
    q_ext, k_ext = queries_ext[rows, :], keys_ext[rows, :]
    ones = jnp.ones_like(values)

    def one(mine, q, k, v):
        scores = dot_nt(jnp.where(mine, q, q_ext), jnp.where(mine, k, k_ext))
        top = jnp.max(scores, axis=-1, keepdims=True)
        weight = jnp.exp(scores - top).astype(bf16)
        return top, dot(weight, jnp.where(mine, v, ones))

    top_a, sum_a = one(low_half, queries, keys, values)
    top_b, sum_b = one(~low_half, queries, keys, values)
    top_c, sum_c = one(low_half, both, keys_two, values_two)
    denom = pltpu.roll(jnp.where(low_half, sum_b, sum_a), HD, 1)
    denom_c = pltpu.roll(sum_c, HD, 1)
    context_out[0, :, :PAIR] = (jnp.where(low_half, sum_a, sum_b) / denom).astype(bf16)
    context_out[0, :, PAIR:] = (sum_c / denom_c)[:, :HD].astype(bf16)
    lse_ab = jnp.where(low_half, top_a, top_b) + jnp.log(denom)
    lse_c = top_c + jnp.log(denom_c)
    every = jnp.where((lane >= 32) & low_half, lse_c, lse_ab).T
    lse_out[0:1, :] = every[0:1]
    lse_out[1:2, :] = every[HD:HD + 1]
    lse_out[2:3, :] = every[32:33]

    @pl.when(step == pl.num_programs(0) - 1)
    def _():
        onward.wait()


def w_out_fsdp(place, depth):
    return (place.shape[0] - 2 * depth - 1) // 5


def attend_one(away, fsdp, place, bucket, lengths, x, own, other, ext, shared):
    t, d = x.shape
    depth = axis_facts()[2]
    height, width = own.shape
    tall, narrow = (height - 16) // depth, d // fsdp
    shapes = [(fsdp, t, narrow), (fsdp, depth, 2, tall, width), (fsdp, 16, width)]
    j = lambda place: neighbour_of(place, away, depth, fsdp)
    any_space = pl.BlockSpec(memory_space=pl.ANY)
    return call(
        functools.partial(attend_one_kernel, away), "attend", (t // PLEN,),
        [held(), any_space, any_space] + [held()] * len(ext)
        + [any_space] * len(shared),
        [
            pl.BlockSpec((1, PLEN, narrow), lambda s, place, *_: (j(place), s, 0)), any_space,
            pl.BlockSpec((1, 16, width), lambda s, place, *_: (j(place), 0, 0)),
            pl.BlockSpec((PLEN, USED), lambda s, *_: (s, 0)), pl.BlockSpec((8, PLEN), lambda s, *_: (0, s)),
        ] + ([] if away else [held()] * 2),
        [sds(shape, bf16) for shape in shapes] + [sds((t, USED), bf16), sds((8, t), f32)]
        + ([] if away else [pltpu.VMEM((t, PAIR), bf16)] * 2),
        ([pltpu.VMEM((8, PAIR), bf16)] * 2 if away else [])
        + [pltpu.VMEM((depth, 2, tall, width), bf16), pltpu.SemaphoreType.DMA((4,))],
        prefetch=3, cost=guess(5e9, 8e6), limit=SMALL, free=pl.ANY,
        aliases={6 + len(ext) + n: n for n in range(len(shared))},
    )(place, bucket, lengths, x, own, other, *ext, *shared)


def attend_back_one_kernel(
    away, depth, place, x_t_far, kept, grad_context, lse, delta, gow_far, inner, outer, gub, queries_ext, keys_ext,
    send, keep, grads_out,
    grads, found, sums, x_t, gow, sems,
):
    height, width = send.shape
    tall = (height - 16) // depth
    step, steps = pl.program_id(0), pl.num_programs(0)
    fsdp = w_out_fsdp(place, depth)
    core, j = core_of(place, depth, fsdp), neighbour_of(place, away, depth, fsdp)
    copies = [
        pltpu.make_async_copy(source, target, sems.at[n])
        for n, (source, target) in enumerate(((x_t_far, x_t), (gow_far.at[j], gow)))
    ]

    @pl.when(step == 0)
    def _():
        for copy in copies:
            copy.start()
        sums[...] = jnp.zeros_like(sums)

    lane = lax.broadcasted_iota(jnp.int32, (PLEN, PAIR), 1)
    low_half = lane < HD
    scale = HD ** (-0.5)

    rows = pl.ds(pl.multiple_of(step * PLEN, PLEN), PLEN)
    queries, keys, values, both, values_two = (kept[:, n * PAIR:(n + 1) * PAIR] for n in range(5))
    keys_two = pltpu.roll(both.astype(f32), HD, 1).astype(bf16)
    q_ext, k_ext = queries_ext[rows, :], keys_ext[rows, :]
    nothing = jnp.zeros_like(values)
    grad_two = jnp.concatenate([grad_context[0, :, PAIR:]] * 2, axis=1)

    def one(a, mine, q, k, v, grad_ctx):
        scores = dot_nt(jnp.where(mine, k, k_ext), jnp.where(mine, q, q_ext))
        probs = jnp.exp(scores - lse[a:a + 1, :])
        grad_probs = dot_nt(jnp.where(mine, v, nothing), grad_ctx)
        grad_scores = (probs * (grad_probs - delta[0, a:a + 1, :])).astype(bf16)
        grad_v = dot(probs.astype(bf16), grad_ctx)
        grad_k = dot(grad_scores, q)
        grad_q = dot_tn(grad_scores, k) * scale
        return grad_q, grad_k, grad_v

    grad_pair = grad_context[0, :, :PAIR]
    q_a, k_a, v_a = one(0, low_half, queries, keys, values, grad_pair)
    q_b, k_b, v_b = one(1, ~low_half, queries, keys, values, grad_pair)
    q_c, k_c, v_c = one(2, low_half, both, keys_two, values_two, grad_two)
    made = [
        jnp.where(low_half, q_a, q_b), jnp.where(low_half, k_a, k_b), jnp.where(low_half, v_a, v_b),
        jnp.where(low_half, q_c, pltpu.roll(k_c, HD, 1)), jnp.where(low_half, v_c, 0.0),
    ]
    for n in range(5):
        low = made[n].astype(bf16)
        lanes = slice(n * PAIR, (n + 1) * PAIR)
        grads[rows, lanes] = low
        grads_out[:, lanes] = low
        sums[0:1, lanes] += jnp.sum(low.astype(f32), axis=0, keepdims=True)

    @pl.when(step == steps - 1)
    def _():
        for copy in copies:
            copy.wait()
        columns = grads[...]
        product = dot(x_t[...], columns)
        found[:, :4 * PAIR] = product[:, :4 * PAIR].astype(bf16)
        found[:, 4 * PAIR:] = jnp.concatenate(
            [product[:, 4 * PAIR:4 * PAIR + HD], gow[...].astype(f32)], axis=1
        ).astype(bf16)
        narrow = width // 4
        none = jnp.zeros((1, 3 * narrow), f32)
        inner_rows, outer_rows = inner[0], outer[0]
        first = jnp.concatenate([sums[0:1, :4 * PAIR + HD], inner_rows[2:3]], axis=1)
        second = jnp.concatenate([inner_rows[0:1], inner_rows[1:2], outer_rows[0:1], outer_rows[1:2]], axis=1)
        third = jnp.concatenate([outer_rows[2:3], none], axis=1)
        row = lax.broadcasted_iota(jnp.int32, (16, width), 0)
        rest = jnp.where(row == 1, second, jnp.where(row == 2, third, jnp.where(row == 3, gub[0], 0.0)))
        below = jnp.where(row == 0, first, rest).astype(bf16)
        for n, target in ((1, send), (0, keep)):
            for z in range(depth):
                i = 2 * z + lax.rem(core + n, 2)
                target[z * tall:(z + 1) * tall, :] = found[pl.ds(pl.multiple_of(i * tall, 16), tall), :]
            target[depth * tall:, :] = below


def attend_back_one(
    away, fsdp, depth, place, x_t, kept, grad_context, lse, delta, gow, inner, outer, gub, q_ext, k_ext
):
    d, t = x_t.shape
    tall, narrow, width = d // (2 * depth), d // fsdp, 4 * d // fsdp
    j = lambda place: neighbour_of(place, away, depth, fsdp)
    any_space = pl.BlockSpec(memory_space=pl.ANY)
    small = lambda *shape: pl.BlockSpec((1, *shape), lambda s, place, *_: (j(place), 0, 0))
    sent = (depth * tall + 16, width)
    rows = pl.BlockSpec((PLEN, USED), lambda s, *_: (s, 0))
    return call(
        functools.partial(attend_back_one_kernel, away, depth), "attend_back", (t // PLEN,),
        [any_space, rows, pl.BlockSpec((1, PLEN, narrow), lambda s, place, *_: (j(place), s, 0)),
         pl.BlockSpec((8, PLEN), lambda s, *_: (0, s)),
         pl.BlockSpec((1, 8, PLEN), lambda s, place, *_: (j(place), 0, s)), any_space,
         small(8, narrow), small(8, narrow), small(1, width), held(), held()],
        [whole(sent), whole(sent), rows],
        [sds(sent, bf16)] * 2 + [sds((t, USED), bf16)],
        [pltpu.VMEM((t, USED), bf16), pltpu.VMEM((d, width), bf16), pltpu.VMEM((8, USED), f32), pltpu.VMEM((d, t), bf16),
         pltpu.VMEM((d, narrow), bf16), pltpu.SemaphoreType.DMA((2,))],
        prefetch=1, cost=guess(10e9, 12e6), limit=SMALL, most=1 << 40,
    )(place, x_t, kept, grad_context, lse, delta, gow, inner, outer, gub, q_ext, k_ext)


def input_grad_kernel(place, inner, *refs):
    grads, weights, out = refs[:-2], refs[-2], refs[-1]
    fsdp, depth, _, tall, _ = weights.shape
    total = inner[...]
    for away, columns in enumerate(grads):
        held_weights = weights[neighbour_of(place, away, depth, fsdp)][:, :, :, :USED]
        total += dot_nt(columns[...], held_weights.reshape(2 * depth * tall, USED))
    out[...] = total


def make_input_grad(place, inner, grads, weights):
    t, d = inner.shape
    rows = pl.BlockSpec((ROWS, d), lambda r, *_: (r, 0))
    return [call(
        input_grad_kernel, "input_grad", (t // ROWS,),
        [rows] + [pl.BlockSpec((ROWS, USED), lambda r, *_: (r, 0))] * len(grads) + [whole(weights.shape)],
        rows, sds((t, d), f32), prefetch=1, cost=guess(5e9, 15e6), limit=SMALL,
    )(place, inner, *grads, weights)]


def attend_back_kernel(
    bucket, lengths, x_t, q, k, v, grad_context, lse, delta, qw, kw, vw, grad_inner,
    gqw, gkw, gvw, gqb, gvb, input_grad,
    queries_ext, keys_ext, grads,
):
    pair = pl.program_id(0)
    row_count = q.shape[0]

    @pl.when(pair == 0)
    def _():
        segment_lanes(bucket, lengths, queries_ext, keys_ext)

    low_half = lax.broadcasted_iota(jnp.int32, (PLEN, PAIR), 1) < HD

    def block(b, carry):
        rows = pl.ds(pl.multiple_of(b * PLEN, PLEN), PLEN)
        queries, keys, values, grad_ctx = q[rows, :], k[rows, :], v[rows, :], grad_context[rows, :]
        q_ext, k_ext = queries_ext[rows, :], keys_ext[rows, :]
        nothing = jnp.zeros_like(values)
        got = []
        for half in range(2):
            mine = low_half if half == 0 else ~low_half
            lse_row = lse[pl.ds(half * HD + pair, 1), rows]
            delta_row = delta[pl.ds(half * HD + pair, 1), rows]
            scores = dot_nt(jnp.where(mine, keys, k_ext), jnp.where(mine, queries, q_ext))
            probs = jnp.exp(scores - lse_row)
            grad_probs = dot_nt(jnp.where(mine, values, nothing), grad_ctx)
            grad_scores = (probs * (grad_probs - delta_row)).astype(bf16)
            grad_v = dot(probs.astype(bf16), grad_ctx)
            grad_k = dot(grad_scores, queries)
            grad_q = dot_tn(grad_scores, keys)
            got.append((grad_q, grad_k, grad_v))
        gq = (jnp.where(low_half, got[0][0], got[1][0]) * HD ** (-0.5)).astype(bf16)
        gk = jnp.where(low_half, got[0][1], got[1][1]).astype(bf16)
        gv = jnp.where(low_half, got[0][2], got[1][2]).astype(bf16)
        grads[rows, :PAIR] = gq
        grads[rows, PAIR:2 * PAIR] = gk
        grads[rows, 2 * PAIR:] = gv
        sum_q = jnp.sum(gq.astype(f32), axis=0, keepdims=True)
        sum_v = jnp.sum(gv.astype(f32), axis=0, keepdims=True)
        return (carry[0] + sum_q, carry[1] + sum_v)

    start = jnp.zeros((1, PAIR), f32)
    gqb[...], gvb[...] = lax.fori_loop(0, row_count // PLEN, block, (start, start))

    columns = grads[...]
    weight_grads = dot(x_t[...], columns)
    gqw[...] = weight_grads[:, :PAIR].astype(gqw.dtype)
    gkw[...] = weight_grads[:, PAIR:2 * PAIR].astype(gkw.dtype)
    gvw[...] = weight_grads[:, 2 * PAIR:].astype(gvw.dtype)

    @pl.when(pair == 0)
    def _():
        input_grad[...] = grad_inner[...]

    weights = jnp.concatenate([qw[0], kw[0], vw[0]], axis=1)
    input_grad[...] += dot_nt(columns, weights)


def attend_back(bucket, lengths, x_t, q, k, v, grad_context, lse, delta, weights, grad_inner):
    t, d = q.shape
    pairs = d // PAIR
    column = lambda m: pl.BlockSpec((1, d, PAIR), lambda p, *_: (m, 0, p))
    vector = pl.BlockSpec((1, PAIR), lambda p, *_: (0, p))
    tall = pl.BlockSpec((t, PAIR), lambda p, *_: (0, p))
    made = pl.BlockSpec((d, PAIR), lambda p, *_: (0, p))
    return call(
        attend_back_kernel, "attend_back", (pairs,),
        [whole((d, t)), tall, tall, tall, tall, whole((PAIR, t)), whole((PAIR, t)),
         column(0), column(1), column(2), whole((t, d))],
        [made, made, made, vector, vector, whole((t, d))],
        [sds((d, d), bf16)] * 3 + [sds((1, d), f32)] * 2 + [sds((t, d), f32)],
        [pltpu.VMEM((t, PAIR), bf16), pltpu.VMEM((t, PAIR), bf16), pltpu.VMEM((t, 3 * PAIR), bf16)],
        prefetch=2, cost=guess(30e9, 25e6),
    )(bucket, lengths, x_t, q, k, v, grad_context, lse, delta, weights, weights, weights, grad_inner)


def normed(v):
    centred = v - jnp.mean(v, axis=-1, keepdims=True)
    r = lax.rsqrt(jnp.mean(centred * centred, axis=-1, keepdims=True) + epsilon)
    return centred * r, r


def norm_back(dy, n, r, gain):
    dn = dy * gain
    return r * (dn - jnp.mean(dn, axis=-1, keepdims=True) - n * jnp.mean(dn * n, axis=-1, keepdims=True))


def gelu_parts(u):
    phi = 0.5 + 0.5 * lax.erf(u * 0.5 ** 0.5)
    bell = jnp.exp2(u * u * -0.7213475204444817)
    return u * phi, phi + u * (bell * 0.3989422804014327)


VECTORS = ((0, 2), (0, 3), (1, 0), (1, 1), (1, 2), (1, 3))


def attended_kernel(x, context, ow, slabs, n1_out, r1_out, low_out, low_t, ow_out, vectors):
    rows = pl.ds(pl.multiple_of(pl.program_id(0) * ROWS, ROWS), ROWS)
    parts, _, narrow = context.shape

    @pl.when(pl.program_id(0) == 0)
    def _():
        ow_out[...] = jnp.concatenate([ow[j][:, ow.shape[2] - narrow:] for j in range(parts)], axis=1)
        cuts, _, width = slabs.shape
        piece = width // 4
        held_slabs = [slabs[j].astype(f32) for j in range(cuts)]
        for n, (r, m) in enumerate(VECTORS):
            vectors[n:n + 1, :] = jnp.concatenate(
                [v[r:r + 1, m * piece:(m + 1) * piece] for v in held_slabs], axis=1
            )

    joined = jnp.concatenate([context[j] for j in range(parts)], axis=1)
    ob, g1, b1 = (vectors[n:n + 1, :] for n in range(3))
    attended = dot(joined, ow_out[...]) + ob
    n1, r1 = normed(x[...].astype(f32) + attended)
    n1_out[rows, :] = n1
    r1_out[rows, :] = jnp.broadcast_to(r1, (ROWS, r1_out.shape[1]))
    low = (n1 * g1 + b1).astype(bf16)
    low_out[rows, :] = low
    low_t[:, rows] = low.T


def attended(x, context, ow, last, slabs):
    t, d = x.shape
    parts, _, narrow = context.shape
    wide = ow.shape[2] // (last + 1)
    rows = pl.BlockSpec((ROWS, d), lambda r: (r, 0))
    return call(
        attended_kernel, "attended", (t // ROWS,),
        [rows, pl.BlockSpec((parts, ROWS, narrow), lambda r: (0, r, 0)),
         pl.BlockSpec((parts, d, wide), lambda r: (0, 0, last)), whole(slabs.shape)],
        [held()] * 5 + [whole((8, d))],
        [pltpu.VMEM((t, d), f32), pltpu.VMEM((t, 128), f32), pltpu.VMEM((t, d), bf16), pltpu.VMEM((d, t), bf16),
         pltpu.VMEM((d, d), bf16), sds((8, d), f32)],
        cost=guess(3e9, 10e6), limit=SMALL,
    )(x, context, ow, slabs)


def up_tiles(tile, uw, slabs, act_out, slope_out):
    count, depth, _, tall, columns = uw.shape
    for j in range(act_out.shape[0]):
        hidden = dot(tile, uw[j].reshape(2 * depth * tall, columns)) + slabs[j, 2:3, :].astype(f32)
        active, slope = gelu_parts(hidden)
        act_out[j] = active.astype(bf16)
        slope_out[j] = slope.astype(bf16)


def up_kernel(place, low, slabs, u0, u1, u2, u3, act_out, slope_out, uw, sems):
    rows = pl.ds(pl.multiple_of(pl.program_id(0) * ROWS, ROWS), ROWS)
    copies = block_copies(place, (u0, u1, u2, u3), lambda core, j: uw.at[j, :, core], sems)

    @pl.when(pl.program_id(0) == 0)
    def _():
        for copy in copies:
            copy.start()
        for copy in copies:
            copy.wait()

    up_tiles(low[rows, :], uw, slabs, act_out, slope_out)


def up(place, low, slabs, blocks):
    t, d = low.shape
    half, depth, tall, wide = blocks[0].shape
    f = 2 * half
    high = pl.BlockSpec((f, ROWS, wide), lambda r, *_: (0, r, 0))
    return call(
        up_kernel, "up", (t // ROWS,),
        [held(), whole((f, 16, wide))] + [pl.BlockSpec(memory_space=pl.ANY)] * 4,
        [high, high, whole((f, depth, 2, tall, wide))],
        [sds((f, t, wide), bf16), sds((f, t, wide), bf16), sds((f, depth, 2, tall, wide), bf16)],
        [pltpu.SemaphoreType.DMA((2 * f,))],
        prefetch=1, cost=guess(12e9, 30e6), limit=SMALL, free=pl.ANY,
    )(place, low, slabs, *blocks)


def down_kernel(
    place, bucket, lengths, act_rows, n1, given, cotangent, act_part, d0, d1, d2, d3,
    out, pooled, mixed_out, branch_out, vectors, send, keep, dw,
    branch_t, counts, sums, found, sems,
):
    step = pl.program_id(0)
    tiles = branch_t.shape[1] // ROWS
    f, _, height, width = send.shape
    each = d0.shape[2] // height
    tall, narrow = height * each, width // each
    depth = (place.shape[0] - 1 - 5 * f) // 2
    shared = f == depth

    def target(core, j):
        rows = pl.ds(pl.multiple_of(j * tall, 16), tall)
        if shared:
            return dw.at[:, rows, pl.ds(pl.multiple_of(core * narrow, narrow), narrow)]
        return dw.at[:, core, rows, :]

    copies = block_copies(place, (d0, d1, d2, d3), target, sems)

    @pl.when(step == 0)
    def _():
        for copy in copies:
            copy.start()
        pooled[...] = jnp.zeros_like(pooled)
        counts[...] = jnp.zeros_like(counts)
        sums[...] = jnp.zeros_like(sums)
        for copy in copies:
            copy.wait()

    @pl.when(step < tiles)
    def _():
        rows = pl.ds(pl.multiple_of(step * ROWS, ROWS), ROWS)
        if shared:
            parts = [dot_nt(act_rows[row_of(place, 0, s, depth) // 2], dw[s]) for s in range(f)]
        else:
            parts = [dot_nt(act_rows[i], dw[i // 2, i % 2]) for i in range(f)]
        branch = sum(parts[1:], parts[0])
        g1, b1, db, g2, b2 = (given[n:n + 1, :] for n in range(1, 6))
        residual = n1[rows, :] * g1 + b1 + (branch + db)
        n2, r2 = normed(residual)
        result = n2 * g2 + b2
        out[...] = result.astype(bf16)
        passage = bucket[0] == 1
        for part in range(ROWS // QLEN):
            start = step * ROWS + part * QLEN
            segment = jnp.where(passage, start // PLEN, start // QLEN)
            position = jnp.where(passage, lax.rem(start, PLEN), 0)
            alive = jnp.clip(lengths[segment] - position, 0, QLEN)
            row = lax.broadcasted_iota(jnp.int32, (QLEN, 1), 0)
            picked = jnp.where(row < alive, result[part * QLEN:(part + 1) * QLEN], 0.0)
            pooled[pl.ds(segment, 1), :] += jnp.sum(picked, axis=0, keepdims=True)
            counts[pl.ds(segment, 1), :] += jnp.full((1, 128), 1.0, f32) * alive.astype(f32)
        dy = cotangent[...].astype(f32)
        sums[1:2, :] += jnp.sum(dy * n2, axis=0, keepdims=True)
        sums[2:3, :] += jnp.sum(dy, axis=0, keepdims=True)
        mixed = norm_back(dy, n2, r2, g2)
        mixed_out[rows, :] = mixed
        low = mixed.astype(bf16)
        branch_out[rows, :] = low
        sums[0:1, :] += jnp.sum(low.astype(f32), axis=0, keepdims=True)
        branch_t[:, rows] = low.T

    @pl.when(step == tiles - 1)
    def _():
        pooled[...] = pooled[...] / jnp.maximum(counts[...], 1.0)[:, :1]
        for j in range(vectors.shape[0]):
            vectors[j] = sums[:, j * vectors.shape[2]:(j + 1) * vectors.shape[2]]

    if shared:
        @pl.when(step >= tiles)
        def _():
            core = core_of(place, depth, f)
            found[...] = dot(branch_t[...], act_part[0]).astype(bf16)
            for n, made in ((1, send), (0, keep)):
                lanes = pl.ds(pl.multiple_of(lax.rem(core + n, 2) * narrow, narrow), narrow)
                for j in range(f):
                    slot = slot_of(place, n, j, depth, f)
                    for r in range(each):
                        top = j * tall + r * height
                        made[slot, 0, :, r * narrow:(r + 1) * narrow] = found[top:top + height, lanes]
    else:
        def part(n, made):
            part_found = dot(branch_t[...], act_part[0]).astype(bf16)
            for j in range(f):
                made[slot_of(place, n, j, depth, f), 0] = part_found[j * tall:(j + 1) * tall]

        @pl.when((step >= tiles) & (step < tiles + depth))
        def _():
            part(1, send)

        @pl.when(step >= tiles + depth)
        def _():
            part(0, keep)


def down(cuts, place, bucket, lengths, active, n1, given, cotangent, blocks):
    f, t, wide = active.shape
    d = n1.shape[1]
    tiles = t // ROWS
    slots = lengths.shape[0]
    _, depth, tall, narrow = blocks[0].shape
    shared = f == depth
    parts = f
    weights = (f, d, wide) if shared else (depth, 2, d, narrow)
    each = wide // narrow
    early = lambda s: jnp.minimum(s, tiles - 1)
    if shared:
        late = lambda s, place: place[jnp.maximum(s - tiles, 0)] // 2
    else:
        late = lambda s, place: place[(jnp.maximum(s - tiles, 0) + depth) % parts]
    made = lambda first: pl.BlockSpec(
        (f, 1, tall // each, narrow * each), lambda s, *_: (0, jnp.clip(s - tiles - first, 0, depth - 1), 0, 0)
    )
    rows = pl.BlockSpec((ROWS, d), lambda s, *_: (early(s), 0))
    return call(
        down_kernel, "down", (tiles + parts,),
        [pl.BlockSpec((f, ROWS, wide), lambda s, *_: (0, early(s), 0)), held(), whole((8, d)), rows, pl.BlockSpec((1, t, wide), lambda s, place, *_: (late(s, place), 0, 0))]
        + [pl.BlockSpec(memory_space=pl.ANY)] * 4,
        [rows, whole((slots, d)), held(), held(), whole((cuts, 8, d // cuts)), made(0), made(0 if shared else depth),
         whole(weights)],
        [sds((t, d), bf16), sds((slots, d), f32), pltpu.VMEM((t, d), f32), pltpu.VMEM((t, d), bf16)]
        + [sds((cuts, 8, d // cuts), f32)] + [sds((f, depth, tall // each, narrow * each), bf16)] * 2
        + [sds(weights, bf16)],
        [pltpu.VMEM((d, t), bf16), pltpu.VMEM((slots, 128), f32), pltpu.VMEM((8, d), f32),
         pltpu.VMEM((d, wide), bf16), pltpu.SemaphoreType.DMA((2 * f,))],
        prefetch=3, cost=guess(12e9, 35e6), limit=SMALL, free=pl.ANY,
    )(place, bucket, lengths, active, n1, given, cotangent, active, *blocks)


def feed_back_kernel(
    place, branch, slope, dw, uw, low_t, mixed, *refs,
):
    send, keep, gub, grad_normed, hidden, found = refs[-6:]
    j = pl.program_id(0)
    _, depth, tall, _ = send.shape
    _, t, wide = slope.shape
    tiles = t // FEED_ROWS

    def gelu_rows(r, sums):
        rows = pl.ds(pl.multiple_of(r * FEED_ROWS, FEED_ROWS), FEED_ROWS)
        grad = (slope[0, rows, :].astype(f32) * dot(branch[rows, :], dw[0])).astype(bf16)
        hidden[rows, :] = grad
        return sums + jnp.sum(grad.astype(f32), axis=0, keepdims=True)

    gub[0] = lax.fori_loop(0, tiles, gelu_rows, jnp.zeros((1, wide), f32))
    found[...] = dot(low_t[...], hidden[...]).astype(bf16)
    for n, target in ((1, send), (0, keep)):
        for slot in range(depth):
            i = row_of(place, n, slot, depth)
            target[0, slot] = found[pl.ds(pl.multiple_of(i * tall, 16), tall), :]

    @pl.when(j == 0)
    def _():
        grad_normed[...] = mixed[...]

    def normed_rows(r, carry):
        rows = pl.ds(pl.multiple_of(r * FEED_ROWS, FEED_ROWS), FEED_ROWS)
        grad_normed[rows, :] += dot_nt(hidden[rows, :], uw[0])
        return carry

    lax.fori_loop(0, tiles, normed_rows, 0)


def feed_back(first, count, place, branch, slope, dw, uw, low_t, mixed, shared):
    t = slope.shape[1]
    f, d, wide = uw.shape
    dp, _, depth, _ = axis_facts()
    tall = d // dp
    made = lambda n: pl.BlockSpec(
        (1, depth, tall, wide), lambda j, place: (slot_of(place, n, first + j, depth, f), 0, 0, 0)
    )
    part = lambda *shape: pl.BlockSpec((1, *shape), lambda j, *_: (first + j, 0, 0))
    slot = lambda j, place: row_of(place, 0, first + j, depth) // 2 if f == depth else first + j
    any_space = pl.BlockSpec(memory_space=pl.ANY)
    return call(
        feed_back_kernel, "feed_back", (count,),
        [held(), part(t, wide), pl.BlockSpec((1, d, wide), lambda j, place: (slot(j, place), 0, 0)), part(d, wide),
         held(), held()] + [any_space] * len(shared),
        [made(1), made(0), part(1, wide), held()],
        [sds((f, depth, tall, wide), bf16)] * 2 + [pltpu.HBM((f, 1, wide), f32), pltpu.VMEM((t, d), f32)],
        [pltpu.VMEM((t, wide), bf16), pltpu.VMEM((d, wide), bf16)],
        prefetch=1, cost=guess(15e9, 35e6), limit=SMALL, least=0, aliases={7 + n: n for n in range(len(shared))},
    )(place, branch, slope, dw, uw, low_t, mixed, *shared)


def inner_kernel(
    head_of, grad_normed, n1, r1, given, context, ow,
    inner_out, vectors, gow, grad_context, delta_out,
    weight_grad, sums,
):
    step = pl.program_id(0)
    d = n1.shape[1]
    parts, _, narrow = context.shape

    @pl.when(step == 0)
    def _():
        weight_grad[...] = jnp.zeros_like(weight_grad)
        sums[...] = jnp.zeros_like(sums)

    shape = (delta_out.shape[0], d)
    head = head_of(lax.broadcasted_iota(jnp.int32, shape, 0))
    pick = jnp.where(lax.broadcasted_iota(jnp.int32, shape, 1) // HD == head, 1.0, 0.0).astype(bf16)
    rows = pl.ds(pl.multiple_of(step * ROWS, ROWS), ROWS)
    dy, n = grad_normed[rows, :], n1[rows, :]
    inner = norm_back(dy, n, r1[rows, :1], given[1:2, :])
    inner_out[...] = inner
    low = inner.astype(bf16)
    grad_ctx = dot_nt(low, ow[...]).astype(bf16)
    for j in range(parts):
        grad_context[j] = grad_ctx[:, j * narrow:(j + 1) * narrow]
    joined = jnp.concatenate([context[j] for j in range(parts)], axis=1)
    both = grad_ctx.astype(f32) * joined.astype(f32)
    high = both.astype(bf16)
    rest = (both - high.astype(f32)).astype(bf16)
    delta_out[...] = dot_nt(pick, high) + dot_nt(pick, rest)
    sums[0:1, :] += jnp.sum(dy * n, axis=0, keepdims=True)
    sums[1:2, :] += jnp.sum(dy, axis=0, keepdims=True)
    sums[2:3, :] += jnp.sum(low.astype(f32), axis=0, keepdims=True)
    weight_grad[...] += dot_tn(joined, low)

    @pl.when(step == pl.num_programs(0) - 1)
    def _():
        for j in range(parts):
            columns = slice(j * narrow, (j + 1) * narrow)
            gow[j] = weight_grad[:, columns].astype(bf16)
            vectors[j] = sums[:, columns]


def inner_back(count, head_of, grad_normed, n1, r1, given, context, ow):
    t, d = n1.shape
    parts, _, narrow = context.shape
    tile = pl.BlockSpec((parts, ROWS, narrow), lambda r: (0, r, 0))
    return call(
        functools.partial(inner_kernel, head_of), "inner_back", (t // ROWS,),
        [held(), held(), held(), whole((8, d)), tile, held()],
        [pl.BlockSpec((ROWS, d), lambda r: (r, 0)), whole((parts, 8, narrow)), whole((parts, d, narrow)), tile,
         pl.BlockSpec((count, ROWS), lambda r: (0, r))],
        [sds((t, d), f32), sds((parts, 8, narrow), f32), sds((parts, d, narrow), bf16), sds((parts, t, narrow), bf16),
         sds((count, t), f32)],
        [pltpu.VMEM((d, d), f32), pltpu.VMEM((8, d), f32)],
        cost=guess(4e9, 10e6), limit=SMALL,
    )(grad_normed, n1, r1, given, context, ow)


def shards(
    tokens, bucket, lengths, cotangent,
    query_weight, query_bias, key_weight, value_weight, value_bias, out_weight, out_bias,
    norm1_gain, norm1_bias, up_weight, up_bias, down_weight, down_bias, norm2_gain, norm2_bias,
):
    t, d = tokens.shape
    dp, fsdp = lax.axis_size("dp"), lax.axis_size("fsdp")
    lengths = lengths[0]

    place = places()
    depth = dp // 2
    tall, narrow = d // dp, d // fsdp
    width = 4 * narrow
    by_head = narrow == HEADS * HD and fsdp == 4
    down_t = down_weight.T

    if by_head:
        block, slab = make_block(
            query_weight, key_weight, value_weight, out_weight, query_bias, value_bias, out_bias, norm1_gain,
            norm1_bias, down_bias, norm2_gain, norm2_bias, up_bias,
        )
        along = Once([(block, "dp", along_z(s)) for s in range(1, depth)])
        x_t, = beside([along], lambda x: (x.T,), (tokens,))
        own = [block] + along.got
        own = line_up_rows(place, own, slab)
        swap = lambda v: (v, "dp", across_cores())
        in_plane = lambda v, s: (v, "fsdp", [(f, f ^ s) for f in range(fsdp)])
        paired = Once([swap(own)])
        beside([paired])
        pair_0 = paired.got[0]
        ups = Once([(up_weight, "dp", along_z(s)) for s in range(1, depth)])
        sides = Once([in_plane(own, 1), in_plane(own, 2)])
        one = lambda away: functools.partial(attend_one, away, fsdp)
        run = (bucket, lengths, tokens)
        *shared, kept_0, lse_0, q_ext, k_ext = beside(
            [sides, ups], one(0), (place, *run, own, pair_0, [], []), out=3
        )
        ext = [q_ext, k_ext]
        own_x, own_y = sides.got
        to_u = Gather(line_up(place, [up_weight] + ups.got))
        paired = Once([swap(own_x), swap(own_y)])
        corner = Once([(select_core(own_y, own_x), ("dp", "fsdp"), along_bit(0))])
        beside([paired])
        pair_x, pair_y = paired.got
        downs = Once([(down_t, "dp", along_z(s)) for s in range(1, depth)])
        *shared, kept_1, lse_1 = beside([corner, to_u, downs], one(1), (place, *run, own_x, pair_x, ext, shared), out=3)
        own_c = corner.got[0]
        to_d = Gather(jnp.stack([down_t] + downs.got))

        def last_two(place, own_c):
            pair_c = lax.ppermute(own_c, "dp", across_cores())
            *part, kept_2, lse_2 = one(2)(place, *run, own_y, pair_y, ext, shared)
            *part, kept_3, lse_3 = one(3)(place, *run, own_c, pair_c, ext, part)
            normal = attended(tokens, part[0], part[1].reshape(fsdp, d, width), 2, part[2])
            return [*part, kept_2, lse_2, kept_3, lse_3, *normal]

        results = beside([to_u, to_d], last_two, (place, own_c), out=12)
        shared, (kept_2, lse_2, kept_3, lse_3), normal = results[:3], results[3:7], results[7:]
        context, weights, slabs = shared
        count, head_of = 8 * fsdp, lambda r: jnp.where(r % 8 < HEADS, r // 8 * HEADS + r % 8, -1)
    else:
        block = jnp.concatenate([
            jnp.concatenate([query_weight, key_weight, value_weight, out_weight], axis=1),
            jnp.concatenate([query_bias, value_bias, out_bias, norm1_gain])[None],
            jnp.concatenate([norm1_bias, down_bias, norm2_gain, norm2_bias])[None],
            up_bias[None],
            jnp.zeros((13, width), bf16),
        ])
        to_a, to_u, to_d = Gather(gather_z(block)), Gather(gather_z(up_weight)), Gather(gather_z(down_t))
        finish(to_a)
        weights, vectors, slabs = assemble(place, to_a.blocks)
        qb, vb = (vectors[m, 0:1] for m in range(2))
        q, k, v, context, lse = attend(bucket, lengths, tokens, weights, qb, vb)
        context, ow, last = context[None], weights[3:], 0
        count, head_of = PAIR, lambda r: 2 * (r % HD) + r // HD

    if by_head:
        n1, r1, low, low_t, ow, given = normal

        def up_now(place, low, slabs, sent):
            got = lax.ppermute(sent, "dp", across_cores())
            return up(place, low, slabs, [*to_u.own, to_u.other, got])

        active, slope, uw = beside([to_d], up_now, (place, low, slabs, to_u.own[1]))
    else:
        n1, r1, low, low_t, ow, given = beside(
            [to_u, to_d], attended, (tokens, context, ow, last, slabs), key=4, out=5
        )
        finish(to_u)
        active, slope, uw = beside([to_d], up, (place, low, slabs, to_u.blocks))
    finish(to_d)
    cuts = context.shape[0]
    out, pooled, mixed, branch, down_vectors, send_d, keep_d, dw = down(
        cuts, place, bucket, lengths, active, n1, given, cotangent, to_d.blocks
    )
    of_d = Scatter(keep_d, send_d)
    dw, uw = dw.reshape(fsdp, d, -1), uw.reshape(fsdp, d, -1)
    part = fsdp // 2
    *shared, so_far = beside(
        [of_d], functools.partial(feed_back, 0, part), (place, branch, slope, dw, uw, low_t, mixed, [])
    )
    send_u, keep_u, gub, grad_normed = beside(
        [of_d], functools.partial(feed_back, part, fsdp - part),
        (place, branch, slope, dw, uw, low_t, so_far, shared),
    )
    of_u = Scatter(keep_u, send_u)
    of_u.joined = by_head
    inner, inner_vectors, gow, grad_context, delta = beside(
        [of_d, of_u], functools.partial(inner_back, count, head_of), (grad_normed, n1, r1, given, context, ow),
        key=3, out=2
    )

    if by_head:
        delta = delta.reshape(fsdp, 8, t)

        def back(away, moves, kept, lse):
            args = (place, x_t, kept, grad_context, lse, delta, gow, inner_vectors, down_vectors, gub, q_ext, k_ext)
            return beside(moves, functools.partial(attend_back_one, away, fsdp, depth), args)

        send_3, keep_3, grads_3 = back(3, [of_u, of_d], kept_3, lse_3)
        swap_3 = Once([swap(send_3)])
        send_1, keep_1, grads_1 = back(1, [swap_3, of_u], kept_1, lse_1)
        corner = Once([(add(keep_3, swap_3.got[0]), ("dp", "fsdp"), along_bit(0))])
        both = [(u, "dp", along_z(-s - 1)) for s, u in enumerate(of_u.send)]
        near, rest = Once(both[::2]), Once(both[1::2])
        swap_1 = Once([swap(send_1)])
        send_2, keep_2, grads_2 = back(2, [corner, near, swap_1], kept_2, lse_2)
        swap_2 = Once([swap(send_2)])
        beside([swap_2])
        add_both = lambda *v: sum(u.astype(f32) for u in v)
        through = corner.got[0]
        sum_1 = add_both(keep_1, swap_1.got[0]) + select_core(jnp.zeros_like(through), through).astype(f32)
        sum_2 = add_both(keep_2, swap_2.got[0]) + select_core(through, jnp.zeros_like(through)).astype(f32)
        sides = Once([in_plane(sum_1.astype(bf16), 1), in_plane(sum_2.astype(bf16), 2)])
        send_0, keep_0, grads_0 = back(0, [sides, rest], kept_0, lse_0)
        sums = Once([swap(send_0)])
        beside([sums, of_u])
        mine, *away = make_total(place, [keep_0, sums.got[0], *sides.got])
        along = Once([(v, "dp", along_z(-s - 1)) for s, v in enumerate(away)])
        input_grad, = beside(
            [along, of_u], make_input_grad, (place, inner, (grads_0, grads_1, grads_2, grads_3), weights)
        )
        *made, gqb, gvb, gob, gg1, gb1, gdb, gg2, gb2, gub = unblock(mine, along.got)
        vectors = (gqb, gvb, gob, gg1, gb1, gdb, gg2, gb2)
        got, input_grad = lax.optimization_barrier((near.got + rest.got, input_grad))
        sum_u, sum_d = add_both(of_u.keep, *got), of_d.total
    else:
        gg1, gb1, gob = (inner_vectors[0, n:n + 1] for n in range(3))
        gdb, gg2, gb2 = (down_vectors[0, n:n + 1] for n in range(3))
        gqw, gkw, gvw, gqb, gvb, input_grad = attend_back(
            bucket, lengths, tokens.T, q, k, v, grad_context[0], lse, delta, weights, inner
        )
        firsts = jnp.stack([gqb, gvb, gob, gg1])
        seconds = jnp.stack([gb1, gdb, gg2, gb2])
        vectors = jnp.concatenate([firsts, seconds, jnp.zeros((4, 14, d), f32)], axis=1)
        of_a = Scatter(*reversed(pack(place, (gqw, gkw, gvw, gow[0]), vectors, gub)))
        while not (of_a.done() and of_u.done() and of_d.done()):
            beside([of_a, of_u, of_d])
        made_a = of_a.total
        made = [made_a[:tall, m * narrow:(m + 1) * narrow] for m in range(4)]
        vectors = [made_a[tall + n, m * narrow:(m + 1) * narrow] for n in range(2) for m in range(4)]
        gub = made_a[tall + 2]
    if not by_head:
        sum_u, sum_d = of_u.total, of_d.total
    columns = down_weight.shape[0]
    made_u = sum_u
    made_d = jnp.concatenate([sum_d[:, c:c + columns] for c in range(0, width, columns)])
    return (
        out, pooled, input_grad, made[0], vectors[0], made[1], made[2], vectors[1], made[3], vectors[2], vectors[3],
        vectors[4], made_u, gub, made_d.T, vectors[5], vectors[6], vectors[7],
    )


def solution(mesh):
    tall, square, vector = P(("dp", "fsdp"), None), P("dp", "fsdp"), P("fsdp")
    in_specs = (
        tall, P(("dp", "fsdp")), tall, tall, square, vector, square, square, vector, square, vector,
        vector, vector, square, vector, square, vector, vector, vector,
    )
    out_specs = (
        tall, tall, tall, square, vector, square, square, vector, square, vector, vector, vector,
        square, vector, square, vector, vector, vector,
    )
    return jax.shard_map(shards, mesh=mesh, in_specs=in_specs, out_specs=out_specs, check_vma=False)
```
